32 devices in a mesh: dp: 8 (over y, x, core), mp: 4 (over z).
Axes of the slice: x: 2, y: 2, z: 4, core: 2. Of those that a mesh axis runs over, the one named last changes fastest.
Arguments:
- patches: bfloat16 [16384, 768], P('dp'), may hold values from -6 to 6
- segment: int32 [16384], P('dp'), may hold values from 0 to 16, as said below
- keep: int32 [16384], P('dp'), may hold values 0 or 1
- pos_y: int32 [16384], P('dp'), may hold values from 0 to 31
- pos_x: int32 [16384], P('dp'), may hold values from 0 to 31
- labels: int32 [128], P('dp'), may hold values from 0 to 999
- bucket: int32 [8], P('dp'), may hold values from 0 to 3
- attend_in: float32 [768, 2304], P('dp', 'mp'), may hold values from -0.21875 to 0.21875
- attend_in_first: float32 [768, 2304], P('dp', 'mp'), may hold values from -2.2888184e-05 to 2.2888184e-05
- attend_in_second: float32 [768, 2304], P('dp', 'mp'), may hold values from 5.890625e-12 to 8.246875e-11
- attend_out: float32 [768, 768], P('mp', 'dp'), may hold values from -0.625 to 0.625
- attend_out_first: float32 [768, 768], P('mp', 'dp'), may hold values from -2.2888184e-05 to 2.2888184e-05
- attend_out_second: float32 [768, 768], P('mp', 'dp'), may hold values from 5.890625e-12 to 8.246875e-11
- expand: float32 [768, 3072], P('dp', 'mp'), may hold values from -0.21875 to 0.21875
- expand_first: float32 [768, 3072], P('dp', 'mp'), may hold values from -2.2888184e-05 to 2.2888184e-05
- expand_second: float32 [768, 3072], P('dp', 'mp'), may hold values from 5.890625e-12 to 8.246875e-11
- contract: float32 [3072, 768], P('mp', 'dp'), may hold values from -0.109375 to 0.109375
- contract_first: float32 [3072, 768], P('mp', 'dp'), may hold values from -2.2888184e-05 to 2.2888184e-05
- contract_second: float32 [3072, 768], P('mp', 'dp'), may hold values from 5.890625e-12 to 8.246875e-11
- patch_embed: float32 [768, 768], P('dp'), may hold values from -0.21875 to 0.21875
- patch_embed_first: float32 [768, 768], P('dp'), may hold values from -2.2888184e-05 to 2.2888184e-05
- patch_embed_second: float32 [768, 768], P('dp'), may hold values from 5.890625e-12 to 8.246875e-11
- position_table: float32 [64, 768], P(None, 'dp'), may hold values from -1.5 to 1.5
- position_table_first: float32 [64, 768], P(None, 'dp'), may hold values from -2.2888184e-05 to 2.2888184e-05
- position_table_second: float32 [64, 768], P(None, 'dp'), may hold values from 5.890625e-12 to 8.246875e-11
- class_head: float32 [768, 1000], P('dp'), may hold values from -0.21875 to 0.21875
- class_head_first: float32 [768, 1000], P('dp'), may hold values from -2.2888184e-05 to 2.2888184e-05
- class_head_second: float32 [768, 1000], P('dp'), may hold values from 5.890625e-12 to 8.246875e-11
- norm_gains: float32 [4, 768], P(None, 'dp'), may hold values from 0.5 to 1.5
- norm_gains_first: float32 [4, 768], P(None, 'dp'), may hold values from -9.1552734e-05 to 9.1552734e-05
- norm_gains_second: float32 [4, 768], P(None, 'dp'), may hold values from 9.425e-11 to 1.2959375e-09
- query_gains: float32 [2, 64], P(None, 'dp'), may hold values from 0.5 to 1.5
- query_gains_first: float32 [2, 64], P(None, 'dp'), may hold values from -9.1552734e-05 to 9.1552734e-05
- query_gains_second: float32 [2, 64], P(None, 'dp'), may hold values from 9.425e-11 to 1.2959375e-09
Outputs:
- bucket_loss: float32 [4], replicated
- bucket_count: float32 [4], replicated
- grad_norm: float32 [], replicated
- attend_in_new: float32 [768, 2304], P('dp', 'mp')
- attend_in_first_new: float32 [768, 2304], P('dp', 'mp')
- attend_in_second_new: float32 [768, 2304], P('dp', 'mp')
- attend_out_new: float32 [768, 768], P('mp', 'dp')
- attend_out_first_new: float32 [768, 768], P('mp', 'dp')
- attend_out_second_new: float32 [768, 768], P('mp', 'dp')
- expand_new: float32 [768, 3072], P('dp', 'mp')
- expand_first_new: float32 [768, 3072], P('dp', 'mp')
- expand_second_new: float32 [768, 3072], P('dp', 'mp')
- contract_new: float32 [3072, 768], P('mp', 'dp')
- contract_first_new: float32 [3072, 768], P('mp', 'dp')
- contract_second_new: float32 [3072, 768], P('mp', 'dp')
- patch_embed_new: float32 [768, 768], P('dp')
- patch_embed_first_new: float32 [768, 768], P('dp')
- patch_embed_second_new: float32 [768, 768], P('dp')
- position_table_new: float32 [64, 768], P(None, 'dp')
- position_table_first_new: float32 [64, 768], P(None, 'dp')
- position_table_second_new: float32 [64, 768], P(None, 'dp')
- class_head_new: float32 [768, 1000], P('dp')
- class_head_first_new: float32 [768, 1000], P('dp')
- class_head_second_new: float32 [768, 1000], P('dp')
- norm_gains_new: float32 [4, 768], P(None, 'dp')
- norm_gains_first_new: float32 [4, 768], P(None, 'dp')
- norm_gains_second_new: float32 [4, 768], P(None, 'dp')
- query_gains_new: float32 [2, 64], P(None, 'dp')
- query_gains_first_new: float32 [2, 64], P(None, 'dp')
- query_gains_second_new: float32 [2, 64], P(None, 'dp')
The draws below stay inside these ranges and needn't reach their ends.
Inputs may be any that keep to these rules, and one draw needn't show every extreme that they name: `segment`: within each sequence the image numbers never fall along the slots, images 0 to n - 1 hold one or more slots each, images n to 15 hold none, and the slots after them are padding with number 16.
All inputs are finite; a program needn't handle non-finite values. No bound on the sum of `keep` on one device may be relied on, other than what follows from the above.
Results may differ from the reference program's by a relative error of at most 0.017.
Values may be sent and summed in bfloat16 or wider, within the bound.
No kernel may reach another device: no remote copies, remote signals or barrier semaphores. Data moves between devices by JAX's collectives and lax.ppermute only.
A program may use at most 192 MiB of HBM per device.

```python
import math
import jax
import jax.numpy as jnp
from jax import lax

D = 768
HD = 64
MLP = 3072
CLASSES = 1000
PIX = 768
GRID = 32
PACK = 2048
IMG = 16
NB = 4
STEP = 10
HEADS = 12
TOKENS = 16384
IMAGES = 128
NPARAM = 8488064
N_DP = 8


def draw_segment(key, part):
    key_count, key_pad, key_weight = jax.random.split(key, 3)
    devices = jnp.arange(N_DP)
    base = IMG // 3 + (IMG - IMG // 3) * devices // max(N_DP - 1, 1)
    images = jnp.clip(base - jax.random.randint(key_count, (N_DP,), 0, 2), 1, IMG)
    used = PACK - jax.random.randint(key_pad, (N_DP,), 1, PACK // 8 + 1)
    weights = jax.random.randint(key_weight, (N_DP, IMG), 1, 9) * (jnp.arange(IMG)[None, :] < images[:, None]).astype(jnp.int32)
    running = jnp.cumsum(weights, axis=1)
    starts = running[:, :-1] * used[:, None] // running[:, -1:]
    slots = jnp.arange(PACK)
    ids = jnp.sum((slots[None, :, None] >= starts[:, None, :]).astype(jnp.int32), axis=2)
    ids = ids + (slots[None, :] >= used[:, None]).astype(jnp.int32)
    return ids.reshape(N_DP * PACK).astype(jnp.int32)


def touch_ends(values, rng, smallest, top_value):
    dims = values.shape
    index_at = [jax.random.randint(jax.random.fold_in(rng, axis), (), 0, dims[axis]) for axis in range(len(dims))]
    values = values.at[tuple(index_at)].set(smallest)
    longest = dims.index(max(dims))
    index_at[longest] = (index_at[longest] + 1) % dims[longest]
    return values.at[tuple(index_at)].set(top_value)


def steps_of(own_key, shape, cuts, smallest, top_value):
    factor_of, own = 1.0, jax.random.fold_in(own_key, 6)
    for position, blocks in cuts:
        steps = jnp.exp(jax.random.uniform(jax.random.fold_in(own, position), (blocks,), jnp.float32, smallest / len(cuts), top_value / len(cuts)))
        factor_of = factor_of * jnp.repeat(steps, shape[position] // blocks).reshape([-1 if axis == position else 1 for axis in range(len(shape))])
    return factor_of


def noise(own_key, shape, width, bound, cuts=(), held_as=jnp.bfloat16):
    drawn = width * jax.random.normal(own_key, shape, jnp.float32)
    if cuts:
        drawn = drawn * steps_of(own_key, shape, cuts, -0.22, 0.18)
    return jnp.clip(drawn, -bound, bound).astype(held_as)


def setup_inputs(seed: int = 0) -> dict:
    splits = jax.random.split(jax.random.key(seed), 35)
    patches = noise(splits[0], (TOKENS, PIX), 1.0, 6.0, ((0, 8),))
    segment = draw_segment(jax.random.fold_in(splits[34], 71), 0)
    keep = touch_ends((jax.random.randint(splits[2], (TOKENS,), 0, 4) < 3).astype(jnp.int32), jax.random.fold_in(splits[2], 1), 0, 1)
    pos_y = touch_ends(jax.random.randint(splits[3], (TOKENS,), 0, GRID), jax.random.fold_in(splits[3], 1), 0, GRID - 1).astype(jnp.int32)
    pos_x = touch_ends(jax.random.randint(splits[4], (TOKENS,), 0, GRID), jax.random.fold_in(splits[4], 1), 0, GRID - 1).astype(jnp.int32)
    labels = touch_ends(jax.random.randint(splits[5], (IMAGES,), 0, CLASSES), jax.random.fold_in(splits[5], 1), 0, CLASSES - 1).astype(jnp.int32)
    bucket = touch_ends(jax.random.randint(splits[6], (N_DP,), 0, NB), jax.random.fold_in(splits[6], 1), 0, NB - 1).astype(jnp.int32)
    attend_in = noise(splits[7], (D, 3 * D), D ** -0.5, 0.21875, ((0, 8), (1, 4)), jnp.float32)
    attend_in_first = noise(splits[8], (D, 3 * D), (0.011 * NPARAM ** -0.5), 2.288818359375e-05, ((0, 8), (1, 4)), jnp.float32)
    attend_in_second = jnp.clip(jnp.exp(math.log(8.24687471090435e-11) - 2.6390573 * jax.random.uniform(splits[9], (D, 3 * D), jnp.float32) ** steps_of(splits[9], (D, 3 * D), ((0, 8), (1, 4)), -0.2, 0.2)), 5.8906247935031075e-12, 8.24687471090435e-11)
    attend_out = noise(splits[10], (D, D), (D // 8) ** -0.5, 0.625, ((0, 4), (1, 8)), jnp.float32)
    attend_out_first = noise(splits[11], (D, D), (0.011 * NPARAM ** -0.5), 2.288818359375e-05, ((0, 4), (1, 8)), jnp.float32)
    attend_out_second = jnp.clip(jnp.exp(math.log(8.24687471090435e-11) - 2.6390573 * jax.random.uniform(splits[12], (D, D), jnp.float32) ** steps_of(splits[12], (D, D), ((0, 4), (1, 8)), -0.2, 0.2)), 5.8906247935031075e-12, 8.24687471090435e-11)
    expand = noise(splits[13], (D, MLP), D ** -0.5, 0.21875, ((0, 8), (1, 4)), jnp.float32)
    expand_first = noise(splits[14], (D, MLP), (0.011 * NPARAM ** -0.5), 2.288818359375e-05, ((0, 8), (1, 4)), jnp.float32)
    expand_second = jnp.clip(jnp.exp(math.log(8.24687471090435e-11) - 2.6390573 * jax.random.uniform(splits[15], (D, MLP), jnp.float32) ** steps_of(splits[15], (D, MLP), ((0, 8), (1, 4)), -0.2, 0.2)), 5.8906247935031075e-12, 8.24687471090435e-11)
    contract = noise(splits[16], (MLP, D), MLP ** -0.5, 0.109375, ((0, 4), (1, 8)), jnp.float32)
    contract_first = noise(splits[17], (MLP, D), (0.011 * NPARAM ** -0.5), 2.288818359375e-05, ((0, 4), (1, 8)), jnp.float32)
    contract_second = jnp.clip(jnp.exp(math.log(8.24687471090435e-11) - 2.6390573 * jax.random.uniform(splits[18], (MLP, D), jnp.float32) ** steps_of(splits[18], (MLP, D), ((0, 4), (1, 8)), -0.2, 0.2)), 5.8906247935031075e-12, 8.24687471090435e-11)
    patch_embed = noise(splits[19], (PIX, D), PIX ** -0.5, 0.21875, ((0, 8),), jnp.float32)
    patch_embed_first = noise(splits[20], (PIX, D), (0.011 * NPARAM ** -0.5), 2.288818359375e-05, ((0, 8),), jnp.float32)
    patch_embed_second = jnp.clip(jnp.exp(math.log(8.24687471090435e-11) - 2.6390573 * jax.random.uniform(splits[21], (PIX, D), jnp.float32) ** steps_of(splits[21], (PIX, D), ((0, 8),), -0.2, 0.2)), 5.8906247935031075e-12, 8.24687471090435e-11)
    position_table = noise(splits[22], (2 * GRID, D), 0.25, 1.5, ((1, 8),), jnp.float32)
    position_table_first = noise(splits[23], (2 * GRID, D), (0.011 * NPARAM ** -0.5), 2.288818359375e-05, ((1, 8),), jnp.float32)
    position_table_second = jnp.clip(jnp.exp(math.log(8.24687471090435e-11) - 2.6390573 * jax.random.uniform(splits[24], (2 * GRID, D), jnp.float32) ** steps_of(splits[24], (2 * GRID, D), ((1, 8),), -0.2, 0.2)), 5.8906247935031075e-12, 8.24687471090435e-11)
    class_head = noise(splits[25], (D, CLASSES), D ** -0.5, 0.21875, ((0, 8),), jnp.float32)
    class_head_first = noise(splits[26], (D, CLASSES), (0.011 * NPARAM ** -0.5), 2.288818359375e-05, ((0, 8),), jnp.float32)
    class_head_second = jnp.clip(jnp.exp(math.log(8.24687471090435e-11) - 2.6390573 * jax.random.uniform(splits[27], (D, CLASSES), jnp.float32) ** steps_of(splits[27], (D, CLASSES), ((0, 8),), -0.2, 0.2)), 5.8906247935031075e-12, 8.24687471090435e-11)
    norm_gains = jnp.clip(1.0 + 0.1 * jax.random.normal(splits[28], (4, D), jnp.float32), 0.5, 1.5)
    norm_gains_first = noise(splits[29], (4, D), (0.044 * NPARAM ** -0.5), 9.1552734375e-05, ((1, 8),), jnp.float32)
    norm_gains_second = jnp.clip(jnp.exp(math.log(1.2959374684484715e-09) - 2.621039 * jax.random.uniform(splits[30], (4, D), jnp.float32) ** steps_of(splits[30], (4, D), ((1, 8),), -0.2, 0.2)), 9.424999669604972e-11, 1.2959374684484715e-09)
    query_gains = jnp.clip(1.0 + 0.1 * jax.random.normal(splits[31], (2, HD), jnp.float32), 0.5, 1.5)
    query_gains_first = noise(splits[32], (2, HD), (0.044 * NPARAM ** -0.5), 9.1552734375e-05, ((1, 8),), jnp.float32)
    query_gains_second = jnp.clip(jnp.exp(math.log(1.2959374684484715e-09) - 2.621039 * jax.random.uniform(splits[33], (2, HD), jnp.float32) ** steps_of(splits[33], (2, HD), ((1, 8),), -0.2, 0.2)), 9.424999669604972e-11, 1.2959374684484715e-09)
    return dict(patches=patches, segment=segment, keep=keep, pos_y=pos_y, pos_x=pos_x, labels=labels, bucket=bucket, attend_in=attend_in, attend_in_first=attend_in_first, attend_in_second=attend_in_second, attend_out=attend_out, attend_out_first=attend_out_first, attend_out_second=attend_out_second, expand=expand, expand_first=expand_first, expand_second=expand_second, contract=contract, contract_first=contract_first, contract_second=contract_second, patch_embed=patch_embed, patch_embed_first=patch_embed_first, patch_embed_second=patch_embed_second, position_table=position_table, position_table_first=position_table_first, position_table_second=position_table_second, class_head=class_head, class_head_first=class_head_first, class_head_second=class_head_second, norm_gains=norm_gains, norm_gains_first=norm_gains_first, norm_gains_second=norm_gains_second, query_gains=query_gains, query_gains_first=query_gains_first, query_gains_second=query_gains_second)


HIGH = lax.Precision.HIGHEST
NORM_EPS = 1e-06
CLIP = 0.1
BETA_ONE = 0.9
BETA_TWO = 0.95
RATE_MATRIX = 0.05
RATE_SMALL = 0.2
DECAY = 0.05
ADAM_EPS = 1e-08
NEG = -1e+30

@jax.custom_vjp
def low(v):
    return lax.optimization_barrier(v.astype(jnp.bfloat16)).astype(jnp.float32)

@jax.custom_vjp
def low_back(v):
    return v

def low_keep(v):
    return (low(v), None)

def low_pass(kept, grad):
    return (grad,)

def back_keep(v):
    return (v, None)

def back_low(kept, grad):
    return (low(grad),)
low.defvjp(low_keep, low_pass)
low_back.defvjp(back_keep, back_low)

def layer_norm(values, gain):
    center = values - lax.optimization_barrier(jnp.mean(values, axis=-1, keepdims=True))
    inv_std = lax.rsqrt(lax.optimization_barrier(jnp.mean(center * center, axis=-1, keepdims=True)) + NORM_EPS)
    return center * inv_std * gain

def sequence_loss(weights, patches, segment, keep, pos_y, pos_x, labels):
    in_proj, out_proj, up_proj, down_proj, patch_proj, pos_rows, head_proj, gain_rows, qgain_rows = weights
    length = patches.shape[0]
    kept = (keep == 1) & (segment < IMG)
    onehot_y = (pos_y[:, None] == jnp.arange(GRID)[None, :]).astype(jnp.float32)
    onehot_x = (pos_x[:, None] == jnp.arange(GRID)[None, :]).astype(jnp.float32)
    embed = jnp.dot(patches, patch_proj, precision=HIGH) + jnp.dot(onehot_y, pos_rows[:GRID], precision=HIGH) + jnp.dot(onehot_x, pos_rows[GRID:], precision=HIGH)
    resid_in = low_back(embed)
    normed_a = low(layer_norm(resid_in, gain_rows[0]))
    mixed = low_back(jnp.dot(normed_a, in_proj, precision=HIGH)).reshape(length, HEADS, 3, HD)
    query = low(layer_norm(mixed[:, :, 0], qgain_rows[0]) * 0.125)
    key = low(layer_norm(mixed[:, :, 1], qgain_rows[1]))
    value = low(mixed[:, :, 2])
    scores = low_back(jnp.einsum('thd,uhd->htu', query, key, precision=HIGH))
    slots = jnp.arange(length)
    allowed = (segment[:, None] == segment[None, :]) & kept[None, :] | (slots[:, None] == slots[None, :])
    scores = jnp.where(allowed[None], scores, NEG)
    probs = low(jax.nn.softmax(scores, axis=-1))
    attended = jnp.einsum('htu,uhd->thd', probs, value, precision=HIGH).reshape(length, D)
    attended = low(low_back(attended))
    resid_mid = resid_in + low_back(jnp.dot(attended, out_proj, precision=HIGH))
    normed_b = low(layer_norm(resid_mid, gain_rows[1]))
    upper = low_back(jnp.dot(normed_b, up_proj, precision=HIGH))
    hidden = low(jax.nn.gelu(upper))
    resid_out = resid_mid + low_back(jnp.dot(hidden, down_proj, precision=HIGH))
    final = layer_norm(resid_out, gain_rows[2])
    member = (segment[None, :] == jnp.arange(IMG)[:, None]) & kept[None, :]
    valid = jnp.any(member, axis=1).astype(jnp.float32)
    final_heads = final.reshape(length, HEADS, HD)
    probe = gain_rows[3].reshape(HEADS, HD)
    tok_score = lax.optimization_barrier(jnp.sum(final_heads * probe[None], axis=-1)) * 0.125
    masked = jnp.where(member[:, :, None], tok_score[None], NEG)
    top = lax.optimization_barrier(jnp.max(masked, axis=1, keepdims=True))
    weights_pool = jnp.where(member[:, :, None], jnp.exp(masked - top), 0.0)
    total = lax.optimization_barrier(jnp.sum(weights_pool, axis=1)) + (1.0 - valid)[:, None]
    attn_pool = weights_pool / total[:, None, :]
    pooled = jnp.einsum('ith,thd->ihd', attn_pool, final_heads, precision=HIGH).reshape(IMG, D)
    logits = low_back(jnp.dot(low(pooled), head_proj, precision=HIGH))
    label_hot = (labels[:, None] == jnp.arange(CLASSES)[None, :]).astype(jnp.float32)
    per_image = lax.optimization_barrier(jnp.sum(jax.nn.softplus(logits), axis=1)) - lax.optimization_barrier(jnp.sum(logits * label_hot, axis=1))
    return jnp.sum(per_image * valid)

def reference(patches, segment, keep, pos_y, pos_x, labels, bucket, attend_in, attend_in_first, attend_in_second, attend_out, attend_out_first, attend_out_second, expand, expand_first, expand_second, contract, contract_first, contract_second, patch_embed, patch_embed_first, patch_embed_second, position_table, position_table_first, position_table_second, class_head, class_head_first, class_head_second, norm_gains, norm_gains_first, norm_gains_second, query_gains, query_gains_first, query_gains_second):
    masters = (attend_in, attend_out, expand, contract, patch_embed, position_table, class_head, norm_gains, query_gains)
    firsts = (attend_in_first, attend_out_first, expand_first, contract_first, patch_embed_first, position_table_first, class_head_first, norm_gains_first, query_gains_first)
    seconds = (attend_in_second, attend_out_second, expand_second, contract_second, patch_embed_second, position_table_second, class_head_second, norm_gains_second, query_gains_second)
    pieces = (patches.astype(jnp.float32).reshape(N_DP, PACK, PIX), segment.reshape(N_DP, PACK), keep.reshape(N_DP, PACK), pos_y.reshape(N_DP, PACK), pos_x.reshape(N_DP, PACK), labels.reshape(N_DP, IMG))
    seg_rows = segment.reshape(N_DP, 1, PACK)
    kept_rows = ((keep == 1) & (segment < IMG)).reshape(N_DP, 1, PACK)
    member_all = (seg_rows == jnp.arange(IMG)[None, :, None]) & kept_rows
    counts = lax.optimization_barrier(jnp.sum(jnp.any(member_all, axis=2).astype(jnp.float32), axis=1))
    image_total = jnp.sum(counts)

    def objective(weights):
        lowered = tuple((low(weight) for weight in weights))
        seq_fn = jax.checkpoint(lambda piece: sequence_loss(lowered, *piece))

        def advance(carry, piece):
            value = seq_fn(piece)
            return (carry + value, value)
        summed, each = lax.scan(advance, jnp.zeros((), jnp.float32), pieces)
        return (summed / image_total, each)
    value, pullback, each = jax.vjp(objective, masters, has_aux=True)
    grads = pullback(jnp.ones((), jnp.float32))[0]
    bucket_hot = (bucket[:, None] == jnp.arange(NB)[None, :]).astype(jnp.float32)
    bucket_loss = lax.optimization_barrier(jnp.sum(each[:, None] * bucket_hot, axis=0))
    bucket_count = lax.optimization_barrier(jnp.sum(counts[:, None] * bucket_hot, axis=0))
    squares = sum((jnp.sum(grad * grad) for grad in grads))
    grad_norm = jnp.sqrt(squares)
    factor = jnp.minimum(1.0, CLIP / (grad_norm + 1e-06))
    results = [bucket_loss, bucket_count, grad_norm]
    for index in range(9):
        clipped = grads[index] * factor
        first_new = BETA_ONE * firsts[index] + (1.0 - BETA_ONE) * clipped
        second_new = BETA_TWO * seconds[index] + (1.0 - BETA_TWO) * clipped * clipped
        matrix = index in (0, 1, 2, 3, 4, 6)
        rate = RATE_MATRIX if matrix else RATE_SMALL
        decay = DECAY if matrix else 0.0
        ratio = first_new / (1.0 - BETA_ONE ** STEP) / (jnp.sqrt(second_new / (1.0 - BETA_TWO ** STEP)) + ADAM_EPS)
        results += [masters[index] - rate * (ratio + decay * masters[index]), first_new, second_new]
    return tuple(results)
```

```python
import jax
import jax.numpy as jnp
from jax import lax
from jax.experimental import pallas as pl
from jax.experimental.pallas import tpu as pltpu
from jax.sharding import PartitionSpec as P

D = 768
HD = 64
HID = 3072
CLASSES = 1000
CPAD = 1024
GRID = 32
IMG = 16
NB = 4
STEP = 10
BQ = 256
TOK = 512
NH = 3

HIGH = lax.Precision.HIGHEST
NORM_EPS = 1e-06
CLIP = 0.1
BETA_ONE = 0.9
BETA_TWO = 0.95
RATE_MATRIX = 0.05
RATE_SMALL = 0.2
DECAY = 0.05
ADAM_EPS = 1e-08
BIG = 128.0

bf16 = jnp.bfloat16
f32 = jnp.float32
VLIM = 56 * 1024 * 1024

NN = (((1,), (0,)), ((), ()))
NT = (((1,), (1,)), ((), ()))
TN = (((0,), (0,)), ((), ()))


def dot(a, b, dims=NN, precision=None):
    return lax.dot_general(a, b, dims, precision=precision, preferred_element_type=f32)


def norm_stats(values):
    center = values - jnp.mean(values, axis=-1, keepdims=True)
    inv_std = lax.rsqrt(jnp.mean(center * center, axis=-1, keepdims=True) + NORM_EPS)
    return center * inv_std, inv_std


def norm_back(grad_scaled, scaled, inv_std):
    return inv_std * (
        grad_scaled
        - jnp.mean(grad_scaled, axis=-1, keepdims=True)
        - scaled * jnp.mean(grad_scaled * scaled, axis=-1, keepdims=True)
    )


def split3(x):
    hi = x.astype(bf16).astype(f32)
    rest = x - hi
    mid = rest.astype(bf16).astype(f32)
    return hi, mid, rest - mid


def rows_at(index, size):
    return pl.ds(pl.multiple_of(index * size, size), size)


def load_rows(pieces, me, dst, sems):
    size = pieces[0].shape[0]
    copies = [
        pltpu.make_async_copy(piece, dst.at[rows_at(me ^ r, size), :], sems.at[r])
        for r, piece in enumerate(pieces)
    ]
    for copy in copies:
        copy.start()
    for copy in copies:
        copy.wait()


def x0_kernel(sc, own, other, hot, pos, gains, *rest):
    pieces = rest[:8]
    a_out, x0_out, w, sems = rest[8:]
    i = pl.program_id(0)

    @pl.when(i == 0)
    def _():
        load_rows(pieces, sc[0], w, sems)

    rows = jnp.where(sc[3] == 1, own[...], other[...])
    x0 = dot(rows, w[:, :D]) + dot(hot[...], pos[...])
    scaled, _ = norm_stats(x0)
    a_out[...] = (scaled * gains[0:1, :]).astype(bf16)

    @pl.when(i == sc[1])
    def _():
        x0_out[...] = x0


def qkv_kernel(sc, a, qaux, kaux, vaux, qg, *rest):
    pieces = rest[:4]
    qx, kx, vx, raw, w, sems = rest[4:]
    i = pl.program_id(0)

    @pl.when(i == 0)
    def _():
        load_rows(pieces, sc[4], w, sems)

    mixed = dot(a[...], w[...])
    qa, ka, va = qaux[...], kaux[...], vaux[...]
    for h in range(NH):
        q = mixed[:, h * 192 : h * 192 + 64]
        k = mixed[:, h * 192 + 64 : h * 192 + 128]
        v = mixed[:, h * 192 + 128 : h * 192 + 192]
        raw[2 * h] = q
        raw[2 * h + 1] = k
        qn = (norm_stats(q)[0] * qg[0:1, :] * 0.125).astype(bf16)
        kn = (norm_stats(k)[0] * qg[1:2, :]).astype(bf16)
        qx[h] = jnp.concatenate([qn, qa], axis=1)
        kx[h] = jnp.concatenate([kn, ka], axis=1)
        vx[h] = jnp.concatenate([v.astype(bf16), va], axis=1)


def attn_kernel(sc, qx, kx, vx, o_rel, o_full, ql, acc):
    i = pl.program_id(0)
    acc[...] = jnp.zeros_like(acc)

    def step(j, carry):
        ks = rows_at(j, BQ)
        for h in range(NH):
            s = dot(qx[h], kx[h, ks, :], NT)
            p = jnp.exp(s).astype(bf16)
            acc[h] += dot(p, vx[h, ks, :])
        return carry

    lax.fori_loop(sc[8 + i], sc[16 + i], step, 0)
    mine = rows_at(i, BQ)
    lane = lax.broadcasted_iota(jnp.int32, (BQ, 128), 1)
    outs = []
    for h in range(NH):
        q = qx[h].astype(f32)
        k = kx[h, mine, :].astype(f32)
        v = vx[h, mine, :].astype(f32)
        free = k[:, 84:85]
        diag = jnp.sum(jnp.where(lane < HD, q * k, 0.0), axis=1, keepdims=True)
        p = jnp.exp(diag) * free
        out = acc[h] + p.astype(bf16).astype(f32) * v
        total = out[:, 64:65]
        outs.append(out[:, :HD] / total)
        parts = split3(-jnp.log(total))
        for n, part in enumerate(parts):
            q = jnp.where(lane == 81 + n, part, q)
        ql[h] = q.astype(bf16)
    full = jnp.concatenate(outs, axis=1)
    o_full[...] = full
    o_rel[0] = full.astype(bf16)


def mid_kernel(sc, o, x0, gains, *rest):
    pieces = rest[:8]
    x1_out, b_out, w, sems = rest[8:]
    load_rows(pieces, sc[0], w, sems)
    x1 = x0[...] + dot(o[...], w[...], NT)
    x1_out[...] = x1
    b_out[...] = (norm_stats(x1)[0] * gains[1:2, :]).astype(bf16)


def tile_copies(pieces, me, z, j, dst, sems):
    size = pieces[0].shape[1]
    return [
        pltpu.make_async_copy(
            piece.at[z ^ j], dst.at[j, rows_at(me ^ r, size), :], sems.at[j, r]
        )
        for r, piece in enumerate(pieces)
    ]


def start_tiles(pieces, me, z, dst, sems):
    for j in range(4):
        for copy in tile_copies(pieces, me, z, j, dst, sems):
            copy.start()


def wait_tile(pieces, me, z, j, dst, sems):
    for copy in tile_copies(pieces, me, z, j, dst, sems):
        copy.wait()


GELU_C = 0.7978845608028654


def gelu_tanh(u):
    return jnp.tanh(GELU_C * (u + 0.044715 * u * u * u))


def up_kernel(sc, b, *rest):
    pieces = rest[:8]
    u_out, h_out, w, sems = rest[8:]
    j = pl.program_id(0)

    @pl.when(j == 0)
    def _():
        start_tiles(pieces, sc[0], sc[2], w, sems)

    wait_tile(pieces, sc[0], sc[2], j, w, sems)
    u = dot(b[...], w[j])
    u_out[...] = u
    h_out[...] = (0.5 * u * (1.0 + gelu_tanh(u))).astype(bf16)


def head_ones():
    row = lax.broadcasted_iota(jnp.int32, (D, 128), 0) // HD
    col = lax.broadcasted_iota(jnp.int32, (D, 128), 1)
    return (row == col).astype(f32)


def down_kernel(sc, h, x1, gains, mem, *rest):
    pieces = rest[:8]
    x2_out, ns_out, w, acc, sems = rest[8:]
    j = pl.program_id(0)

    @pl.when(j == 0)
    def _():
        start_tiles(pieces, sc[0], sc[2], w, sems)
        acc[...] = x1[...]

    wait_tile(pieces, sc[0], sc[2], j, w, sems)
    acc[...] += dot(h[...], w[j], NT)

    @pl.when(j == 3)
    def _():
        x2 = acc[...]
        x2_out[...] = x2
        f = norm_stats(x2)[0] * gains[2:3, :]
        ones = head_ones()
        e = jnp.exp(dot(f * gains[3:4, :], ones, NN, HIGH) * 0.125)
        eb = dot(e, ones, NT, HIGH)
        m = mem[...]
        ns_out[:, :D] = dot(m, eb * f, TN, HIGH)
        ns_out[:, D:] = dot(m, e, TN, HIGH)


def head_kernel(sc, ns, lab, vt, *rest):
    pieces = rest[:8]
    pooled_out, gp_out, sinv_out, loss_out, gh_out, gh_send, w, gw, sems = rest[8:]
    load_rows(pieces, sc[0], w, sems)
    valid = vt[:, 0:1]
    scale = vt[:, 1:2]
    total = jnp.where(valid > 0.0, ns[:, D:], 1.0)
    sinv = jnp.where(valid > 0.0, 1.0 / total, 0.0)
    lane = lax.broadcasted_iota(jnp.int32, (IMG, 128), 1)
    sinv = jnp.where(lane < D // HD, sinv, 0.0)
    pooled = ns[:, :D] * dot(sinv, head_ones(), NT, HIGH)
    low = pooled.astype(bf16)
    logits = dot(low, w[...])
    cls = lax.broadcasted_iota(jnp.int32, (IMG, CPAD), 1)
    real = (cls < CLASSES).astype(f32)
    hot = lab[...]
    ex = jnp.exp(-jnp.abs(logits))
    soft = jnp.maximum(logits, 0.0) + jnp.log1p(ex)
    per = jnp.sum(soft * real, axis=1, keepdims=True) - jnp.sum(
        logits * hot, axis=1, keepdims=True
    )
    loss_out[...] = jnp.broadcast_to(per * valid, (IMG, 128))
    sig = jnp.where(logits >= 0.0, 1.0, ex) / (1.0 + ex)
    gl = (scale * (sig * real - hot)).astype(bf16)
    pooled_out[...] = pooled
    sinv_out[...] = sinv
    gp_out[...] = dot(gl, w[...], NT)
    half = jnp.where(sc[2] % 2 == 1, gl[:, 512:].astype(f32), gl[:, :512].astype(f32))
    gw[...] = dot(low, half.astype(bf16), TN)
    size = D // 8
    for p in range(4):
        r = (p >> 1) * 2 + (p & 1) * 4
        gh_out[p] = gw[rows_at(sc[0] ^ r, size), :].astype(bf16)
        gh_send[p] = gw[rows_at(sc[0] ^ (r + 1), size), :].astype(bf16)


def back_kernel(sc, u, x2, x1, gains, mem, pooled, gp, sinv, *rest):
    ex_p, con_p, out_p = rest[:8], rest[8:16], rest[16:24]
    (gu_out, gr_out, gm_out, gmid_out, ga_out, small_out) = rest[24:30]
    wex, wcon, wout, grs, acc, sem_e, sem_c, sem_o = rest[30:]
    j = pl.program_id(0)
    size = D // 8

    @pl.when(j == 0)
    def _():
        start_tiles(con_p, sc[0], sc[2], wcon, sem_c)
        start_tiles(ex_p, sc[0], sc[2], wex, sem_e)
        for r, piece in enumerate(out_p):
            pltpu.make_async_copy(
                piece, wout.at[rows_at(sc[0] ^ r, size), :], sem_o.at[r]
            ).start()
        scaled, inv = norm_stats(x2[...])
        f = scaled * gains[2:3, :]
        probe = gains[3:4, :]
        ones = head_ones()
        e = jnp.exp(dot(f * probe, ones, NN, HIGH) * 0.125)
        m = mem[...]
        gt = dot(m, gp[...], NN, HIGH)
        at = e * dot(m, sinv[...], NN, HIGH)
        gpp = dot(gp[...] * pooled[...], ones, NN, HIGH)
        da = dot(gt * f, ones, NN, HIGH)
        dc = at * (da - dot(m, gpp, NN, HIGH))
        dcb = dot(dc, ones, NT, HIGH) * 0.125
        df = dot(at, ones, NT, HIGH) * gt + dcb * probe
        gr = norm_back(df * gains[2:3, :], scaled, inv)
        grs[...] = gr
        gr_out[...] = gr.astype(bf16)
        small_out[0:1, :] = jnp.sum(df * scaled, axis=0, keepdims=True)
        small_out[1:2, :] = jnp.sum(dcb * f, axis=0, keepdims=True)
        small_out[3:8, :] = jnp.zeros((5, D), f32)
        acc[...] = jnp.zeros_like(acc)

    wait_tile(con_p, sc[0], sc[2], j, wcon, sem_c)
    gh = dot(grs[...].astype(bf16), wcon[j])
    v = u[...]
    t = gelu_tanh(v)
    slope = 0.5 * (1.0 + t) + 0.5 * v * (1.0 - t * t) * GELU_C * (1.0 + 0.134145 * v * v)
    gu = (gh * slope).astype(bf16)
    gu_out[...] = gu
    wait_tile(ex_p, sc[0], sc[2], j, wex, sem_e)
    acc[...] += dot(gu, wex[j], NT)

    @pl.when(j == 3)
    def _():
        for r, piece in enumerate(out_p):
            pltpu.make_async_copy(
                piece, wout.at[rows_at(sc[0] ^ r, size), :], sem_o.at[r]
            ).wait()
        scaled, inv = norm_stats(x1[...])
        gb = acc[...]
        small_out[2:3, :] = jnp.sum(gb * scaled, axis=0, keepdims=True)
        gmid = grs[...] + norm_back(gb * gains[1:2, :], scaled, inv)
        gmid_out[...] = gmid
        low = gmid.astype(bf16)
        gm_out[...] = low
        ga_out[...] = dot(low, wout[...]).astype(bf16)


def rel_order(first):
    m1, m2 = (2, 4) if first == 2 else (4, 2)
    return [(p >> 1) * m1 + (p & 1) * m2 for p in range(4)]


def wgrad_kernel(sc, gr, h, b, gu, gm, o, ek, es, ck, cs, ok, os_, tile):
    j = pl.program_id(0)
    size = D // 8

    def emit(keep, send, first, lead):
        for p, r in enumerate(rel_order(first)):
            at = (p, 0) if lead else (p,)
            keep[at] = tile[rows_at(sc[0] ^ r, size), :].astype(bf16)
            send[at] = tile[rows_at(sc[0] ^ (r + 1), size), :].astype(bf16)

    tile[...] = dot(gr[...], h[...], TN)
    emit(ck, cs, 4, True)
    tile[...] = dot(b[...], gu[...], TN)
    emit(ek, es, 2, True)

    @pl.when(j == 3)
    def _():
        tile[...] = dot(gm[...], o[...], TN)
        emit(ok, os_, 2, False)


def attn_back_kernel(sc, ql, of, do, kx, vx, raw, a, qg, *rest):
    pieces = rest[:4]
    gna, gin_out, qg_out, dq, dk, dv, gin, w, sems = rest[4:]
    i = pl.program_id(0)
    nq = dk.shape[1] // BQ

    @pl.when(i == 0)
    def _():
        dk[...] = jnp.zeros_like(dk)
        dv[...] = jnp.zeros_like(dv)
        gin[...] = jnp.zeros_like(gin)
        qg_out[...] = jnp.zeros_like(qg_out)
        load_rows(pieces, sc[4], w, sems)

    @pl.when(i < nq)
    def _():
        mine = rows_at(i, BQ)
        lane = lax.broadcasted_iota(jnp.int32, (BQ, 128), 1)
        for h in range(NH):
            dof = do[0, :, h * HD : h * HD + HD].astype(f32)
            delta = jnp.sum(dof * of[:, h * HD : h * HD + HD], axis=1, keepdims=True)
            pad = jnp.zeros((BQ, HD), f32)
            dox = jnp.concatenate([dof, pad], axis=1)
            for n, part in enumerate(split3(-delta)):
                dox = jnp.where(lane == HD + n, part, dox)
            q = ql[h].astype(f32)
            k = kx[h, mine, :].astype(f32)
            v = vx[h, mine, :].astype(f32)
            free = k[:, 84:85]
            inner = (lane < HD) | ((lane >= 81) & (lane < 84))
            p = jnp.exp(jnp.sum(jnp.where(inner, q * k, 0.0), axis=1, keepdims=True)) * free
            ds = p * jnp.sum(jnp.where(lane < HD + 3, dox * v, 0.0), axis=1, keepdims=True)
            ds = ds.astype(bf16).astype(f32)
            dq[h, mine, :] = ds * k
            dk[h, mine, :] += ds * q
            dv[h, mine, :] += p.astype(bf16).astype(f32) * dox
            dob = dox.astype(bf16)
            qb = ql[h]

            def step(j, carry):
                ks = rows_at(j, BQ)
                kb = kx[h, ks, :]
                pt = jnp.exp(dot(kb, qb, NT))
                dpt = dot(vx[h, ks, :], dob, NT)
                dst = (pt * dpt).astype(bf16)
                dv[h, ks, :] += dot(pt.astype(bf16), dob)
                dk[h, ks, :] += dot(dst, qb)
                dq[h, mine, :] += dot(dst, kb, TN)
                return carry

            lax.fori_loop(sc[8 + i], sc[16 + i], step, 0)

    @pl.when(i >= nq)
    def _():
        rows = rows_at(i - nq, TOK)
        parts = []
        gq = jnp.zeros((1, HD), f32)
        gk = jnp.zeros((1, HD), f32)
        for h in range(NH):
            gradq = dq[h, rows, :][:, :HD] * 0.125
            gradk = dk[h, rows, :][:, :HD]
            qs, qi = norm_stats(raw[2 * h])
            ks, ki = norm_stats(raw[2 * h + 1])
            gq += jnp.sum(gradq * qs, axis=0, keepdims=True)
            gk += jnp.sum(gradk * ks, axis=0, keepdims=True)
            parts.append(norm_back(gradq * qg[0:1, :], qs, qi))
            parts.append(norm_back(gradk * qg[1:2, :], ks, ki))
            parts.append(dv[h, rows, :][:, :HD])
        qg_out[0:1, :] += gq
        qg_out[1:2, :] += gk
        mix = jnp.concatenate(parts, axis=1).astype(bf16)
        gna[0] = dot(mix, w[...], NT).astype(bf16)
        gin[...] += dot(a[...], mix, TN)

    @pl.when(i == pl.num_programs(0) - 1)
    def _():
        size = D // 4
        for p in range(4):
            r = (p >> 1) + (p & 1) * 2
            gin_out[p] = gin[rows_at(sc[4] ^ r, size), :].astype(bf16)


def tail_kernel(sc, gna, gna_in, gmid, x0, gains, own, other, hot, pk, ps, post, ga_out, tile):
    size = D // 8
    grad = gna[...].astype(f32) + gna_in[...].astype(f32)
    scaled, inv = norm_stats(x0[...])
    ga_out[0:1, :] = jnp.sum(grad * scaled, axis=0, keepdims=True)
    ga_out[1:8, :] = jnp.zeros((7, D), f32)
    ge = (gmid[...] + norm_back(grad * gains[0:1, :], scaled, inv)).astype(bf16)
    rows = jnp.where(sc[3] == 1, own[...], other[...])
    tile[...] = dot(rows, ge, TN)
    for p, r in enumerate(rel_order(2)):
        pk[p] = tile[rows_at(sc[0] ^ r, size), :].astype(bf16)
        ps[p] = tile[rows_at(sc[0] ^ (r + 1), size), :].astype(bf16)
    post[...] = dot(ge, hot[...], TN)


ANY = pl.BlockSpec(memory_space=pl.ANY)


def call(kernel, grid, sc, ins, specs, outs, out_specs, scratch, flops=0, nbytes=0):
    return pl.pallas_call(
        kernel,
        out_shape=outs,
        grid_spec=pltpu.PrefetchScalarGridSpec(
            num_scalar_prefetch=1,
            grid=grid,
            in_specs=specs,
            out_specs=out_specs,
            scratch_shapes=scratch,
        ),
        compiler_params=pltpu.CompilerParams(vmem_limit_bytes=VLIM),
        cost_estimate=pl.CostEstimate(flops=int(flops), bytes_accessed=int(nbytes), transcendentals=0),
    )(sc, *ins)


def whole(shape):
    return pl.BlockSpec(shape, lambda i, s: (0,) * len(shape))


def sds(shape, dtype):
    return jax.ShapeDtypeStruct(shape, dtype)


DMA = pltpu.SemaphoreType.DMA


def make_local(n_dp, n_mp):
    extra = n_dp // 8
    masks = [extra, 2 * extra, 4 * extra]
    low_bits = []
    m = 1
    while m < extra:
        low_bits.append(m)
        m *= 2
    cextra = n_dp // 8
    col_low = [2 * b for b in low_bits]
    col_masks = [2 * cextra, 4 * cextra]

    def pp(x, dmask, zmask=0):
        perm = [
            (d * n_mp + z, (d ^ dmask) * n_mp + (z ^ zmask))
            for d in range(n_dp)
            for z in range(n_mp)
        ]
        return lax.ppermute(x, ("dp", "mp"), perm)

    def local(
        patches, segment, keep, pos_y, pos_x, labels, bucket, *state
    ):
        masters, firsts, seconds = state[0::3], state[1::3], state[2::3]
        (attend_in, attend_out, expand, contract, patch_embed, pos_table, class_head,
         norm_gains, query_gains) = masters
        length = patches.shape[0]
        rows = patch_embed.shape[0]
        nq = length // BQ
        dp = lax.axis_index("dp")
        z = lax.axis_index("mp")
        core = dp % 2
        z1, z0 = z // 2, z % 2
        g = z0 + 2 * core
        me = dp // extra
        mecol = (dp // 2) // cextra
        mine = core == z1

        perm_core = [
            (d * n_mp + zz, (d ^ 1) * n_mp + zz)
            for d in range(n_dp)
            for zz in range(n_mp)
            if d % 2 == zz // 2
        ]
        patches_in = lax.ppermute(patches, ("dp", "mp"), perm_core)
        meta = jnp.stack([segment, keep, pos_y, pos_x])
        tag = jnp.concatenate([labels, bucket, jnp.zeros((length - IMG - 1,), jnp.int32)])
        meta = jnp.concatenate([meta, tag[None]], axis=0)
        meta = jnp.where(mine, meta, lax.ppermute(meta, ("dp", "mp"), perm_core))

        own_kept = (keep == 1) & (segment < IMG)
        own_valid = jnp.any(
            (segment[None, :] == jnp.arange(IMG)[:, None]) & own_kept[None, :], axis=1
        )
        own_hot = (bucket[0] == jnp.arange(128)).astype(f32)
        counts = jnp.broadcast_to(
            (own_hot * jnp.sum(own_valid.astype(f32)))[None, :], (8, 128)
        )

        def sum_dp(x):
            x = x + pp(x, 1)
            m = 2
            while m < n_dp:
                x = (x + pp(x, m)) + (pp(x, 2 * m) + pp(x, 3 * m))
                m *= 4
            return x

        def sum_z(x):
            return (x + pp(x, 0, 1)) + (pp(x, 0, 2) + pp(x, 0, 3))

        counts = sum_dp(counts)
        image_total = jnp.sum(counts[0])

        def bit_of(mask):
            return (dp // mask) % 2 == 1

        def swap(flag, x, y, axis):
            return jnp.where(
                flag, jnp.concatenate([y, x], axis=axis), jnp.concatenate([x, y], axis=axis)
            )

        def gather(x, low, order, unit):
            for b in low:
                x = swap(bit_of(b), x, pp(x, b), -2)
            got = {0: x}
            for m in order:
                for r in list(got):
                    got[r + m // unit] = pp(got[r], m)
            return [got[r] for r in range(len(got))]

        def gather_dp(x, first):
            a, b = (masks[1], masks[2]) if first == 2 else (masks[2], masks[1])
            return gather(x, low_bits, [a, b, masks[0]], extra)

        qcols = query_gains.shape[1]
        small = jnp.concatenate(
            [
                pos_table.T,
                norm_gains.T,
                jnp.pad(query_gains.reshape(2 * qcols, 1), ((0, rows - 2 * qcols), (0, 0))),
                jnp.zeros((rows, 59), f32),
            ],
            axis=1,
        )
        patch_p = gather_dp(
            jnp.concatenate([patch_embed, small], axis=1).astype(bf16), 2
        )

        perm_a, perm_b, back_b = [], [], []
        for d in range(n_dp):
            for zz in range(n_mp):
                c, a1, a0 = d % 2, zz // 2, zz % 2
                src = d * n_mp + zz
                perm_a.append((src, (d - c + a1) * n_mp + a0 + 2 * c))
                perm_b.append((src, (d - c + a1) * n_mp + a0 + 2 * (1 - c)))
                back_b.append((src, (d - c + 1 - a1) * n_mp + a0 + 2 * c))
        in_low = attend_in.astype(bf16)
        in_a = lax.ppermute(in_low, ("dp", "mp"), perm_a)
        in_b = lax.ppermute(in_low, ("dp", "mp"), perm_b)
        in_p = gather(swap(z1 == 1, in_a, in_b, 0), col_low, col_masks, 2 * cextra)

        def gather_z(x):
            return [x, pp(x, 0, 1), pp(x, 0, 2), pp(x, 0, 3)]

        def pick4(parts, index, axis):
            odd, high = index % 2 == 1, index // 2 == 1
            lo = swap(odd, parts[0], parts[1], axis)
            hi = swap(odd, parts[2], parts[3], axis)
            return swap(high, lo, hi, axis)

        out_p = gather_dp(pick4(gather_z(attend_out.T.astype(bf16)), z, 1), 2)
        head_p = gather_dp(
            jnp.pad(class_head, ((0, 0), (0, CPAD - CLASSES))).astype(bf16), 4
        )
        ex_p = gather_dp(jnp.stack(gather_z(expand.astype(bf16))), 2)
        con_p = gather_dp(jnp.stack(gather_z(contract.T.astype(bf16))), 4)

        size = D // 8

        def pick8(parts, axis):
            odd = me % 2 == 1
            pairs = [swap(odd, parts[2 * n], parts[2 * n + 1], axis) for n in range(4)]
            return pick4(pairs, me // 2, axis)

        small_all = pick8([p[:, D:] for p in patch_p], 0).T
        pos_rows = small_all[: 2 * GRID]
        gains = jnp.pad(small_all[2 * GRID : 2 * GRID + 4].astype(f32), ((0, 4), (0, 0)))
        qg = small_all[2 * GRID + 4].astype(f32).reshape(n_dp, rows)[:, : 2 * qcols]
        qg = qg.reshape(n_dp, 2, qcols).transpose(1, 0, 2).reshape(2, HD)
        qg = jnp.pad(qg, ((0, 6), (0, 0)))

        seg, kp, py, px = meta[0], meta[1], meta[2], meta[3]
        labs = meta[4, :IMG]
        buck = meta[4, IMG]
        kept = (kp == 1) & (seg < IMG)
        ids64 = jnp.arange(64)[None, :]
        hot_pos = ((py[:, None] == ids64) | (px[:, None] + GRID == ids64)).astype(bf16)
        same = seg[:, None] == ids64
        qaux = jnp.where((ids64 < IMG) & same, BIG, jnp.where(ids64 == IMG, 1.0, 0.0)).astype(bf16)
        kaux = jnp.where(
            (ids64 < IMG) & same & kept[:, None],
            1.0,
            jnp.where(
                ids64 == IMG,
                -BIG,
                jnp.where(
                    (ids64 > IMG) & (ids64 < IMG + 4),
                    1.0,
                    jnp.where((ids64 == IMG + 4) & ~kept[:, None], 1.0, 0.0),
                ),
            ),
        ).astype(bf16)
        vaux = jnp.broadcast_to(jnp.where(ids64 < 3, 1.0, 0.0).astype(bf16), (length, 64))
        first_seg, last_seg = seg[::BQ], jnp.minimum(seg[BQ - 1 :: BQ], IMG - 1)
        lo = jnp.sum((seg[None, :] < first_seg[:, None]).astype(jnp.int32), axis=1) // BQ
        hi = (jnp.sum((seg[None, :] <= last_seg[:, None]).astype(jnp.int32), axis=1) + BQ - 1) // BQ
        sc = jnp.concatenate(
            [
                jnp.stack([me, g, z, mine.astype(jnp.int32), mecol, mecol, mecol, mecol]),
                lo,
                hi,
            ]
        ).astype(jnp.int32)
        mem_all = ((seg[:, None] == jnp.arange(128)[None, :]) & kept[:, None]).astype(f32)
        mem_all = jnp.where(jnp.arange(128)[None, :] < IMG, mem_all, 0.0)[:, :IMG]
        valid = jnp.max(mem_all, axis=0)
        mem = lax.dynamic_slice_in_dim(mem_all, g * TOK, TOK, 0)
        hot_own = lax.dynamic_slice_in_dim(hot_pos, g * TOK, TOK, 0)
        vt = jnp.stack([valid, valid / image_total], axis=1)
        vt = jnp.pad(vt, ((0, 0), (0, 126)))
        lab_hot = (labs[:, None] == jnp.arange(CPAD)[None, :]).astype(f32)

        nt = length // TOK
        a, x0 = call(
            x0_kernel,
            (nt,),
            sc,
            [patches, patches_in, hot_pos, pos_rows, gains] + patch_p,
            [
                pl.BlockSpec((TOK, D), lambda i, s: (jnp.where(s[3] == 1, i, 0), 0)),
                pl.BlockSpec((TOK, D), lambda i, s: (jnp.where(s[3] == 1, 0, i), 0)),
                pl.BlockSpec((TOK, 64), lambda i, s: (i, 0)),
                whole((64, D)),
                whole((8, D)),
            ]
            + [ANY] * 8,
            (sds((length, D), bf16), sds((TOK, D), f32)),
            (pl.BlockSpec((TOK, D), lambda i, s: (i, 0)), whole((TOK, D))),
            [pltpu.VMEM((D, D + 128), bf16), DMA((8,))],
            2 * length * D * D,
            10e6,
        )
        qx, kx, vx, raw = call(
            qkv_kernel,
            (nt,),
            sc,
            [a, qaux, kaux, vaux, qg] + in_p,
            [
                pl.BlockSpec((TOK, D), lambda i, s: (i, 0)),
                pl.BlockSpec((TOK, 64), lambda i, s: (i, 0)),
                pl.BlockSpec((TOK, 64), lambda i, s: (i, 0)),
                pl.BlockSpec((TOK, 64), lambda i, s: (i, 0)),
                whole((8, HD)),
            ]
            + [ANY] * 4,
            tuple([sds((NH, length, 128), bf16)] * 3 + [sds((2 * NH, length, HD), f32)]),
            tuple(
                [pl.BlockSpec((NH, TOK, 128), lambda i, s: (0, i, 0))] * 3
                + [pl.BlockSpec((2 * NH, TOK, HD), lambda i, s: (0, i, 0))]
            ),
            [pltpu.VMEM((D, 576), bf16), DMA((4,))],
            2 * length * D * 576,
            10e6,
        )
        per_tok = TOK // BQ
        o_rel, o_full, ql = call(
            attn_kernel,
            (nq,),
            sc,
            [qx, kx, vx],
            [
                pl.BlockSpec((NH, BQ, 128), lambda i, s: (0, i, 0)),
                whole((NH, length, 128)),
                whole((NH, length, 128)),
            ],
            (
                sds((4, TOK, NH * HD), bf16),
                sds((length, NH * HD), f32),
                sds((NH, length, 128), bf16),
            ),
            (
                pl.BlockSpec(
                    (1, BQ, NH * HD), lambda i, s: (s[1] ^ (i // per_tok), i % per_tok, 0)
                ),
                pl.BlockSpec((BQ, NH * HD), lambda i, s: (i, 0)),
                pl.BlockSpec((NH, BQ, 128), lambda i, s: (0, i, 0)),
            ),
            [pltpu.VMEM((NH, BQ, 128), f32)],
            8e9,
            8e6,
        )

        def trade(parts):
            return [
                parts[0],
                pp(parts[1], 0, 1),
                pp(parts[2], 1, 0),
                pp(parts[3], 1, 1),
            ]

        o_cat = pick4(trade([o_rel[r] for r in range(4)]), g, 1)
        x1, b = call(
            mid_kernel,
            (1,),
            sc,
            [o_cat, x0, gains] + out_p,
            [whole((TOK, D)), whole((TOK, D)), whole((8, D))] + [ANY] * 8,
            (sds((TOK, D), f32), sds((TOK, D), bf16)),
            (whole((TOK, D)), whole((TOK, D))),
            [pltpu.VMEM((D, D), bf16), DMA((8,))],
            2 * TOK * D * D,
            6e6,
        )
        tile_spec = pl.BlockSpec((TOK, D), lambda j, s: (0, j))
        u, h = call(
            up_kernel,
            (4,),
            sc,
            [b] + ex_p,
            [whole((TOK, D))] + [ANY] * 8,
            (sds((TOK, HID), f32), sds((TOK, HID), bf16)),
            (tile_spec, tile_spec),
            [pltpu.VMEM((4, D, D), bf16), DMA((4, 8))],
            2 * TOK * D * HID,
            14e6,
        )
        x2, ns = call(
            down_kernel,
            (4,),
            sc,
            [h, x1, gains, mem] + con_p,
            [tile_spec, whole((TOK, D)), whole((8, D)), whole((TOK, IMG))] + [ANY] * 8,
            (sds((TOK, D), f32), sds((IMG, D + 128), f32)),
            (whole((TOK, D)), whole((IMG, D + 128))),
            [pltpu.VMEM((4, D, D), bf16), pltpu.VMEM((TOK, D), f32), DMA((4, 8))],
            2 * TOK * D * HID,
            12e6,
        )
        ns = ns + pp(ns, 1, 0)
        ns = ns + pp(ns, 0, 1)
        pooled, gp, sinv, loss, gh, gh_send = call(
            head_kernel,
            (1,),
            sc,
            [ns, lab_hot, vt] + head_p,
            [whole((IMG, D + 128)), whole((IMG, CPAD)), whole((IMG, 128))] + [ANY] * 8,
            (
                sds((IMG, D), f32),
                sds((IMG, D), f32),
                sds((IMG, 128), f32),
                sds((IMG, 128), f32),
                sds((4, size, CPAD // 2), bf16),
                sds((4, size, CPAD // 2), bf16),
            ),
            (
                whole((IMG, D)),
                whole((IMG, D)),
                whole((IMG, 128)),
                whole((IMG, 128)),
                whole((4, size, CPAD // 2)),
                whole((4, size, CPAD // 2)),
            ),
            [pltpu.VMEM((D, CPAD), bf16), pltpu.VMEM((D, CPAD // 2), f32), DMA((8,))],
            1e8,
            3e6,
        )

        gu, gr, gm, gmid, ga, small_b = call(
            back_kernel,
            (4,),
            sc,
            [u, x2, x1, gains, mem, pooled, gp, sinv] + ex_p + con_p + out_p,
            [
                tile_spec,
                whole((TOK, D)),
                whole((TOK, D)),
                whole((8, D)),
                whole((TOK, IMG)),
                whole((IMG, D)),
                whole((IMG, D)),
                whole((IMG, 128)),
            ]
            + [ANY] * 24,
            (
                sds((TOK, HID), bf16),
                sds((TOK, D), bf16),
                sds((TOK, D), bf16),
                sds((TOK, D), f32),
                sds((TOK, D), bf16),
                sds((8, D), f32),
            ),
            (
                tile_spec,
                whole((TOK, D)),
                whole((TOK, D)),
                whole((TOK, D)),
                whole((TOK, D)),
                whole((8, D)),
            ),
            [
                pltpu.VMEM((4, D, D), bf16),
                pltpu.VMEM((4, D, D), bf16),
                pltpu.VMEM((D, D), bf16),
                pltpu.VMEM((TOK, D), f32),
                pltpu.VMEM((TOK, D), f32),
                DMA((4, 8)),
                DMA((4, 8)),
                DMA((8,)),
            ],
            4 * TOK * D * HID,
            24e6,
        )
        ga4 = ga.reshape(TOK, 4, NH * HD).transpose(1, 0, 2)
        ga_rel = pick4([ga4[n : n + 1] for n in range(4)], g, 0)
        do = pick4([t[None] for t in trade([ga_rel[r] for r in range(4)])], g, 0)

        wide = pl.BlockSpec((4, 1, size, D), lambda j, s: (0, s[2] ^ j, 0, 0))
        ek, es, ck, cs, ok, os_ = call(
            wgrad_kernel,
            (4,),
            sc,
            [gr, h, b, gu, gm, o_cat],
            [whole((TOK, D)), tile_spec, whole((TOK, D)), tile_spec, whole((TOK, D)), whole((TOK, D))],
            tuple([sds((4, 4, size, D), bf16)] * 4 + [sds((4, size, D), bf16)] * 2),
            tuple([wide] * 4 + [whole((4, size, D))] * 2),
            [pltpu.VMEM((D, D), f32)],
            4 * TOK * D * HID,
            20e6,
        )

        def add(x, y):
            return x.astype(f32) + y.astype(f32)

        def low_rows(x, low):
            for b in reversed(low):
                half = x.shape[-2] // 2
                first, second = x[..., :half, :], x[..., half:, :]
                flag = bit_of(b)
                send = jnp.where(flag, first, second)
                stay = jnp.where(flag, second, first)
                x = add(stay, pp(send.astype(bf16), b))
            return x

        def scatter4(stay, low, m1, m2):
            x = add(stay[:2], pp(stay[2:].astype(bf16), m1))
            x = add(x[0].astype(bf16), pp(x[1].astype(bf16), m2))
            return low_rows(x, low)

        def scatter8(stay, send, first):
            x = add(stay, pp(send, masks[0])).astype(bf16)
            m1, m2 = (masks[1], masks[2]) if first == 2 else (masks[2], masks[1])
            return scatter4(x, low_bits, m1, m2)

        def scatter_z(parts):
            return (parts[0].astype(f32) + pp(parts[1], 0, 1)) + (
                pp(parts[2], 0, 2).astype(f32) + pp(parts[3], 0, 3)
            )

        def split_z(x):
            return scatter_z([x[r].astype(bf16) for r in range(4)])

        if extra == 1:
            gh = scatter4(gh, low_bits, masks[1], masks[2])
        else:
            gh = 0.5 * scatter8(gh, gh_send, 2)
        gh = add(gh.astype(bf16), pp(gh.astype(bf16), 0, 2))
        gh = swap(z0 == 1, gh, pp(gh, 0, 1), 1)[:, :CLASSES]

        share_ex = split_z(scatter8(ek, es, 2))
        share_con = split_z(scatter8(ck, cs, 4)).T
        go = scatter8(ok, os_, 2)
        go4 = go.reshape(rows, 4, NH * HD).transpose(1, 0, 2)
        share_out = split_z(pick4([go4[n : n + 1] for n in range(4)], z, 0)).T

        nsteps = nq + nt
        gna, gin, qgrad = call(
            attn_back_kernel,
            (nsteps,),
            sc,
            [ql, o_full, do, kx, vx, raw, a, qg] + in_p,
            [
                pl.BlockSpec((NH, BQ, 128), lambda i, s: (0, jnp.minimum(i, nq - 1), 0)),
                pl.BlockSpec((BQ, NH * HD), lambda i, s: (jnp.minimum(i, nq - 1), 0)),
                pl.BlockSpec(
                    (1, BQ, NH * HD),
                    lambda i, s: (
                        jnp.minimum(i, nq - 1) // per_tok,
                        jnp.minimum(i, nq - 1) % per_tok,
                        0,
                    ),
                ),
                whole((NH, length, 128)),
                whole((NH, length, 128)),
                pl.BlockSpec((2 * NH, TOK, HD), lambda i, s: (0, jnp.maximum(i - nq, 0), 0)),
                pl.BlockSpec((TOK, D), lambda i, s: (jnp.maximum(i - nq, 0), 0)),
                whole((8, HD)),
            ]
            + [ANY] * 4,
            (sds((4, TOK, D), bf16), sds((4, D // 4, 576), bf16), sds((8, HD), f32)),
            (
                pl.BlockSpec((1, TOK, D), lambda i, s: (s[1] ^ jnp.maximum(i - nq, 0), 0, 0)),
                whole((4, D // 4, 576)),
                whole((8, HD)),
            ),
            [
                pltpu.VMEM((NH, length, 128), f32),
                pltpu.VMEM((NH, length, 128), f32),
                pltpu.VMEM((NH, length, 128), f32),
                pltpu.VMEM((D, 576), f32),
                pltpu.VMEM((D, 576), bf16),
                DMA((4,)),
            ],
            20e9,
            20e6,
        )
        part = add(gna[:2], pp(gna[2:], 1)).astype(bf16)
        gna_in = pp(part[1], 0, 1)

        gin = scatter4(gin, col_low, col_masks[0], col_masks[1])
        gin = gin.astype(bf16).reshape(2, rows, 3 * NH * HD)
        share_in = add(
            lax.ppermute(jnp.where(z1 == 1, gin[1], gin[0]), ("dp", "mp"), perm_a),
            lax.ppermute(jnp.where(z1 == 1, gin[0], gin[1]), ("dp", "mp"), back_b),
        )

        own_rows = pl.BlockSpec((TOK, D), lambda i, s: (s[1], 0))
        pk, ps, post, gain_a = call(
            tail_kernel,
            (1,),
            sc,
            [part[0], gna_in, gmid, x0, gains, patches, patches_in, hot_own],
            [
                whole((TOK, D)),
                whole((TOK, D)),
                whole((TOK, D)),
                whole((TOK, D)),
                whole((8, D)),
                own_rows,
                own_rows,
                whole((TOK, 64)),
            ],
            (
                sds((4, size, D), bf16),
                sds((4, size, D), bf16),
                sds((D, 64), f32),
                sds((8, D), f32),
            ),
            (whole((4, size, D)), whole((4, size, D)), whole((D, 64)), whole((8, D))),
            [pltpu.VMEM((D, D), f32)],
            2 * TOK * D * D,
            8e6,
        )
        qg_cols = qgrad[:2].reshape(2, n_dp, qcols).transpose(1, 0, 2).reshape(n_dp, 2 * qcols)
        qg_cols = jnp.pad(qg_cols, ((0, 0), (0, rows - 2 * qcols))).reshape(D, 1)
        gain_cols = jnp.stack([gain_a[0], small_b[2], small_b[0], small_b[1]], axis=1)
        tiny = jnp.concatenate(
            [post, gain_cols, qg_cols, jnp.zeros((D, 59), f32)], axis=1
        ).astype(bf16)
        tiny = tiny.reshape(8, 1, size, 128)
        tiny = pick8([tiny[n] for n in range(8)], 0)
        order = rel_order(2)
        tk = jnp.stack([tiny[r] for r in order])
        ts = jnp.stack([tiny[r + 1] for r in order])
        gpatch = scatter8(pk, ps, 2).astype(bf16)
        gtiny = scatter8(tk, ts, 2).astype(bf16)
        quarter = rows // 4

        def z_rows(x):
            x4 = x.reshape(4, quarter, x.shape[-1])
            rel = pick4([x4[n : n + 1] for n in range(4)], z, 0)
            return scatter_z([rel[r] for r in range(4)])

        qpatch, qtiny = z_rows(gpatch), z_rows(gtiny)

        once = (z == 0).astype(f32)
        squares = (
            jnp.sum(share_in * share_in)
            + jnp.sum(share_out * share_out)
            + jnp.sum(share_ex * share_ex)
            + jnp.sum(share_con * share_con)
            + once * jnp.sum(gh * gh)
            + jnp.sum(qpatch * qpatch)
            + jnp.sum(qtiny * qtiny)
        )
        lane = jnp.arange(128)
        buck_hot = (lane == buck + 1).astype(f32) * (g == 0).astype(f32)
        stats = jnp.where(lane == 0, squares, 0.0) + buck_hot * jnp.sum(loss[:, 0])
        stats = sum_z(sum_dp(jnp.broadcast_to(stats[None, :], (8, 128))))
        grad_norm = jnp.sqrt(stats[0, 0])
        bucket_loss = stats[0, 1 : 1 + NB]
        factor = jnp.minimum(1.0, CLIP / (grad_norm + 1e-06))

        share_patch = pick4(gather_z(qpatch), z, 0)
        share_tiny = pick4(gather_z(qtiny), z, 0)
        shares = (
            share_in,
            share_out,
            share_ex,
            share_con,
            share_patch,
            share_tiny[:, : 2 * GRID].T,
            gh,
            share_tiny[:, 2 * GRID : 2 * GRID + 4].T,
            share_tiny[: 2 * qcols, 2 * GRID + 4].reshape(2, qcols),
        )
        results = [bucket_loss, counts[0, :NB], grad_norm]
        for index in range(9):
            clipped = shares[index] * factor
            first_new = BETA_ONE * firsts[index] + (1.0 - BETA_ONE) * clipped
            second_new = BETA_TWO * seconds[index] + (1.0 - BETA_TWO) * clipped * clipped
            matrix = index in (0, 1, 2, 3, 4, 6)
            rate = RATE_MATRIX if matrix else RATE_SMALL
            decay = DECAY if matrix else 0.0
            ratio = (
                first_new
                / (1.0 - BETA_ONE**STEP)
                / (jnp.sqrt(second_new / (1.0 - BETA_TWO**STEP)) + ADAM_EPS)
            )
            results += [
                masters[index] - rate * (ratio + decay * masters[index]),
                first_new,
                second_new,
            ]
        return tuple(results)

    return local


def solution(mesh):
    shard = {
        "in": P("dp", "mp"),
        "out": P("mp", "dp"),
        "row": P("dp", None),
        "col": P(None, "dp"),
    }
    kinds = ["in", "out", "in", "out", "row", "col", "row", "col", "col"]
    triples = tuple(shard[k] for k in kinds for _ in range(3))
    in_specs = (P("dp", None),) + (P("dp"),) * 6 + triples
    out_specs = (P(), P(), P()) + triples
    return jax.shard_map(
        make_local(mesh.shape["dp"], mesh.shape["mp"]),
        mesh=mesh,
        in_specs=in_specs,
        out_specs=out_specs,
        check_vma=False,
    )
```

```python
import jax
import jax.numpy as jnp
from jax import lax
from jax.experimental import pallas as pl
from jax.experimental.pallas import tpu as pltpu
from jax.sharding import PartitionSpec as P

D = 768
HD = 64
HID = 3072
CLASSES = 1000
CPAD = 1024
GRID = 32
IMG = 16
NB = 4
STEP = 10
BQ = 256
TOK = 512
NH = 3
QK = 2 * NH * HD
SUB = D // 8
SMALL = 128
LANE_GAIN = 64
LANE_QG = 68
LANE_COUNT = 72

HIGH = lax.Precision.HIGHEST
NORM_EPS = 1e-06
CLIP = 0.1
BETA_ONE = 0.9
BETA_TWO = 0.95
RATE_MATRIX = 0.05
RATE_SMALL = 0.2
DECAY = 0.05
ADAM_EPS = 1e-08
BIG = 128.0

bf16 = jnp.bfloat16
f32 = jnp.float32
VLIM = 56 * 1024 * 1024

NN = (((1,), (0,)), ((), ()))
NT = (((1,), (1,)), ((), ()))
TN = (((0,), (0,)), ((), ()))


def dot(a, b, dims=NN, precision=None):
    return lax.dot_general(a, b, dims, precision=precision, preferred_element_type=f32)


def norm_stats(values):
    center = values - jnp.mean(values, axis=-1, keepdims=True)
    inv_std = lax.rsqrt(jnp.mean(center * center, axis=-1, keepdims=True) + NORM_EPS)
    return center * inv_std, inv_std


def norm_back(grad_scaled, scaled, inv_std):
    return inv_std * (
        grad_scaled
        - jnp.mean(grad_scaled, axis=-1, keepdims=True)
        - scaled * jnp.mean(grad_scaled * scaled, axis=-1, keepdims=True)
    )


def splits(x, n):
    out = []
    for _ in range(n - 1):
        part = x.astype(bf16)
        out.append(part)
        x = x - part.astype(f32)
    out.append(x.astype(bf16))
    return out


def dot_split(x, exact, n, dims=NN):
    total = None
    for part in splits(x, n):
        term = dot(part, exact, dims)
        total = term if total is None else total + term
    return total


def eye(rows, cols, offset=0):
    row = lax.broadcasted_iota(jnp.int32, (rows, cols), 0)
    col = lax.broadcasted_iota(jnp.int32, (rows, cols), 1)
    return (row + offset == col).astype(f32)


def rows_at(index, size):
    return pl.ds(pl.multiple_of(index * size, size), size)


def pack_kernel(w_in, w_out, w_up, w_down, w_patch, w_pos, w_gain, w_qg, cnt,
                patch_o, in_o, z_o, out_o):
    rows = w_patch.shape[0]
    patch_o[:, :D] = w_patch[...].astype(bf16)
    low = lambda ref: ref[...].astype(bf16).astype(f32)
    small = dot(low(w_pos), eye(64, SMALL), TN)
    small += dot(low(w_gain), eye(4, SMALL, LANE_GAIN), TN)
    qg = dot(low(w_qg), eye(2, SMALL, LANE_QG), TN)
    small += dot(eye(rows, qg.shape[0]), qg)
    small += dot(eye(rows, 8), cnt[...])
    patch_o[:, D:] = small.astype(bf16)
    w = w_in[...].astype(bf16)
    parts = [
        w[:, h * 192 + part * HD : h * 192 + part * HD + HD]
        for part in range(3)
        for h in range(NH)
    ]
    in_o[...] = jnp.concatenate(parts, axis=1)
    z_o[0] = w_up[...].astype(bf16)
    z_o[1] = w_down[...].astype(bf16)
    out_o[...] = dot(eye(rows, rows).astype(bf16), w_out[...].astype(bf16), NT).astype(bf16)


def ordered(flag, x, y):
    return jnp.where(flag, jnp.concatenate([y, x], axis=1), jnp.concatenate([x, y], axis=1))


def xor_columns(parts, index):
    odd, high = index % 2 == 1, index // 2 == 1
    return ordered(high, ordered(odd, parts[0], parts[1]), ordered(odd, parts[2], parts[3]))


def first_kernel(sc, z_w, o0, o1, o2, o3, head, f_out):
    f_out[:, :D] = z_w[0]
    f_out[:, D : 2 * D] = z_w[1]
    outs = [o[...].astype(f32) for o in (o0, o1, o2, o3)]
    f_out[:, 2 * D : 3 * D] = xor_columns(outs, sc[2]).astype(bf16)
    f_out[:, 3 * D :] = jnp.zeros_like(f_out[:, 3 * D :])
    f_out[:, 3 * D : 3 * D + CLASSES] = head[...].astype(bf16)


def second_kernel(z1, z2, z3, g_out):
    for n, ref in enumerate((z1, z2, z3)):
        g_out[2 * n] = ref[0]
        g_out[2 * n + 1] = ref[1]


REL = [0, 2, 4, 6, 1, 3, 5, 7]


def row_copies(refs, me, dst, sems, rel=REL):
    out = []
    for n, ref in enumerate(refs):
        size = ref.shape[0]
        out.append(pltpu.make_async_copy(ref, dst.at[rows_at(me ^ rel[n], size), :], sems.at[n]))
    return out


def columns(refs, lo, width):
    return [ref.at[:, pl.ds(lo, width)] for ref in refs]


def start(copies):
    for copy in copies:
        copy.start()


def wait(copies):
    for copy in copies:
        copy.wait()


def x0_kernel(sc, own, other, hot, *rest):
    refs = rest[:8]
    a_out, x0_out, gx_out, w, sems = rest[8:]
    i = pl.program_id(0)

    @pl.when(i == 0)
    def _():
        copies = row_copies(refs, sc[0], w, sems)
        start(copies)
        wait(copies)
        row = lax.broadcasted_iota(jnp.int32, (16, SMALL), 0)
        col = lax.broadcasted_iota(jnp.int32, (16, SMALL), 1)
        pick = (row + LANE_GAIN == col).astype(f32).astype(bf16)
        gx_out[...] = dot(pick, w[:, D:], NT)

    rows = jnp.where(sc[3] == 1, own[...], other[...])
    x0 = dot(rows, w[:, :D]) + dot(hot[...], w[:, D:], NT)
    scaled, _ = norm_stats(x0)
    a_out[...] = (scaled * gx_out[0:1, :]).astype(bf16)

    @pl.when(i == sc[1])
    def _():
        x0_out[...] = x0


IN_REL = [0, 1, 2, 3]


def qkv_kernel(sc, a, qaux, kaux, vaux, gain, avg, *rest):
    refs = rest[:4]
    qx, kx, vx, xh_out, inv_out, w, sems = rest[4:]
    i = pl.program_id(0)

    @pl.when(i == 0)
    def _():
        copies = row_copies(refs, sc[4], w, sems, IN_REL)
        start(copies)
        wait(copies)

    mixed = dot(a[...], w[...])
    qk = mixed[:, :QK]
    v = mixed[:, QK:].astype(bf16)
    ones = avg[...]
    center = qk - dot_split(qk, ones, 2)
    inv = lax.rsqrt(dot_split(center * center, ones, 2) + NORM_EPS)
    scaled = center * inv
    xh_out[...] = scaled
    inv_out[...] = inv
    low = (scaled * gain[0:1, :]).astype(bf16)
    qa, ka, va = qaux[...], kaux[...], vaux[...]
    for h in range(NH):
        qx[h] = jnp.concatenate([low[:, h * HD : h * HD + HD], qa], axis=1)
        kx[h] = jnp.concatenate([low[:, (NH + h) * HD : (NH + h) * HD + HD], ka], axis=1)
        vx[h] = jnp.concatenate([v[:, h * HD : h * HD + HD], va], axis=1)


def attn_kernel(sc, qx, kx, vx, o_rel, o_full, ql, acc):
    i = pl.program_id(0)
    acc[...] = jnp.zeros_like(acc)
    lo, hi = sc[8 + i], sc[16 + i]

    def tile(start_row, size):
        ks = pl.ds(pl.multiple_of(start_row, BQ), size)
        scores = [dot(qx[h], kx[h, ks, :], NT) for h in range(NH)]
        probs = [jnp.exp(s).astype(bf16) for s in scores]
        for h in range(NH):
            acc[h] += dot(probs[h], vx[h, ks, :])

    pairs = (hi - lo) // 2

    def step(j, carry):
        tile((lo + 2 * j) * BQ, 2 * BQ)
        return carry

    lax.fori_loop(0, pairs, step, 0)

    @pl.when((hi - lo) % 2 == 1)
    def _():
        tile((hi - 1) * BQ, BQ)

    mine = rows_at(i, BQ)
    lane = lax.broadcasted_iota(jnp.int32, (BQ, 128), 1)
    outs = []
    for h in range(NH):
        q = qx[h].astype(f32)
        k = kx[h, mine, :].astype(f32)
        v = vx[h, mine, :].astype(f32)
        free = k[:, 84:85]
        diag = jnp.sum(jnp.where(lane < HD, q * k, 0.0), axis=1, keepdims=True)
        p = jnp.exp(diag) * free
        out = acc[h] + p.astype(bf16).astype(f32) * v
        total = out[:, 64:65]
        outs.append(out[:, :HD] / total)
        for n, part in enumerate(splits(-jnp.log(total), 3)):
            q = jnp.where(lane == 81 + n, part.astype(f32), q)
        ql[h] = q.astype(bf16)
    full = jnp.concatenate(outs, axis=1)
    o_full[...] = full
    o_rel[0] = full.astype(bf16)


GELU_C = 0.7978845608028654


def gelu_tanh(u):
    return jnp.tanh(GELU_C * (u + 0.044715 * u * u * u))


def mlp_tile(b, w, u_out, h_out):
    u = dot(b, w[0])
    u_out[...] = u
    h = (0.5 * u * (1.0 + gelu_tanh(u))).astype(bf16)
    h_out[...] = h
    return dot(h, w[1], NT)


def first_tile(refs, me, dst, sems):
    return row_copies(columns(refs, 0, D), me, dst.at[0], sems.at[0]) + row_copies(
        columns(refs, D, D), me, dst.at[1], sems.at[1]
    )


def later_tile(refs, t, me, dst, sems):
    return row_copies([r.at[2 * t] for r in refs], me, dst.at[0], sems.at[0]) + row_copies(
        [r.at[2 * t + 1] for r in refs], me, dst.at[1], sems.at[1]
    )


def mlp_one_kernel(sc, o, x0, gx, *rest):
    refs = rest[:8]
    x1_out, b_out, u_out, h_out, acc, w_o, w_t, sem_o, sem_t = rest[8:]
    first = row_copies(columns(refs, 2 * D, D), sc[0], w_o, sem_o)
    tile = first_tile(refs, sc[0], w_t, sem_t)
    start(first)
    start(tile)
    wait(first)
    x1 = x0[...] + dot(o[...], w_o[...], NT)
    x1_out[...] = x1
    b_out[...] = (norm_stats(x1)[0] * gx[1:2, :]).astype(bf16)
    wait(tile)
    acc[...] = x1 + mlp_tile(b_out[...], w_t, u_out, h_out)


def mlp_two_kernel(sc, b, acc_in, gx, mem, heads, *rest):
    refs = rest[:8]
    u_out, h_out, x2, ns_out, w_t, sem_t = rest[8:]
    j = pl.program_id(0)

    @pl.when(j == 0)
    def _():
        for t in range(3):
            start(later_tile(refs, t, sc[0], w_t.at[t], sem_t.at[t]))
        x2[...] = acc_in[...]

    for t in range(3):

        @pl.when(j == t)
        def _():
            wait(later_tile(refs, t, sc[0], w_t.at[t], sem_t.at[t]))

    x2[...] += mlp_tile(b[...], w_t.at[j], u_out, h_out)

    @pl.when(j == 2)
    def _():
        f = norm_stats(x2[...])[0] * gx[2:3, :]
        ones = heads[...]
        e = jnp.exp(dot_split(f * gx[3:4, :], ones, 3) * 0.125)
        eb = dot_split(e, ones, 2, NT)
        m = mem[...]
        num = jnp.zeros((IMG, D), f32)
        for part in splits(eb * f, 3):
            num += dot(m, part, TN)
        den = jnp.zeros((IMG, 128), f32)
        for part in splits(e, 3):
            den += dot(m, part, TN)
        ns_out[:, :D] = num
        ns_out[:, D:] = den


def head_kernel(sc, ns_a, ns_b, lab, vt, heads, *rest):
    pooled_out, gp_out, sinv_out, loss_out, gh_out, gh_send, w, gw, sems = rest[8:]
    copies = row_copies(columns(rest[:8], 3 * D, CPAD), sc[0], w, sems)
    start(copies)
    ns = ns_a[...] + ns_b[...]
    valid = vt[:, 0:1]
    scale = vt[:, 1:2]
    total = jnp.where(valid > 0.0, ns[:, D:], 1.0)
    sinv = jnp.where(valid > 0.0, 1.0 / total, 0.0)
    lane = lax.broadcasted_iota(jnp.int32, (IMG, 128), 1)
    sinv = jnp.where(lane < D // HD, sinv, 0.0)
    pooled = ns[:, :D] * dot_split(sinv, heads[...], 3, NT)
    low = pooled.astype(bf16)
    wait(copies)
    logits = dot(low, w[...])
    cls = lax.broadcasted_iota(jnp.int32, (IMG, CPAD), 1)
    real = (cls < CLASSES).astype(f32)
    hot = lab[...]
    ex = jnp.exp(-jnp.abs(logits))
    soft = jnp.maximum(logits, 0.0) + jnp.log1p(ex)
    per = jnp.sum(soft * real, axis=1, keepdims=True) - jnp.sum(
        logits * hot, axis=1, keepdims=True
    )
    loss_out[...] = jnp.broadcast_to(per * valid, (IMG, 128))
    sig = jnp.where(logits >= 0.0, 1.0, ex) / (1.0 + ex)
    gl = (scale * (sig * real - hot)).astype(bf16)
    pooled_out[...] = pooled
    sinv_out[...] = sinv
    gp_out[...] = dot(gl, w[...], NT)
    half = jnp.where(sc[2] % 2 == 1, gl[:, 512:].astype(f32), gl[:, :512].astype(f32))
    gw[...] = dot(low, half.astype(bf16), TN)
    for p, r in enumerate(rel_order(2)):
        gh_out[p] = gw[rows_at(sc[0] ^ r, SUB), :].astype(bf16)
        gh_send[p] = gw[rows_at(sc[0] ^ (r + 1), SUB), :].astype(bf16)


def rel_order(first):
    m1, m2 = (2, 4) if first == 2 else (4, 2)
    return [(p >> 1) * m1 + (p & 1) * m2 for p in range(4)]


def back_kernel(sc, u_a, u_b, x2, x1, gx, mem, pooled, gp, sinv, heads, *rest):
    refs, later = rest[:8], rest[8:16]
    gu_out, gr_out, gm_out, gmid_out, ga_out, small_out = rest[16:22]
    w_t, w_o, grs, acc, sem_t, sem_o = rest[22:]
    j = pl.program_id(0)

    def tile(t):
        if t == 0:
            return first_tile(refs, sc[0], w_t.at[0], sem_t.at[0])
        return later_tile(later, t - 1, sc[0], w_t.at[t], sem_t.at[t])

    def out_rows():
        return row_copies(columns(refs, 2 * D, D), sc[0], w_o, sem_o)

    @pl.when(j == 0)
    def _():
        for t in range(4):
            start(tile(t))
        start(out_rows())
        scaled, inv = norm_stats(x2[...])
        f = scaled * gx[2:3, :]
        probe = gx[3:4, :]
        ones = heads[...]
        e = jnp.exp(dot_split(f * probe, ones, 3) * 0.125)
        m = mem[...]
        m3 = jnp.concatenate([m, m, m], axis=1)

        def spread(x):
            return dot(m3, jnp.concatenate(splits(x, 3), axis=0))

        gt = spread(gp[...])
        at = e * spread(sinv[...])
        gpp = dot_split(gp[...] * pooled[...], ones, 3)
        da = dot_split(gt * f, ones, 3)
        dc = at * (da - spread(gpp))
        dcb = dot_split(dc, ones, 2, NT) * 0.125
        df = dot_split(at, ones, 2, NT) * gt + dcb * probe
        gr = norm_back(df * gx[2:3, :], scaled, inv)
        grs[...] = gr
        gr_out[...] = gr.astype(bf16)
        small_out[2:3, :] = jnp.sum(df * scaled, axis=0, keepdims=True)
        small_out[3:4, :] = jnp.sum(dcb * f, axis=0, keepdims=True)
        small_out[0:1, :] = jnp.zeros((1, D), f32)
        small_out[4:8, :] = jnp.zeros((4, D), f32)
        acc[...] = jnp.zeros_like(acc)

    for t in range(4):

        @pl.when(j == t)
        def _():
            wait(tile(t))

    gh = dot(gr_out[...], w_t[j, 1])
    v = jnp.where(j < 1, u_a[...], u_b[...])
    t = gelu_tanh(v)
    slope = 0.5 * (1.0 + t) + 0.5 * v * (1.0 - t * t) * GELU_C * (1.0 + 0.134145 * v * v)
    gu = (gh * slope).astype(bf16)
    gu_out[...] = gu
    acc[...] += dot(gu, w_t[j, 0], NT)

    @pl.when(j == 3)
    def _():
        wait(out_rows())
        scaled, inv = norm_stats(x1[...])
        gb = acc[...]
        small_out[1:2, :] = jnp.sum(gb * scaled, axis=0, keepdims=True)
        gmid = grs[...] + norm_back(gb * gx[1:2, :], scaled, inv)
        gmid_out[...] = gmid
        low = gmid.astype(bf16)
        gm_out[...] = low
        ga_out[...] = dot(low, w_o[...]).astype(bf16)


def wgrad_kernel(sc, gr, h_a, h_b, b, gu, gm, o, ek, es, ck, cs, tile):
    j = pl.program_id(0)

    def emit(keep, send, first):
        for p, r in enumerate(rel_order(first)):
            keep[p, 0] = tile[rows_at(sc[0] ^ r, SUB), :].astype(bf16)
            send[p, 0] = tile[rows_at(sc[0] ^ (r + 1), SUB), :].astype(bf16)

    @pl.when(j < 4)
    def _():
        h = jnp.where(j < 1, h_a[...].astype(f32), h_b[...].astype(f32)).astype(bf16)
        tile[...] = dot(gr[...], h, TN)
        emit(ck, cs, 4)
        tile[...] = dot(b[...], gu[...], TN)
        emit(ek, es, 2)

    @pl.when(j == 4)
    def _():
        tile[...] = dot(gm[...], o[...], TN)
        emit(ek, es, 2)


def attn_back_kernel(sc, ql, of, do, kx, vx, g_out, dq, dk, dv):
    i = pl.program_id(0)
    nq = dk.shape[1] // BQ

    @pl.when(i == 0)
    def _():
        dk[...] = jnp.zeros_like(dk)
        dv[...] = jnp.zeros_like(dv)

    @pl.when(i < nq)
    def _():
        mine = rows_at(i, BQ)
        lane = lax.broadcasted_iota(jnp.int32, (BQ, 128), 1)
        dob, qb = [], []
        for h in range(NH):
            dof = do[0, :, h * HD : h * HD + HD].astype(f32)
            delta = jnp.sum(dof * of[:, h * HD : h * HD + HD], axis=1, keepdims=True)
            dox = jnp.concatenate([dof, jnp.zeros((BQ, HD), f32)], axis=1)
            for n, part in enumerate(splits(-delta, 3)):
                dox = jnp.where(lane == HD + n, part.astype(f32), dox)
            q = ql[h].astype(f32)
            k = kx[h, mine, :].astype(f32)
            v = vx[h, mine, :].astype(f32)
            free = k[:, 84:85]
            inner = (lane < HD) | ((lane >= 81) & (lane < 84))
            p = jnp.exp(jnp.sum(jnp.where(inner, q * k, 0.0), axis=1, keepdims=True)) * free
            ds = p * jnp.sum(jnp.where(lane < HD + 3, dox * v, 0.0), axis=1, keepdims=True)
            ds = ds.astype(bf16).astype(f32)
            dq[h, mine, :] = ds * k
            dk[h, mine, :] += ds * q
            dv[h, mine, :] += p.astype(bf16).astype(f32) * dox
            dob.append(dox.astype(bf16))
            qb.append(ql[h])

        def step(j, carry):
            ks = rows_at(j, BQ)
            pts = [jnp.exp(dot(kx[h, ks, :], qb[h], NT)) for h in range(NH)]
            dpts = [dot(vx[h, ks, :], dob[h], NT) for h in range(NH)]
            dsts = [(pts[h] * dpts[h]).astype(bf16) for h in range(NH)]
            for h in range(NH):
                dv[h, ks, :] += dot(pts[h].astype(bf16), dob[h])
                dk[h, ks, :] += dot(dsts[h], qb[h])
                dq[h, mine, :] += dot(dsts[h], kx[h, ks, :], TN)
            return carry

        lax.fori_loop(sc[8 + i], sc[16 + i], step, 0)

    @pl.when(i >= nq)
    def _():
        rows = rows_at(i - nq, TOK)
        g_out[...] = jnp.concatenate(
            [ref[h, rows, :][:, :HD] for ref in (dq, dk, dv) for h in range(NH)], axis=1
        )


def mix_kernel(sc, grad, xh, inv, a, gain, avg, *rest):
    refs = rest[:4]
    g_send, g_one, g_own, in_keep, in_send, qg_out, gin, w, sems = rest[4:]
    n = pl.program_id(0)

    @pl.when(n == 0)
    def _():
        copies = row_copies(refs, sc[4], w, sems, IN_REL)
        start(copies)
        gin[...] = jnp.zeros_like(gin)
        qg_out[...] = jnp.zeros_like(qg_out)
        wait(copies)

    grads = grad[:, :QK]
    scaled = xh[...]
    ones = avg[...]
    qg_out[0:1, :] += jnp.sum(grads * scaled, axis=0, keepdims=True)
    dg = grads * gain[0:1, :]
    back = inv[...] * (
        dg - dot_split(dg, ones, 2) - scaled * dot_split(dg * scaled, ones, 2)
    )
    mix = jnp.concatenate([back, grad[:, QK:]], axis=1).astype(bf16)
    out = dot(mix, w[...], NT).astype(bf16)
    gin[...] += dot(a[...], mix, TN)

    @pl.when(n < 2)
    def _():
        g_send[0] = out

    @pl.when(n == 2)
    def _():
        g_one[...] = out

    @pl.when(n == 3)
    def _():
        g_own[...] = out
        size = D // 4
        for p in range(2):
            in_keep[p] = gin[rows_at(sc[4] ^ (2 * p), size), :].astype(bf16)
            in_send[p] = gin[rows_at(sc[4] ^ (2 * p + 1), size), :].astype(bf16)


def add(x, y):
    return x.astype(f32) + y.astype(f32)


def split_kernel(count, *refs):
    ins, outs = refs[1 : 1 + 2 * count], refs[1 + 2 * count :]
    p = pl.program_id(0)
    total = pl.num_programs(0)
    for n in range(count):
        value = add(ins[2 * n][...], ins[2 * n + 1][...]).astype(bf16)

        @pl.when(p < total // 2)
        def _():
            outs[2 * n][...] = value

        @pl.when(p >= total // 2)
        def _():
            outs[2 * n + 1][...] = value


def z_parts_kernel(sc, up, up_r, down, down_r, z_out):
    for r in range(4):
        z_out[r, :, :D] = add(up[r], up_r[r]).astype(bf16)
        z_out[r, :, D : 2 * D] = add(down[r], down_r[r]).astype(bf16)
    out = add(up[4], up_r[4])
    width = D // 4
    out = xor_columns([out[:, n * width : (n + 1) * width] for n in range(4)], sc[2])
    for r in range(4):
        z_out[r, :, 2 * D :] = out[:, r * width : (r + 1) * width].astype(bf16)


def in_parts_kernel(sc, kept, got, a_out, b_out):
    half = a_out.shape[0]
    first = sc[5]
    mine, other = rows_at(first, half), rows_at(1 - first, half)
    a_out[...] = add(kept[mine, :], got[mine, :]).astype(bf16)
    b_out[...] = add(kept[other, :], got[other, :]).astype(bf16)


def share_kernel(sc, z0, z1, z2, z3, in_a, in_b, h_own, h_got,
                 up_o, down_o, out_o, in_o, head_o, sq_o):
    rows = up_o.shape[0]
    total = add(z0[0], z1[...]) + add(z2[...], z3[...])
    up_o[...] = total[:, :D]
    down_o[...] = total[:, D : 2 * D]
    out_o[...] = dot(total[:, 2 * D :], eye(rows, rows), TN, HIGH)
    grad = add(in_a[...], in_b[...])
    in_o[...] = jnp.concatenate(
        [
            grad[:, part * NH * HD + h * HD : part * NH * HD + h * HD + HD]
            for h in range(NH)
            for part in range(3)
        ],
        axis=1,
    )
    head = ordered(sc[2] % 2 == 1, h_own[...], h_got[...])
    head_o[...] = head[:, :CLASSES]
    squares = jnp.sum(total * total, keepdims=True) + jnp.sum(grad * grad, keepdims=True)
    once = jnp.where(sc[2] == 0, 1.0, 0.0)
    squares += once * jnp.sum(head * head, keepdims=True)
    sq_o[...] = jnp.broadcast_to(squares, sq_o.shape)


def patch_parts_kernel(sc, kept, got, out, tile):
    tile[...] = add(kept[0], got[0])
    size = out.shape[1]
    for r in range(4):
        out[r] = tile[rows_at(sc[2] ^ r, size), :].astype(bf16)


def patch_sum_kernel(sc, own, q1, q2, q3, sq, extra_row, out):
    size = own.shape[1]
    total = add(own[0], q1[...]) + add(q2[...], q3[...])
    out[...] = jnp.zeros_like(out)
    out[:size, :] = total
    squares = jnp.sum(total * total, keepdims=True) + sq[0:1, 0:1]
    lane = lax.broadcasted_iota(jnp.int32, (1, D + SMALL), 1)
    out[size : size + 1, :] = jnp.where(lane == 0, squares, extra_row[0:1, :])


def tail_kernel(n_dp, sc, g_own, g_core, g_z, gmid, x0, gx, own, other, hot, small_b, qgrad,
                pk, ps, tile):
    grad = g_own[...].astype(f32) + g_core[0].astype(f32) + g_z[...].astype(f32)
    scaled, inv = norm_stats(x0[...])
    gain_a = jnp.sum(grad * scaled, axis=0, keepdims=True)
    ge = (gmid[...] + norm_back(grad * gx[0:1, :], scaled, inv)).astype(bf16)
    rows = jnp.where(sc[3] == 1, own[...], other[...])
    tile[:, :D] = dot(rows, ge, TN)
    row8 = lax.broadcasted_iota(jnp.int32, (8, D), 0)
    gains = jnp.where(row8 == 0, gain_a, small_b[...])
    small = dot(ge, hot[...], TN) + dot(gains, eye(8, SMALL, LANE_GAIN), TN)
    part = HD // n_dp
    kk = lax.broadcasted_iota(jnp.int32, (HD, D), 0)
    rr = lax.broadcasted_iota(jnp.int32, (HD, D), 1)
    spot = ((kk // part) * (D // n_dp) + kk % part == rr).astype(f32)
    lane = lax.broadcasted_iota(jnp.int32, (8, SMALL), 1)
    row = lax.broadcasted_iota(jnp.int32, (8, SMALL), 0)
    q_lane = ((lane == LANE_QG + row) & (row < 2)).astype(f32)
    q_cols = dot(qgrad[...], q_lane, TN, HIGH)
    small += dot(spot, q_cols, TN)
    tile[:, D:] = small
    for p, r in enumerate(rel_order(2)):
        pk[p] = tile[rows_at(sc[0] ^ r, SUB), :].astype(bf16)
        ps[p] = tile[rows_at(sc[0] ^ (r + 1), SUB), :].astype(bf16)


def update_kernel(stats, *rest):
    shares = rest[:6]
    state = rest[6:33]
    head_out, outs = rest[33], rest[34:]
    total = stats[0:1, :]
    norm = jnp.sqrt(total)
    head_out[...] = jnp.where(
        lax.broadcasted_iota(jnp.int32, (8, 128), 1) == 0, norm, total
    )
    factor = jnp.minimum(1.0, CLIP / (norm[:, 0:1] + 1e-06))
    s_in, s_out, s_up, s_down, s_patch, s_head = shares
    rows = s_patch.shape[0]
    small = dot(eye(SMALL, SMALL), s_patch[:, D:], NT, HIGH)
    part = state[24].shape[1]
    grads = [
        s_in[...],
        s_out[...],
        s_up[...],
        s_down[...],
        s_patch[:, :D],
        small[: 2 * GRID, :],
        s_head[...],
        small[LANE_GAIN : LANE_GAIN + 4, :],
        small[LANE_QG : LANE_QG + 2, :part],
    ]
    for n in range(9):
        master, first, second = state[3 * n : 3 * n + 3]
        clipped = grads[n] * factor
        first_new = BETA_ONE * first[...] + (1.0 - BETA_ONE) * clipped
        second_new = BETA_TWO * second[...] + (1.0 - BETA_TWO) * clipped * clipped
        matrix = n in (0, 1, 2, 3, 4, 6)
        rate = RATE_MATRIX if matrix else RATE_SMALL
        decay = DECAY if matrix else 0.0
        ratio = (
            first_new
            / (1.0 - BETA_ONE**STEP)
            / (jnp.sqrt(second_new / (1.0 - BETA_TWO**STEP)) + ADAM_EPS)
        )
        value = master[...]
        outs[3 * n][...] = value - rate * (ratio + decay * value)
        outs[3 * n + 1][...] = first_new
        outs[3 * n + 2][...] = second_new


ANY = pl.BlockSpec(memory_space=pl.ANY)


def without(kernel, count, deps):
    if not deps:
        return kernel
    return lambda *refs: kernel(*refs[:count], *refs[count + len(deps) :])


def call(kernel, grid, sc, ins, specs, outs, out_specs, scratch, us=5, deps=()):
    return pl.pallas_call(
        without(kernel, 1 + len(ins), deps),
        out_shape=outs,
        grid_spec=pltpu.PrefetchScalarGridSpec(
            num_scalar_prefetch=1,
            grid=grid,
            in_specs=list(specs) + [ANY] * len(deps),
            out_specs=out_specs,
            scratch_shapes=scratch,
        ),
        compiler_params=pltpu.CompilerParams(vmem_limit_bytes=VLIM),
        cost_estimate=pl.CostEstimate(
            flops=int(us * 1.15e9), bytes_accessed=1000000, transcendentals=0
        ),
    )(sc, *ins, *deps)


def flat_call(kernel, sc, ins, outs, scratch=(), us=3, deps=()):
    return call(
        kernel,
        (1,),
        sc,
        ins,
        [whole(x.shape) for x in ins],
        outs,
        tuple(whole(o.shape) for o in outs),
        list(scratch),
        us,
        deps,
    )


def simple_call(kernel, ins, outs, us=3, deps=()):
    return pl.pallas_call(
        without(kernel, len(ins), deps),
        out_shape=outs,
        in_specs=[pl.BlockSpec(memory_space=pltpu.VMEM)] * len(ins) + [ANY] * len(deps),
        compiler_params=pltpu.CompilerParams(vmem_limit_bytes=VLIM),
        cost_estimate=pl.CostEstimate(
            flops=int(us * 1.15e9), bytes_accessed=1000000, transcendentals=0
        ),
    )(*ins, *deps)


def whole(shape):
    return pl.BlockSpec(shape, lambda i, s: (0,) * len(shape))


def sds(shape, dtype):
    return jax.ShapeDtypeStruct(shape, dtype)


DMA = pltpu.SemaphoreType.DMA


def make_local(n_dp, n_mp):
    extra = n_dp // 8
    masks = [extra, 2 * extra, 4 * extra]
    low_bits = [b for b in (1, 2, 4, 8, 16, 32) if b < extra]
    col_low = [2 * b for b in low_bits]
    col_masks = [2 * extra, 4 * extra]

    def pp(x, dmask, zmask=0):
        perm = [
            (d * n_mp + z, (d ^ dmask) * n_mp + (z ^ zmask))
            for d in range(n_dp)
            for z in range(n_mp)
        ]
        return lax.ppermute(x, ("dp", "mp"), perm)

    def local(patches, segment, keep, pos_y, pos_x, labels, bucket, *state):
        masters = state[0::3]
        (attend_in, attend_out, expand, contract, patch_embed, pos_table, class_head,
         norm_gains, query_gains) = masters
        length = patches.shape[0]
        rows = patch_embed.shape[0]
        nq = length // BQ
        dp = lax.axis_index("dp")
        z = lax.axis_index("mp")
        core = dp % 2
        z1, z0 = z // 2, z % 2
        g = z0 + 2 * core
        me = dp // extra
        mecol = (dp // 2) // extra
        mine = core == z1

        def bit_of(mask):
            return (dp // mask) % 2 == 1

        def swap(flag, x, y, axis):
            return jnp.where(
                flag, jnp.concatenate([y, x], axis=axis), jnp.concatenate([x, y], axis=axis)
            )

        def pick4(parts, index, axis):
            odd, high = index % 2 == 1, index // 2 == 1
            lo = swap(odd, parts[0], parts[1], axis)
            hi = swap(odd, parts[2], parts[3], axis)
            return swap(high, lo, hi, axis)

        own_kept = (keep == 1) & (segment < IMG)
        own_valid = jnp.any(
            (segment[None, :] == jnp.arange(IMG)[:, None]) & own_kept[None, :], axis=1
        )
        lanes = jnp.arange(SMALL)
        cnt = jnp.where(lanes == bucket[0] + LANE_COUNT, jnp.sum(own_valid.astype(f32)), 0.0)
        cnt = jnp.pad(cnt[None, :], ((0, 7), (0, 0)))
        patch_w, in_w, z_w, out_w = simple_call(
            pack_kernel,
            [attend_in, attend_out, expand, contract.T, patch_embed, pos_table, norm_gains,
             query_gains, cnt],
            (
                sds((rows, D + SMALL), bf16),
                sds((rows, 576), bf16),
                sds((2, rows, D), bf16),
                sds((rows, 192), bf16),
            ),
        )

        perm_core = [
            (d * n_mp + zz, (d ^ 1) * n_mp + zz)
            for d in range(n_dp)
            for zz in range(n_mp)
            if d % 2 == zz // 2
        ]
        patches_in = lax.ppermute(patches, ("dp", "mp"), perm_core)
        meta = jnp.stack([segment, keep, pos_y, pos_x])
        tag = jnp.concatenate([labels, bucket, jnp.zeros((length - IMG - 1,), jnp.int32)])
        meta = jnp.concatenate([meta, tag[None]], axis=0)
        meta = jnp.where(mine, meta, lax.ppermute(meta, ("dp", "mp"), perm_core))

        def widen(x, low):
            for b in low:
                x = swap(bit_of(b), x, pp(x, b), -2)
            return x

        def direct8(x):
            chips = [x] + [pp(x, m) for m in (masks[1], masks[2], masks[1] | masks[2])]
            return chips + [pp(y, masks[0]) for y in chips]

        patch_p = direct8(widen(patch_w, low_bits))

        perm_a, perm_b, back_b = [], [], []
        for d in range(n_dp):
            for zz in range(n_mp):
                c, a1, a0 = d % 2, zz // 2, zz % 2
                src = d * n_mp + zz
                perm_a.append((src, (d - c + a1) * n_mp + a0 + 2 * c))
                perm_b.append((src, (d - c + a1) * n_mp + a0 + 2 * (1 - c)))
                back_b.append((src, (d - c + 1 - a1) * n_mp + a0 + 2 * c))
        in_a = lax.ppermute(in_w, ("dp", "mp"), perm_a)
        in_b = lax.ppermute(in_w, ("dp", "mp"), perm_b)
        in_own = widen(swap(z1 == 1, in_a, in_b, 0), col_low)
        in_p = [in_own] + [pp(in_own, m) for m in (col_masks[0], col_masks[1], col_masks[0] | col_masks[1])]
        out_z = [out_w, pp(out_w, 0, 1), pp(out_w, 0, 2), pp(out_w, 0, 3)]
        z_in = [pp(z_w, 0, r) for r in (1, 2, 3)]

        seg, kp, py, px = meta[0], meta[1], meta[2], meta[3]
        labs = meta[4, :IMG]
        buck = meta[4, IMG]
        kept = (kp == 1) & (seg < IMG)
        ids = jnp.arange(128)[None, :]
        ids64 = ids[:, :64]
        hot_pos = ((py[:, None] == ids) | (px[:, None] + GRID == ids)).astype(bf16)
        match = seg[:, None] == ids64
        qaux = jnp.where((ids64 < IMG) & match, BIG, jnp.where(ids64 == IMG, 1.0, 0.0)).astype(bf16)
        kaux = jnp.where(
            (ids64 < IMG) & match & kept[:, None],
            1.0,
            jnp.where(
                ids64 == IMG,
                -BIG,
                jnp.where(
                    (ids64 > IMG) & (ids64 < IMG + 4),
                    1.0,
                    jnp.where((ids64 == IMG + 4) & ~kept[:, None], 1.0, 0.0),
                ),
            ),
        ).astype(bf16)
        vaux = jnp.broadcast_to(jnp.where(jnp.arange(64) < 3, 1.0, 0.0).astype(bf16), (TOK, 64))
        first_seg, last_seg = seg[::BQ], jnp.minimum(seg[BQ - 1 :: BQ], IMG - 1)
        lo = jnp.sum((seg[None, :] < first_seg[:, None]).astype(jnp.int32), axis=1) // BQ
        hi = (jnp.sum((seg[None, :] <= last_seg[:, None]).astype(jnp.int32), axis=1) + BQ - 1) // BQ
        sc = jnp.concatenate(
            [
                jnp.stack([me, g, z, mine.astype(jnp.int32), mecol, z1, z1, z1]),
                lo,
                hi,
            ]
        ).astype(jnp.int32)
        own_seg = lax.dynamic_slice_in_dim(seg, g * TOK, TOK, 0)
        own_kp = lax.dynamic_slice_in_dim(kept, g * TOK, TOK, 0)
        mem = (
            (own_seg[:, None] == jnp.arange(IMG)[None, :]) & own_kp[:, None]
        ).astype(bf16)
        valid = jnp.max(
            ((seg[None, :] == jnp.arange(IMG)[:, None]) & kept[None, :]).astype(f32), axis=1
        )
        lab_hot = (labs[:, None] == jnp.arange(CPAD)[None, :]).astype(f32)
        block = jnp.arange(QK) // HD
        avg = jnp.where(block[:, None] == block[None, :], 1.0 / HD, 0.0).astype(bf16)
        heads = (jnp.arange(D)[:, None] // HD == ids).astype(bf16)

        nt = length // TOK
        f_w = flat_call(
            first_kernel,
            sc,
            [z_w] + out_z + [class_head],
            (sds((rows, 3 * D + CPAD), bf16),),
            us=2,
            deps=patch_p[1:4],
        )[0]
        f_p = direct8(widen(f_w, low_bits))
        a, x0, gx = call(
            x0_kernel,
            (nt,),
            sc,
            [patches, patches_in, hot_pos] + patch_p,
            [
                pl.BlockSpec((TOK, D), lambda i, s: (jnp.where(s[3] == 1, i, 0), 0)),
                pl.BlockSpec((TOK, D), lambda i, s: (jnp.where(s[3] == 1, 0, i), 0)),
                pl.BlockSpec((TOK, 128), lambda i, s: (i, 0)),
            ]
            + [ANY] * 8,
            (sds((length, D), bf16), sds((TOK, D), f32), sds((16, D), f32)),
            (pl.BlockSpec((TOK, D), lambda i, s: (i, 0)), whole((TOK, D)), whole((16, D))),
            [pltpu.VMEM((D, D + SMALL), bf16), DMA((8,))],
            10,
            deps=[f_w],
        )
        g_w = simple_call(
            second_kernel, z_in, sds((6, rows, D), bf16), 2, deps=[a]
        )
        g_p = direct8(widen(g_w, low_bits))
        qcols = query_gains.shape[1]
        counts = jnp.sum(gx[LANE_COUNT - LANE_GAIN : LANE_COUNT - LANE_GAIN + NB], axis=1)
        image_total = jnp.sum(counts)
        qg = gx[4:6].reshape(2, n_dp, rows)[:, :, :qcols].reshape(2, 1, HD)
        gain = jnp.tile(qg * jnp.array([0.125, 1.0], f32)[:, None, None], (1, NH, 1))
        gain = jnp.pad(gain.reshape(1, QK), ((0, 7), (0, 0)))
        vt = jnp.stack([valid, valid / image_total], axis=1)
        vt = jnp.pad(vt, ((0, 0), (0, 126)))

        row_block = lambda width: pl.BlockSpec((TOK, width), lambda i, s: (i, 0))
        head_block = pl.BlockSpec((NH, TOK, 128), lambda i, s: (0, i, 0))
        qx, kx, vx, xh, inv = call(
            qkv_kernel,
            (nt,),
            sc,
            [a, qaux, kaux, vaux, gain, avg] + in_p,
            [row_block(D), row_block(64), row_block(64), whole((TOK, 64)), whole((8, QK)),
             whole((QK, QK))]
            + [ANY] * 4,
            tuple([sds((NH, length, 128), bf16)] * 3 + [sds((length, QK), f32)] * 2),
            tuple([head_block] * 3 + [row_block(QK)] * 2),
            [pltpu.VMEM((D, 576), bf16), DMA((4,))],
            10,
            deps=[g_w],
        )
        per_tok = TOK // BQ
        o_rel, o_full, ql = call(
            attn_kernel,
            (nq,),
            sc,
            [qx, kx, vx],
            [
                pl.BlockSpec((NH, BQ, 128), lambda i, s: (0, i, 0)),
                whole((NH, length, 128)),
                whole((NH, length, 128)),
            ],
            (
                sds((4, TOK, NH * HD), bf16),
                sds((length, NH * HD), f32),
                sds((NH, length, 128), bf16),
            ),
            (
                pl.BlockSpec(
                    (1, BQ, NH * HD), lambda i, s: (s[1] ^ (i // per_tok), i % per_tok, 0)
                ),
                pl.BlockSpec((BQ, NH * HD), lambda i, s: (i, 0)),
                pl.BlockSpec((NH, BQ, 128), lambda i, s: (0, i, 0)),
            ),
            [pltpu.VMEM((NH, BQ, 128), f32)],
            20,
        )

        def trade(parts):
            return [parts[0], pp(parts[1], 0, 1), pp(parts[2], 1, 0), pp(parts[3], 1, 1)]

        o_cat = pick4(trade([o_rel[r] for r in range(4)]), g, 1)
        tile_spec = pl.BlockSpec((TOK, D), lambda j, s: (0, j))
        x1, b, u_a, h_a, acc = call(
            mlp_one_kernel,
            (1,),
            sc,
            [o_cat, x0, gx] + f_p,
            [whole((TOK, D)), whole((TOK, D)), whole((16, D))] + [ANY] * 8,
            (
                sds((TOK, D), f32),
                sds((TOK, D), bf16),
                sds((TOK, D), f32),
                sds((TOK, D), bf16),
                sds((TOK, D), f32),
            ),
            tuple([whole((TOK, D))] * 5),
            [pltpu.VMEM((D, D), bf16), pltpu.VMEM((2, D, D), bf16), DMA((8,)), DMA((2, 8))],
            10,
        )
        u_b, h_b, x2, ns = call(
            mlp_two_kernel,
            (3,),
            sc,
            [b, acc, gx, mem, heads] + g_p,
            [whole((TOK, D)), whole((TOK, D)), whole((16, D)), whole((TOK, IMG)), whole((D, 128))]
            + [ANY] * 8,
            (
                sds((TOK, 3 * D), f32),
                sds((TOK, 3 * D), bf16),
                sds((TOK, D), f32),
                sds((IMG, D + 128), f32),
            ),
            (tile_spec, tile_spec, whole((TOK, D)), whole((IMG, D + 128))),
            [pltpu.VMEM((3, 2, D, D), bf16), DMA((3, 2, 8))],
            13,
        )
        ns = ns + pp(ns, 1, 0)
        half_shape = (4, SUB, CPAD // 2)
        pooled, gp, sinv, loss, gh, gh_send = call(
            head_kernel,
            (1,),
            sc,
            [ns, pp(ns, 0, 1), lab_hot, vt, heads] + f_p,
            [whole((IMG, D + 128))] * 2
            + [whole((IMG, CPAD)), whole((IMG, 128)), whole((D, 128))]
            + [ANY] * 8,
            (
                sds((IMG, D), f32),
                sds((IMG, D), f32),
                sds((IMG, 128), f32),
                sds((IMG, 128), f32),
                sds(half_shape, bf16),
                sds(half_shape, bf16),
            ),
            (
                whole((IMG, D)),
                whole((IMG, D)),
                whole((IMG, 128)),
                whole((IMG, 128)),
                whole(half_shape),
                whole(half_shape),
            ),
            [pltpu.VMEM((D, CPAD), bf16), pltpu.VMEM((D, CPAD // 2), f32), DMA((8,))],
            5,
        )

        low_spec = whole((TOK, D))
        high_spec = pl.BlockSpec((TOK, D), lambda j, s: (0, jnp.clip(j - 1, 0, 2)))
        gu, gr, gm, gmid, ga, small_b = call(
            back_kernel,
            (4,),
            sc,
            [u_a, u_b, x2, x1, gx, mem, pooled, gp, sinv, heads]
            + f_p + g_p,
            [
                low_spec,
                high_spec,
                whole((TOK, D)),
                whole((TOK, D)),
                whole((16, D)),
                whole((TOK, IMG)),
                whole((IMG, D)),
                whole((IMG, D)),
                whole((IMG, 128)),
                whole((D, 128)),
            ]
            + [ANY] * 16,
            (
                sds((TOK, HID), bf16),
                sds((TOK, D), bf16),
                sds((TOK, D), bf16),
                sds((TOK, D), f32),
                sds((TOK, D), bf16),
                sds((8, D), f32),
            ),
            (
                tile_spec,
                whole((TOK, D)),
                whole((TOK, D)),
                whole((TOK, D)),
                whole((TOK, D)),
                whole((8, D)),
            ),
            [
                pltpu.VMEM((4, 2, D, D), bf16),
                pltpu.VMEM((D, D), bf16),
                pltpu.VMEM((TOK, D), f32),
                pltpu.VMEM((TOK, D), f32),
                DMA((4, 2, 8)),
                DMA((8,)),
            ],
            20,
        )
        ga4 = [ga[:, n * NH * HD : (n + 1) * NH * HD][None] for n in range(4)]
        ga_rel = pick4(ga4, g, 0)
        do = pick4([t[None] for t in trade([ga_rel[r] for r in range(4)])], g, 0)

        up_block = pl.BlockSpec((4, 1, SUB, D), lambda j, s: (0, j, 0, 0))
        down_block = pl.BlockSpec((4, 1, SUB, D), lambda j, s: (0, jnp.minimum(j, 3), 0, 0))
        ek, es, ck, cs = call(
            wgrad_kernel,
            (5,),
            sc,
            [gr, h_a, h_b, b, gu, gm, o_cat],
            [
                whole((TOK, D)),
                low_spec,
                high_spec,
                whole((TOK, D)),
                pl.BlockSpec((TOK, D), lambda j, s: (0, jnp.minimum(j, 3))),
                whole((TOK, D)),
                whole((TOK, D)),
            ],
            tuple([sds((4, 5, SUB, D), bf16)] * 2 + [sds((4, 4, SUB, D), bf16)] * 2),
            (up_block, up_block, down_block, down_block),
            [pltpu.VMEM((D, D), f32)],
            14,
        )

        def low_rows(x, low):
            for b in reversed(low):
                half = x.shape[-2] // 2
                first, second = x[..., :half, :], x[..., half:, :]
                flag = bit_of(b)
                send = jnp.where(flag, first, second)
                stay = jnp.where(flag, second, first)
                x = add(stay, pp(send.astype(bf16), b))
            return x

        def scatter4(stay, low, m1, m2):
            x = add(stay[:2], pp(stay[2:].astype(bf16), m1))
            x = add(x[0].astype(bf16), pp(x[1].astype(bf16), m2))
            return low_rows(x, low)

        def core_sum(stay, send):
            return add(stay, pp(send, masks[0])).astype(bf16)

        def chip_sum(x, first):
            m1, m2 = (masks[1], masks[2]) if first == 2 else (masks[2], masks[1])
            return scatter4(x, low_bits, m1, m2)

        if extra == 1:
            gh = chip_sum(gh, 2)
        else:
            gh = 0.5 * chip_sum(core_sum(gh, gh_send), 2)
        gh = add(gh.astype(bf16), pp(gh.astype(bf16), 0, 2))

        def halves(pairs, us, deps=()):
            count = pairs[0][0].shape[0]
            half = count // 2
            ins, specs, outs, out_specs = [], [], [], []
            for kept, got in pairs:
                shape = kept.shape[1:]
                block = (1,) + shape
                tail = (0,) * len(shape)
                ins += [kept, got]
                specs += [pl.BlockSpec(block, lambda p, s, tail=tail: (p,) + tail)] * 2
                outs += [sds((half,) + shape, bf16)] * 2
                out_specs += [
                    pl.BlockSpec(block, lambda p, s, tail=tail: (jnp.minimum(p, half - 1),) + tail),
                    pl.BlockSpec(block, lambda p, s, tail=tail: (jnp.maximum(p - half, 0),) + tail),
                ]
            n = len(pairs)
            out = call(
                lambda *refs: split_kernel(n, *refs), (count,), sc, ins, specs, tuple(outs),
                tuple(out_specs), [], us, deps,
            )
            return [(out[2 * i], out[2 * i + 1]) for i in range(n)]

        (uk, us_), (vk, vs) = halves([(ek, pp(es, masks[0])), (ck, pp(cs, masks[0]))], 5)
        us_got, vs_got = pp(us_, masks[1]), pp(vs, masks[2])

        last = nq - 1
        grads = call(
            attn_back_kernel,
            (nq + nt,),
            sc,
            [ql, o_full, do, kx, vx],
            [
                pl.BlockSpec((NH, BQ, 128), lambda i, s: (0, jnp.minimum(i, last), 0)),
                pl.BlockSpec((BQ, NH * HD), lambda i, s: (jnp.minimum(i, last), 0)),
                pl.BlockSpec(
                    (1, BQ, NH * HD),
                    lambda i, s: (
                        jnp.minimum(i, last) // per_tok,
                        jnp.minimum(i, last) % per_tok,
                        0,
                    ),
                ),
                whole((NH, length, 128)),
                whole((NH, length, 128)),
            ],
            (sds((length, 576), f32),),
            (pl.BlockSpec((TOK, 576), lambda i, s: (jnp.maximum(i - nq, 0), 0)),),
            [
                pltpu.VMEM((NH, length, 128), f32),
                pltpu.VMEM((NH, length, 128), f32),
                pltpu.VMEM((NH, length, 128), f32),
            ],
            35,
            deps=[us_, vs],
        )[0]
        (uk2, us2), (vk2, vs2) = halves([(uk, us_got), (vk, vs_got)], 4, deps=[grads])
        us2_got, vs2_got = pp(us2, masks[2]), pp(vs2, masks[1])
        rel_tok = lambda n, s: s[1] ^ jnp.where(n < 2, n + 2, 3 - n)
        tok_block = lambda width: pl.BlockSpec((TOK, width), lambda n, s: (rel_tok(n, s), 0))
        in_shape = (2, D // 4, 576)
        g_send, g_one, g_own, in_keep, in_send, qgrad = call(
            mix_kernel,
            (nt,),
            sc,
            [grads, xh, inv, a, gain, avg] + in_p,
            [tok_block(576), tok_block(QK), tok_block(QK), tok_block(D), whole((8, QK)),
             whole((QK, QK))]
            + [ANY] * 4,
            (
                sds((2, TOK, D), bf16),
                sds((TOK, D), bf16),
                sds((TOK, D), bf16),
                sds(in_shape, bf16),
                sds(in_shape, bf16),
                sds((8, QK), f32),
            ),
            (
                pl.BlockSpec((1, TOK, D), lambda n, s: (jnp.minimum(n, 1), 0, 0)),
                whole((TOK, D)),
                whole((TOK, D)),
                whole(in_shape),
                whole(in_shape),
                whole((8, QK)),
            ),
            [pltpu.VMEM((D, 576), f32), pltpu.VMEM((D, 576), bf16), DMA((4,))],
            14,
            deps=[us2, vs2],
        )
        g_core = pp(g_send, 1)
        g_z = pp(add(g_one, g_core[1]).astype(bf16), 0, 1)

        in_got = pp(in_send, col_masks[0])
        if extra == 1:
            z_ins = [uk2[0], us2_got[0], vk2[0], vs2_got[0]]
        else:
            up = low_rows(add(uk2[0], us2_got[0]), low_bits).astype(bf16)
            down = low_rows(add(vk2[0], vs2_got[0]), low_bits).astype(bf16)
            z_ins = [up, jnp.zeros_like(up), down, jnp.zeros_like(down)]
        z_out = flat_call(
            z_parts_kernel, sc, z_ins, (sds((4, rows, 2 * D + 192), bf16),), us=4, deps=[g_core]
        )[0]
        z_got = [pp(z_out[r], 0, r) for r in (1, 2, 3)]
        (ik, is_), = halves([(in_keep, in_got)], 2, deps=[z_out])
        is_got = pp(is_, col_masks[1])

        qg_rows = qgrad[0].reshape(2, NH, HD).sum(axis=1) * jnp.array([0.125, 1.0], f32)[:, None]
        qg_rows = jnp.pad(qg_rows, ((0, 6), (0, 0)))
        hot_own = pl.BlockSpec((TOK, 128), lambda i, s: (s[1], 0))
        own_rows = pl.BlockSpec((TOK, D), lambda i, s: (s[1], 0))

        def tail_body(*refs):
            tail_kernel(n_dp, *refs)

        pk, ps = call(
            tail_body,
            (1,),
            sc,
            [g_own, g_core, g_z, gmid, x0, gx, patches, patches_in, hot_pos, small_b, qg_rows],
            [
                whole((TOK, D)),
                pl.BlockSpec((1, TOK, D), lambda i, s: (0, 0, 0)),
                whole((TOK, D)),
                whole((TOK, D)),
                whole((TOK, D)),
                whole((16, D)),
                own_rows,
                own_rows,
                hot_own,
                whole((8, D)),
                whole((8, HD)),
            ],
            (sds((4, SUB, D + SMALL), bf16), sds((4, SUB, D + SMALL), bf16)),
            (whole((4, SUB, D + SMALL)), whole((4, SUB, D + SMALL))),
            [pltpu.VMEM((D, D + SMALL), f32)],
            6,
            deps=[is_],
        )
        (pk1, ps1), = halves([(pk, pp(ps, masks[0]))], 2)
        ps1_got = pp(ps1, masks[1])
        if extra == 1:
            in_a, in_b = flat_call(
                in_parts_kernel, sc, [ik[0], is_got[0]], (sds((rows, 576), bf16),) * 2, us=2,
                deps=[ps1],
            )
        else:
            both = low_rows(add(ik[0], is_got[0]), col_low).astype(bf16).reshape(2, rows, 576)
            in_a = jnp.where(z1 == 1, both[1], both[0])
            in_b = jnp.where(z1 == 1, both[0], both[1])
        in_a = lax.ppermute(in_a, ("dp", "mp"), perm_a)
        in_b = lax.ppermute(in_b, ("dp", "mp"), back_b)
        (pk2, ps2), = halves([(pk1, ps1_got)], 2)
        ps2_got = pp(ps2, masks[2])
        s_up, s_down, s_out, s_in, s_head, sq = flat_call(
            share_kernel,
            sc,
            [z_out] + z_got + [in_a, in_b, gh, pp(gh, 0, 1)],
            (
                sds((rows, D), f32),
                sds((rows, D), f32),
                sds((192, rows), f32),
                sds((rows, 576), f32),
                sds((rows, CLASSES), f32),
                sds((8, 128), f32),
            ),
            us=4,
            deps=[ps2],
        )
        quarter = rows // 4
        if rows % 32 == 0:
            rel = flat_call(
                patch_parts_kernel, sc, [pk2, ps2_got], (sds((4, quarter, D + SMALL), bf16),),
                [pltpu.VMEM((rows, D + SMALL), f32)], 2, deps=[sq],
            )[0]
        else:
            rel = low_rows(add(pk2[0], ps2_got[0]), low_bits).astype(bf16)
            rel = rel.reshape(4, quarter, D + SMALL)
            rel = pick4([rel[n : n + 1] for n in range(4)], z, 0)
        q_got = [pp(rel[r], 0, r) for r in (1, 2, 3)]

        wide = jnp.arange(D + SMALL)
        extra_row = jnp.where((wide == buck + 1) & (g == 0), jnp.sum(loss[:, 0]), 0.0)
        extra_row = jnp.broadcast_to(extra_row[None, :], (8, D + SMALL))
        mine_q = flat_call(
            patch_sum_kernel, sc, [rel] + q_got + [sq, extra_row],
            (sds((quarter + 8, D + SMALL), f32),), us=2,
        )[0]
        around = [mine_q, pp(mine_q, 0, 1), pp(mine_q, 0, 2), pp(mine_q, 0, 3)]
        stats = [q[quarter : quarter + 1, :SMALL] for q in around]
        stats = (stats[0] + stats[1]) + (stats[2] + stats[3])
        stats = jnp.broadcast_to(stats, (8, SMALL))
        stats = stats + pp(stats, 1)
        m = 2
        while m < n_dp:
            stats = (stats + pp(stats, m)) + (pp(stats, 2 * m) + pp(stats, 3 * m))
            m *= 4
        share_patch = pick4([q[:quarter] for q in around], z, 0)

        shares = [s_in, s_out, s_up, s_down, share_patch, s_head]
        turned = [x.T if n // 3 == 3 else x for n, x in enumerate(state)]
        news = simple_call(
            update_kernel,
            [stats] + shares + turned,
            tuple([sds((8, 128), f32)] + [sds(s.shape, f32) for s in turned]),
            6,
        )
        top = news[0]
        outs = [x.T if n // 3 == 3 else x for n, x in enumerate(news[1:])]
        return (top[0, 1 : 1 + NB], counts, top[0, 0]) + tuple(outs)

    return local


def solution(mesh):
    shard = {
        "in": P("dp", "mp"),
        "out": P("mp", "dp"),
        "row": P("dp", None),
        "col": P(None, "dp"),
    }
    kinds = ["in", "out", "in", "out", "row", "col", "row", "col", "col"]
    triples = tuple(shard[k] for k in kinds for _ in range(3))
    in_specs = (P("dp", None),) + (P("dp"),) * 6 + triples
    out_specs = (P(), P(), P()) + triples
    return jax.shard_map(
        make_local(mesh.shape["dp"], mesh.shape["mp"]),
        mesh=mesh,
        in_specs=in_specs,
        out_specs=out_specs,
        check_vma=False,
    )
```

```python
import jax
import jax.numpy as jnp
from jax import lax
from jax.experimental import pallas as pl
from jax.experimental.pallas import tpu as pltpu
from jax.sharding import PartitionSpec as P

D = 768
HD = 64
HID = 3072
CLASSES = 1000
CPAD = 1024
GRID = 32
IMG = 16
NB = 4
STEP = 10
BQ = 256
TOK = 512
NH = 3
QK = 2 * NH * HD
SUB = D // 8
SMALL = 128
OW = 256
HEAD_AT = 4 * OW
LANE_GAIN = 64
LANE_QG = 68
LANE_COUNT = 72

HIGH = lax.Precision.HIGHEST
NORM_EPS = 1e-06
CLIP = 0.1
BETA_ONE = 0.9
BETA_TWO = 0.95
RATE_MATRIX = 0.05
RATE_SMALL = 0.2
DECAY = 0.05
ADAM_EPS = 1e-08
BIG = 128.0

bf16 = jnp.bfloat16
f32 = jnp.float32
VLIM = 56 * 1024 * 1024
COST = 0.1 * 1.15e9

NN = (((1,), (0,)), ((), ()))
NT = (((1,), (1,)), ((), ()))
TN = (((0,), (0,)), ((), ()))


def dot(a, b, dims=NN, precision=None):
    return lax.dot_general(a, b, dims, precision=precision, preferred_element_type=f32)


def norm_stats(values):
    center = values - jnp.mean(values, axis=-1, keepdims=True)
    inv_std = lax.rsqrt(jnp.mean(center * center, axis=-1, keepdims=True) + NORM_EPS)
    return center * inv_std, inv_std


def norm_back(grad_scaled, scaled, inv_std):
    return inv_std * (
        grad_scaled
        - jnp.mean(grad_scaled, axis=-1, keepdims=True)
        - scaled * jnp.mean(grad_scaled * scaled, axis=-1, keepdims=True)
    )


def splits(x, n):
    out = []
    for _ in range(n - 1):
        part = x.astype(bf16)
        out.append(part)
        x = x - part.astype(f32)
    out.append(x.astype(bf16))
    return out


def dot_split(x, exact, n, dims=NN):
    total = None
    for part in splits(x, n):
        term = dot(part, exact, dims)
        total = term if total is None else total + term
    return total


def head_mean(x, ones, n):
    return jnp.concatenate(
        [dot_split(x[:, c : c + 128], ones, n) for c in range(0, QK, 128)], axis=1
    )


def eye(rows, cols, offset=0):
    row = lax.broadcasted_iota(jnp.int32, (rows, cols), 0)
    col = lax.broadcasted_iota(jnp.int32, (rows, cols), 1)
    return (row + offset == col).astype(f32)


def rows_at(index, size):
    return pl.ds(pl.multiple_of(index * size, size), size)


def pack_kernel(w_patch, w_pos, w_gain, w_qg, seg, keep, bucket, w_in, w_out, w_up, w_down,
                patch_o, in_o, t_o, out_o):
    rows = w_patch.shape[0]
    patch_o[:, :D] = w_patch[...].astype(bf16)
    low = lambda ref: ref[...].astype(bf16).astype(f32)
    small = dot(low(w_pos), eye(64, SMALL), TN)
    small += dot(low(w_gain), eye(4, SMALL, LANE_GAIN), TN)
    qg = dot(low(w_qg), eye(2, SMALL, LANE_QG), TN)
    small += dot(eye(rows, qg.shape[0]), qg)
    kept = keep[...] == 1
    count = jnp.zeros((1, 1), f32)
    for n in range(IMG):
        held = jnp.where((seg[...] == n) & kept, 1.0, 0.0)
        count += jnp.max(held, keepdims=True)
    row = lax.broadcasted_iota(jnp.int32, (rows, SMALL), 0)
    col = lax.broadcasted_iota(jnp.int32, (rows, SMALL), 1)
    small += jnp.where((row == 0) & (col == LANE_COUNT + bucket[0]), count, 0.0)
    patch_o[:, D:] = small.astype(bf16)

    w = w_in[...].astype(bf16)
    parts = [
        w[:, h * 192 + part * HD : h * 192 + part * HD + HD]
        for part in range(3)
        for h in range(NH)
    ]
    in_o[...] = jnp.concatenate(parts, axis=1)
    t_o[:, :D] = w_up[...].astype(bf16)
    t_o[:, D:] = w_down[...].astype(bf16)
    turned = dot(eye(rows, rows).astype(bf16), w_out[...].astype(bf16), NT)
    out_o[...] = jnp.concatenate([turned, jnp.zeros((rows, OW - 192), f32)], axis=1).astype(bf16)


def ordered(flag, x, y):
    return jnp.where(flag, jnp.concatenate([y, x], axis=1), jnp.concatenate([x, y], axis=1))


def lanes_at(index, width):
    return pl.ds(pl.multiple_of(index * width, width), width)


def second_kernel(sc, o0, o1, o2, o3, head, out):
    for r, ref in enumerate((o0, o1, o2, o3)):
        out[:, lanes_at(sc[2] ^ r, OW)] = ref[...]
    out[:, HEAD_AT:] = jnp.zeros((out.shape[0], CPAD), bf16)
    out[:, HEAD_AT : HEAD_AT + CLASSES] = head[...].astype(bf16)


def eight(refs):
    return list(refs[:4]) + [refs[4].at[n] for n in range(4)]


REL = [0, 2, 4, 6, 1, 3, 5, 7]


def stack_kernel(a, b, c, d, out):
    for n, ref in enumerate((a, b, c, d)):
        out[n] = ref[...]


def row_copies(refs, me, dst, sems, rel=REL):
    out = []
    for n, ref in enumerate(refs):
        size = ref.shape[0]
        out.append(pltpu.make_async_copy(ref, dst.at[rows_at(me ^ rel[n], size), :], sems.at[n]))
    return out


def columns(refs, lo, width):
    return [ref.at[:, pl.ds(lo, width)] for ref in refs]


def start(copies):
    for copy in copies:
        copy.start()


def wait(copies):
    for copy in copies:
        copy.wait()


def x0_kernel(sc, own, other, hot, *rest):
    refs = eight(rest[:5])
    a_out, x0_out, gx_out, w, sems = rest[5:]
    i = pl.program_id(0)

    @pl.when(i == 0)
    def _():
        copies = row_copies(refs, sc[0], w, sems)
        start(copies)
        wait(copies)
        row = lax.broadcasted_iota(jnp.int32, (16, SMALL), 0)
        col = lax.broadcasted_iota(jnp.int32, (16, SMALL), 1)
        pick = (row + LANE_GAIN == col).astype(f32).astype(bf16)
        gx_out[...] = dot(pick, w[:, D:], NT)

    rows = jnp.where(sc[3] == 1, own[...], other[...])
    x0 = dot(rows, w[:, :D]) + dot(hot[...], w[:, D:], NT)
    scaled, _ = norm_stats(x0)
    a_out[...] = (scaled * gx_out[0:1, :]).astype(bf16)

    @pl.when(i == sc[1])
    def _():
        x0_out[...] = x0


IN_REL = [0, 1, 2, 3]


def qkv_kernel(sc, a, qaux, kaux, vaux, gain, avg, *rest):
    refs = rest[:4]
    qx, kx, vx, xh_out, inv_out, w, sems = rest[4:]
    i = pl.program_id(0)

    @pl.when(i == 0)
    def _():
        copies = row_copies(refs, sc[4], w, sems, IN_REL)
        start(copies)
        wait(copies)

    mixed = dot(a[...], w[...])
    qk = mixed[:, :QK]
    v = mixed[:, QK:].astype(bf16)
    ones = avg[...]
    center = qk - head_mean(qk, ones, 2)
    inv = lax.rsqrt(head_mean(center * center, ones, 2) + NORM_EPS)
    scaled = center * inv
    xh_out[...] = scaled
    inv_out[...] = inv
    low = (scaled * gain[0:1, :]).astype(bf16)
    qa, ka, va = qaux[...], kaux[...], vaux[...]
    for h in range(NH):
        qx[h] = jnp.concatenate([low[:, h * HD : h * HD + HD], qa], axis=1)
        kx[h] = jnp.concatenate([low[:, (NH + h) * HD : (NH + h) * HD + HD], ka], axis=1)
        vx[h] = jnp.concatenate([v[:, h * HD : h * HD + HD], va], axis=1)


def attn_kernel(rel, sc, qx, kx, vx, o_rel, o_full, ql, acc):
    step_id = pl.program_id(0)
    i = 2 * (sc[1] ^ jnp.where(step_id < 2, rel[0], rel[1])) + step_id % 2
    acc[...] = jnp.zeros_like(acc)
    lo, hi = sc[8 + i], sc[16 + i]

    def tile(start_row, size):
        ks = pl.ds(pl.multiple_of(start_row, BQ), size)
        scores = [dot(qx[h], kx[h, ks, :], NT) for h in range(NH)]
        probs = [jnp.exp(s).astype(bf16) for s in scores]
        for h in range(NH):
            acc[h] += dot(probs[h], vx[h, ks, :])

    pairs = (hi - lo) // 2

    def step(j, carry):
        tile((lo + 2 * j) * BQ, 2 * BQ)
        return carry

    lax.fori_loop(0, pairs, step, 0)

    @pl.when((hi - lo) % 2 == 1)
    def _():
        tile((hi - 1) * BQ, BQ)

    mine = rows_at(i, BQ)
    lane = lax.broadcasted_iota(jnp.int32, (BQ, 128), 1)
    outs = []
    for h in range(NH):
        q = qx[h].astype(f32)
        k = kx[h, mine, :].astype(f32)
        v = vx[h, mine, :].astype(f32)
        free = k[:, 84:85]
        diag = jnp.sum(jnp.where(lane < HD, q * k, 0.0), axis=1, keepdims=True)
        p = jnp.exp(diag) * free
        out = acc[h] + p.astype(bf16).astype(f32) * v
        total = out[:, 64:65]
        outs.append(out[:, :HD] / total)
        for n, part in enumerate(splits(-jnp.log(total), 3)):
            q = jnp.where(lane == 81 + n, part.astype(f32), q)
        ql[h] = q.astype(bf16)
    full = jnp.concatenate(outs, axis=1)
    o_full[...] = full
    o_rel[0] = jnp.concatenate([full, jnp.zeros((BQ, OW - NH * HD), f32)], axis=1).astype(bf16)


GELU_C = 0.7978845608028654


def gelu_tanh(u):
    return jnp.tanh(GELU_C * (u + 0.044715 * u * u * u))


def mlp_tile(b, w, u_out, h_out):
    u = dot(b, w[0])
    u_out[...] = u
    h = (0.5 * u * (1.0 + gelu_tanh(u))).astype(bf16)
    h_out[...] = h
    return dot(h, w[1], NT)


def tile_copies(w_all, j, dst, sems):
    size = D // 8
    return [
        pltpu.make_async_copy(
            w_all.at[d, j, :, pl.ds(part * D, D)],
            dst.at[part, pl.ds(d * size, size), :],
            sems.at[part, d],
        )
        for part in range(2)
        for d in range(8)
    ]


def mlp_kernel(sc, o0, o1, o2, o3, x0, gx, mem, heads, *rest):
    refs, w_all = eight(rest[:5]), rest[5]
    x1_out, b_out, u_out, h_out, x2, ns_out, w_o, w_t, sem_o, sem_t = rest[6:]
    j = pl.program_id(0)

    @pl.when(j == 0)
    def _():
        first = row_copies(columns(refs, 0, 4 * OW), sc[0], w_o, sem_o)
        start(first)
        for t in range(4):
            start(tile_copies(w_all, t, w_t.at[t], sem_t.at[t]))
        wait(first)
        x1 = x0[...]
        for r, ref in enumerate((o0, o1, o2, o3)):
            x1 += dot(ref[...], w_o[:, lanes_at(sc[1] ^ r, OW)], NT)
        x1_out[...] = x1
        b_out[...] = (norm_stats(x1)[0] * gx[1:2, :]).astype(bf16)
        x2[...] = x1

    wait(tile_copies(w_all, j, w_t.at[j], sem_t.at[j]))
    x2[...] += mlp_tile(b_out[...], w_t.at[j], u_out, h_out)

    @pl.when(j == 3)
    def _():
        f = norm_stats(x2[...])[0] * gx[2:3, :]
        ones = heads[...]
        e = jnp.exp(dot_split(f * gx[3:4, :], ones, 3) * 0.125)
        eb = dot_split(e, ones, 2, NT)
        m = mem[...]
        num = jnp.zeros((IMG, D), f32)
        for part in splits(eb * f, 3):
            num += dot(m, part, TN)
        den = jnp.zeros((IMG, 128), f32)
        for part in splits(e, 3):
            den += dot(m, part, TN)
        ns_out[:, :D] = num
        ns_out[:, D:] = den


def head_kernel(sc, ns_a, ns_b, lab, vt, heads, *rest):
    pooled_out, gp_out, sinv_out, loss_out, gh_out, gh_send, w, gw, sems = rest[5:]
    copies = row_copies(columns(eight(rest[:5]), HEAD_AT, CPAD), sc[0], w, sems)
    start(copies)
    ns = ns_a[...] + ns_b[...]
    valid = vt[:, 0:1]
    scale = vt[:, 1:2]
    total = jnp.where(valid > 0.0, ns[:, D:], 1.0)
    sinv = jnp.where(valid > 0.0, 1.0 / total, 0.0)
    lane = lax.broadcasted_iota(jnp.int32, (IMG, 128), 1)
    sinv = jnp.where(lane < D // HD, sinv, 0.0)
    pooled = ns[:, :D] * dot_split(sinv, heads[...], 3, NT)
    low = pooled.astype(bf16)
    wait(copies)
    logits = dot(low, w[...])
    cls = lax.broadcasted_iota(jnp.int32, (IMG, CPAD), 1)
    real = (cls < CLASSES).astype(f32)
    hot = lab[...]
    ex = jnp.exp(-jnp.abs(logits))
    soft = jnp.maximum(logits, 0.0) + jnp.log1p(ex)
    per = jnp.sum(soft * real, axis=1, keepdims=True) - jnp.sum(
        logits * hot, axis=1, keepdims=True
    )
    loss_out[...] = jnp.broadcast_to(per * valid, (IMG, 128))
    sig = jnp.where(logits >= 0.0, 1.0, ex) / (1.0 + ex)
    gl = (scale * (sig * real - hot)).astype(bf16)
    pooled_out[...] = pooled
    sinv_out[...] = sinv
    gp_out[...] = dot(gl, w[...], NT)
    half = jnp.where(sc[2] % 2 == 1, gl[:, 512:].astype(f32), gl[:, :512].astype(f32))
    gw[...] = dot(low, half.astype(bf16), TN)
    for p, r in enumerate(rel_order(2)):
        gh_out[p] = gw[rows_at(sc[0] ^ r, SUB), :].astype(bf16)
        gh_send[p] = gw[rows_at(sc[0] ^ (r + 1), SUB), :].astype(bf16)


def rel_order(first):
    m1, m2 = (2, 4) if first == 2 else (4, 2)
    return [(p >> 1) * m1 + (p & 1) * m2 for p in range(4)]


def back_kernel(sc, u, x2, x1, gx, mem, pooled, gp, sinv, heads, *rest):
    refs, w_all = eight(rest[:5]), rest[5]
    gu_out, gr_out, gm_out, gmid_out, ga_out, small_out = rest[6:12]
    w_t, w_o, grs, acc, sem_t, sem_o = rest[12:]
    j = pl.program_id(0)

    def out_rows():
        return row_copies(columns(refs, 0, 4 * OW), sc[0], w_o, sem_o)

    @pl.when(j == 0)
    def _():
        for t in range(4):
            start(tile_copies(w_all, t, w_t.at[t], sem_t.at[t]))
        start(out_rows())
        scaled, inv = norm_stats(x2[...])
        f = scaled * gx[2:3, :]
        probe = gx[3:4, :]
        ones = heads[...]
        e = jnp.exp(dot_split(f * probe, ones, 3) * 0.125)
        m = mem[...]
        m3 = jnp.concatenate([m, m, m], axis=1)

        def spread(x):
            return dot(m3, jnp.concatenate(splits(x, 3), axis=0))

        gt = spread(gp[...])
        at = e * spread(sinv[...])
        gpp = dot_split(gp[...] * pooled[...], ones, 3)
        da = dot_split(gt * f, ones, 3)
        dc = at * (da - spread(gpp))
        dcb = dot_split(dc, ones, 2, NT) * 0.125
        df = dot_split(at, ones, 2, NT) * gt + dcb * probe
        gr = norm_back(df * gx[2:3, :], scaled, inv)
        grs[...] = gr
        gr_out[...] = gr.astype(bf16)
        small_out[2:3, :] = jnp.sum(df * scaled, axis=0, keepdims=True)
        small_out[3:4, :] = jnp.sum(dcb * f, axis=0, keepdims=True)
        small_out[0:1, :] = jnp.zeros((1, D), f32)
        small_out[4:8, :] = jnp.zeros((4, D), f32)
        acc[...] = jnp.zeros_like(acc)

    wait(tile_copies(w_all, j, w_t.at[j], sem_t.at[j]))
    gh = dot(gr_out[...], w_t[j, 1])
    v = u[...]
    t = gelu_tanh(v)
    slope = 0.5 * (1.0 + t) + 0.5 * v * (1.0 - t * t) * GELU_C * (1.0 + 0.134145 * v * v)
    gu = (gh * slope).astype(bf16)
    gu_out[...] = gu
    acc[...] += dot(gu, w_t[j, 0], NT)

    @pl.when(j == 3)
    def _():
        wait(out_rows())
        scaled, inv = norm_stats(x1[...])
        gb = acc[...]
        small_out[1:2, :] = jnp.sum(gb * scaled, axis=0, keepdims=True)
        gmid = grs[...] + norm_back(gb * gx[1:2, :], scaled, inv)
        gmid_out[...] = gmid
        low = gmid.astype(bf16)
        gm_out[...] = low
        for r in range(4):
            ga_out[r] = dot(low, w_o[:, lanes_at(sc[1] ^ r, OW)]).astype(bf16)


def wgrad_kernel(sc, gr, h, b, gu, gm, o0, o1, o2, o3, out, os):
    j = pl.program_id(0)

    @pl.when(j == 0)
    def _():
        for r, ref in enumerate((o0, o1, o2, o3)):
            os[r] = ref[...]

    parts = [
        (0, dot(b[...], gu[...], TN)),
        (D, dot(gr[...], h[...], TN)),
        (2 * D, dot(gm[...], os[sc[1] ^ j], TN)),
    ]
    for lo, value in parts:
        width = value.shape[1]
        for d in range(8):
            out[d, 0, :, lo : lo + width] = value[d * SUB : (d + 1) * SUB, :].astype(bf16)


def attn_back_kernel(sc, ql_a, ql_b, of_a, of_b, d0, d1, d2, d3, kx, vx, g_out, dq, dk, dv, dos):
    i = pl.program_id(0)
    nq = dk.shape[1] // BQ

    @pl.when(i == 0)
    def _():
        for n, ref in enumerate((d3, d1, d2, d0)):
            dos[n] = ref[...]

    @pl.when(i == 0)
    def _():
        dk[...] = jnp.zeros_like(dk)
        dv[...] = jnp.zeros_like(dv)

    @pl.when(i < nq)
    def _():
        n = i // 2
        block = 2 * (sc[1] ^ jnp.where(n < 2, 3 - 2 * n, 6 - 2 * n)) + i % 2
        mine = rows_at(block, BQ)
        lane = lax.broadcasted_iota(jnp.int32, (BQ, 128), 1)
        inner = (lane < HD) | ((lane >= 81) & (lane < 84))
        first = i < nq // 2
        of = jnp.where(first, of_a[...], of_b[...])
        do = dos[n, rows_at(i % 2, BQ), :].astype(f32)
        dob, qb = [], []
        for h in range(NH):
            dof = do[:, h * HD : h * HD + HD]
            delta = jnp.sum(dof * of[:, h * HD : h * HD + HD], axis=1, keepdims=True)
            dox = jnp.concatenate([dof, jnp.zeros((BQ, HD), f32)], axis=1)
            for m, part in enumerate(splits(-delta, 3)):
                dox = jnp.where(lane == HD + m, part.astype(f32), dox)
            q = jnp.where(first, ql_a[h].astype(f32), ql_b[h].astype(f32))
            k = kx[h, mine, :].astype(f32)
            v = vx[h, mine, :].astype(f32)
            free = k[:, 84:85]
            p = jnp.exp(jnp.sum(jnp.where(inner, q * k, 0.0), axis=1, keepdims=True)) * free
            ds = p * jnp.sum(jnp.where(lane < HD + 3, dox * v, 0.0), axis=1, keepdims=True)
            ds = ds.astype(bf16).astype(f32)
            dq[h, mine, :] = ds * k
            dk[h, mine, :] += ds * q
            dv[h, mine, :] += p.astype(bf16).astype(f32) * dox
            dob.append(dox.astype(bf16))
            qb.append(q.astype(bf16))

        def tile(start_row, size):
            ks = pl.ds(pl.multiple_of(start_row, BQ), size)
            pts = [jnp.exp(dot(kx[h, ks, :], qb[h], NT)) for h in range(NH)]
            dpts = [dot(vx[h, ks, :], dob[h], NT) for h in range(NH)]
            dsts = [(pts[h] * dpts[h]).astype(bf16) for h in range(NH)]
            for h in range(NH):
                dv[h, ks, :] += dot(pts[h].astype(bf16), dob[h])
                dk[h, ks, :] += dot(dsts[h], qb[h])
                dq[h, mine, :] += dot(dsts[h], kx[h, ks, :], TN)

        lo, hi = sc[8 + block], sc[16 + block]

        def step(j, carry):
            tile((lo + 2 * j) * BQ, 2 * BQ)
            return carry

        lax.fori_loop(0, (hi - lo) // 2, step, 0)

        @pl.when((hi - lo) % 2 == 1)
        def _():
            tile((hi - 1) * BQ, BQ)

    @pl.when(i >= nq)
    def _():
        rows = rows_at(i - nq, TOK)
        g_out[...] = jnp.concatenate(
            [ref[h, rows, :][:, :HD] for ref in (dq, dk, dv) for h in range(NH)], axis=1
        )


def mix_kernel(sc, grad, xh, inv, a, gain, avg, *rest):
    refs = rest[:4]
    g_send, g_one, g_own, in_keep, in_send, qg_out, gin, w, sems = rest[4:]
    n = pl.program_id(0)

    @pl.when(n == 0)
    def _():
        copies = row_copies(refs, sc[4], w, sems, IN_REL)
        start(copies)
        gin[...] = jnp.zeros_like(gin)
        qg_out[...] = jnp.zeros_like(qg_out)
        wait(copies)

    grads = grad[:, :QK]
    scaled = xh[...]
    ones = avg[...]
    qg_out[0:1, :] += jnp.sum(grads * scaled, axis=0, keepdims=True)
    dg = grads * gain[0:1, :]
    back = inv[...] * (
        dg - head_mean(dg, ones, 2) - scaled * head_mean(dg * scaled, ones, 2)
    )
    mix = jnp.concatenate([back, grad[:, QK:]], axis=1).astype(bf16)
    out = dot(mix, w[...], NT).astype(bf16)
    gin[...] += dot(a[...], mix, TN)

    @pl.when(n < 2)
    def _():
        g_send[0] = out

    @pl.when(n == 2)
    def _():
        g_one[...] = out

    @pl.when(n == 3)
    def _():
        g_own[...] = out
        size = D // 4
        for p in range(2):
            in_keep[p] = gin[rows_at(sc[4] ^ (2 * p), size), :].astype(bf16)
            in_send[p] = gin[rows_at(sc[4] ^ (2 * p + 1), size), :].astype(bf16)


def add(x, y):
    return x.astype(f32) + y.astype(f32)


def split_kernel(count, *refs):
    ins, outs = refs[1 : 1 + 2 * count], refs[1 + 2 * count :]
    p = pl.program_id(0)
    total = pl.num_programs(0)
    for n in range(count):
        value = add(ins[2 * n][...], ins[2 * n + 1][...]).astype(bf16)

        @pl.when(p < total // 2)
        def _():
            outs[2 * n][...] = value

        @pl.when(p >= total // 2)
        def _():
            outs[2 * n + 1][...] = value


def in_parts_kernel(sc, kept, got, a_out, b_out):
    half = a_out.shape[0]
    first = sc[5]
    mine, other = rows_at(first, half), rows_at(1 - first, half)
    a_out[...] = add(kept[mine, :], got[mine, :]).astype(bf16)
    b_out[...] = add(kept[other, :], got[other, :]).astype(bf16)


def share_z_kernel(sc, z0, z1, z2, z3, up_o, down_o, out_o, sq_o):
    rows = up_o.shape[0]
    total = add(z0[0], z1[...]) + add(z2[...], z3[...])
    up_o[...] = total[:, :D]
    down_o[...] = total[:, D : 2 * D]
    out_o[...] = dot(total[:, 2 * D :], eye(rows, rows), TN, HIGH)[:192, :]
    sq_o[...] = jnp.broadcast_to(jnp.sum(total * total, keepdims=True), sq_o.shape)


def share_kernel(sc, sq_z, in_a, in_b, h_own, h_got, in_o, head_o, sq_o):
    grad = add(in_a[...], in_b[...])
    in_o[...] = jnp.concatenate(
        [
            grad[:, part * NH * HD + h * HD : part * NH * HD + h * HD + HD]
            for h in range(NH)
            for part in range(3)
        ],
        axis=1,
    )
    head = ordered(sc[2] % 2 == 1, h_own[...], h_got[...])
    head_o[...] = head[:, :CLASSES]
    squares = jnp.sum(grad * grad, keepdims=True)
    once = jnp.where(sc[2] == 0, 1.0, 0.0)
    squares += once * jnp.sum(head * head, keepdims=True)
    sq_o[...] = sq_z[...] + squares


def patch_row_kernel(sc, kept, got, sq, extra_row, out):
    rows = kept.shape[1]
    out[:rows, :] = add(kept[0], got[0]).astype(bf16)
    lane = lax.broadcasted_iota(jnp.int32, (16, D + SMALL), 1)
    row = lax.broadcasted_iota(jnp.int32, (16, D + SMALL), 0)
    value = jnp.where(lane == 0, sq[0:1, 0:1], extra_row[0:1, :])
    tail = jnp.zeros((16, D + SMALL), f32)
    for n, part in enumerate(splits(value, 3)):
        tail = jnp.where(row == n, part.astype(f32), tail)
    out[rows:, :] = tail.astype(bf16)


def patch_sum_kernel(sc, own, q1, q2, q3, share_o, stats_o):
    rows = share_o.shape[0]
    total = add(own[...], q1[...]) + add(q2[...], q3[...])
    patch = total[:rows, :]
    share_o[...] = patch
    sums = total[rows : rows + 1, :SMALL] + total[rows + 1 : rows + 2, :SMALL]
    sums += total[rows + 2 : rows + 3, :SMALL]
    lane = lax.broadcasted_iota(jnp.int32, (8, SMALL), 1)
    squares = jnp.sum(patch * patch, keepdims=True)
    stats_o[...] = sums + jnp.where(lane == 0, squares, 0.0)


def tail_kernel(n_dp, sc, g_own, g_core, g_z, gmid, x0, gx, own, other, hot, small_b, qgrad,
                pk, ps, tile):
    grad = g_own[...].astype(f32) + g_core[0].astype(f32) + g_z[...].astype(f32)
    scaled, inv = norm_stats(x0[...])
    gain_a = jnp.sum(grad * scaled, axis=0, keepdims=True)
    ge = (gmid[...] + norm_back(grad * gx[0:1, :], scaled, inv)).astype(bf16)
    rows = jnp.where(sc[3] == 1, own[...], other[...])
    tile[:, :D] = dot(rows, ge, TN)
    row8 = lax.broadcasted_iota(jnp.int32, (8, D), 0)
    gains = jnp.where(row8 == 0, gain_a, small_b[...])
    small = dot(ge, hot[...], TN) + dot(gains, eye(8, SMALL, LANE_GAIN), TN)
    part = HD // n_dp
    kk = lax.broadcasted_iota(jnp.int32, (HD, D), 0)
    rr = lax.broadcasted_iota(jnp.int32, (HD, D), 1)
    spot = ((kk // part) * (D // n_dp) + kk % part == rr).astype(f32)
    lane = lax.broadcasted_iota(jnp.int32, (8, SMALL), 1)
    row = lax.broadcasted_iota(jnp.int32, (8, SMALL), 0)
    q_lane = ((lane == LANE_QG + row) & (row < 2)).astype(f32)
    q_cols = dot(qgrad[...], q_lane, TN, HIGH)
    small += dot(spot, q_cols, TN)
    tile[:, D:] = small
    for p, r in enumerate(rel_order(2)):
        pk[p] = tile[rows_at(sc[0] ^ r, SUB), :].astype(bf16)
        ps[p] = tile[rows_at(sc[0] ^ (r + 1), SUB), :].astype(bf16)


def update_kernel(stats, *rest):
    shares = rest[:6]
    state = rest[6:33]
    norm_out, loss_out, outs = rest[33], rest[34], rest[35:]
    total = stats[0:1, :]
    norm = jnp.sqrt(total)
    norm_out[...] = norm[:, 0:1]
    loss_out[...] = total[:, 1 : 1 + NB]
    factor = jnp.minimum(1.0, CLIP / (norm[:, 0:1] + 1e-06))
    s_in, s_out, s_up, s_down, s_patch, s_head = shares
    rows = s_patch.shape[0]
    small = dot(eye(SMALL, SMALL), s_patch[:, D:], NT, HIGH)
    part = state[24].shape[1]
    grads = [
        s_in[...],
        s_out[...],
        s_up[...],
        s_down[...],
        s_patch[:, :D],
        small[: 2 * GRID, :],
        s_head[...],
        small[LANE_GAIN : LANE_GAIN + 4, :],
        small[LANE_QG : LANE_QG + 2, :part],
    ]
    for n in range(9):
        master, first, second = state[3 * n : 3 * n + 3]
        clipped = grads[n] * factor
        first_new = BETA_ONE * first[...] + (1.0 - BETA_ONE) * clipped
        second_new = BETA_TWO * second[...] + (1.0 - BETA_TWO) * clipped * clipped
        matrix = n in (0, 1, 2, 3, 4, 6)
        rate = RATE_MATRIX if matrix else RATE_SMALL
        decay = DECAY if matrix else 0.0
        ratio = (
            first_new
            / (1.0 - BETA_ONE**STEP)
            / (jnp.sqrt(second_new / (1.0 - BETA_TWO**STEP)) + ADAM_EPS)
        )
        value = master[...]
        outs[3 * n][...] = value - rate * (ratio + decay * value)
        outs[3 * n + 1][...] = first_new
        outs[3 * n + 2][...] = second_new


ANY = pl.BlockSpec(memory_space=pl.ANY)


def without(kernel, count, deps):
    if not deps:
        return kernel
    return lambda *refs: kernel(*refs[:count], *refs[count + len(deps) :])


def call(kernel, grid, sc, ins, specs, outs, out_specs, scratch, us=5, deps=()):
    return pl.pallas_call(
        without(kernel, 1 + len(ins), deps),
        out_shape=outs,
        grid_spec=pltpu.PrefetchScalarGridSpec(
            num_scalar_prefetch=1,
            grid=grid,
            in_specs=list(specs) + [ANY] * len(deps),
            out_specs=out_specs,
            scratch_shapes=scratch,
        ),
        compiler_params=pltpu.CompilerParams(vmem_limit_bytes=VLIM),
        cost_estimate=pl.CostEstimate(
            flops=int(us * COST), bytes_accessed=1000, transcendentals=0
        ),
    )(sc, *ins, *deps)


def flat_call(kernel, sc, ins, outs, scratch=(), us=3, deps=()):
    return call(
        kernel,
        (1,),
        sc,
        ins,
        [whole(x.shape) for x in ins],
        outs,
        tuple(whole(o.shape) for o in outs),
        list(scratch),
        us,
        deps,
    )


def simple_call(kernel, ins, outs, us=3, deps=()):
    return pl.pallas_call(
        without(kernel, len(ins), deps),
        out_shape=outs,
        in_specs=[pl.BlockSpec(memory_space=pltpu.VMEM)] * len(ins) + [ANY] * len(deps),
        compiler_params=pltpu.CompilerParams(vmem_limit_bytes=VLIM),
        cost_estimate=pl.CostEstimate(
            flops=int(us * COST), bytes_accessed=1000, transcendentals=0
        ),
    )(*ins, *deps)


def whole(shape):
    return pl.BlockSpec(shape, lambda i, s: (0,) * len(shape))


def sds(shape, dtype):
    return jax.ShapeDtypeStruct(shape, dtype)


DMA = pltpu.SemaphoreType.DMA


def make_local(n_dp, n_mp):
    extra = n_dp // 8
    masks = [extra, 2 * extra, 4 * extra]
    low_bits = [b for b in (1, 2, 4, 8, 16, 32) if b < extra]
    col_low = [2 * b for b in low_bits]
    col_masks = [2 * extra, 4 * extra]

    def pp(x, dmask, zmask=0):
        perm = [
            (d * n_mp + z, (d ^ dmask) * n_mp + (z ^ zmask))
            for d in range(n_dp)
            for z in range(n_mp)
        ]
        return lax.ppermute(x, ("dp", "mp"), perm)

    def local(patches, segment, keep, pos_y, pos_x, labels, bucket, *state):
        masters = state[0::3]
        (attend_in, attend_out, expand, contract, patch_embed, pos_table, class_head,
         norm_gains, query_gains) = masters
        length = patches.shape[0]
        rows = patch_embed.shape[0]
        nq = length // BQ
        dp = lax.axis_index("dp")
        z = lax.axis_index("mp")
        core = dp % 2
        z1, z0 = z // 2, z % 2
        g = z0 + 2 * core
        me = dp // extra
        mecol = (dp // 2) // extra
        mine = core == z1

        def bit_of(mask):
            return (dp // mask) % 2 == 1

        def swap(flag, x, y, axis):
            return jnp.where(
                flag, jnp.concatenate([y, x], axis=axis), jnp.concatenate([x, y], axis=axis)
            )

        def pick4(parts, index, axis):
            odd, high = index % 2 == 1, index // 2 == 1
            lo = swap(odd, parts[0], parts[1], axis)
            hi = swap(odd, parts[2], parts[3], axis)
            return swap(high, lo, hi, axis)

        patch_w, in_w, t_w, out_w = pl.pallas_call(
            pack_kernel,
            out_shape=(
                sds((rows, D + SMALL), bf16),
                sds((rows, 576), bf16),
                sds((rows, 2 * D), bf16),
                sds((rows, OW), bf16),
            ),
            in_specs=[pl.BlockSpec(memory_space=pltpu.VMEM)] * 6
            + [pl.BlockSpec(memory_space=pltpu.SMEM)]
            + [pl.BlockSpec(memory_space=pltpu.VMEM)] * 4,
            compiler_params=pltpu.CompilerParams(vmem_limit_bytes=VLIM),
        )(patch_embed, pos_table, norm_gains, query_gains, segment.reshape(-1, 128),
          keep.reshape(-1, 128), bucket, attend_in, attend_out, expand, contract.T)
        w_all = lax.all_gather(t_w, ("dp", "mp"), axis=0, tiled=True)
        w_all = w_all.reshape(8, extra, n_mp, rows, 2 * D)
        if extra > 1:
            w_all = w_all.transpose(0, 2, 1, 3, 4)
        w_all = w_all.reshape(8, n_mp, SUB, 2 * D)

        perm_core = [
            (d * n_mp + zz, (d ^ 1) * n_mp + zz)
            for d in range(n_dp)
            for zz in range(n_mp)
            if d % 2 == zz // 2
        ]
        patches_in = lax.ppermute(patches, ("dp", "mp"), perm_core)
        meta = jnp.stack([segment, keep, pos_y, pos_x])
        tag = jnp.concatenate([labels, bucket, jnp.zeros((length - IMG - 1,), jnp.int32)])
        meta = jnp.concatenate([meta, tag[None]], axis=0)
        meta_in = lax.ppermute(meta, ("dp", "mp"), perm_core)
        meta = jnp.where(mine, meta, meta_in)

        def widen(x, low):
            for b in low:
                x = swap(bit_of(b), x, pp(x, b), -2)
            return x

        def across(x):
            one, two = pp(x, masks[1]), pp(x, masks[2])
            return [x, one, two, pp(one, masks[2])]

        def stack(parts, deps):
            high, width = parts[0].shape
            cuts = 1 if width < 2048 else 4
            step = width // cuts
            return pl.pallas_call(
                without(stack_kernel, 4, deps),
                out_shape=sds((4, high, width), bf16),
                grid=(cuts,),
                in_specs=[pl.BlockSpec((high, step), lambda i: (0, i))] * 4 + [ANY] * len(deps),
                out_specs=pl.BlockSpec((4, high, step), lambda i: (0, 0, i)),
                compiler_params=pltpu.CompilerParams(vmem_limit_bytes=VLIM),
                cost_estimate=pl.CostEstimate(flops=int(COST), bytes_accessed=1000, transcendentals=0),
            )(*parts, *deps)

        def halved(x):
            one, two = pp(x, masks[1]), pp(x, masks[2])
            half = x.shape[0] // 2
            far = jnp.concatenate([pp(one[:half], masks[2]), pp(two[half:], masks[1])])
            return [x, one, two, far]

        def all8(parts, deps=()):
            stacked = stack(parts, deps)
            return parts + [pp(stacked, masks[0])], stacked

        patch_c = across(widen(patch_w, low_bits))

        perm_a, perm_b, back_b = [], [], []
        for d in range(n_dp):
            for zz in range(n_mp):
                c, a1, a0 = d % 2, zz // 2, zz % 2
                src = d * n_mp + zz
                perm_a.append((src, (d - c + a1) * n_mp + a0 + 2 * c))
                perm_b.append((src, (d - c + a1) * n_mp + a0 + 2 * (1 - c)))
                back_b.append((src, (d - c + 1 - a1) * n_mp + a0 + 2 * c))
        in_a = lax.ppermute(in_w, ("dp", "mp"), perm_a)
        in_b = lax.ppermute(in_w, ("dp", "mp"), perm_b)
        patch_p, _ = all8(patch_c, [patches_in, meta_in, in_a, in_b])
        in_own = widen(swap(z1 == 1, in_a, in_b, 0), col_low)
        in_one, in_two = pp(in_own, col_masks[0]), pp(in_own, col_masks[1])
        in_p = [in_own, in_one, in_two, pp(in_one, col_masks[1])]
        o_one, o_two = pp(out_w, 0, 1), pp(out_w, 0, 2)
        out_z = [out_w, o_one, o_two, pp(o_two, 0, 1)]

        seg, kp, py, px = meta[0], meta[1], meta[2], meta[3]
        labs = meta[4, :IMG]
        buck = meta[4, IMG]
        kept = (kp == 1) & (seg < IMG)
        ids = jnp.arange(128)[None, :]
        ids64 = ids[:, :64]
        hot_pos = ((py[:, None] == ids) | (px[:, None] + GRID == ids)).astype(bf16)
        match = seg[:, None] == ids64
        qaux = jnp.where((ids64 < IMG) & match, BIG, jnp.where(ids64 == IMG, 1.0, 0.0)).astype(bf16)
        kaux = jnp.where(
            (ids64 < IMG) & match & kept[:, None],
            1.0,
            jnp.where(
                ids64 == IMG,
                -BIG,
                jnp.where(
                    (ids64 > IMG) & (ids64 < IMG + 4),
                    1.0,
                    jnp.where((ids64 == IMG + 4) & ~kept[:, None], 1.0, 0.0),
                ),
            ),
        ).astype(bf16)
        vaux = jnp.broadcast_to(jnp.where(jnp.arange(64) < 3, 1.0, 0.0).astype(bf16), (TOK, 64))
        first_seg, last_seg = seg[::BQ], jnp.minimum(seg[BQ - 1 :: BQ], IMG - 1)
        lo = jnp.sum((seg[None, :] < first_seg[:, None]).astype(jnp.int32), axis=1) // BQ
        hi = (jnp.sum((seg[None, :] <= last_seg[:, None]).astype(jnp.int32), axis=1) + BQ - 1) // BQ
        sc = jnp.concatenate(
            [
                jnp.stack([me, g, z, mine.astype(jnp.int32), mecol, z1, z1, z1]),
                lo,
                hi,
            ]
        ).astype(jnp.int32)
        own_seg = lax.dynamic_slice_in_dim(seg, g * TOK, TOK, 0)
        own_kp = lax.dynamic_slice_in_dim(kept, g * TOK, TOK, 0)
        mem = (
            (own_seg[:, None] == jnp.arange(IMG)[None, :]) & own_kp[:, None]
        ).astype(bf16)
        valid = jnp.max(
            ((seg[None, :] == jnp.arange(IMG)[:, None]) & kept[None, :]).astype(f32), axis=1
        )
        lab_hot = (labs[:, None] == jnp.arange(CPAD)[None, :]).astype(f32)
        block = jnp.arange(128) // HD
        avg = jnp.where(block[:, None] == block[None, :], 1.0 / HD, 0.0).astype(bf16)
        heads = (jnp.arange(D)[:, None] // HD == ids).astype(bf16)

        nt = length // TOK
        a, x0, gx = call(
            x0_kernel,
            (nt,),
            sc,
            [patches, patches_in, hot_pos] + patch_p,
            [
                pl.BlockSpec((TOK, D), lambda i, s: (jnp.where(s[3] == 1, i, 0), 0)),
                pl.BlockSpec((TOK, D), lambda i, s: (jnp.where(s[3] == 1, 0, i), 0)),
                pl.BlockSpec((TOK, 128), lambda i, s: (i, 0)),
            ]
            + [ANY] * 5,
            (sds((length, D), bf16), sds((TOK, D), f32), sds((16, D), f32)),
            (pl.BlockSpec((TOK, D), lambda i, s: (i, 0)), whole((TOK, D)), whole((16, D))),
            [pltpu.VMEM((D, D + SMALL), bf16), DMA((8,))],
            10,
        )
        f_w = flat_call(
            second_kernel, sc, out_z + [class_head], (sds((rows, 4 * OW + CPAD), bf16),), us=2,
            deps=[a],
        )[0]
        f_c = halved(widen(f_w, low_bits))
        qcols = query_gains.shape[1]
        counts = jnp.sum(gx[LANE_COUNT - LANE_GAIN : LANE_COUNT - LANE_GAIN + NB], axis=1)
        image_total = jnp.sum(counts)
        qg = gx[4:6].reshape(2, n_dp, rows)[:, :, :qcols].reshape(2, 1, HD)
        gain = jnp.tile(qg * jnp.array([0.125, 1.0], f32)[:, None, None], (1, NH, 1))
        gain = jnp.pad(gain.reshape(1, QK), ((0, 7), (0, 0)))
        vt = jnp.stack([valid, valid / image_total], axis=1)
        vt = jnp.pad(vt, ((0, 0), (0, 126)))

        row_block = lambda width: pl.BlockSpec((TOK, width), lambda i, s: (i, 0))
        head_block = pl.BlockSpec((NH, TOK, 128), lambda i, s: (0, i, 0))
        qx, kx, vx, xh, inv = call(
            qkv_kernel,
            (nt,),
            sc,
            [a, qaux, kaux, vaux, gain, avg] + in_p,
            [row_block(D), row_block(64), row_block(64), whole((TOK, 64)), whole((8, QK)),
             whole((128, 128))]
            + [ANY] * 4,
            tuple([sds((NH, length, 128), bf16)] * 3 + [sds((length, QK), f32)] * 2),
            tuple([head_block] * 3 + [row_block(QK)] * 2),
            [pltpu.VMEM((D, 576), bf16), DMA((4,))],
            10,
            deps=[f_w],
        )
        per_tok = TOK // BQ
        def attend(rel, us, deps):
            half = nq // 2
            block = lambda i, s: 2 * (s[1] ^ jnp.where(i < 2, rel[0], rel[1])) + i % 2
            return call(
                lambda *refs: attn_kernel(rel, *refs),
                (half,),
                sc,
                [qx, kx, vx],
                [
                    pl.BlockSpec((NH, BQ, 128), lambda i, s: (0, block(i, s), 0)),
                    whole((NH, length, 128)),
                    whole((NH, length, 128)),
                ],
                (
                    sds((2, TOK, OW), bf16),
                    sds((half * BQ, NH * HD), f32),
                    sds((NH, half * BQ, 128), bf16),
                ),
                (
                    pl.BlockSpec((1, BQ, OW), lambda i, s: (i // per_tok, i % per_tok, 0)),
                    pl.BlockSpec((BQ, NH * HD), lambda i, s: (i, 0)),
                    pl.BlockSpec((NH, BQ, 128), lambda i, s: (0, i, 0)),
                ),
                [pltpu.VMEM((NH, BQ, 128), f32)],
                us,
                deps,
            )

        o_a, of_a, ql_a = attend((3, 1), 11, ())
        f_p, f_stack = all8(f_c, [o_a])
        o_b, of_b, ql_b = attend((2, 0), 11, [f_stack])

        def trade(parts):
            return [parts[0], pp(parts[1], 0, 1), pp(parts[2], 1, 0), pp(parts[3], 1, 1)]

        o_p = trade([o_b[1], o_a[1], o_b[0], o_a[0]])
        tile_spec = pl.BlockSpec((TOK, D), lambda j, s: (0, j))
        x1, b, u, h, x2, ns = call(
            mlp_kernel,
            (4,),
            sc,
            o_p + [x0, gx, mem, heads] + f_p + [w_all],
            [whole((TOK, OW))] * 4
            + [whole((TOK, D)), whole((16, D)), whole((TOK, IMG)), whole((D, 128))]
            + [ANY] * 6,
            (
                sds((TOK, D), f32),
                sds((TOK, D), bf16),
                sds((TOK, HID), f32),
                sds((TOK, HID), bf16),
                sds((TOK, D), f32),
                sds((IMG, D + 128), f32),
            ),
            (whole((TOK, D)), whole((TOK, D)), tile_spec, tile_spec, whole((TOK, D)),
             whole((IMG, D + 128))),
            [
                pltpu.VMEM((D, 4 * OW), bf16),
                pltpu.VMEM((4, 2, D, D), bf16),
                DMA((8,)),
                DMA((4, 2, 8)),
            ],
            18,
        )
        ns = ns + pp(ns, 1, 0)
        half_shape = (4, SUB, CPAD // 2)
        pooled, gp, sinv, loss, gh, gh_send = call(
            head_kernel,
            (1,),
            sc,
            [ns, pp(ns, 0, 1), lab_hot, vt, heads] + f_p,
            [whole((IMG, D + 128))] * 2
            + [whole((IMG, CPAD)), whole((IMG, 128)), whole((D, 128))]
            + [ANY] * 5,
            (
                sds((IMG, D), f32),
                sds((IMG, D), f32),
                sds((IMG, 128), f32),
                sds((IMG, 128), f32),
                sds(half_shape, bf16),
                sds(half_shape, bf16),
            ),
            (
                whole((IMG, D)),
                whole((IMG, D)),
                whole((IMG, 128)),
                whole((IMG, 128)),
                whole(half_shape),
                whole(half_shape),
            ),
            [pltpu.VMEM((D, CPAD), bf16), pltpu.VMEM((D, CPAD // 2), f32), DMA((8,))],
            5,
        )

        gu, gr, gm, gmid, ga, small_b = call(
            back_kernel,
            (4,),
            sc,
            [u, x2, x1, gx, mem, pooled, gp, sinv, heads] + f_p + [w_all],
            [
                tile_spec,
                whole((TOK, D)),
                whole((TOK, D)),
                whole((16, D)),
                whole((TOK, IMG)),
                whole((IMG, D)),
                whole((IMG, D)),
                whole((IMG, 128)),
                whole((D, 128)),
            ]
            + [ANY] * 6,
            (
                sds((TOK, HID), bf16),
                sds((TOK, D), bf16),
                sds((TOK, D), bf16),
                sds((TOK, D), f32),
                sds((4, TOK, OW), bf16),
                sds((8, D), f32),
            ),
            (
                tile_spec,
                whole((TOK, D)),
                whole((TOK, D)),
                whole((TOK, D)),
                whole((4, TOK, OW)),
                whole((8, D)),
            ),
            [
                pltpu.VMEM((4, 2, D, D), bf16),
                pltpu.VMEM((D, 4 * OW), bf16),
                pltpu.VMEM((TOK, D), f32),
                pltpu.VMEM((TOK, D), f32),
                DMA((4, 2, 8)),
                DMA((8,)),
            ],
            20,
        )
        ga_parts = [ga[r] for r in range(4)]
        do_p = trade(ga_parts)

        if extra == 1:
            gh_one = add(gh[:2], pp(gh[2:], masks[1])).astype(bf16)
        else:
            gh_one = add(gh, pp(gh_send, masks[0])).astype(bf16)

        tile_of = pl.BlockSpec((TOK, D), lambda j, s: (0, j))
        width = 2 * D + OW
        wgrad = call(
            wgrad_kernel,
            (4,),
            sc,
            [gr, h, b, gu, gm] + o_p,
            [whole((TOK, D)), tile_of, whole((TOK, D)), tile_of, whole((TOK, D))]
            + [whole((TOK, OW))] * 4,
            (sds((8, 4, SUB, width), bf16),),
            (pl.BlockSpec((8, 1, SUB, width), lambda j, s: (0, s[2] ^ j, 0, 0)),),
            [pltpu.VMEM((4, TOK, OW), bf16)],
            14,
            deps=ga_parts + [gh_one],
        )[0]
        if extra > 1:
            wgrad = wgrad.reshape(8, 4, extra, rows, width).transpose(0, 2, 1, 3, 4)
        wgrad = wgrad.reshape(n_dp * 4 * rows, width)
        z_out = lax.psum_scatter(wgrad, "dp", scatter_dimension=0, tiled=True)
        z_out = z_out.reshape(4, rows, width)
        z_got = [pp(z_out[r], 0, r) for r in (1, 2, 3)]

        def low_rows(x, low):
            for b in reversed(low):
                half = x.shape[-2] // 2
                first, second = x[..., :half, :], x[..., half:, :]
                flag = bit_of(b)
                send = jnp.where(flag, first, second)
                stay = jnp.where(flag, second, first)
                x = add(stay, pp(send.astype(bf16), b))
            return x

        def scatter4(stay, low, m1, m2):
            x = add(stay[:2], pp(stay[2:].astype(bf16), m1))
            x = add(x[0].astype(bf16), pp(x[1].astype(bf16), m2))
            return low_rows(x, low)

        def core_sum(stay, send):
            return add(stay, pp(send, masks[0])).astype(bf16)

        def chip_sum(x, first):
            m1, m2 = (masks[1], masks[2]) if first == 2 else (masks[2], masks[1])
            return scatter4(x, low_bits, m1, m2)

        if extra == 1:
            gh = add(gh_one[0], pp(gh_one[1], masks[2])).astype(bf16)
        else:
            gh = (0.5 * chip_sum(gh_one, 2)).astype(bf16)

        def halves(pairs, us, deps=()):
            count = pairs[0][0].shape[0]
            half = count // 2
            ins, specs, outs, out_specs = [], [], [], []
            for kept, got in pairs:
                shape = kept.shape[1:]
                block = (1,) + shape
                tail = (0,) * len(shape)
                ins += [kept, got]
                specs += [pl.BlockSpec(block, lambda p, s, tail=tail: (p,) + tail)] * 2
                outs += [sds((half,) + shape, bf16)] * 2
                out_specs += [
                    pl.BlockSpec(block, lambda p, s, tail=tail: (jnp.minimum(p, half - 1),) + tail),
                    pl.BlockSpec(block, lambda p, s, tail=tail: (jnp.maximum(p - half, 0),) + tail),
                ]
            n = len(pairs)
            out = call(
                lambda *refs: split_kernel(n, *refs), (count,), sc, ins, specs, tuple(outs),
                tuple(out_specs), [], us, deps,
            )
            return [(out[2 * i], out[2 * i + 1]) for i in range(n)]

        gh = add(gh, pp(gh, 0, 2))
        gh_got = pp(gh, 0, 1)

        half = nq // 2
        grads = call(
            attn_back_kernel,
            (nq + nt,),
            sc,
            [ql_a, ql_b, of_a, of_b] + do_p + [kx, vx],
            [
                pl.BlockSpec((NH, BQ, 128), lambda i, s: (0, jnp.minimum(i, half - 1), 0)),
                pl.BlockSpec((NH, BQ, 128), lambda i, s: (0, jnp.clip(i - half, 0, half - 1), 0)),
                pl.BlockSpec((BQ, NH * HD), lambda i, s: (jnp.minimum(i, half - 1), 0)),
                pl.BlockSpec((BQ, NH * HD), lambda i, s: (jnp.clip(i - half, 0, half - 1), 0)),
            ]
            + [whole((TOK, OW))] * 4
            + [whole((NH, length, 128)), whole((NH, length, 128))],
            (sds((length, 576), f32),),
            (pl.BlockSpec((TOK, 576), lambda i, s: (jnp.maximum(i - nq, 0), 0)),),
            [
                pltpu.VMEM((NH, length, 128), f32),
                pltpu.VMEM((NH, length, 128), f32),
                pltpu.VMEM((NH, length, 128), f32),
                pltpu.VMEM((4, TOK, OW), bf16),
            ],
            35,
            deps=[gh],
        )[0]
        rel_tok = lambda n, s: s[1] ^ jnp.where(n < 2, n + 2, 3 - n)
        tok_block = lambda width: pl.BlockSpec((TOK, width), lambda n, s: (rel_tok(n, s), 0))
        in_shape = (2, D // 4, 576)
        g_send, g_one, g_own, in_keep, in_send, qgrad = call(
            mix_kernel,
            (nt,),
            sc,
            [grads, xh, inv, a, gain, avg] + in_p,
            [tok_block(576), tok_block(QK), tok_block(QK), tok_block(D), whole((8, QK)),
             whole((128, 128))]
            + [ANY] * 4,
            (
                sds((2, TOK, D), bf16),
                sds((TOK, D), bf16),
                sds((TOK, D), bf16),
                sds(in_shape, bf16),
                sds(in_shape, bf16),
                sds((8, QK), f32),
            ),
            (
                pl.BlockSpec((1, TOK, D), lambda n, s: (jnp.minimum(n, 1), 0, 0)),
                whole((TOK, D)),
                whole((TOK, D)),
                whole(in_shape),
                whole(in_shape),
                whole((8, QK)),
            ),
            [pltpu.VMEM((D, 576), f32), pltpu.VMEM((D, 576), bf16), DMA((4,))],
            14,
            deps=[gh_got],
        )
        g_core = pp(g_send, 1)
        g_z = pp(add(g_one, g_core[1]).astype(bf16), 0, 1)

        in_got = pp(in_send, col_masks[0])
        (ik, is_), = halves([(in_keep, in_got)], 2, deps=[g_core])
        is_got = pp(is_, col_masks[1])

        qg_rows = qgrad[0].reshape(2, NH, HD).sum(axis=1) * jnp.array([0.125, 1.0], f32)[:, None]
        qg_rows = jnp.pad(qg_rows, ((0, 6), (0, 0)))
        hot_own = pl.BlockSpec((TOK, 128), lambda i, s: (s[1], 0))
        own_rows = pl.BlockSpec((TOK, D), lambda i, s: (s[1], 0))

        def tail_body(*refs):
            tail_kernel(n_dp, *refs)

        pk, ps = call(
            tail_body,
            (1,),
            sc,
            [g_own, g_core, g_z, gmid, x0, gx, patches, patches_in, hot_pos, small_b, qg_rows],
            [
                whole((TOK, D)),
                pl.BlockSpec((1, TOK, D), lambda i, s: (0, 0, 0)),
                whole((TOK, D)),
                whole((TOK, D)),
                whole((TOK, D)),
                whole((16, D)),
                own_rows,
                own_rows,
                hot_own,
                whole((8, D)),
                whole((8, HD)),
            ],
            (sds((4, SUB, D + SMALL), bf16), sds((4, SUB, D + SMALL), bf16)),
            (whole((4, SUB, D + SMALL)), whole((4, SUB, D + SMALL))),
            [pltpu.VMEM((D, D + SMALL), f32)],
            6,
            deps=[is_],
        )
        (pk1, ps1), = halves([(pk, pp(ps, masks[0]))], 2)
        ps1_got = pp(ps1, masks[1])
        if extra == 1:
            in_a, in_b = flat_call(
                in_parts_kernel, sc, [ik[0], is_got[0]], (sds((rows, 576), bf16),) * 2, us=2,
                deps=[ps1],
            )
        else:
            both = low_rows(add(ik[0], is_got[0]), col_low).astype(bf16).reshape(2, rows, 576)
            in_a = jnp.where(z1 == 1, both[1], both[0])
            in_b = jnp.where(z1 == 1, both[0], both[1])
        in_a = lax.ppermute(in_a, ("dp", "mp"), perm_a)
        in_b = lax.ppermute(in_b, ("dp", "mp"), back_b)
        (pk2, ps2), = halves([(pk1, ps1_got)], 2)
        ps2_got = pp(ps2, masks[2])
        s_up, s_down, s_out, sq_z = flat_call(
            share_z_kernel,
            sc,
            [z_out] + z_got,
            (
                sds((rows, D), f32),
                sds((rows, D), f32),
                sds((192, rows), f32),
                sds((8, 128), f32),
            ),
            us=3,
            deps=[ps2],
        )
        s_in, s_head, sq = flat_call(
            share_kernel,
            sc,
            [sq_z, in_a, in_b, gh, gh_got],
            (sds((rows, 576), f32), sds((rows, CLASSES), f32), sds((8, 128), f32)),
            us=2,
            deps=[ps2],
        )
        if extra == 1:
            p_ins = [pk2, ps2_got]
        else:
            total = low_rows(add(pk2[0], ps2_got[0]), low_bits).astype(bf16)[None]
            p_ins = [total, jnp.zeros_like(total)]
        wide = jnp.arange(D + SMALL)
        extra_row = jnp.where((wide == buck + 1) & (g == 0), jnp.sum(loss[:, 0]), 0.0)
        extra_row = jnp.broadcast_to(extra_row[None, :], (8, D + SMALL))
        mine_q = flat_call(
            patch_row_kernel, sc, p_ins + [sq, extra_row], (sds((rows + 16, D + SMALL), bf16),), us=2
        )[0]
        share_patch, stats = flat_call(
            patch_sum_kernel,
            sc,
            [mine_q, pp(mine_q, 0, 1), pp(mine_q, 0, 2), pp(mine_q, 0, 3)],
            (sds((rows, D + SMALL), f32), sds((8, SMALL), f32)),
            us=2,
        )
        stats = stats + pp(stats, 1)
        m = 2
        while m < n_dp:
            stats = (stats + pp(stats, m)) + (pp(stats, 2 * m) + pp(stats, 3 * m))
            m *= 4

        shares = [s_in, s_out, s_up, s_down, share_patch, s_head]
        turned = [x.T if n // 3 == 3 else x for n, x in enumerate(state)]
        news = simple_call(
            update_kernel,
            [stats] + shares + turned,
            tuple([sds((1, 1), f32), sds((1, NB), f32)] + [sds(s.shape, f32) for s in turned]),
            6,
        )
        outs = [x.T if n // 3 == 3 else x for n, x in enumerate(news[2:])]
        return (news[1].reshape(NB), counts, news[0].reshape(())) + tuple(outs)

    return local


def solution(mesh):
    shard = {
        "in": P("dp", "mp"),
        "out": P("mp", "dp"),
        "row": P("dp", None),
        "col": P(None, "dp"),
    }
    kinds = ["in", "out", "in", "out", "row", "col", "row", "col", "col"]
    triples = tuple(shard[k] for k in kinds for _ in range(3))
    in_specs = (P("dp", None),) + (P("dp"),) * 6 + triples
    out_specs = (P(), P(), P()) + triples
    return jax.shard_map(
        make_local(mesh.shape["dp"], mesh.shape["mp"]),
        mesh=mesh,
        in_specs=in_specs,
        out_specs=out_specs,
        check_vma=False,
    )
```

```python
import jax
import jax.numpy as jnp
from jax import lax
from jax.experimental import pallas as pl
from jax.experimental.pallas import tpu as pltpu
from jax.sharding import PartitionSpec as P

D = 768
HD = 64
HID = 3072
CLASSES = 1000
CPAD = 1024
GRID = 32
IMG = 16
NB = 4
STEP = 10
BQ = 256
TOK = 512
NH = 3
QK = 2 * NH * HD
SUB = D // 8
SMALL = 128
OW = 256
LANE_GAIN = 64
LANE_QG = 68
LANE_COUNT = 72

HIGH = lax.Precision.HIGHEST
NORM_EPS = 1e-06
CLIP = 0.1
BETA_ONE = 0.9
BETA_TWO = 0.95
RATE_MATRIX = 0.05
RATE_SMALL = 0.2
DECAY = 0.05
ADAM_EPS = 1e-08
BIG = 128.0

bf16 = jnp.bfloat16
f32 = jnp.float32
VLIM = 56 * 1024 * 1024
COST = 0.001 * 1.15e9

NN = (((1,), (0,)), ((), ()))
NT = (((1,), (1,)), ((), ()))
TN = (((0,), (0,)), ((), ()))


def dot(a, b, dims=NN, precision=None):
    return lax.dot_general(a, b, dims, precision=precision, preferred_element_type=f32)


def norm_stats(values):
    center = values - jnp.mean(values, axis=-1, keepdims=True)
    inv_std = lax.rsqrt(jnp.mean(center * center, axis=-1, keepdims=True) + NORM_EPS)
    return center * inv_std, inv_std


def norm_back(grad_scaled, scaled, inv_std):
    return inv_std * (
        grad_scaled
        - jnp.mean(grad_scaled, axis=-1, keepdims=True)
        - scaled * jnp.mean(grad_scaled * scaled, axis=-1, keepdims=True)
    )


def splits(x, n):
    out = []
    for _ in range(n - 1):
        part = x.astype(bf16)
        out.append(part)
        x = x - part.astype(f32)
    out.append(x.astype(bf16))
    return out


def dot_split(x, exact, n, dims=NN):
    total = None
    for part in splits(x, n):
        term = dot(part, exact, dims)
        total = term if total is None else total + term
    return total


def head_mean(x, ones, n):
    return jnp.concatenate(
        [dot_split(x[:, c : c + 128], ones, n) for c in range(0, QK, 128)], axis=1
    )


def eye(rows, cols, offset=0):
    row = lax.broadcasted_iota(jnp.int32, (rows, cols), 0)
    col = lax.broadcasted_iota(jnp.int32, (rows, cols), 1)
    return (row + offset == col).astype(f32)


def rows_at(index, size):
    return pl.ds(pl.multiple_of(index * size, size), size)


def pack_kernel(w_patch, w_pos, w_gain, w_qg, seg, keep, bucket, w_up, w_down,
                patch_o, t_o):
    rows = w_patch.shape[0]
    patch_o[:, :D] = w_patch[...].astype(bf16)
    low = lambda ref: ref[...].astype(bf16).astype(f32)
    small = dot(low(w_pos), eye(64, SMALL), TN)
    small += dot(low(w_gain), eye(4, SMALL, LANE_GAIN), TN)
    qg = dot(low(w_qg), eye(2, SMALL, LANE_QG), TN)
    small += dot(eye(rows, qg.shape[0]), qg)
    kept = keep[...] == 1
    count = jnp.zeros((1, 1), f32)
    for n in range(IMG):
        held = jnp.where((seg[...] == n) & kept, 1.0, 0.0)
        count += jnp.max(held, keepdims=True)
    row = lax.broadcasted_iota(jnp.int32, (rows, SMALL), 0)
    col = lax.broadcasted_iota(jnp.int32, (rows, SMALL), 1)
    small += jnp.where((row == 0) & (col == LANE_COUNT + bucket[0]), count, 0.0)
    patch_o[:, D:] = small.astype(bf16)

    t_o[:, :D] = w_up[...].astype(bf16)
    t_o[:, D:] = w_down[...].astype(bf16)


def pack_rest_kernel(w_in, w_out, in_o, out_o):
    rows = w_in.shape[0]
    w = w_in[...].astype(bf16)
    parts = [
        w[:, h * 192 + part * HD : h * 192 + part * HD + HD]
        for part in range(3)
        for h in range(NH)
    ]
    in_o[...] = jnp.concatenate(parts, axis=1)
    turned = dot(eye(rows, rows).astype(bf16), w_out[...].astype(bf16), NT)
    out_o[...] = jnp.concatenate([turned, jnp.zeros((rows, OW - 192), f32)], axis=1).astype(bf16)


def ordered(flag, x, y):
    return jnp.where(flag, jnp.concatenate([y, x], axis=1), jnp.concatenate([x, y], axis=1))


def lanes_at(index, width):
    return pl.ds(pl.multiple_of(index * width, width), width)


def out_kernel(sc, o0, o1, o2, o3, out):
    for r, ref in enumerate((o0, o1, o2, o3)):
        out[:, lanes_at(sc[2] ^ r, OW)] = ref[...]


def head_pack_kernel(head, out):
    out[...] = jnp.zeros_like(out)
    out[:, :CLASSES] = head[...].astype(bf16)


def eight(refs):
    return list(refs[:4]) + [refs[4].at[n] for n in range(4)]


REL = [0, 2, 4, 6, 1, 3, 5, 7]


def stack_kernel(a, b, c, d, out):
    for n, ref in enumerate((a, b, c, d)):
        out[n] = ref[...]


def row_copies(refs, me, dst, sems, rel=REL):
    out = []
    for n, ref in enumerate(refs):
        size = ref.shape[0]
        out.append(pltpu.make_async_copy(ref, dst.at[rows_at(me ^ rel[n], size), :], sems.at[n]))
    return out


def columns(refs, lo, width):
    return [ref.at[:, pl.ds(lo, width)] for ref in refs]


def start(copies):
    for copy in copies:
        copy.start()


def wait(copies):
    for copy in copies:
        copy.wait()


def x0_kernel(sc, own, other, hot, *rest):
    refs = eight(rest[:5])
    a_out, x0_out, gx_out, w, sems = rest[5:]
    i = pl.program_id(0)

    @pl.when(i == 0)
    def _():
        copies = row_copies(refs, sc[0], w, sems)
        start(copies)
        wait(copies)
        row = lax.broadcasted_iota(jnp.int32, (16, SMALL), 0)
        col = lax.broadcasted_iota(jnp.int32, (16, SMALL), 1)
        pick = (row + LANE_GAIN == col).astype(f32).astype(bf16)
        gx_out[...] = dot(pick, w[:, D:], NT)

    rows = jnp.where(sc[3] == 1, own[...], other[...])
    x0 = dot(rows, w[:, :D]) + dot(hot[...], w[:, D:], NT)
    scaled, _ = norm_stats(x0)
    a_out[...] = (scaled * gx_out[0:1, :]).astype(bf16)

    @pl.when(i == sc[1])
    def _():
        x0_out[...] = x0


IN_REL = [0, 1, 2, 3]


def qkv_kernel(sc, a, qaux, kaux, vaux, gain, avg, *rest):
    refs = rest[:4]
    qx, kx, vx, xh_out, inv_out, w, sems = rest[4:]
    i = pl.program_id(0)

    @pl.when(i == 0)
    def _():
        copies = row_copies(refs, sc[4], w, sems, IN_REL)
        start(copies)
        wait(copies)

    mixed = dot(a[...], w[...])
    qk = mixed[:, :QK]
    v = mixed[:, QK:].astype(bf16)
    ones = avg[...]
    center = qk - head_mean(qk, ones, 2)
    inv = lax.rsqrt(head_mean(center * center, ones, 2) + NORM_EPS)
    scaled = center * inv
    xh_out[...] = scaled
    inv_out[...] = inv
    low = (scaled * gain[0:1, :]).astype(bf16)
    qa, ka, va = qaux[...], kaux[...], vaux[...]
    for h in range(NH):
        qx[h] = jnp.concatenate([low[:, h * HD : h * HD + HD], qa], axis=1)
        kx[h] = jnp.concatenate([low[:, (NH + h) * HD : (NH + h) * HD + HD], ka], axis=1)
        vx[h] = jnp.concatenate([v[:, h * HD : h * HD + HD], va], axis=1)


def attn_kernel(rel, sc, qx, kx, vx, o_first, o_second, o_full, ql, acc):
    step_id = pl.program_id(0)
    i = 2 * (sc[1] ^ jnp.where(step_id < 2, rel[0], rel[1])) + step_id % 2
    acc[...] = jnp.zeros_like(acc)
    lo, hi = sc[8 + i], sc[16 + i]

    def tile(start_row, size):
        ks = pl.ds(pl.multiple_of(start_row, BQ), size)
        scores = [dot(qx[h], kx[h, ks, :], NT) for h in range(NH)]
        probs = [jnp.exp(s).astype(bf16) for s in scores]
        for h in range(NH):
            acc[h] += dot(probs[h], vx[h, ks, :])

    pairs = (hi - lo) // 2

    def step(j, carry):
        tile((lo + 2 * j) * BQ, 2 * BQ)
        return carry

    lax.fori_loop(0, pairs, step, 0)

    @pl.when((hi - lo) % 2 == 1)
    def _():
        tile((hi - 1) * BQ, BQ)

    mine = rows_at(i, BQ)
    lane = lax.broadcasted_iota(jnp.int32, (BQ, 128), 1)
    outs = []
    for h in range(NH):
        q = qx[h].astype(f32)
        k = kx[h, mine, :].astype(f32)
        v = vx[h, mine, :].astype(f32)
        free = k[:, 84:85]
        diag = jnp.sum(jnp.where(lane < HD, q * k, 0.0), axis=1, keepdims=True)
        p = jnp.exp(diag) * free
        out = acc[h] + p.astype(bf16).astype(f32) * v
        total = out[:, 64:65]
        outs.append(out[:, :HD] / total)
        for n, part in enumerate(splits(-jnp.log(total), 3)):
            q = jnp.where(lane == 81 + n, part.astype(f32), q)
        ql[h] = q.astype(bf16)
    full = jnp.concatenate(outs, axis=1)
    o_full[...] = full
    low = jnp.concatenate([full, jnp.zeros((BQ, OW - NH * HD), f32)], axis=1).astype(bf16)

    @pl.when(step_id < 2)
    def _():
        o_first[...] = low

    @pl.when(step_id >= 2)
    def _():
        o_second[...] = low


GELU_C = 0.7978845608028654


def gelu_tanh(u):
    return jnp.tanh(GELU_C * (u + 0.044715 * u * u * u))


def mlp_tile(b, w, u_out, h_out):
    u = dot(b, w[0])
    u_out[...] = u
    h = (0.5 * u * (1.0 + gelu_tanh(u))).astype(bf16)
    h_out[...] = h
    return dot(h, w[1], NT)


def tile_copies(w_all, j, dst, sems):
    size = D // 8
    return [
        pltpu.make_async_copy(
            w_all.at[d, j, :, pl.ds(part * D, D)],
            dst.at[part, pl.ds(d * size, size), :],
            sems.at[part, d],
        )
        for part in range(2)
        for d in range(8)
    ]


def mlp_kernel(sc, o0, o1, o2, o3, x0, gx, mem, heads, *rest):
    refs, w_all = eight(rest[:5]), rest[5]
    x1_out, b_out, u_out, h_out, x2, ns_out, w_o, w_t, sem_o, sem_t = rest[6:]
    j = pl.program_id(0)

    @pl.when(j == 0)
    def _():
        first = row_copies(refs, sc[0], w_o, sem_o)
        start(first)
        for t in range(4):
            start(tile_copies(w_all, t, w_t.at[t], sem_t.at[t]))
        wait(first)
        x1 = x0[...]
        for r, ref in enumerate((o0, o1, o2, o3)):
            x1 += dot(ref[...], w_o[:, lanes_at(sc[1] ^ r, OW)], NT)
        x1_out[...] = x1
        b_out[...] = (norm_stats(x1)[0] * gx[1:2, :]).astype(bf16)
        x2[...] = x1

    wait(tile_copies(w_all, j, w_t.at[j], sem_t.at[j]))
    x2[...] += mlp_tile(b_out[...], w_t.at[j], u_out, h_out)

    @pl.when(j == 3)
    def _():
        f = norm_stats(x2[...])[0] * gx[2:3, :]
        ones = heads[...]
        e = jnp.exp(dot_split(f * gx[3:4, :], ones, 3) * 0.125)
        eb = dot_split(e, ones, 2, NT)
        m = mem[...]
        num = jnp.zeros((IMG, D), f32)
        for part in splits(eb * f, 3):
            num += dot(m, part, TN)
        den = jnp.zeros((IMG, 128), f32)
        for part in splits(e, 3):
            den += dot(m, part, TN)
        ns_out[:, :D] = num
        ns_out[:, D:] = den


def head_kernel(sc, ns_a, ns_b, lab, vt, heads, *rest):
    pooled_out, gp_out, sinv_out, loss_out, gh_out, gh_send, w, gw, sems = rest[5:]
    copies = row_copies(eight(rest[:5]), sc[0], w, sems)
    start(copies)
    ns = ns_a[...] + ns_b[...]
    valid = vt[:, 0:1]
    scale = vt[:, 1:2]
    total = jnp.where(valid > 0.0, ns[:, D:], 1.0)
    sinv = jnp.where(valid > 0.0, 1.0 / total, 0.0)
    lane = lax.broadcasted_iota(jnp.int32, (IMG, 128), 1)
    sinv = jnp.where(lane < D // HD, sinv, 0.0)
    pooled = ns[:, :D] * dot_split(sinv, heads[...], 3, NT)
    low = pooled.astype(bf16)
    wait(copies)
    logits = dot(low, w[...])
    cls = lax.broadcasted_iota(jnp.int32, (IMG, CPAD), 1)
    real = (cls < CLASSES).astype(f32)
    hot = lab[...]
    ex = jnp.exp(-jnp.abs(logits))
    soft = jnp.maximum(logits, 0.0) + jnp.log1p(ex)
    per = jnp.sum(soft * real, axis=1, keepdims=True) - jnp.sum(
        logits * hot, axis=1, keepdims=True
    )
    loss_out[...] = jnp.broadcast_to(per * valid, (IMG, 128))
    sig = jnp.where(logits >= 0.0, 1.0, ex) / (1.0 + ex)
    gl = (scale * (sig * real - hot)).astype(bf16)
    pooled_out[...] = pooled
    sinv_out[...] = sinv
    gp_out[...] = dot(gl, w[...], NT)
    half = jnp.where(sc[2] % 2 == 1, gl[:, 512:].astype(f32), gl[:, :512].astype(f32))
    gw[...] = dot(low, half.astype(bf16), TN)
    for p, r in enumerate(rel_order(2)):
        gh_out[p] = gw[rows_at(sc[0] ^ r, SUB), :].astype(bf16)
        gh_send[p] = gw[rows_at(sc[0] ^ (r + 1), SUB), :].astype(bf16)


def rel_order(first):
    m1, m2 = (2, 4) if first == 2 else (4, 2)
    return [(p >> 1) * m1 + (p & 1) * m2 for p in range(4)]


def back_kernel(sc, u, x2, x1, gx, mem, pooled, gp, sinv, heads, *rest):
    refs, w_all = eight(rest[:5]), rest[5]
    gu_out, gr_out, gm_out, gmid_out = rest[6:10]
    ga_out, small_out = rest[10:14], rest[14]
    w_t, w_o, grs, acc, sem_t, sem_o = rest[15:]
    j = pl.program_id(0)

    def out_rows():
        return row_copies(refs, sc[0], w_o, sem_o)

    @pl.when(j == 0)
    def _():
        for t in range(4):
            start(tile_copies(w_all, t, w_t.at[t], sem_t.at[t]))
        start(out_rows())
        scaled, inv = norm_stats(x2[...])
        f = scaled * gx[2:3, :]
        probe = gx[3:4, :]
        ones = heads[...]
        e = jnp.exp(dot_split(f * probe, ones, 3) * 0.125)
        m = mem[...]
        m3 = jnp.concatenate([m, m, m], axis=1)

        def spread(x):
            return dot(m3, jnp.concatenate(splits(x, 3), axis=0))

        gt = spread(gp[...])
        at = e * spread(sinv[...])
        gpp = dot_split(gp[...] * pooled[...], ones, 3)
        da = dot_split(gt * f, ones, 3)
        dc = at * (da - spread(gpp))
        dcb = dot_split(dc, ones, 2, NT) * 0.125
        df = dot_split(at, ones, 2, NT) * gt + dcb * probe
        gr = norm_back(df * gx[2:3, :], scaled, inv)
        grs[...] = gr
        gr_out[...] = gr.astype(bf16)
        small_out[2:3, :] = jnp.sum(df * scaled, axis=0, keepdims=True)
        small_out[3:4, :] = jnp.sum(dcb * f, axis=0, keepdims=True)
        small_out[0:1, :] = jnp.zeros((1, D), f32)
        small_out[4:8, :] = jnp.zeros((4, D), f32)
        acc[...] = jnp.zeros_like(acc)

    wait(tile_copies(w_all, j, w_t.at[j], sem_t.at[j]))
    gh = dot(gr_out[...], w_t[j, 1])
    v = u[...]
    t = gelu_tanh(v)
    slope = 0.5 * (1.0 + t) + 0.5 * v * (1.0 - t * t) * GELU_C * (1.0 + 0.134145 * v * v)
    gu = (gh * slope).astype(bf16)
    gu_out[...] = gu
    acc[...] += dot(gu, w_t[j, 0], NT)

    @pl.when(j == 3)
    def _():
        wait(out_rows())
        scaled, inv = norm_stats(x1[...])
        gb = acc[...]
        small_out[1:2, :] = jnp.sum(gb * scaled, axis=0, keepdims=True)
        gmid = grs[...] + norm_back(gb * gx[1:2, :], scaled, inv)
        gmid_out[...] = gmid
        low = gmid.astype(bf16)
        gm_out[...] = low
        for r in range(4):
            ga_out[r][...] = dot(low, w_o[:, lanes_at(sc[1] ^ r, OW)]).astype(bf16)


def wgrad_kernel(sc, gr, h, b, gu, gm, o0, o1, o2, o3, out, os):
    j = pl.program_id(0)

    @pl.when(j == 0)
    def _():
        for r, ref in enumerate((o0, o1, o2, o3)):
            os[r] = ref[...]

    parts = [
        (0, dot(b[...], gu[...], TN)),
        (D, dot(gr[...], h[...], TN)),
        (2 * D, dot(gm[...], os[sc[1] ^ j], TN)),
    ]
    for lo, value in parts:
        width = value.shape[1]
        for d in range(8):
            out[d, 0, :, lo : lo + width] = value[d * SUB : (d + 1) * SUB, :].astype(bf16)


def attn_back_kernel(sc, ql_a, ql_b, of_a, of_b, d0, d1, d2, d3, kx, vx, g_out, dq, dk, dv, dos):
    i = pl.program_id(0)
    nq = dk.shape[1] // BQ

    @pl.when(i == 0)
    def _():
        for n, ref in enumerate((d3, d1, d2, d0)):
            dos[n] = ref[...]

    @pl.when(i == 0)
    def _():
        dk[...] = jnp.zeros_like(dk)
        dv[...] = jnp.zeros_like(dv)

    @pl.when(i < nq)
    def _():
        n = i // 2
        block = 2 * (sc[1] ^ jnp.where(n < 2, 3 - 2 * n, 6 - 2 * n)) + i % 2
        mine = rows_at(block, BQ)
        lane = lax.broadcasted_iota(jnp.int32, (BQ, 128), 1)
        inner = (lane < HD) | ((lane >= 81) & (lane < 84))
        first = i < nq // 2
        of = jnp.where(first, of_a[...], of_b[...])
        do = dos[n, rows_at(i % 2, BQ), :].astype(f32)
        dob, qb = [], []
        for h in range(NH):
            dof = do[:, h * HD : h * HD + HD]
            delta = jnp.sum(dof * of[:, h * HD : h * HD + HD], axis=1, keepdims=True)
            dox = jnp.concatenate([dof, jnp.zeros((BQ, HD), f32)], axis=1)
            for m, part in enumerate(splits(-delta, 3)):
                dox = jnp.where(lane == HD + m, part.astype(f32), dox)
            q = jnp.where(first, ql_a[h].astype(f32), ql_b[h].astype(f32))
            k = kx[h, mine, :].astype(f32)
            v = vx[h, mine, :].astype(f32)
            free = k[:, 84:85]
            p = jnp.exp(jnp.sum(jnp.where(inner, q * k, 0.0), axis=1, keepdims=True)) * free
            ds = p * jnp.sum(jnp.where(lane < HD + 3, dox * v, 0.0), axis=1, keepdims=True)
            ds = ds.astype(bf16).astype(f32)
            dq[h, mine, :] = ds * k
            dk[h, mine, :] += ds * q
            dv[h, mine, :] += p.astype(bf16).astype(f32) * dox
            dob.append(dox.astype(bf16))
            qb.append(q.astype(bf16))

        def tile(start_row, size):
            ks = pl.ds(pl.multiple_of(start_row, BQ), size)
            pts = [jnp.exp(dot(kx[h, ks, :], qb[h], NT)) for h in range(NH)]
            dpts = [dot(vx[h, ks, :], dob[h], NT) for h in range(NH)]
            dsts = [(pts[h] * dpts[h]).astype(bf16) for h in range(NH)]
            for h in range(NH):
                dv[h, ks, :] += dot(pts[h].astype(bf16), dob[h])
                dk[h, ks, :] += dot(dsts[h], qb[h])
                dq[h, mine, :] += dot(dsts[h], kx[h, ks, :], TN)

        lo, hi = sc[8 + block], sc[16 + block]

        def step(j, carry):
            tile((lo + 2 * j) * BQ, 2 * BQ)
            return carry

        lax.fori_loop(0, (hi - lo) // 2, step, 0)

        @pl.when((hi - lo) % 2 == 1)
        def _():
            tile((hi - 1) * BQ, BQ)

    @pl.when(i >= nq)
    def _():
        rows = rows_at(i - nq, TOK)
        g_out[...] = jnp.concatenate(
            [ref[h, rows, :][:, :HD] for ref in (dq, dk, dv) for h in range(NH)], axis=1
        )


def mix_kernel(sc, grad, xh, inv, a, gain, avg, *rest):
    refs = rest[:4]
    g_send, g_one, g_own, in_keep, in_send, qg_out, gin, w, sems = rest[4:]
    n = pl.program_id(0)

    @pl.when(n == 0)
    def _():
        copies = row_copies(refs, sc[4], w, sems, IN_REL)
        start(copies)
        gin[...] = jnp.zeros_like(gin)
        qg_out[...] = jnp.zeros_like(qg_out)
        wait(copies)

    grads = grad[:, :QK]
    scaled = xh[...]
    ones = avg[...]
    qg_out[0:1, :] += jnp.sum(grads * scaled, axis=0, keepdims=True)
    dg = grads * gain[0:1, :]
    back = inv[...] * (
        dg - head_mean(dg, ones, 2) - scaled * head_mean(dg * scaled, ones, 2)
    )
    mix = jnp.concatenate([back, grad[:, QK:]], axis=1).astype(bf16)
    out = dot(mix, w[...], NT).astype(bf16)
    gin[...] += dot(a[...], mix, TN)

    @pl.when(n < 2)
    def _():
        g_send[0] = out

    @pl.when(n == 2)
    def _():
        g_one[...] = out

    @pl.when(n == 3)
    def _():
        g_own[...] = out
        size = D // 4
        for p in range(2):
            in_keep[p] = gin[rows_at(sc[4] ^ (2 * p), size), :].astype(bf16)
            in_send[p] = gin[rows_at(sc[4] ^ (2 * p + 1), size), :].astype(bf16)


def add(x, y):
    return x.astype(f32) + y.astype(f32)


def halve_kernel(sc, kept, got, keep_o, send_o):
    half = keep_o.shape[0]
    for n in range(half):
        keep_o[n] = add(kept[n], got[n]).astype(bf16)
        send_o[n] = add(kept[half + n], got[half + n]).astype(bf16)


def in_parts_kernel(sc, kept, got, a_out, b_out):
    half = a_out.shape[0]
    first = sc[5]
    mine, other = rows_at(first, half), rows_at(1 - first, half)
    a_out[...] = add(kept[mine, :], got[mine, :]).astype(bf16)
    b_out[...] = add(kept[other, :], got[other, :]).astype(bf16)


def share_z_kernel(sc, z0, z1, z2, z3, up_o, down_o, out_o, sq_o):
    rows = up_o.shape[0]
    total = add(z0[0], z1[...]) + add(z2[...], z3[...])
    up_o[...] = total[:, :D]
    down_o[...] = total[:, D : 2 * D]
    out_o[...] = dot(total[:, 2 * D :], eye(rows, rows), TN, HIGH)[:192, :]
    sq_o[...] = jnp.broadcast_to(jnp.sum(total * total, keepdims=True), sq_o.shape)


def share_kernel(sc, sq_z, in_a, in_b, h_own, h_got, in_o, head_o, sq_o):
    grad = add(in_a[...], in_b[...])
    in_o[...] = jnp.concatenate(
        [
            grad[:, part * NH * HD + h * HD : part * NH * HD + h * HD + HD]
            for h in range(NH)
            for part in range(3)
        ],
        axis=1,
    )
    head = ordered(sc[2] % 2 == 1, h_own[...], h_got[...])
    head_o[...] = head[:, :CLASSES]
    squares = jnp.sum(grad * grad, keepdims=True)
    once = jnp.where(sc[2] == 0, 1.0, 0.0)
    squares += once * jnp.sum(head * head, keepdims=True)
    sq_o[...] = sq_z[...] + squares


def patch_row_kernel(sc, kept, got, sq, extra_row, out):
    rows = kept.shape[1]
    out[:rows, :] = add(kept[0], got[0]).astype(bf16)
    lane = lax.broadcasted_iota(jnp.int32, (16, D + SMALL), 1)
    row = lax.broadcasted_iota(jnp.int32, (16, D + SMALL), 0)
    value = jnp.where(lane == 0, sq[0:1, 0:1], extra_row[0:1, :])
    tail = jnp.zeros((16, D + SMALL), f32)
    for n, part in enumerate(splits(value, 3)):
        tail = jnp.where(row == n, part.astype(f32), tail)
    out[rows:, :] = tail.astype(bf16)


def patch_sum_kernel(sc, own, q1, q2, q3, share_o, stats_o):
    rows = share_o.shape[0]
    total = add(own[...], q1[...]) + add(q2[...], q3[...])
    patch = total[:rows, :]
    share_o[...] = patch
    sums = total[rows : rows + 1, :SMALL] + total[rows + 1 : rows + 2, :SMALL]
    sums += total[rows + 2 : rows + 3, :SMALL]
    lane = lax.broadcasted_iota(jnp.int32, (8, SMALL), 1)
    squares = jnp.sum(patch * patch, keepdims=True)
    stats_o[...] = sums + jnp.where(lane == 0, squares, 0.0)


def tail_kernel(n_dp, sc, g_own, g_core, g_z, gmid, x0, gx, own, other, hot, small_b, qgrad,
                pk, ps, tile):
    grad = g_own[...].astype(f32) + g_core[0].astype(f32) + g_z[...].astype(f32)
    scaled, inv = norm_stats(x0[...])
    gain_a = jnp.sum(grad * scaled, axis=0, keepdims=True)
    ge = (gmid[...] + norm_back(grad * gx[0:1, :], scaled, inv)).astype(bf16)
    rows = jnp.where(sc[3] == 1, own[...], other[...])
    tile[:, :D] = dot(rows, ge, TN)
    row8 = lax.broadcasted_iota(jnp.int32, (8, D), 0)
    gains = jnp.where(row8 == 0, gain_a, small_b[...])
    small = dot(ge, hot[...], TN) + dot(gains, eye(8, SMALL, LANE_GAIN), TN)
    part = HD // n_dp
    kk = lax.broadcasted_iota(jnp.int32, (HD, D), 0)
    rr = lax.broadcasted_iota(jnp.int32, (HD, D), 1)
    spot = ((kk // part) * (D // n_dp) + kk % part == rr).astype(f32)
    lane = lax.broadcasted_iota(jnp.int32, (8, SMALL), 1)
    row = lax.broadcasted_iota(jnp.int32, (8, SMALL), 0)
    q_lane = ((lane == LANE_QG + row) & (row < 2)).astype(f32)
    q_cols = dot(qgrad[...], q_lane, TN, HIGH)
    small += dot(spot, q_cols, TN)
    tile[:, D:] = small
    for p, r in enumerate(rel_order(2)):
        pk[p] = tile[rows_at(sc[0] ^ r, SUB), :].astype(bf16)
        ps[p] = tile[rows_at(sc[0] ^ (r + 1), SUB), :].astype(bf16)


def update_kernel(stats, *rest):
    shares = rest[:6]
    state = rest[6:33]
    norm_out, loss_out, outs = rest[33], rest[34], rest[35:]
    total = stats[0:1, :]
    norm = jnp.sqrt(total)
    norm_out[...] = norm[:, 0:1]
    loss_out[...] = total[:, 1 : 1 + NB]
    factor = jnp.minimum(1.0, CLIP / (norm[:, 0:1] + 1e-06))
    s_in, s_out, s_up, s_down, s_patch, s_head = shares
    rows = s_patch.shape[0]
    small = dot(eye(SMALL, SMALL), s_patch[:, D:], NT, HIGH)
    part = state[24].shape[1]
    grads = [
        s_in[...],
        s_out[...],
        s_up[...],
        s_down[...],
        s_patch[:, :D],
        small[: 2 * GRID, :],
        s_head[...],
        small[LANE_GAIN : LANE_GAIN + 4, :],
        small[LANE_QG : LANE_QG + 2, :part],
    ]
    for n in range(9):
        master, first, second = state[3 * n : 3 * n + 3]
        clipped = grads[n] * factor
        first_new = BETA_ONE * first[...] + (1.0 - BETA_ONE) * clipped
        second_new = BETA_TWO * second[...] + (1.0 - BETA_TWO) * clipped * clipped
        matrix = n in (0, 1, 2, 3, 4, 6)
        rate = RATE_MATRIX if matrix else RATE_SMALL
        decay = DECAY if matrix else 0.0
        ratio = (
            first_new
            / (1.0 - BETA_ONE**STEP)
            / (jnp.sqrt(second_new / (1.0 - BETA_TWO**STEP)) + ADAM_EPS)
        )
        value = master[...]
        outs[3 * n][...] = value - rate * (ratio + decay * value)
        outs[3 * n + 1][...] = first_new
        outs[3 * n + 2][...] = second_new


ANY = pl.BlockSpec(memory_space=pl.ANY)


def without(kernel, count, deps):
    if not deps:
        return kernel
    return lambda *refs: kernel(*refs[:count], *refs[count + len(deps) :])


def call(kernel, grid, sc, ins, specs, outs, out_specs, scratch, us=5, deps=()):
    return pl.pallas_call(
        without(kernel, 1 + len(ins), deps),
        out_shape=outs,
        grid_spec=pltpu.PrefetchScalarGridSpec(
            num_scalar_prefetch=1,
            grid=grid,
            in_specs=list(specs) + [ANY] * len(deps),
            out_specs=out_specs,
            scratch_shapes=scratch,
        ),
        compiler_params=pltpu.CompilerParams(vmem_limit_bytes=VLIM),
        cost_estimate=pl.CostEstimate(
            flops=int(us * COST), bytes_accessed=1000, transcendentals=0
        ),
    )(sc, *ins, *deps)


def flat_call(kernel, sc, ins, outs, scratch=(), us=3, deps=()):
    return call(
        kernel,
        (1,),
        sc,
        ins,
        [whole(x.shape) for x in ins],
        outs,
        tuple(whole(o.shape) for o in outs),
        list(scratch),
        us,
        deps,
    )


def simple_call(kernel, ins, outs, us=3, deps=()):
    return pl.pallas_call(
        without(kernel, len(ins), deps),
        out_shape=outs,
        in_specs=[pl.BlockSpec(memory_space=pltpu.VMEM)] * len(ins) + [ANY] * len(deps),
        compiler_params=pltpu.CompilerParams(vmem_limit_bytes=VLIM),
        cost_estimate=pl.CostEstimate(
            flops=int(us * COST), bytes_accessed=1000, transcendentals=0
        ),
    )(*ins, *deps)


def whole(shape):
    return pl.BlockSpec(shape, lambda i, s: (0,) * len(shape))


def sds(shape, dtype):
    return jax.ShapeDtypeStruct(shape, dtype)


DMA = pltpu.SemaphoreType.DMA


def make_local(n_dp, n_mp):
    extra = n_dp // 8
    masks = [extra, 2 * extra, 4 * extra]
    low_bits = [b for b in (1, 2, 4, 8, 16, 32) if b < extra]
    col_low = [2 * b for b in low_bits]
    col_masks = [2 * extra, 4 * extra]

    def pp(x, dmask, zmask=0):
        perm = [
            (d * n_mp + z, (d ^ dmask) * n_mp + (z ^ zmask))
            for d in range(n_dp)
            for z in range(n_mp)
        ]
        return lax.ppermute(x, ("dp", "mp"), perm)

    def local(patches, segment, keep, pos_y, pos_x, labels, bucket, *state):
        masters = state[0::3]
        (attend_in, attend_out, expand, contract, patch_embed, pos_table, class_head,
         norm_gains, query_gains) = masters
        length = patches.shape[0]
        rows = patch_embed.shape[0]
        nq = length // BQ
        dp = lax.axis_index("dp")
        z = lax.axis_index("mp")
        core = dp % 2
        z1, z0 = z // 2, z % 2
        g = z0 + 2 * core
        me = dp // extra
        mecol = (dp // 2) // extra
        mine = core == z1

        def bit_of(mask):
            return (dp // mask) % 2 == 1

        def swap(flag, x, y, axis):
            return jnp.where(
                flag, jnp.concatenate([y, x], axis=axis), jnp.concatenate([x, y], axis=axis)
            )

        def pick4(parts, index, axis):
            odd, high = index % 2 == 1, index // 2 == 1
            lo = swap(odd, parts[0], parts[1], axis)
            hi = swap(odd, parts[2], parts[3], axis)
            return swap(high, lo, hi, axis)

        patch_w, t_w = pl.pallas_call(
            pack_kernel,
            out_shape=(
                sds((rows, D + SMALL), bf16),
                sds((rows, 2 * D), bf16),
            ),
            in_specs=[pl.BlockSpec(memory_space=pltpu.VMEM)] * 6
            + [pl.BlockSpec(memory_space=pltpu.SMEM)]
            + [pl.BlockSpec(memory_space=pltpu.VMEM)] * 2,
            compiler_params=pltpu.CompilerParams(vmem_limit_bytes=VLIM),
        )(patch_embed, pos_table, norm_gains, query_gains, segment.reshape(-1, 128),
          keep.reshape(-1, 128), bucket, expand, contract.T)
        w_all = lax.all_gather(t_w, ("dp", "mp"), axis=0, tiled=True)
        w_all = w_all.reshape(8, extra, n_mp, rows, 2 * D)
        if extra > 1:
            w_all = w_all.transpose(0, 2, 1, 3, 4)
        w_all = w_all.reshape(8, n_mp, SUB, 2 * D)

        perm_core = [
            (d * n_mp + zz, (d ^ 1) * n_mp + zz)
            for d in range(n_dp)
            for zz in range(n_mp)
            if d % 2 == zz // 2
        ]
        patches_in = lax.ppermute(patches, ("dp", "mp"), perm_core)
        meta = jnp.stack([segment, keep, pos_y, pos_x])
        tag = jnp.concatenate([labels, bucket, jnp.zeros((length - IMG - 1,), jnp.int32)])
        meta = jnp.concatenate([meta, tag[None]], axis=0)
        meta_in = lax.ppermute(meta, ("dp", "mp"), perm_core)
        meta = jnp.where(mine, meta, meta_in)

        def widen(x, low):
            for b in low:
                x = swap(bit_of(b), x, pp(x, b), -2)
            return x

        def across(x):
            one, two = pp(x, masks[1]), pp(x, masks[2])
            return [x, one, two, pp(one, masks[2])]

        def stack(parts, deps):
            high, width = parts[0].shape
            cuts = 1 if width < 2048 else 4
            step = width // cuts
            return pl.pallas_call(
                without(stack_kernel, 4, deps),
                out_shape=sds((4, high, width), bf16),
                grid=(cuts,),
                in_specs=[pl.BlockSpec((high, step), lambda i: (0, i))] * 4 + [ANY] * len(deps),
                out_specs=pl.BlockSpec((4, high, step), lambda i: (0, 0, i)),
                compiler_params=pltpu.CompilerParams(vmem_limit_bytes=VLIM),
                cost_estimate=pl.CostEstimate(flops=int(COST), bytes_accessed=1000, transcendentals=0),
            )(*parts, *deps)

        def direct(x):
            return [x] + [pp(x, m) for m in (masks[1], masks[2], masks[1] | masks[2])]

        def all8(parts, deps=()):
            stacked = stack(parts, deps)
            return parts + [pp(stacked, masks[0])], stacked

        patch_c = direct(widen(patch_w, low_bits))
        in_w, out_w = simple_call(
            pack_rest_kernel,
            [attend_in, attend_out],
            (sds((rows, 576), bf16), sds((rows, OW), bf16)),
            deps=[meta_in],
        )

        perm_a, perm_b, back_b = [], [], []
        for d in range(n_dp):
            for zz in range(n_mp):
                c, a1, a0 = d % 2, zz // 2, zz % 2
                src = d * n_mp + zz
                perm_a.append((src, (d - c + a1) * n_mp + a0 + 2 * c))
                perm_b.append((src, (d - c + a1) * n_mp + a0 + 2 * (1 - c)))
                back_b.append((src, (d - c + 1 - a1) * n_mp + a0 + 2 * c))
        in_a = lax.ppermute(in_w, ("dp", "mp"), perm_a)
        in_b = lax.ppermute(in_w, ("dp", "mp"), perm_b)
        patch_p, _ = all8(patch_c, [patches_in])
        in_own = widen(swap(z1 == 1, in_a, in_b, 0), col_low)
        in_one, in_two = pp(in_own, col_masks[0]), pp(in_own, col_masks[1])
        in_p = [in_own, in_one, in_two, pp(in_own, col_masks[0] | col_masks[1])]
        o_one, o_two = pp(out_w, 0, 1), pp(out_w, 0, 2)
        out_z = [out_w, o_one, o_two, pp(o_two, 0, 1)]

        seg, kp, py, px = meta[0], meta[1], meta[2], meta[3]
        labs = meta[4, :IMG]
        buck = meta[4, IMG]
        kept = (kp == 1) & (seg < IMG)
        ids = jnp.arange(128)[None, :]
        ids64 = ids[:, :64]
        hot_pos = ((py[:, None] == ids) | (px[:, None] + GRID == ids)).astype(bf16)
        match = seg[:, None] == ids64
        qaux = jnp.where((ids64 < IMG) & match, BIG, jnp.where(ids64 == IMG, 1.0, 0.0)).astype(bf16)
        kaux = jnp.where(
            (ids64 < IMG) & match & kept[:, None],
            1.0,
            jnp.where(
                ids64 == IMG,
                -BIG,
                jnp.where(
                    (ids64 > IMG) & (ids64 < IMG + 4),
                    1.0,
                    jnp.where((ids64 == IMG + 4) & ~kept[:, None], 1.0, 0.0),
                ),
            ),
        ).astype(bf16)
        vaux = jnp.broadcast_to(jnp.where(jnp.arange(64) < 3, 1.0, 0.0).astype(bf16), (TOK, 64))
        first_seg, last_seg = seg[::BQ], jnp.minimum(seg[BQ - 1 :: BQ], IMG - 1)
        lo = jnp.sum((seg[None, :] < first_seg[:, None]).astype(jnp.int32), axis=1) // BQ
        hi = (jnp.sum((seg[None, :] <= last_seg[:, None]).astype(jnp.int32), axis=1) + BQ - 1) // BQ
        sc = jnp.concatenate(
            [
                jnp.stack([me, g, z, mine.astype(jnp.int32), mecol, z1, z1, z1]),
                lo,
                hi,
            ]
        ).astype(jnp.int32)
        own_seg = lax.dynamic_slice_in_dim(seg, g * TOK, TOK, 0)
        own_kp = lax.dynamic_slice_in_dim(kept, g * TOK, TOK, 0)
        mem = (
            (own_seg[:, None] == jnp.arange(IMG)[None, :]) & own_kp[:, None]
        ).astype(bf16)
        valid = jnp.max(
            ((seg[None, :] == jnp.arange(IMG)[:, None]) & kept[None, :]).astype(f32), axis=1
        )
        lab_hot = (labs[:, None] == jnp.arange(CPAD)[None, :]).astype(f32)
        block = jnp.arange(128) // HD
        avg = jnp.where(block[:, None] == block[None, :], 1.0 / HD, 0.0).astype(bf16)
        heads = (jnp.arange(D)[:, None] // HD == ids).astype(bf16)

        nt = length // TOK
        a, x0, gx = call(
            x0_kernel,
            (nt,),
            sc,
            [patches, patches_in, hot_pos] + patch_p,
            [
                pl.BlockSpec((TOK, D), lambda i, s: (jnp.where(s[3] == 1, i, 0), 0)),
                pl.BlockSpec((TOK, D), lambda i, s: (jnp.where(s[3] == 1, 0, i), 0)),
                pl.BlockSpec((TOK, 128), lambda i, s: (i, 0)),
            ]
            + [ANY] * 5,
            (sds((length, D), bf16), sds((TOK, D), f32), sds((16, D), f32)),
            (pl.BlockSpec((TOK, D), lambda i, s: (i, 0)), whole((TOK, D)), whole((16, D))),
            [pltpu.VMEM((D, D + SMALL), bf16), DMA((8,))],
            10,
        )
        qcols = query_gains.shape[1]
        counts = jnp.sum(gx[LANE_COUNT - LANE_GAIN : LANE_COUNT - LANE_GAIN + NB], axis=1)
        image_total = jnp.sum(counts)
        qg = gx[4:6].reshape(2, n_dp, rows)[:, :, :qcols].reshape(2, 1, HD)
        gain = jnp.tile(qg * jnp.array([0.125, 1.0], f32)[:, None, None], (1, NH, 1))
        gain = jnp.pad(gain.reshape(1, QK), ((0, 7), (0, 0)))
        vt = jnp.stack([valid, valid / image_total], axis=1)
        vt = jnp.pad(vt, ((0, 0), (0, 126)))

        row_block = lambda width: pl.BlockSpec((TOK, width), lambda i, s: (i, 0))
        head_block = pl.BlockSpec((NH, TOK, 128), lambda i, s: (0, i, 0))
        qx, kx, vx, xh, inv = call(
            qkv_kernel,
            (nt,),
            sc,
            [a, qaux, kaux, vaux, gain, avg] + in_p,
            [row_block(D), row_block(64), row_block(64), whole((TOK, 64)), whole((8, QK)),
             whole((128, 128))]
            + [ANY] * 4,
            tuple([sds((NH, length, 128), bf16)] * 3 + [sds((length, QK), f32)] * 2),
            tuple([head_block] * 3 + [row_block(QK)] * 2),
            [pltpu.VMEM((D, 576), bf16), DMA((4,))],
            10,
        )
        f_w = flat_call(
            out_kernel, sc, out_z, (sds((rows, 4 * OW), bf16),), us=2, deps=[a]
        )[0]
        f_c = direct(widen(f_w, low_bits))
        per_tok = TOK // BQ
        def attend(rel, us, deps):
            half = nq // 2
            block = lambda i, s: 2 * (s[1] ^ jnp.where(i < 2, rel[0], rel[1])) + i % 2
            return call(
                lambda *refs: attn_kernel(rel, *refs),
                (half,),
                sc,
                [qx, kx, vx],
                [
                    pl.BlockSpec((NH, BQ, 128), lambda i, s: (0, block(i, s), 0)),
                    whole((NH, length, 128)),
                    whole((NH, length, 128)),
                ],
                (
                    sds((TOK, OW), bf16),
                    sds((TOK, OW), bf16),
                    sds((half * BQ, NH * HD), f32),
                    sds((NH, half * BQ, 128), bf16),
                ),
                (
                    pl.BlockSpec((BQ, OW), lambda i, s: (jnp.minimum(i, 1), 0)),
                    pl.BlockSpec((BQ, OW), lambda i, s: (jnp.maximum(i - 2, 0), 0)),
                    pl.BlockSpec((BQ, NH * HD), lambda i, s: (i, 0)),
                    pl.BlockSpec((NH, BQ, 128), lambda i, s: (0, i, 0)),
                ),
                [pltpu.VMEM((NH, BQ, 128), f32)],
                us,
                deps,
            )

        o_3, o_1, of_a, ql_a = attend((3, 1), 11, [f_w])
        f_p, f_stack = all8(f_c, [o_1])
        o_2, o_0, of_b, ql_b = attend((2, 0), 11, [f_stack])
        head_w = simple_call(
            head_pack_kernel, [class_head], sds((rows, CPAD), bf16), deps=[o_0]
        )
        head_c = direct(widen(head_w, low_bits))

        def trade(parts):
            return [parts[0], pp(parts[1], 0, 1), pp(parts[2], 1, 0), pp(parts[3], 1, 1)]

        o_p = trade([o_0, o_1, o_2, o_3])
        tile_spec = pl.BlockSpec((TOK, D), lambda j, s: (0, j))
        x1, b, u, h, x2, ns = call(
            mlp_kernel,
            (4,),
            sc,
            o_p + [x0, gx, mem, heads] + f_p + [w_all],
            [whole((TOK, OW))] * 4
            + [whole((TOK, D)), whole((16, D)), whole((TOK, IMG)), whole((D, 128))]
            + [ANY] * 6,
            (
                sds((TOK, D), f32),
                sds((TOK, D), bf16),
                sds((TOK, HID), f32),
                sds((TOK, HID), bf16),
                sds((TOK, D), f32),
                sds((IMG, D + 128), f32),
            ),
            (whole((TOK, D)), whole((TOK, D)), tile_spec, tile_spec, whole((TOK, D)),
             whole((IMG, D + 128))),
            [
                pltpu.VMEM((D, 4 * OW), bf16),
                pltpu.VMEM((4, 2, D, D), bf16),
                DMA((8,)),
                DMA((4, 2, 8)),
            ],
            18,
        )
        head_p, _ = all8(head_c, [x1])
        ns = ns + pp(ns, 1, 0)
        half_shape = (4, SUB, CPAD // 2)
        pooled, gp, sinv, loss, gh, gh_send = call(
            head_kernel,
            (1,),
            sc,
            [ns, pp(ns, 0, 1), lab_hot, vt, heads] + head_p,
            [whole((IMG, D + 128))] * 2
            + [whole((IMG, CPAD)), whole((IMG, 128)), whole((D, 128))]
            + [ANY] * 5,
            (
                sds((IMG, D), f32),
                sds((IMG, D), f32),
                sds((IMG, 128), f32),
                sds((IMG, 128), f32),
                sds(half_shape, bf16),
                sds(half_shape, bf16),
            ),
            (
                whole((IMG, D)),
                whole((IMG, D)),
                whole((IMG, 128)),
                whole((IMG, 128)),
                whole(half_shape),
                whole(half_shape),
            ),
            [pltpu.VMEM((D, CPAD), bf16), pltpu.VMEM((D, CPAD // 2), f32), DMA((8,))],
            5,
        )

        gu, gr, gm, gmid, *ga_parts, small_b = call(
            back_kernel,
            (4,),
            sc,
            [u, x2, x1, gx, mem, pooled, gp, sinv, heads] + f_p + [w_all],
            [
                tile_spec,
                whole((TOK, D)),
                whole((TOK, D)),
                whole((16, D)),
                whole((TOK, IMG)),
                whole((IMG, D)),
                whole((IMG, D)),
                whole((IMG, 128)),
                whole((D, 128)),
            ]
            + [ANY] * 6,
            (
                sds((TOK, HID), bf16),
                sds((TOK, D), bf16),
                sds((TOK, D), bf16),
                sds((TOK, D), f32),
                sds((TOK, OW), bf16),
                sds((TOK, OW), bf16),
                sds((TOK, OW), bf16),
                sds((TOK, OW), bf16),
                sds((8, D), f32),
            ),
            (
                tile_spec,
                whole((TOK, D)),
                whole((TOK, D)),
                whole((TOK, D)),
                whole((TOK, OW)),
                whole((TOK, OW)),
                whole((TOK, OW)),
                whole((TOK, OW)),
                whole((8, D)),
            ),
            [
                pltpu.VMEM((4, 2, D, D), bf16),
                pltpu.VMEM((D, 4 * OW), bf16),
                pltpu.VMEM((TOK, D), f32),
                pltpu.VMEM((TOK, D), f32),
                DMA((4, 2, 8)),
                DMA((8,)),
            ],
            20,
        )
        do_p = trade(ga_parts)

        if extra == 1:
            gh_one = add(gh[:2], pp(gh[2:], masks[1])).astype(bf16)
        else:
            gh_one = add(gh, pp(gh_send, masks[0])).astype(bf16)

        tile_of = pl.BlockSpec((TOK, D), lambda j, s: (0, j))
        width = 2 * D + OW
        wgrad = call(
            wgrad_kernel,
            (4,),
            sc,
            [gr, h, b, gu, gm] + o_p,
            [whole((TOK, D)), tile_of, whole((TOK, D)), tile_of, whole((TOK, D))]
            + [whole((TOK, OW))] * 4,
            (sds((8, 4, SUB, width), bf16),),
            (pl.BlockSpec((8, 1, SUB, width), lambda j, s: (0, s[2] ^ j, 0, 0)),),
            [pltpu.VMEM((4, TOK, OW), bf16)],
            14,
            deps=[do_p[2], gh_one],
        )[0]
        if extra > 1:
            wgrad = wgrad.reshape(8, 4, extra, rows, width).transpose(0, 2, 1, 3, 4)
        wgrad = wgrad.reshape(n_dp * 4 * rows, width)
        z_out = lax.psum_scatter(wgrad, "dp", scatter_dimension=0, tiled=True)
        z_out = z_out.reshape(4, rows, width)
        z_got = [pp(z_out[r], 0, r) for r in (1, 2, 3)]

        def low_rows(x, low):
            for b in reversed(low):
                half = x.shape[-2] // 2
                first, second = x[..., :half, :], x[..., half:, :]
                flag = bit_of(b)
                send = jnp.where(flag, first, second)
                stay = jnp.where(flag, second, first)
                x = add(stay, pp(send.astype(bf16), b))
            return x

        def scatter4(stay, low, m1, m2):
            x = add(stay[:2], pp(stay[2:].astype(bf16), m1))
            x = add(x[0].astype(bf16), pp(x[1].astype(bf16), m2))
            return low_rows(x, low)

        def core_sum(stay, send):
            return add(stay, pp(send, masks[0])).astype(bf16)

        def chip_sum(x, first):
            m1, m2 = (masks[1], masks[2]) if first == 2 else (masks[2], masks[1])
            return scatter4(x, low_bits, m1, m2)

        if extra == 1:
            gh_m2 = add(gh_one[0], pp(gh_one[1], masks[2])).astype(bf16)
        else:
            gh_m2 = (0.5 * chip_sum(gh_one, 2)).astype(bf16)

        def halves(pairs, us, deps=()):
            kept, got = pairs[0]
            out = sds((kept.shape[0] // 2,) + kept.shape[1:], bf16)
            return (tuple(flat_call(halve_kernel, sc, [kept, got], (out, out), us=us, deps=deps)),)

        gh = add(gh_m2, pp(gh_m2, 0, 2))
        gh_got = pp(gh, 0, 1)
        half = nq // 2
        grads = call(
            attn_back_kernel,
            (nq + nt,),
            sc,
            [ql_a, ql_b, of_a, of_b] + do_p + [kx, vx],
            [
                pl.BlockSpec((NH, BQ, 128), lambda i, s: (0, jnp.minimum(i, half - 1), 0)),
                pl.BlockSpec((NH, BQ, 128), lambda i, s: (0, jnp.clip(i - half, 0, half - 1), 0)),
                pl.BlockSpec((BQ, NH * HD), lambda i, s: (jnp.minimum(i, half - 1), 0)),
                pl.BlockSpec((BQ, NH * HD), lambda i, s: (jnp.clip(i - half, 0, half - 1), 0)),
            ]
            + [whole((TOK, OW))] * 4
            + [whole((NH, length, 128)), whole((NH, length, 128))],
            (sds((length, 576), f32),),
            (pl.BlockSpec((TOK, 576), lambda i, s: (jnp.maximum(i - nq, 0), 0)),),
            [
                pltpu.VMEM((NH, length, 128), f32),
                pltpu.VMEM((NH, length, 128), f32),
                pltpu.VMEM((NH, length, 128), f32),
                pltpu.VMEM((4, TOK, OW), bf16),
            ],
            35,
        )[0]
        rel_tok = lambda n, s: s[1] ^ jnp.where(n < 2, n + 2, 3 - n)
        tok_block = lambda width: pl.BlockSpec((TOK, width), lambda n, s: (rel_tok(n, s), 0))
        in_shape = (2, D // 4, 576)
        g_send, g_one, g_own, in_keep, in_send, qgrad = call(
            mix_kernel,
            (nt,),
            sc,
            [grads, xh, inv, a, gain, avg] + in_p,
            [tok_block(576), tok_block(QK), tok_block(QK), tok_block(D), whole((8, QK)),
             whole((128, 128))]
            + [ANY] * 4,
            (
                sds((2, TOK, D), bf16),
                sds((TOK, D), bf16),
                sds((TOK, D), bf16),
                sds(in_shape, bf16),
                sds(in_shape, bf16),
                sds((8, QK), f32),
            ),
            (
                pl.BlockSpec((1, TOK, D), lambda n, s: (jnp.minimum(n, 1), 0, 0)),
                whole((TOK, D)),
                whole((TOK, D)),
                whole(in_shape),
                whole(in_shape),
                whole((8, QK)),
            ),
            [pltpu.VMEM((D, 576), f32), pltpu.VMEM((D, 576), bf16), DMA((4,))],
            14,
            deps=[gh_m2],
        )
        g_core = pp(g_send, 1)
        g_z_in = add(g_one, g_core[1]).astype(bf16)
        g_z = pp(g_z_in, 0, 1)

        in_got = pp(in_send, col_masks[0])
        (ik, is_), = halves([(in_keep, in_got)], 2, deps=[g_z_in, gh, z_out])
        is_got = pp(is_, col_masks[1])

        qg_rows = qgrad[0].reshape(2, NH, HD).sum(axis=1) * jnp.array([0.125, 1.0], f32)[:, None]
        qg_rows = jnp.pad(qg_rows, ((0, 6), (0, 0)))
        hot_own = pl.BlockSpec((TOK, 128), lambda i, s: (s[1], 0))
        own_rows = pl.BlockSpec((TOK, D), lambda i, s: (s[1], 0))

        def tail_body(*refs):
            tail_kernel(n_dp, *refs)

        pk, ps = call(
            tail_body,
            (1,),
            sc,
            [g_own, g_core, g_z, gmid, x0, gx, patches, patches_in, hot_pos, small_b, qg_rows],
            [
                whole((TOK, D)),
                pl.BlockSpec((1, TOK, D), lambda i, s: (0, 0, 0)),
                whole((TOK, D)),
                whole((TOK, D)),
                whole((TOK, D)),
                whole((16, D)),
                own_rows,
                own_rows,
                hot_own,
                whole((8, D)),
                whole((8, HD)),
            ],
            (sds((4, SUB, D + SMALL), bf16), sds((4, SUB, D + SMALL), bf16)),
            (whole((4, SUB, D + SMALL)), whole((4, SUB, D + SMALL))),
            [pltpu.VMEM((D, D + SMALL), f32)],
            6,
            deps=[is_],
        )
        (pk1, ps1), = halves([(pk, pp(ps, masks[0]))], 2)
        ps1_got = pp(ps1, masks[1])
        if extra == 1:
            in_a, in_b = flat_call(
                in_parts_kernel, sc, [ik[0], is_got[0]], (sds((rows, 576), bf16),) * 2, us=2,
                deps=[ps1],
            )
        else:
            both = low_rows(add(ik[0], is_got[0]), col_low).astype(bf16).reshape(2, rows, 576)
            in_a = jnp.where(z1 == 1, both[1], both[0])
            in_b = jnp.where(z1 == 1, both[0], both[1])
        in_parts = in_a
        in_a = lax.ppermute(in_a, ("dp", "mp"), perm_a)
        in_b = lax.ppermute(in_b, ("dp", "mp"), back_b)
        (pk2, ps2), = halves([(pk1, ps1_got)], 2, deps=[in_parts])
        ps2_got = pp(ps2, masks[2])
        s_up, s_down, s_out, sq_z = flat_call(
            share_z_kernel,
            sc,
            [z_out] + z_got,
            (
                sds((rows, D), f32),
                sds((rows, D), f32),
                sds((192, rows), f32),
                sds((8, 128), f32),
            ),
            us=3,
            deps=[ps2],
        )
        s_in, s_head, sq = flat_call(
            share_kernel,
            sc,
            [sq_z, in_a, in_b, gh, gh_got],
            (sds((rows, 576), f32), sds((rows, CLASSES), f32), sds((8, 128), f32)),
            us=2,
            deps=[sq_z],
        )
        if extra == 1:
            p_ins = [pk2, ps2_got]
        else:
            total = low_rows(add(pk2[0], ps2_got[0]), low_bits).astype(bf16)[None]
            p_ins = [total, jnp.zeros_like(total)]
        wide = jnp.arange(D + SMALL)
        extra_row = jnp.where((wide == buck + 1) & (g == 0), jnp.sum(loss[:, 0]), 0.0)
        extra_row = jnp.broadcast_to(extra_row[None, :], (8, D + SMALL))
        mine_q = flat_call(
            patch_row_kernel, sc, p_ins + [sq, extra_row], (sds((rows + 16, D + SMALL), bf16),), us=2
        )[0]
        share_patch, stats = flat_call(
            patch_sum_kernel,
            sc,
            [mine_q, pp(mine_q, 0, 1), pp(mine_q, 0, 2), pp(mine_q, 0, 3)],
            (sds((rows, D + SMALL), f32), sds((8, SMALL), f32)),
            us=2,
        )
        stats = stats + pp(stats, 1)
        m = 2
        while m < n_dp:
            stats = (stats + pp(stats, m)) + (pp(stats, 2 * m) + pp(stats, 3 * m))
            m *= 4

        shares = [s_in, s_out, s_up, s_down, share_patch, s_head]
        turned = [x.T if n // 3 == 3 else x for n, x in enumerate(state)]
        news = simple_call(
            update_kernel,
            [stats] + shares + turned,
            tuple([sds((1, 1), f32), sds((1, NB), f32)] + [sds(s.shape, f32) for s in turned]),
            6,
        )
        outs = [x.T if n // 3 == 3 else x for n, x in enumerate(news[2:])]
        return (news[1].reshape(NB), counts, news[0].reshape(())) + tuple(outs)

    return local


def solution(mesh):
    shard = {
        "in": P("dp", "mp"),
        "out": P("mp", "dp"),
        "row": P("dp", None),
        "col": P(None, "dp"),
    }
    kinds = ["in", "out", "in", "out", "row", "col", "row", "col", "col"]
    triples = tuple(shard[k] for k in kinds for _ in range(3))
    in_specs = (P("dp", None),) + (P("dp"),) * 6 + triples
    out_specs = (P(), P(), P()) + triples
    return jax.shard_map(
        make_local(mesh.shape["dp"], mesh.shape["mp"]),
        mesh=mesh,
        in_specs=in_specs,
        out_specs=out_specs,
        check_vma=False,
    )
```

```python
import jax
import jax.numpy as jnp
from jax import lax
from jax.experimental import pallas as pl
from jax.experimental.pallas import tpu as pltpu
from jax.sharding import PartitionSpec as P

D = 768
HD = 64
HID = 3072
CLASSES = 1000
CPAD = 1024
GRID = 32
IMG = 16
NB = 4
STEP = 10
BQ = 256
TOK = 512
NH = 3
QK = 2 * NH * HD
SUB = D // 8
SMALL = 128
OW = 256
LANE_GAIN = 64
LANE_QG = 68
LANE_COUNT = 72

HIGH = lax.Precision.HIGHEST
NORM_EPS = 1e-06
CLIP = 0.1
BETA_ONE = 0.9
BETA_TWO = 0.95
RATE_MATRIX = 0.05
RATE_SMALL = 0.2
DECAY = 0.05
ADAM_EPS = 1e-08
BIG = 128.0

bf16 = jnp.bfloat16
f32 = jnp.float32
VLIM = 56 * 1024 * 1024
COST = 0.001 * 1.15e9

NN = (((1,), (0,)), ((), ()))
NT = (((1,), (1,)), ((), ()))
TN = (((0,), (0,)), ((), ()))


def dot(a, b, dims=NN, precision=None):
    return lax.dot_general(a, b, dims, precision=precision, preferred_element_type=f32)


def norm_stats(values):
    center = values - jnp.mean(values, axis=-1, keepdims=True)
    inv_std = lax.rsqrt(jnp.mean(center * center, axis=-1, keepdims=True) + NORM_EPS)
    return center * inv_std, inv_std


def norm_back(grad_scaled, scaled, inv_std):
    return inv_std * (
        grad_scaled
        - jnp.mean(grad_scaled, axis=-1, keepdims=True)
        - scaled * jnp.mean(grad_scaled * scaled, axis=-1, keepdims=True)
    )


def splits(x, n):
    out = []
    for _ in range(n - 1):
        part = x.astype(bf16)
        out.append(part)
        x = x - part.astype(f32)
    out.append(x.astype(bf16))
    return out


def dot_split(x, exact, n, dims=NN):
    total = None
    for part in splits(x, n):
        term = dot(part, exact, dims)
        total = term if total is None else total + term
    return total


def head_mean(x, ones, n):
    return jnp.concatenate(
        [dot_split(x[:, c : c + 128], ones, n) for c in range(0, QK, 128)], axis=1
    )


def eye(rows, cols, offset=0):
    row = lax.broadcasted_iota(jnp.int32, (rows, cols), 0)
    col = lax.broadcasted_iota(jnp.int32, (rows, cols), 1)
    return (row + offset == col).astype(f32)


def rows_at(index, size):
    return pl.ds(pl.multiple_of(index * size, size), size)


def pack_kernel(w_patch, w_pos, w_gain, w_qg, seg, keep, bucket, w_up, w_down,
                patch_o, t_o):
    rows = w_patch.shape[0]
    patch_o[:, :D] = w_patch[...].astype(bf16)
    low = lambda ref: ref[...].astype(bf16).astype(f32)
    small = dot(low(w_pos), eye(64, SMALL), TN)
    small += dot(low(w_gain), eye(4, SMALL, LANE_GAIN), TN)
    qg = dot(low(w_qg), eye(2, SMALL, LANE_QG), TN)
    small += dot(eye(rows, qg.shape[0]), qg)
    kept = keep[...] == 1
    count = jnp.zeros((1, 1), f32)
    for n in range(IMG):
        held = jnp.where((seg[...] == n) & kept, 1.0, 0.0)
        count += jnp.max(held, keepdims=True)
    row = lax.broadcasted_iota(jnp.int32, (rows, SMALL), 0)
    col = lax.broadcasted_iota(jnp.int32, (rows, SMALL), 1)
    small += jnp.where((row == 0) & (col == LANE_COUNT + bucket[0]), count, 0.0)
    patch_o[:, D:] = small.astype(bf16)

    t_o[:, :D] = w_up[...].astype(bf16)
    t_o[:, D:] = w_down[...].astype(bf16)


def pack_rest_kernel(w_in, w_out, in_o, out_o):
    rows = w_in.shape[0]
    w = w_in[...].astype(bf16)
    parts = [
        w[:, h * 192 + part * HD : h * 192 + part * HD + HD]
        for part in range(3)
        for h in range(NH)
    ]
    in_o[...] = jnp.concatenate(parts, axis=1)
    turned = dot(eye(rows, rows).astype(bf16), w_out[...].astype(bf16), NT)
    out_o[...] = jnp.concatenate([turned, jnp.zeros((rows, OW - 192), f32)], axis=1).astype(bf16)


def ordered(flag, x, y):
    return jnp.where(flag, jnp.concatenate([y, x], axis=1), jnp.concatenate([x, y], axis=1))


def lanes_at(index, width):
    return pl.ds(pl.multiple_of(index * width, width), width)


def out_kernel(sc, o0, o1, o2, o3, out):
    for r, ref in enumerate((o0, o1, o2, o3)):
        out[:, lanes_at(sc[2] ^ r, OW)] = ref[...]


def head_pack_kernel(head, out):
    out[...] = jnp.zeros_like(out)
    out[:, :CLASSES] = head[...].astype(bf16)


def eight(refs):
    return list(refs[:4]) + [refs[4].at[n] for n in range(4)]


REL = [0, 2, 4, 6, 1, 3, 5, 7]


def stack_kernel(a, b, c, d, out):
    for n, ref in enumerate((a, b, c, d)):
        out[n] = ref[...]


def row_copies(refs, me, dst, sems, rel=REL):
    out = []
    for n, ref in enumerate(refs):
        size = ref.shape[0]
        out.append(pltpu.make_async_copy(ref, dst.at[rows_at(me ^ rel[n], size), :], sems.at[n]))
    return out


def columns(refs, lo, width):
    return [ref.at[:, pl.ds(lo, width)] for ref in refs]


def start(copies):
    for copy in copies:
        copy.start()


def wait(copies):
    for copy in copies:
        copy.wait()


def x0_kernel(sc, own, other, hot, *rest):
    refs = eight(rest[:5])
    a_out, x0_out, gx_out, w, sems = rest[5:]
    i = pl.program_id(0)

    @pl.when(i == 0)
    def _():
        copies = row_copies(refs, sc[0], w, sems)
        start(copies)
        wait(copies)
        row = lax.broadcasted_iota(jnp.int32, (16, SMALL), 0)
        col = lax.broadcasted_iota(jnp.int32, (16, SMALL), 1)
        pick = (row + LANE_GAIN == col).astype(f32).astype(bf16)
        gx_out[...] = dot(pick, w[:, D:], NT)

    rows = jnp.where(sc[3] == 1, own[...], other[...])
    x0 = dot(rows, w[:, :D]) + dot(hot[...], w[:, D:], NT)
    scaled, _ = norm_stats(x0)
    a_out[...] = (scaled * gx_out[0:1, :]).astype(bf16)

    @pl.when(i == sc[1])
    def _():
        x0_out[...] = x0


IN_REL = [0, 1, 2, 3]


def qkv_kernel(sc, a, qaux, kaux, vaux, gain, avg, *rest):
    refs = rest[:4]
    qx, kx, vx, xh_out, inv_out, w, sems = rest[4:]
    i = pl.program_id(0)

    @pl.when(i == 0)
    def _():
        copies = row_copies(refs, sc[4], w, sems, IN_REL)
        start(copies)
        wait(copies)

    mixed = dot(a[...], w[...])
    qk = mixed[:, :QK]
    v = mixed[:, QK:].astype(bf16)
    ones = avg[...]
    center = qk - head_mean(qk, ones, 2)
    inv = lax.rsqrt(head_mean(center * center, ones, 2) + NORM_EPS)
    scaled = center * inv
    xh_out[...] = scaled
    inv_out[...] = inv
    low = (scaled * gain[0:1, :]).astype(bf16)
    qa, ka, va = qaux[...], kaux[...], vaux[...]
    for h in range(NH):
        qx[h] = jnp.concatenate([low[:, h * HD : h * HD + HD], qa], axis=1)
        kx[h] = jnp.concatenate([low[:, (NH + h) * HD : (NH + h) * HD + HD], ka], axis=1)
        vx[h] = jnp.concatenate([v[:, h * HD : h * HD + HD], va], axis=1)


def attn_kernel(rel, sc, qx, kx, vx, free, o_first, o_second, o_full, ql, acc):
    step_id = pl.program_id(0)
    i = 2 * (sc[1] ^ jnp.where(step_id < 2, rel[0], rel[1])) + step_id % 2
    acc[...] = jnp.zeros_like(acc)
    lo, hi = sc[8 + i], sc[16 + i]

    def tile(start_row, size):
        ks = pl.ds(pl.multiple_of(start_row, BQ), size)
        row = lax.broadcasted_iota(jnp.int32, (BQ, size), 0)
        col = lax.broadcasted_iota(jnp.int32, (BQ, size), 1)
        own = jnp.where(row + (i * BQ - start_row) == col, free[0:1, ks], 0.0)
        scores = [dot(qx[h], kx[h, ks, :], NT) + own for h in range(NH)]
        probs = [jnp.exp(s).astype(bf16) for s in scores]
        for h in range(NH):
            acc[h] += dot(probs[h], vx[h, ks, :])

    pairs = (hi - lo) // 2

    def step(j, carry):
        tile((lo + 2 * j) * BQ, 2 * BQ)
        return carry

    lax.fori_loop(0, pairs, step, 0)

    @pl.when((hi - lo) % 2 == 1)
    def _():
        tile((hi - 1) * BQ, BQ)

    lane = lax.broadcasted_iota(jnp.int32, (BQ, HD), 1)
    outs = []
    for h in range(NH):
        out = acc[h]
        total = out[:, HD:]
        outs.append(out[:, :HD] / total)
        aux = qx[h][:, HD:].astype(f32)
        for n, part in enumerate(splits(-jnp.log(total), 3)):
            aux = jnp.where(lane == IMG + 1 + n, part.astype(f32), aux)
        ql[h] = jnp.concatenate([qx[h][:, :HD], aux.astype(bf16)], axis=1)
    full = jnp.concatenate(outs, axis=1)
    o_full[...] = full
    low = jnp.concatenate([full, jnp.zeros((BQ, OW - NH * HD), f32)], axis=1).astype(bf16)

    @pl.when(step_id < 2)
    def _():
        o_first[...] = low

    @pl.when(step_id >= 2)
    def _():
        o_second[...] = low


GELU_C = 0.7978845608028654


def gelu_tanh(u):
    return jnp.tanh(GELU_C * (u + 0.044715 * u * u * u))


def mlp_tile(b, w, u_out, h_out):
    u = dot(b, w[0])
    u_out[...] = u
    h = (0.5 * u * (1.0 + gelu_tanh(u))).astype(bf16)
    h_out[...] = h
    return dot(h, w[1], NT)


def tile_copies(w_all, j, dst, sems):
    size = D // 8
    return [
        pltpu.make_async_copy(
            w_all.at[d, j, :, pl.ds(part * D, D)],
            dst.at[part, pl.ds(d * size, size), :],
            sems.at[part, d],
        )
        for part in range(2)
        for d in range(8)
    ]


def mlp_kernel(sc, o0, o1, o2, o3, x0, gx, mem, heads, *rest):
    refs, w_all = eight(rest[:5]), rest[5]
    x1_out, b_out, u_out, h_out, x2, ns_out, w_o, w_t, sem_o, sem_t = rest[6:]
    j = pl.program_id(0)

    @pl.when(j == 0)
    def _():
        first = row_copies(refs, sc[0], w_o, sem_o)
        start(first)
        for t in range(4):
            start(tile_copies(w_all, t, w_t.at[t], sem_t.at[t]))
        wait(first)
        x1 = x0[...]
        for r, ref in enumerate((o0, o1, o2, o3)):
            x1 += dot(ref[...], w_o[:, lanes_at(sc[1] ^ r, OW)], NT)
        x1_out[...] = x1
        b_out[...] = (norm_stats(x1)[0] * gx[1:2, :]).astype(bf16)
        x2[...] = x1

    wait(tile_copies(w_all, j, w_t.at[j], sem_t.at[j]))
    x2[...] += mlp_tile(b_out[...], w_t.at[j], u_out, h_out)

    @pl.when(j == 3)
    def _():
        f = norm_stats(x2[...])[0] * gx[2:3, :]
        ones = heads[...]
        e = jnp.exp(dot_split(f * gx[3:4, :], ones, 3) * 0.125)
        eb = dot_split(e, ones, 2, NT)
        m = mem[...]
        num = jnp.zeros((IMG, D), f32)
        for part in splits(eb * f, 3):
            num += dot(m, part, TN)
        den = jnp.zeros((IMG, 128), f32)
        for part in splits(e, 3):
            den += dot(m, part, TN)
        ns_out[:, :D] = num
        ns_out[:, D:] = den


def head_kernel(sc, ns_a, ns_b, lab, vt, heads, *rest):
    pooled_out, gp_out, sinv_out, loss_out, gh_out, gh_send, w, gw, sems = rest[5:]
    copies = row_copies(eight(rest[:5]), sc[0], w, sems)
    start(copies)
    ns = ns_a[...] + ns_b[...]
    valid = vt[:, 0:1]
    scale = vt[:, 1:2]
    total = jnp.where(valid > 0.0, ns[:, D:], 1.0)
    sinv = jnp.where(valid > 0.0, 1.0 / total, 0.0)
    lane = lax.broadcasted_iota(jnp.int32, (IMG, 128), 1)
    sinv = jnp.where(lane < D // HD, sinv, 0.0)
    pooled = ns[:, :D] * dot_split(sinv, heads[...], 3, NT)
    low = pooled.astype(bf16)
    wait(copies)
    logits = dot(low, w[...])
    cls = lax.broadcasted_iota(jnp.int32, (IMG, CPAD), 1)
    real = (cls < CLASSES).astype(f32)
    hot = lab[...]
    ex = jnp.exp(-jnp.abs(logits))
    soft = jnp.maximum(logits, 0.0) + jnp.log1p(ex)
    per = jnp.sum(soft * real, axis=1, keepdims=True) - jnp.sum(
        logits * hot, axis=1, keepdims=True
    )
    loss_out[...] = jnp.broadcast_to(per * valid, (IMG, 128))
    sig = jnp.where(logits >= 0.0, 1.0, ex) / (1.0 + ex)
    gl = (scale * (sig * real - hot)).astype(bf16)
    pooled_out[...] = pooled
    sinv_out[...] = sinv
    gp_out[...] = dot(gl, w[...], NT)
    half = jnp.where(sc[2] % 2 == 1, gl[:, 512:].astype(f32), gl[:, :512].astype(f32))
    gw[...] = dot(low, half.astype(bf16), TN)
    for p, r in enumerate(rel_order(2)):
        gh_out[p] = gw[rows_at(sc[0] ^ r, SUB), :].astype(bf16)
        gh_send[p] = gw[rows_at(sc[0] ^ (r + 1), SUB), :].astype(bf16)


def rel_order(first):
    m1, m2 = (2, 4) if first == 2 else (4, 2)
    return [(p >> 1) * m1 + (p & 1) * m2 for p in range(4)]


def back_kernel(sc, u, x2, x1, gx, mem, pooled, gp, sinv, heads, *rest):
    refs, w_all = eight(rest[:5]), rest[5]
    gu_out, gr_out, gm_out, gmid_out = rest[6:10]
    ga_out, small_out = rest[10:14], rest[14]
    w_t, w_o, grs, acc, sem_t, sem_o = rest[15:]
    j = pl.program_id(0)

    def out_rows():
        return row_copies(refs, sc[0], w_o, sem_o)

    @pl.when(j == 0)
    def _():
        for t in range(4):
            start(tile_copies(w_all, t, w_t.at[t], sem_t.at[t]))
        start(out_rows())
        scaled, inv = norm_stats(x2[...])
        f = scaled * gx[2:3, :]
        probe = gx[3:4, :]
        ones = heads[...]
        e = jnp.exp(dot_split(f * probe, ones, 3) * 0.125)
        m = mem[...]
        m3 = jnp.concatenate([m, m, m], axis=1)

        def spread(x):
            return dot(m3, jnp.concatenate(splits(x, 3), axis=0))

        gt = spread(gp[...])
        at = e * spread(sinv[...])
        gpp = dot_split(gp[...] * pooled[...], ones, 3)
        da = dot_split(gt * f, ones, 3)
        dc = at * (da - spread(gpp))
        dcb = dot_split(dc, ones, 2, NT) * 0.125
        df = dot_split(at, ones, 2, NT) * gt + dcb * probe
        gr = norm_back(df * gx[2:3, :], scaled, inv)
        grs[...] = gr
        gr_out[...] = gr.astype(bf16)
        small_out[2:3, :] = jnp.sum(df * scaled, axis=0, keepdims=True)
        small_out[3:4, :] = jnp.sum(dcb * f, axis=0, keepdims=True)
        small_out[0:1, :] = jnp.zeros((1, D), f32)
        small_out[4:8, :] = jnp.zeros((4, D), f32)
        acc[...] = jnp.zeros_like(acc)

    wait(tile_copies(w_all, j, w_t.at[j], sem_t.at[j]))
    gh = dot(gr_out[...], w_t[j, 1])
    v = u[...]
    t = gelu_tanh(v)
    slope = 0.5 * (1.0 + t) + 0.5 * v * (1.0 - t * t) * GELU_C * (1.0 + 0.134145 * v * v)
    gu = (gh * slope).astype(bf16)
    gu_out[...] = gu
    acc[...] += dot(gu, w_t[j, 0], NT)

    @pl.when(j == 3)
    def _():
        wait(out_rows())
        scaled, inv = norm_stats(x1[...])
        gb = acc[...]
        small_out[1:2, :] = jnp.sum(gb * scaled, axis=0, keepdims=True)
        gmid = grs[...] + norm_back(gb * gx[1:2, :], scaled, inv)
        gmid_out[...] = gmid
        low = gmid.astype(bf16)
        gm_out[...] = low
        for r in range(4):
            ga_out[r][...] = dot(low, w_o[:, lanes_at(sc[1] ^ r, OW)]).astype(bf16)


def wgrad_kernel(sc, gr, h, b, gu, gm, o0, o1, o2, o3, out, os):
    j = pl.program_id(0)

    @pl.when(j == 0)
    def _():
        for r, ref in enumerate((o0, o1, o2, o3)):
            os[r] = ref[...]

    parts = [
        (0, dot(b[...], gu[...], TN)),
        (D, dot(gr[...], h[...], TN)),
        (2 * D, dot(gm[...], os[sc[1] ^ j], TN)),
    ]
    for lo, value in parts:
        width = value.shape[1]
        for d in range(8):
            out[d, 0, :, lo : lo + width] = value[d * SUB : (d + 1) * SUB, :].astype(bf16)


def attn_back_kernel(sc, ql_a, ql_b, of_a, of_b, d0, d1, d2, d3, kx, vx, free, g_out, dq, dk, dv, dos):
    i = pl.program_id(0)
    nq = dk.shape[1] // BQ

    @pl.when(i == 0)
    def _():
        for n, ref in enumerate((d3, d1, d2, d0)):
            dos[n] = ref[...]

    @pl.when(i == 0)
    def _():
        dk[...] = jnp.zeros_like(dk)
        dv[...] = jnp.zeros_like(dv)

    @pl.when(i < nq)
    def _():
        n = i // 2
        block = 2 * (sc[1] ^ jnp.where(n < 2, 3 - 2 * n, 6 - 2 * n)) + i % 2
        mine = rows_at(block, BQ)
        lane = lax.broadcasted_iota(jnp.int32, (BQ, HD), 1)
        first = i < nq // 2
        of = jnp.where(first, of_a[...], of_b[...])
        do = dos[n, rows_at(i % 2, BQ), :].astype(f32)
        width = NH * HD
        head_r = lax.broadcasted_iota(jnp.int32, (width, width), 0) // HD
        head_c = lax.broadcasted_iota(jnp.int32, (width, width), 1) // HD
        same_head = (head_r == head_c).astype(f32).astype(bf16)
        deltas = dot_split(do[:, :width] * of, same_head, 3)
        dob, qb = [], []
        for h in range(NH):
            dof = do[:, h * HD : h * HD + HD]
            delta = deltas[:, h * HD : h * HD + HD]
            aux = jnp.zeros((BQ, HD), f32)
            for m, part in enumerate(splits(-delta, 3)):
                aux = jnp.where(lane == m, part.astype(f32), aux)
            dob.append(jnp.concatenate([dof, aux], axis=1).astype(bf16))
            q = jnp.where(first, ql_a[h].astype(f32), ql_b[h].astype(f32))
            qb.append(q.astype(bf16))
            dq[h, mine, :] = jnp.zeros((BQ, 128), f32)
        own_free = free[0:1, pl.ds(pl.multiple_of(block * BQ, BQ), BQ)]

        def tile(start_row, size):
            ks = pl.ds(pl.multiple_of(start_row, BQ), size)
            row = lax.broadcasted_iota(jnp.int32, (size, BQ), 0)
            col = lax.broadcasted_iota(jnp.int32, (size, BQ), 1)
            own = jnp.where(row + (start_row - block * BQ) == col, own_free, 0.0)
            pts = [jnp.exp(dot(kx[h, ks, :], qb[h], NT) + own) for h in range(NH)]
            dpts = [dot(vx[h, ks, :], dob[h], NT) for h in range(NH)]
            dsts = [(pts[h] * dpts[h]).astype(bf16) for h in range(NH)]
            for h in range(NH):
                dv[h, ks, :] += dot(pts[h].astype(bf16), dob[h])
                dk[h, ks, :] += dot(dsts[h], qb[h])
                dq[h, mine, :] += dot(dsts[h], kx[h, ks, :], TN)

        lo, hi = sc[8 + block], sc[16 + block]

        def step(j, carry):
            tile((lo + 2 * j) * BQ, 2 * BQ)
            return carry

        lax.fori_loop(0, (hi - lo) // 2, step, 0)

        @pl.when((hi - lo) % 2 == 1)
        def _():
            tile((hi - 1) * BQ, BQ)

    @pl.when(i >= nq)
    def _():
        rows = rows_at(i - nq, TOK)
        g_out[...] = jnp.concatenate(
            [ref[h, rows, :][:, :HD] for ref in (dq, dk, dv) for h in range(NH)], axis=1
        )


def mix_kernel(sc, grad, xh, inv, a, gain, avg, *rest):
    refs = rest[:4]
    g_send, g_one, g_own, in_keep, in_send, qg_out, gin, w, sems = rest[4:]
    n = pl.program_id(0)

    @pl.when(n == 0)
    def _():
        copies = row_copies(refs, sc[4], w, sems, IN_REL)
        start(copies)
        gin[...] = jnp.zeros_like(gin)
        qg_out[...] = jnp.zeros_like(qg_out)
        wait(copies)

    grads = grad[:, :QK]
    scaled = xh[...]
    ones = avg[...]
    qg_out[0:1, :] += jnp.sum(grads * scaled, axis=0, keepdims=True)
    dg = grads * gain[0:1, :]
    back = inv[...] * (
        dg - head_mean(dg, ones, 2) - scaled * head_mean(dg * scaled, ones, 2)
    )
    mix = jnp.concatenate([back, grad[:, QK:]], axis=1).astype(bf16)
    out = dot(mix, w[...], NT).astype(bf16)
    gin[...] += dot(a[...], mix, TN)

    @pl.when(n < 2)
    def _():
        g_send[0] = out

    @pl.when(n == 2)
    def _():
        g_one[...] = out

    @pl.when(n == 3)
    def _():
        g_own[...] = out
        size = D // 4
        for p in range(2):
            in_keep[p] = gin[rows_at(sc[4] ^ (2 * p), size), :].astype(bf16)
            in_send[p] = gin[rows_at(sc[4] ^ (2 * p + 1), size), :].astype(bf16)


def add(x, y):
    return x.astype(f32) + y.astype(f32)


def halve_kernel(sc, kept, got, keep_o, send_o):
    half = keep_o.shape[0]
    for n in range(half):
        keep_o[n] = add(kept[n], got[n]).astype(bf16)
        send_o[n] = add(kept[half + n], got[half + n]).astype(bf16)


def in_parts_kernel(sc, kept, got, a_out, b_out):
    half = a_out.shape[0]
    first = sc[5]
    mine, other = rows_at(first, half), rows_at(1 - first, half)
    a_out[...] = add(kept[mine, :], got[mine, :]).astype(bf16)
    b_out[...] = add(kept[other, :], got[other, :]).astype(bf16)


def share_z_kernel(sc, z0, z1, z2, z3, up_o, down_o, out_o, sq_o):
    rows = up_o.shape[0]
    total = add(z0[0], z1[...]) + add(z2[...], z3[...])
    up_o[...] = total[:, :D]
    down_o[...] = total[:, D : 2 * D]
    out_o[...] = dot(total[:, 2 * D :], eye(rows, rows), TN, HIGH)[:192, :]
    sq_o[...] = jnp.broadcast_to(jnp.sum(total * total, keepdims=True), sq_o.shape)


def share_kernel(sc, sq_z, in_a, in_b, h_own, h_got, in_o, head_o, sq_o):
    grad = add(in_a[...], in_b[...])
    in_o[...] = jnp.concatenate(
        [
            grad[:, part * NH * HD + h * HD : part * NH * HD + h * HD + HD]
            for h in range(NH)
            for part in range(3)
        ],
        axis=1,
    )
    head = ordered(sc[2] % 2 == 1, h_own[...], h_got[...])
    head_o[...] = head[:, :CLASSES]
    squares = jnp.sum(grad * grad, keepdims=True)
    once = jnp.where(sc[2] == 0, 1.0, 0.0)
    squares += once * jnp.sum(head * head, keepdims=True)
    sq_o[...] = sq_z[...] + squares


def patch_row_kernel(sc, kept, got, sq, extra_row, out):
    rows = kept.shape[1]
    out[:rows, :] = add(kept[0], got[0]).astype(bf16)
    lane = lax.broadcasted_iota(jnp.int32, (16, D + SMALL), 1)
    row = lax.broadcasted_iota(jnp.int32, (16, D + SMALL), 0)
    value = jnp.where(lane == 0, sq[0:1, 0:1], extra_row[0:1, :])
    tail = jnp.zeros((16, D + SMALL), f32)
    for n, part in enumerate(splits(value, 3)):
        tail = jnp.where(row == n, part.astype(f32), tail)
    out[rows:, :] = tail.astype(bf16)


def patch_sum_kernel(sc, own, q1, q2, q3, share_o, stats_o):
    rows = share_o.shape[0]
    total = add(own[...], q1[...]) + add(q2[...], q3[...])
    patch = total[:rows, :]
    share_o[...] = patch
    sums = total[rows : rows + 1, :SMALL] + total[rows + 1 : rows + 2, :SMALL]
    sums += total[rows + 2 : rows + 3, :SMALL]
    lane = lax.broadcasted_iota(jnp.int32, (8, SMALL), 1)
    squares = jnp.sum(patch * patch, keepdims=True)
    stats_o[...] = sums + jnp.where(lane == 0, squares, 0.0)


def tail_kernel(n_dp, sc, g_own, g_core, g_z, gmid, x0, gx, own, other, hot, small_b, qgrad,
                pk, ps, tile):
    grad = g_own[...].astype(f32) + g_core[0].astype(f32) + g_z[...].astype(f32)
    scaled, inv = norm_stats(x0[...])
    gain_a = jnp.sum(grad * scaled, axis=0, keepdims=True)
    ge = (gmid[...] + norm_back(grad * gx[0:1, :], scaled, inv)).astype(bf16)
    rows = jnp.where(sc[3] == 1, own[...], other[...])
    tile[:, :D] = dot(rows, ge, TN)
    row8 = lax.broadcasted_iota(jnp.int32, (8, D), 0)
    gains = jnp.where(row8 == 0, gain_a, small_b[...])
    small = dot(ge, hot[...], TN) + dot(gains, eye(8, SMALL, LANE_GAIN), TN)
    part = HD // n_dp
    kk = lax.broadcasted_iota(jnp.int32, (HD, D), 0)
    rr = lax.broadcasted_iota(jnp.int32, (HD, D), 1)
    spot = ((kk // part) * (D // n_dp) + kk % part == rr).astype(f32)
    lane = lax.broadcasted_iota(jnp.int32, (8, SMALL), 1)
    row = lax.broadcasted_iota(jnp.int32, (8, SMALL), 0)
    q_lane = ((lane == LANE_QG + row) & (row < 2)).astype(f32)
    q_cols = dot(qgrad[...], q_lane, TN, HIGH)
    small += dot(spot, q_cols, TN)
    tile[:, D:] = small
    for p, r in enumerate(rel_order(2)):
        pk[p] = tile[rows_at(sc[0] ^ r, SUB), :].astype(bf16)
        ps[p] = tile[rows_at(sc[0] ^ (r + 1), SUB), :].astype(bf16)


def update_kernel(stats, *rest):
    shares = rest[:6]
    state = rest[6:33]
    norm_out, loss_out, outs = rest[33], rest[34], rest[35:]
    total = stats[0:1, :]
    norm = jnp.sqrt(total)
    norm_out[...] = norm[:, 0:1]
    loss_out[...] = total[:, 1 : 1 + NB]
    factor = jnp.minimum(1.0, CLIP / (norm[:, 0:1] + 1e-06))
    s_in, s_out, s_up, s_down, s_patch, s_head = shares
    rows = s_patch.shape[0]
    small = dot(eye(SMALL, SMALL), s_patch[:, D:], NT, HIGH)
    part = state[24].shape[1]
    grads = [
        s_in[...],
        s_out[...],
        s_up[...],
        s_down[...],
        s_patch[:, :D],
        small[: 2 * GRID, :],
        s_head[...],
        small[LANE_GAIN : LANE_GAIN + 4, :],
        small[LANE_QG : LANE_QG + 2, :part],
    ]
    for n in range(9):
        master, first, second = state[3 * n : 3 * n + 3]
        clipped = grads[n] * factor
        first_new = BETA_ONE * first[...] + (1.0 - BETA_ONE) * clipped
        second_new = BETA_TWO * second[...] + (1.0 - BETA_TWO) * clipped * clipped
        matrix = n in (0, 1, 2, 3, 4, 6)
        rate = RATE_MATRIX if matrix else RATE_SMALL
        decay = DECAY if matrix else 0.0
        ratio = (
            first_new
            / (1.0 - BETA_ONE**STEP)
            / (jnp.sqrt(second_new / (1.0 - BETA_TWO**STEP)) + ADAM_EPS)
        )
        value = master[...]
        outs[3 * n][...] = value - rate * (ratio + decay * value)
        outs[3 * n + 1][...] = first_new
        outs[3 * n + 2][...] = second_new


ANY = pl.BlockSpec(memory_space=pl.ANY)


def without(kernel, count, deps):
    if not deps:
        return kernel
    return lambda *refs: kernel(*refs[:count], *refs[count + len(deps) :])


def call(kernel, grid, sc, ins, specs, outs, out_specs, scratch, us=5, deps=()):
    return pl.pallas_call(
        without(kernel, 1 + len(ins), deps),
        out_shape=outs,
        grid_spec=pltpu.PrefetchScalarGridSpec(
            num_scalar_prefetch=1,
            grid=grid,
            in_specs=list(specs) + [ANY] * len(deps),
            out_specs=out_specs,
            scratch_shapes=scratch,
        ),
        compiler_params=pltpu.CompilerParams(vmem_limit_bytes=VLIM),
        cost_estimate=pl.CostEstimate(
            flops=int(us * COST), bytes_accessed=1000, transcendentals=0
        ),
    )(sc, *ins, *deps)


def flat_call(kernel, sc, ins, outs, scratch=(), us=3, deps=()):
    return call(
        kernel,
        (1,),
        sc,
        ins,
        [whole(x.shape) for x in ins],
        outs,
        tuple(whole(o.shape) for o in outs),
        list(scratch),
        us,
        deps,
    )


def pass_on(x, deps):
    return pl.pallas_call(
        lambda *refs: None,
        out_shape=sds(x.shape, x.dtype),
        in_specs=[ANY] * (1 + len(deps)),
        out_specs=ANY,
        input_output_aliases={0: 0},
        cost_estimate=pl.CostEstimate(flops=0, bytes_accessed=1000, transcendentals=0),
    )(x, *deps)


def simple_call(kernel, ins, outs, us=3, deps=()):
    return pl.pallas_call(
        without(kernel, len(ins), deps),
        out_shape=outs,
        in_specs=[pl.BlockSpec(memory_space=pltpu.VMEM)] * len(ins) + [ANY] * len(deps),
        compiler_params=pltpu.CompilerParams(vmem_limit_bytes=VLIM),
        cost_estimate=pl.CostEstimate(
            flops=int(us * COST), bytes_accessed=1000, transcendentals=0
        ),
    )(*ins, *deps)


def whole(shape):
    return pl.BlockSpec(shape, lambda i, s: (0,) * len(shape))


def sds(shape, dtype):
    return jax.ShapeDtypeStruct(shape, dtype)


DMA = pltpu.SemaphoreType.DMA


def make_local(n_dp, n_mp):
    extra = n_dp // 8
    masks = [extra, 2 * extra, 4 * extra]
    low_bits = [b for b in (1, 2, 4, 8, 16, 32) if b < extra]
    col_low = [2 * b for b in low_bits]
    col_masks = [2 * extra, 4 * extra]

    def pp(x, dmask, zmask=0):
        perm = [
            (d * n_mp + z, (d ^ dmask) * n_mp + (z ^ zmask))
            for d in range(n_dp)
            for z in range(n_mp)
        ]
        return lax.ppermute(x, ("dp", "mp"), perm)

    def local(patches, segment, keep, pos_y, pos_x, labels, bucket, *state):
        masters = state[0::3]
        (attend_in, attend_out, expand, contract, patch_embed, pos_table, class_head,
         norm_gains, query_gains) = masters
        length = patches.shape[0]
        rows = patch_embed.shape[0]
        nq = length // BQ
        dp = lax.axis_index("dp")
        z = lax.axis_index("mp")
        core = dp % 2
        z1, z0 = z // 2, z % 2
        g = z0 + 2 * core
        me = dp // extra
        mecol = (dp // 2) // extra
        mine = core == z1

        def bit_of(mask):
            return (dp // mask) % 2 == 1

        def swap(flag, x, y, axis):
            return jnp.where(
                flag, jnp.concatenate([y, x], axis=axis), jnp.concatenate([x, y], axis=axis)
            )

        def pick4(parts, index, axis):
            odd, high = index % 2 == 1, index // 2 == 1
            lo = swap(odd, parts[0], parts[1], axis)
            hi = swap(odd, parts[2], parts[3], axis)
            return swap(high, lo, hi, axis)

        patch_w, t_w = pl.pallas_call(
            pack_kernel,
            out_shape=(
                sds((rows, D + SMALL), bf16),
                sds((rows, 2 * D), bf16),
            ),
            in_specs=[pl.BlockSpec(memory_space=pltpu.VMEM)] * 6
            + [pl.BlockSpec(memory_space=pltpu.SMEM)]
            + [pl.BlockSpec(memory_space=pltpu.VMEM)] * 2,
            compiler_params=pltpu.CompilerParams(vmem_limit_bytes=VLIM),
        )(patch_embed, pos_table, norm_gains, query_gains, segment.reshape(-1, 128),
          keep.reshape(-1, 128), bucket, expand, contract.T)
        w_all = lax.all_gather(t_w, ("dp", "mp"), axis=0, tiled=True)
        w_all = w_all.reshape(8, extra, n_mp, rows, 2 * D)
        if extra > 1:
            w_all = w_all.transpose(0, 2, 1, 3, 4)
        w_all = w_all.reshape(8, n_mp, SUB, 2 * D)

        perm_core = [
            (d * n_mp + zz, (d ^ 1) * n_mp + zz)
            for d in range(n_dp)
            for zz in range(n_mp)
            if d % 2 == zz // 2
        ]
        patches_in = lax.ppermute(patches, ("dp", "mp"), perm_core)
        meta = jnp.stack([segment, keep, pos_y, pos_x])
        tag = jnp.concatenate([labels, bucket, jnp.zeros((length - IMG - 1,), jnp.int32)])
        meta = jnp.concatenate([meta, tag[None]], axis=0)
        meta_in = lax.ppermute(meta, ("dp", "mp"), perm_core)
        meta = jnp.where(mine, meta, meta_in)

        def widen(x, low):
            for b in low:
                x = swap(bit_of(b), x, pp(x, b), -2)
            return x

        def across(x):
            one, two = pp(x, masks[1]), pp(x, masks[2])
            return [x, one, two, pp(one, masks[2])]

        def stack(parts, deps):
            high, width = parts[0].shape
            cuts = 1 if width < 2048 else 4
            step = width // cuts
            return pl.pallas_call(
                without(stack_kernel, 4, deps),
                out_shape=sds((4, high, width), bf16),
                grid=(cuts,),
                in_specs=[pl.BlockSpec((high, step), lambda i: (0, i))] * 4 + [ANY] * len(deps),
                out_specs=pl.BlockSpec((4, high, step), lambda i: (0, 0, i)),
                compiler_params=pltpu.CompilerParams(vmem_limit_bytes=VLIM),
                cost_estimate=pl.CostEstimate(flops=int(COST), bytes_accessed=1000, transcendentals=0),
            )(*parts, *deps)

        def direct(x):
            return [x] + [pp(x, m) for m in (masks[1], masks[2], masks[1] | masks[2])]

        def all8(parts, deps=()):
            stacked = stack(parts, deps)
            return parts + [pp(stacked, masks[0])], stacked

        patch_c = direct(widen(patch_w, low_bits))
        in_w, out_w = simple_call(
            pack_rest_kernel,
            [attend_in, attend_out],
            (sds((rows, 576), bf16), sds((rows, OW), bf16)),
            deps=[meta_in],
        )

        perm_a, perm_b, back_b = [], [], []
        for d in range(n_dp):
            for zz in range(n_mp):
                c, a1, a0 = d % 2, zz // 2, zz % 2
                src = d * n_mp + zz
                perm_a.append((src, (d - c + a1) * n_mp + a0 + 2 * c))
                perm_b.append((src, (d - c + a1) * n_mp + a0 + 2 * (1 - c)))
                back_b.append((src, (d - c + 1 - a1) * n_mp + a0 + 2 * c))
        in_a = lax.ppermute(in_w, ("dp", "mp"), perm_a)
        in_b = lax.ppermute(in_w, ("dp", "mp"), perm_b)
        patch_p, _ = all8(patch_c, [patches_in])
        in_own = widen(swap(z1 == 1, in_a, in_b, 0), col_low)
        in_one, in_two = pp(in_own, col_masks[0]), pp(in_own, col_masks[1])
        in_p = [in_own, in_one, in_two, pp(in_own, col_masks[0] | col_masks[1])]
        o_one, o_two = pp(out_w, 0, 1), pp(out_w, 0, 2)
        out_z = [out_w, o_one, o_two, pp(o_two, 0, 1)]

        seg, kp, py, px = meta[0], meta[1], meta[2], meta[3]
        labs = meta[4, :IMG]
        buck = meta[4, IMG]
        kept = (kp == 1) & (seg < IMG)
        ids = jnp.arange(128)[None, :]
        ids64 = ids[:, :64]
        hot_pos = ((py[:, None] == ids) | (px[:, None] + GRID == ids)).astype(bf16)
        match = seg[:, None] == ids64
        qaux = jnp.where((ids64 < IMG) & match, BIG, jnp.where(ids64 == IMG, 1.0, 0.0)).astype(bf16)
        kaux = jnp.where(
            (ids64 < IMG) & match & kept[:, None],
            1.0,
            jnp.where(
                ids64 == IMG,
                -BIG,
                jnp.where(
                    (ids64 > IMG) & (ids64 < IMG + 4),
                    1.0,
                    0.0,
                ),
            ),
        ).astype(bf16)
        vaux = jnp.broadcast_to(jnp.ones((64,), bf16), (TOK, 64))
        first_seg, last_seg = seg[::BQ], jnp.minimum(seg[BQ - 1 :: BQ], IMG - 1)
        lo = jnp.sum((seg[None, :] < first_seg[:, None]).astype(jnp.int32), axis=1) // BQ
        hi = (jnp.sum((seg[None, :] <= last_seg[:, None]).astype(jnp.int32), axis=1) + BQ - 1) // BQ
        blocks = jnp.arange(nq)
        lo, hi = jnp.minimum(lo, blocks), jnp.maximum(hi, blocks + 1)
        free_row = jnp.broadcast_to(jnp.where(kept, 0.0, BIG)[None, :], (8, length))
        sc = jnp.concatenate(
            [
                jnp.stack([me, g, z, mine.astype(jnp.int32), mecol, z1, z1, z1]),
                lo,
                hi,
            ]
        ).astype(jnp.int32)
        own_seg = lax.dynamic_slice_in_dim(seg, g * TOK, TOK, 0)
        own_kp = lax.dynamic_slice_in_dim(kept, g * TOK, TOK, 0)
        mem = (
            (own_seg[:, None] == jnp.arange(IMG)[None, :]) & own_kp[:, None]
        ).astype(bf16)
        valid = jnp.max(
            ((seg[None, :] == jnp.arange(IMG)[:, None]) & kept[None, :]).astype(f32), axis=1
        )
        lab_hot = (labs[:, None] == jnp.arange(CPAD)[None, :]).astype(f32)
        block = jnp.arange(128) // HD
        avg = jnp.where(block[:, None] == block[None, :], 1.0 / HD, 0.0).astype(bf16)
        heads = (jnp.arange(D)[:, None] // HD == ids).astype(bf16)

        nt = length // TOK
        a, x0, gx = call(
            x0_kernel,
            (nt,),
            sc,
            [patches, patches_in, hot_pos] + patch_p,
            [
                pl.BlockSpec((TOK, D), lambda i, s: (jnp.where(s[3] == 1, i, 0), 0)),
                pl.BlockSpec((TOK, D), lambda i, s: (jnp.where(s[3] == 1, 0, i), 0)),
                pl.BlockSpec((TOK, 128), lambda i, s: (i, 0)),
            ]
            + [ANY] * 5,
            (sds((length, D), bf16), sds((TOK, D), f32), sds((16, D), f32)),
            (pl.BlockSpec((TOK, D), lambda i, s: (i, 0)), whole((TOK, D)), whole((16, D))),
            [pltpu.VMEM((D, D + SMALL), bf16), DMA((8,))],
            10,
        )
        qcols = query_gains.shape[1]
        counts = jnp.sum(gx[LANE_COUNT - LANE_GAIN : LANE_COUNT - LANE_GAIN + NB], axis=1)
        image_total = jnp.sum(counts)
        qg = gx[4:6].reshape(2, n_dp, rows)[:, :, :qcols].reshape(2, 1, HD)
        gain = jnp.tile(qg * jnp.array([0.125, 1.0], f32)[:, None, None], (1, NH, 1))
        gain = jnp.pad(gain.reshape(1, QK), ((0, 7), (0, 0)))
        vt = jnp.stack([valid, valid / image_total], axis=1)
        vt = jnp.pad(vt, ((0, 0), (0, 126)))

        row_block = lambda width: pl.BlockSpec((TOK, width), lambda i, s: (i, 0))
        head_block = pl.BlockSpec((NH, TOK, 128), lambda i, s: (0, i, 0))
        qx, kx, vx, xh, inv = call(
            qkv_kernel,
            (nt,),
            sc,
            [a, qaux, kaux, vaux, gain, avg] + in_p,
            [row_block(D), row_block(64), row_block(64), whole((TOK, 64)), whole((8, QK)),
             whole((128, 128))]
            + [ANY] * 4,
            tuple([sds((NH, length, 128), bf16)] * 3 + [sds((length, QK), f32)] * 2),
            tuple([head_block] * 3 + [row_block(QK)] * 2),
            [pltpu.VMEM((D, 576), bf16), DMA((4,))],
            10,
        )
        f_w = flat_call(
            out_kernel, sc, out_z, (sds((rows, 4 * OW), bf16),), us=2, deps=[a]
        )[0]
        f_c = direct(widen(f_w, low_bits))
        per_tok = TOK // BQ
        def attend(rel, us, deps):
            half = nq // 2
            block = lambda i, s: 2 * (s[1] ^ jnp.where(i < 2, rel[0], rel[1])) + i % 2
            return call(
                lambda *refs: attn_kernel(rel, *refs),
                (half,),
                sc,
                [qx, kx, vx, free_row],
                [
                    pl.BlockSpec((NH, BQ, 128), lambda i, s: (0, block(i, s), 0)),
                    whole((NH, length, 128)),
                    whole((NH, length, 128)),
                    whole((8, length)),
                ],
                (
                    sds((TOK, OW), bf16),
                    sds((TOK, OW), bf16),
                    sds((half * BQ, NH * HD), f32),
                    sds((NH, half * BQ, 128), bf16),
                ),
                (
                    pl.BlockSpec((BQ, OW), lambda i, s: (jnp.minimum(i, 1), 0)),
                    pl.BlockSpec((BQ, OW), lambda i, s: (jnp.maximum(i - 2, 0), 0)),
                    pl.BlockSpec((BQ, NH * HD), lambda i, s: (i, 0)),
                    pl.BlockSpec((NH, BQ, 128), lambda i, s: (0, i, 0)),
                ),
                [pltpu.VMEM((NH, BQ, 128), f32)],
                us,
                deps,
            )

        o_3, o_1, of_a, ql_a = attend((3, 1), 11, [f_w])
        f_p, f_stack = all8(f_c, [o_1])
        o_2, o_0, of_b, ql_b = attend((2, 0), 11, [f_stack])
        head_w = simple_call(
            head_pack_kernel, [class_head], sds((rows, CPAD), bf16), deps=[o_0]
        )
        head_c = direct(widen(head_w, low_bits))

        def trade(parts):
            return [parts[0], pp(parts[1], 0, 1), pp(parts[2], 1, 0), pp(parts[3], 1, 1)]

        o_p = trade([o_0, o_1, o_2, o_3])
        tile_spec = pl.BlockSpec((TOK, D), lambda j, s: (0, j))
        x1, b, u, h, x2, ns = call(
            mlp_kernel,
            (4,),
            sc,
            o_p + [x0, gx, mem, heads] + f_p + [w_all],
            [whole((TOK, OW))] * 4
            + [whole((TOK, D)), whole((16, D)), whole((TOK, IMG)), whole((D, 128))]
            + [ANY] * 6,
            (
                sds((TOK, D), f32),
                sds((TOK, D), bf16),
                sds((TOK, HID), f32),
                sds((TOK, HID), bf16),
                sds((TOK, D), f32),
                sds((IMG, D + 128), f32),
            ),
            (whole((TOK, D)), whole((TOK, D)), tile_spec, tile_spec, whole((TOK, D)),
             whole((IMG, D + 128))),
            [
                pltpu.VMEM((D, 4 * OW), bf16),
                pltpu.VMEM((4, 2, D, D), bf16),
                DMA((8,)),
                DMA((4, 2, 8)),
            ],
            18,
        )
        ns = ns + pp(ns, 1, 0)
        head_p, _ = all8(head_c, [ns])
        half_shape = (4, SUB, CPAD // 2)
        pooled, gp, sinv, loss, gh, gh_send = call(
            head_kernel,
            (1,),
            sc,
            [ns, pp(ns, 0, 1), lab_hot, vt, heads] + head_p,
            [whole((IMG, D + 128))] * 2
            + [whole((IMG, CPAD)), whole((IMG, 128)), whole((D, 128))]
            + [ANY] * 5,
            (
                sds((IMG, D), f32),
                sds((IMG, D), f32),
                sds((IMG, 128), f32),
                sds((IMG, 128), f32),
                sds(half_shape, bf16),
                sds(half_shape, bf16),
            ),
            (
                whole((IMG, D)),
                whole((IMG, D)),
                whole((IMG, 128)),
                whole((IMG, 128)),
                whole(half_shape),
                whole(half_shape),
            ),
            [pltpu.VMEM((D, CPAD), bf16), pltpu.VMEM((D, CPAD // 2), f32), DMA((8,))],
            5,
        )

        gu, gr, gm, gmid, *ga_parts, small_b = call(
            back_kernel,
            (4,),
            sc,
            [u, x2, x1, gx, mem, pooled, gp, sinv, heads] + f_p + [w_all],
            [
                tile_spec,
                whole((TOK, D)),
                whole((TOK, D)),
                whole((16, D)),
                whole((TOK, IMG)),
                whole((IMG, D)),
                whole((IMG, D)),
                whole((IMG, 128)),
                whole((D, 128)),
            ]
            + [ANY] * 6,
            (
                sds((TOK, HID), bf16),
                sds((TOK, D), bf16),
                sds((TOK, D), bf16),
                sds((TOK, D), f32),
                sds((TOK, OW), bf16),
                sds((TOK, OW), bf16),
                sds((TOK, OW), bf16),
                sds((TOK, OW), bf16),
                sds((8, D), f32),
            ),
            (
                tile_spec,
                whole((TOK, D)),
                whole((TOK, D)),
                whole((TOK, D)),
                whole((TOK, OW)),
                whole((TOK, OW)),
                whole((TOK, OW)),
                whole((TOK, OW)),
                whole((8, D)),
            ),
            [
                pltpu.VMEM((4, 2, D, D), bf16),
                pltpu.VMEM((D, 4 * OW), bf16),
                pltpu.VMEM((TOK, D), f32),
                pltpu.VMEM((TOK, D), f32),
                DMA((4, 2, 8)),
                DMA((8,)),
            ],
            20,
        )
        do_p = trade(ga_parts)

        if extra == 1:
            gh_one = add(gh[:2], pp(gh[2:], masks[1])).astype(bf16)
        else:
            gh_one = add(gh, pp(gh_send, masks[0])).astype(bf16)

        tile_of = pl.BlockSpec((TOK, D), lambda j, s: (0, j))
        width = 2 * D + OW
        wgrad = call(
            wgrad_kernel,
            (4,),
            sc,
            [gr, h, b, gu, gm] + o_p,
            [whole((TOK, D)), tile_of, whole((TOK, D)), tile_of, whole((TOK, D))]
            + [whole((TOK, OW))] * 4,
            (sds((8, 4, SUB, width), bf16),),
            (pl.BlockSpec((8, 1, SUB, width), lambda j, s: (0, s[2] ^ j, 0, 0)),),
            [pltpu.VMEM((4, TOK, OW), bf16)],
            14,
            deps=[gh_one],
        )[0]
        wgrad = pass_on(wgrad, [do_p[1], do_p[2], do_p[3]])
        if extra > 1:
            wgrad = wgrad.reshape(8, 4, extra, rows, width).transpose(0, 2, 1, 3, 4)
        wgrad = wgrad.reshape(n_dp * 4 * rows, width)
        z_out = lax.psum_scatter(wgrad, "dp", scatter_dimension=0, tiled=True)
        z_out = z_out.reshape(4, rows, width)
        z_got = [pp(z_out[r], 0, r) for r in (1, 2, 3)]

        def low_rows(x, low):
            for b in reversed(low):
                half = x.shape[-2] // 2
                first, second = x[..., :half, :], x[..., half:, :]
                flag = bit_of(b)
                send = jnp.where(flag, first, second)
                stay = jnp.where(flag, second, first)
                x = add(stay, pp(send.astype(bf16), b))
            return x

        def scatter4(stay, low, m1, m2):
            x = add(stay[:2], pp(stay[2:].astype(bf16), m1))
            x = add(x[0].astype(bf16), pp(x[1].astype(bf16), m2))
            return low_rows(x, low)

        def core_sum(stay, send):
            return add(stay, pp(send, masks[0])).astype(bf16)

        def chip_sum(x, first):
            m1, m2 = (masks[1], masks[2]) if first == 2 else (masks[2], masks[1])
            return scatter4(x, low_bits, m1, m2)

        if extra == 1:
            gh_m2 = add(gh_one[0], pp(gh_one[1], masks[2])).astype(bf16)
        else:
            gh_m2 = (0.5 * chip_sum(gh_one, 2)).astype(bf16)

        def halves(pairs, us, deps=()):
            kept, got = pairs[0]
            out = sds((kept.shape[0] // 2,) + kept.shape[1:], bf16)
            return (tuple(flat_call(halve_kernel, sc, [kept, got], (out, out), us=us, deps=deps)),)

        gh = add(gh_m2, pp(gh_m2, 0, 2))
        gh_got = pp(gh, 0, 1)
        half = nq // 2
        grads = call(
            attn_back_kernel,
            (nq + nt,),
            sc,
            [ql_a, ql_b, of_a, of_b] + do_p + [kx, vx, free_row],
            [
                pl.BlockSpec((NH, BQ, 128), lambda i, s: (0, jnp.minimum(i, half - 1), 0)),
                pl.BlockSpec((NH, BQ, 128), lambda i, s: (0, jnp.clip(i - half, 0, half - 1), 0)),
                pl.BlockSpec((BQ, NH * HD), lambda i, s: (jnp.minimum(i, half - 1), 0)),
                pl.BlockSpec((BQ, NH * HD), lambda i, s: (jnp.clip(i - half, 0, half - 1), 0)),
            ]
            + [whole((TOK, OW))] * 4
            + [whole((NH, length, 128)), whole((NH, length, 128)), whole((8, length))],
            (sds((length, 576), f32),),
            (pl.BlockSpec((TOK, 576), lambda i, s: (jnp.maximum(i - nq, 0), 0)),),
            [
                pltpu.VMEM((NH, length, 128), f32),
                pltpu.VMEM((NH, length, 128), f32),
                pltpu.VMEM((NH, length, 128), f32),
                pltpu.VMEM((4, TOK, OW), bf16),
            ],
            35,
        )[0]
        rel_tok = lambda n, s: s[1] ^ jnp.where(n < 2, n + 2, 3 - n)
        tok_block = lambda width: pl.BlockSpec((TOK, width), lambda n, s: (rel_tok(n, s), 0))
        in_shape = (2, D // 4, 576)
        g_send, g_one, g_own, in_keep, in_send, qgrad = call(
            mix_kernel,
            (nt,),
            sc,
            [grads, xh, inv, a, gain, avg] + in_p,
            [tok_block(576), tok_block(QK), tok_block(QK), tok_block(D), whole((8, QK)),
             whole((128, 128))]
            + [ANY] * 4,
            (
                sds((2, TOK, D), bf16),
                sds((TOK, D), bf16),
                sds((TOK, D), bf16),
                sds(in_shape, bf16),
                sds(in_shape, bf16),
                sds((8, QK), f32),
            ),
            (
                pl.BlockSpec((1, TOK, D), lambda n, s: (jnp.minimum(n, 1), 0, 0)),
                whole((TOK, D)),
                whole((TOK, D)),
                whole(in_shape),
                whole(in_shape),
                whole((8, QK)),
            ),
            [pltpu.VMEM((D, 576), f32), pltpu.VMEM((D, 576), bf16), DMA((4,))],
            14,
            deps=[gh_m2],
        )
        g_core = pp(g_send, 1)
        g_z_in = add(g_one, g_core[1]).astype(bf16)
        g_z = pp(g_z_in, 0, 1)

        in_got = pp(in_send, col_masks[0])
        (ik, is_), = halves([(in_keep, in_got)], 2, deps=[g_z_in])
        is_got = pp(is_, col_masks[1])

        if extra == 1:
            in_a, in_b = flat_call(
                in_parts_kernel, sc, [ik[0], is_got[0]], (sds((rows, 576), bf16),) * 2, us=2,
                deps=[is_],
            )
        else:
            both = low_rows(add(ik[0], is_got[0]), col_low).astype(bf16).reshape(2, rows, 576)
            in_a = jnp.where(z1 == 1, both[1], both[0])
            in_b = jnp.where(z1 == 1, both[0], both[1])
        in_parts = in_a
        in_a = lax.ppermute(in_a, ("dp", "mp"), perm_a)
        in_b = lax.ppermute(in_b, ("dp", "mp"), back_b)
        qg_rows = qgrad[0].reshape(2, NH, HD).sum(axis=1) * jnp.array([0.125, 1.0], f32)[:, None]
        qg_rows = jnp.pad(qg_rows, ((0, 6), (0, 0)))
        hot_own = pl.BlockSpec((TOK, 128), lambda i, s: (s[1], 0))
        own_rows = pl.BlockSpec((TOK, D), lambda i, s: (s[1], 0))

        def tail_body(*refs):
            tail_kernel(n_dp, *refs)

        pk, ps = call(
            tail_body,
            (1,),
            sc,
            [g_own, g_core, g_z, gmid, x0, gx, patches, patches_in, hot_pos, small_b, qg_rows],
            [
                whole((TOK, D)),
                pl.BlockSpec((1, TOK, D), lambda i, s: (0, 0, 0)),
                whole((TOK, D)),
                whole((TOK, D)),
                whole((TOK, D)),
                whole((16, D)),
                own_rows,
                own_rows,
                hot_own,
                whole((8, D)),
                whole((8, HD)),
            ],
            (sds((4, SUB, D + SMALL), bf16), sds((4, SUB, D + SMALL), bf16)),
            (whole((4, SUB, D + SMALL)), whole((4, SUB, D + SMALL))),
            [pltpu.VMEM((D, D + SMALL), f32)],
            6,
            deps=[is_],
        )
        (pk1, ps1), = halves([(pk, pp(ps, masks[0]))], 2, deps=[z_out])
        ps1_got = pp(ps1, masks[1])
        (pk2, ps2), = halves([(pk1, ps1_got)], 2, deps=[gh, in_parts])
        ps2_got = pp(ps2, masks[2])
        s_up, s_down, s_out, sq_z = flat_call(
            share_z_kernel,
            sc,
            [z_out] + z_got,
            (
                sds((rows, D), f32),
                sds((rows, D), f32),
                sds((192, rows), f32),
                sds((8, 128), f32),
            ),
            us=3,
            deps=[ps2],
        )
        s_in, s_head, sq = flat_call(
            share_kernel,
            sc,
            [sq_z, in_a, in_b, gh, gh_got],
            (sds((rows, 576), f32), sds((rows, CLASSES), f32), sds((8, 128), f32)),
            us=2,
            deps=[sq_z],
        )
        if extra == 1:
            p_ins = [pk2, ps2_got]
        else:
            total = low_rows(add(pk2[0], ps2_got[0]), low_bits).astype(bf16)[None]
            p_ins = [total, jnp.zeros_like(total)]
        wide = jnp.arange(D + SMALL)
        extra_row = jnp.where((wide == buck + 1) & (g == 0), jnp.sum(loss[:, 0]), 0.0)
        extra_row = jnp.broadcast_to(extra_row[None, :], (8, D + SMALL))
        mine_q = flat_call(
            patch_row_kernel, sc, p_ins + [sq, extra_row], (sds((rows + 16, D + SMALL), bf16),), us=2
        )[0]
        share_patch, stats = flat_call(
            patch_sum_kernel,
            sc,
            [mine_q, pp(mine_q, 0, 1), pp(mine_q, 0, 2), pp(mine_q, 0, 3)],
            (sds((rows, D + SMALL), f32), sds((8, SMALL), f32)),
            us=2,
        )
        stats = stats + pp(stats, 1)
        m = 2
        while m < n_dp:
            stats = (stats + pp(stats, m)) + (pp(stats, 2 * m) + pp(stats, 3 * m))
            m *= 4

        shares = [s_in, s_out, s_up, s_down, share_patch, s_head]
        turned = [x.T if n // 3 == 3 else x for n, x in enumerate(state)]
        news = simple_call(
            update_kernel,
            [stats] + shares + turned,
            tuple([sds((1, 1), f32), sds((1, NB), f32)] + [sds(s.shape, f32) for s in turned]),
            6,
        )
        outs = [x.T if n // 3 == 3 else x for n, x in enumerate(news[2:])]
        return (news[1].reshape(NB), counts, news[0].reshape(())) + tuple(outs)

    return local


def solution(mesh):
    shard = {
        "in": P("dp", "mp"),
        "out": P("mp", "dp"),
        "row": P("dp", None),
        "col": P(None, "dp"),
    }
    kinds = ["in", "out", "in", "out", "row", "col", "row", "col", "col"]
    triples = tuple(shard[k] for k in kinds for _ in range(3))
    in_specs = (P("dp", None),) + (P("dp"),) * 6 + triples
    out_specs = (P(), P(), P()) + triples
    return jax.shard_map(
        make_local(mesh.shape["dp"], mesh.shape["mp"]),
        mesh=mesh,
        in_specs=in_specs,
        out_specs=out_specs,
        check_vma=False,
    )
```

```python
import jax
import jax.numpy as jnp
from jax import lax
from jax.experimental import pallas as pl
from jax.experimental.pallas import tpu as pltpu
from jax.sharding import PartitionSpec as P

D = 768
HD = 64
HID = 3072
CLASSES = 1000
CPAD = 1024
GRID = 32
IMG = 16
NB = 4
STEP = 10
BQ = 256
TOK = 512
NH = 3
QK = 2 * NH * HD
SUB = D // 8
SMALL = 128
OW = 256
LANE_GAIN = 64
LANE_QG = 68
LANE_COUNT = 72

HIGH = lax.Precision.HIGHEST
NORM_EPS = 1e-06
CLIP = 0.1
BETA_ONE = 0.9
BETA_TWO = 0.95
RATE_MATRIX = 0.05
RATE_SMALL = 0.2
DECAY = 0.05
ADAM_EPS = 1e-08
BIG = 128.0

bf16 = jnp.bfloat16
f32 = jnp.float32
VLIM = 56 * 1024 * 1024
COST = 0.001 * 1.15e9

NN = (((1,), (0,)), ((), ()))
NT = (((1,), (1,)), ((), ()))
TN = (((0,), (0,)), ((), ()))


def dot(a, b, dims=NN, precision=None):
    return lax.dot_general(a, b, dims, precision=precision, preferred_element_type=f32)


def norm_stats(values):
    center = values - jnp.mean(values, axis=-1, keepdims=True)
    inv_std = lax.rsqrt(jnp.mean(center * center, axis=-1, keepdims=True) + NORM_EPS)
    return center * inv_std, inv_std


def norm_back(grad_scaled, scaled, inv_std):
    return inv_std * (
        grad_scaled
        - jnp.mean(grad_scaled, axis=-1, keepdims=True)
        - scaled * jnp.mean(grad_scaled * scaled, axis=-1, keepdims=True)
    )


def splits(x, n):
    out = []
    for _ in range(n - 1):
        part = x.astype(bf16)
        out.append(part)
        x = x - part.astype(f32)
    out.append(x.astype(bf16))
    return out


def dot_split(x, exact, n, dims=NN):
    total = None
    for part in splits(x, n):
        term = dot(part, exact, dims)
        total = term if total is None else total + term
    return total


def head_mean(x, ones, n):
    return jnp.concatenate(
        [dot_split(x[:, c : c + 128], ones, n) for c in range(0, QK, 128)], axis=1
    )


def eye(rows, cols, offset=0):
    row = lax.broadcasted_iota(jnp.int32, (rows, cols), 0)
    col = lax.broadcasted_iota(jnp.int32, (rows, cols), 1)
    return (row + offset == col).astype(f32)


def rows_at(index, size):
    return pl.ds(pl.multiple_of(index * size, size), size)


def pack_kernel(w_patch, w_pos, w_gain, w_qg, seg, keep, bucket, w_up, w_down,
                patch_o, t_o):
    rows = w_patch.shape[0]
    patch_o[:, :D] = w_patch[...].astype(bf16)
    low = lambda ref: ref[...].astype(bf16).astype(f32)
    small = dot(low(w_pos), eye(64, SMALL), TN)
    small += dot(low(w_gain), eye(4, SMALL, LANE_GAIN), TN)
    qg = dot(low(w_qg), eye(2, SMALL, LANE_QG), TN)
    small += dot(eye(rows, qg.shape[0]), qg)
    kept = keep[...] == 1
    count = jnp.zeros((1, 1), f32)
    for n in range(IMG):
        held = jnp.where((seg[...] == n) & kept, 1.0, 0.0)
        count += jnp.max(held, keepdims=True)
    row = lax.broadcasted_iota(jnp.int32, (rows, SMALL), 0)
    col = lax.broadcasted_iota(jnp.int32, (rows, SMALL), 1)
    small += jnp.where((row == 0) & (col == LANE_COUNT + bucket[0]), count, 0.0)
    patch_o[:, D:] = small.astype(bf16)

    t_o[:, :D] = w_up[...].astype(bf16)
    t_o[:, D:] = w_down[...].astype(bf16)


def pack_rest_kernel(w_in, w_out, in_o, out_o):
    rows = w_in.shape[0]
    w = w_in[...].astype(bf16)
    parts = [
        w[:, h * 192 + part * HD : h * 192 + part * HD + HD]
        for part in range(3)
        for h in range(NH)
    ]
    in_o[...] = jnp.concatenate(parts, axis=1)
    turned = dot(eye(rows, rows).astype(bf16), w_out[...].astype(bf16), NT)
    out_o[...] = jnp.concatenate([turned, jnp.zeros((rows, OW - 192), f32)], axis=1).astype(bf16)


def ordered(flag, x, y):
    return jnp.where(flag, jnp.concatenate([y, x], axis=1), jnp.concatenate([x, y], axis=1))


def lanes_at(index, width):
    return pl.ds(pl.multiple_of(index * width, width), width)


def out_kernel(sc, o0, o1, o2, o3, out):
    for r, ref in enumerate((o0, o1, o2, o3)):
        out[:, lanes_at(sc[2] ^ r, OW)] = ref[...]


def head_pack_kernel(head, out):
    out[...] = jnp.zeros_like(out)
    out[:, :CLASSES] = head[...].astype(bf16)


def eight(refs):
    return list(refs[:4]) + [refs[4].at[n] for n in range(4)]


REL = [0, 2, 4, 6, 1, 3, 5, 7]


def stack_kernel(a, b, c, d, out):
    for n, ref in enumerate((a, b, c, d)):
        out[n] = ref[...]


def row_copies(refs, me, dst, sems, rel=REL):
    out = []
    for n, ref in enumerate(refs):
        size = ref.shape[0]
        out.append(pltpu.make_async_copy(ref, dst.at[rows_at(me ^ rel[n], size), :], sems.at[n]))
    return out


def columns(refs, lo, width):
    return [ref.at[:, pl.ds(lo, width)] for ref in refs]


def start(copies):
    for copy in copies:
        copy.start()


def wait(copies):
    for copy in copies:
        copy.wait()


def x0_kernel(sc, own, other, hot, *rest):
    refs = eight(rest[:5])
    a_out, x0_out, gx_out, w, sems = rest[5:]
    i = pl.program_id(0)

    @pl.when(i == 0)
    def _():
        copies = row_copies(refs, sc[0], w, sems)
        start(copies)
        wait(copies)
        row = lax.broadcasted_iota(jnp.int32, (16, SMALL), 0)
        col = lax.broadcasted_iota(jnp.int32, (16, SMALL), 1)
        pick = (row + LANE_GAIN == col).astype(f32).astype(bf16)
        gx_out[...] = dot(pick, w[:, D:], NT)

    rows = jnp.where(sc[3] == 1, own[...], other[...])
    x0 = dot(rows, w[:, :D]) + dot(hot[...], w[:, D:], NT)
    scaled, _ = norm_stats(x0)
    a_out[...] = (scaled * gx_out[0:1, :]).astype(bf16)

    @pl.when(i == sc[1])
    def _():
        x0_out[...] = x0


IN_REL = [0, 1, 2, 3]


def qkv_kernel(sc, a, qaux, kaux, vaux, gain, avg, *rest):
    refs = rest[:4]
    qx, kx, vx, xh_out, inv_out, w, sems = rest[4:]
    i = pl.program_id(0)

    @pl.when(i == 0)
    def _():
        copies = row_copies(refs, sc[4], w, sems, IN_REL)
        start(copies)
        wait(copies)

    mixed = dot(a[...], w[...])
    qk = mixed[:, :QK]
    v = mixed[:, QK:].astype(bf16)
    ones = avg[...]
    center = qk - head_mean(qk, ones, 2)
    inv = lax.rsqrt(head_mean(center * center, ones, 2) + NORM_EPS)
    scaled = center * inv
    xh_out[...] = scaled
    inv_out[...] = inv
    low = (scaled * gain[0:1, :]).astype(bf16)
    qa, ka, va = qaux[...], kaux[...], vaux[...]
    for h in range(NH):
        qx[h] = jnp.concatenate([low[:, h * HD : h * HD + HD], qa], axis=1)
        kx[h] = jnp.concatenate([low[:, (NH + h) * HD : (NH + h) * HD + HD], ka], axis=1)
        vx[h] = jnp.concatenate([v[:, h * HD : h * HD + HD], va], axis=1)


def attn_kernel(rel, sc, qx, kx, vx, free, o_first, o_second, o_full, ql, acc):
    step_id = pl.program_id(0)
    i = 2 * (sc[1] ^ jnp.where(step_id < 2, rel[0], rel[1])) + step_id % 2
    acc[...] = jnp.zeros_like(acc)
    lo, hi = sc[8 + i], sc[16 + i]

    def tile(start_row, size):
        ks = pl.ds(pl.multiple_of(start_row, BQ), size)
        row = lax.broadcasted_iota(jnp.int32, (BQ, size), 0)
        col = lax.broadcasted_iota(jnp.int32, (BQ, size), 1)
        own = jnp.where(row + (i * BQ - start_row) == col, free[0:1, ks], 0.0)
        scores = [dot(qx[h], kx[h, ks, :], NT) + own for h in range(NH)]
        probs = [jnp.exp(s).astype(bf16) for s in scores]
        for h in range(NH):
            acc[h] += dot(probs[h], vx[h, ks, :])

    pairs = (hi - lo) // 2

    def step(j, carry):
        tile((lo + 2 * j) * BQ, 2 * BQ)
        return carry

    lax.fori_loop(0, pairs, step, 0)

    @pl.when((hi - lo) % 2 == 1)
    def _():
        tile((hi - 1) * BQ, BQ)

    lane = lax.broadcasted_iota(jnp.int32, (BQ, HD), 1)
    outs = []
    for h in range(NH):
        out = acc[h]
        total = out[:, HD:]
        outs.append(out[:, :HD] / total)
        aux = qx[h][:, HD:].astype(f32)
        for n, part in enumerate(splits(-jnp.log(total), 3)):
            aux = jnp.where(lane == IMG + 1 + n, part.astype(f32), aux)
        ql[h] = jnp.concatenate([qx[h][:, :HD], aux.astype(bf16)], axis=1)
    full = jnp.concatenate(outs, axis=1)
    o_full[...] = full
    low = jnp.concatenate([full, jnp.zeros((BQ, OW - NH * HD), f32)], axis=1).astype(bf16)

    @pl.when(step_id < 2)
    def _():
        o_first[...] = low

    @pl.when(step_id >= 2)
    def _():
        o_second[...] = low


GELU_C = 0.7978845608028654


def gelu_tanh(u):
    return jnp.tanh(GELU_C * (u + 0.044715 * u * u * u))


def mlp_tile(b, w, u_out, h_out):
    u = dot(b, w[0])
    u_out[...] = u
    h = (0.5 * u * (1.0 + gelu_tanh(u))).astype(bf16)
    h_out[...] = h
    return dot(h, w[1], NT)


def tile_copies(w_all, j, dst, sems):
    size = D // 8
    return [
        pltpu.make_async_copy(
            w_all.at[d, j, :, pl.ds(part * D, D)],
            dst.at[part, pl.ds(d * size, size), :],
            sems.at[part, d],
        )
        for part in range(2)
        for d in range(8)
    ]


def mlp_kernel(sc, o0, o1, o2, o3, x0, gx, mem, heads, *rest):
    refs, w_all = eight(rest[:5]), rest[5]
    x1_out, b_out, u_out, h_out, x2, ns_out, w_o, w_t, sem_o, sem_t = rest[6:]
    j = pl.program_id(0)

    @pl.when(j == 0)
    def _():
        first = row_copies(refs, sc[0], w_o, sem_o)
        start(first)
        for t in range(4):
            start(tile_copies(w_all, t, w_t.at[t], sem_t.at[t]))
        wait(first)
        x1 = x0[...]
        for r, ref in enumerate((o0, o1, o2, o3)):
            x1 += dot(ref[...], w_o[:, lanes_at(sc[1] ^ r, OW)], NT)
        x1_out[...] = x1
        b_out[...] = (norm_stats(x1)[0] * gx[1:2, :]).astype(bf16)
        x2[...] = x1

    wait(tile_copies(w_all, j, w_t.at[j], sem_t.at[j]))
    x2[...] += mlp_tile(b_out[...], w_t.at[j], u_out, h_out)

    @pl.when(j == 3)
    def _():
        f = norm_stats(x2[...])[0] * gx[2:3, :]
        ones = heads[...]
        e = jnp.exp(dot_split(f * gx[3:4, :], ones, 3) * 0.125)
        eb = dot_split(e, ones, 2, NT)
        m = mem[...]
        num = jnp.zeros((IMG, D), f32)
        for part in splits(eb * f, 3):
            num += dot(m, part, TN)
        den = jnp.zeros((IMG, 128), f32)
        for part in splits(e, 3):
            den += dot(m, part, TN)
        ns_out[:, :D] = num
        ns_out[:, D:] = den


def head_kernel(sc, ns_a, ns_b, lab, vt, heads, *rest):
    pooled_out, gp_out, sinv_out, loss_out, gh_out, gh_send, w, gw, sems = rest[5:]
    copies = row_copies(eight(rest[:5]), sc[0], w, sems)
    start(copies)
    ns = ns_a[...] + ns_b[...]
    valid = vt[:, 0:1]
    scale = vt[:, 1:2]
    total = jnp.where(valid > 0.0, ns[:, D:], 1.0)
    sinv = jnp.where(valid > 0.0, 1.0 / total, 0.0)
    lane = lax.broadcasted_iota(jnp.int32, (IMG, 128), 1)
    sinv = jnp.where(lane < D // HD, sinv, 0.0)
    pooled = ns[:, :D] * dot_split(sinv, heads[...], 3, NT)
    low = pooled.astype(bf16)
    wait(copies)
    logits = dot(low, w[...])
    cls = lax.broadcasted_iota(jnp.int32, (IMG, CPAD), 1)
    real = (cls < CLASSES).astype(f32)
    hot = lab[...]
    ex = jnp.exp(-jnp.abs(logits))
    soft = jnp.maximum(logits, 0.0) + jnp.log1p(ex)
    per = jnp.sum(soft * real, axis=1, keepdims=True) - jnp.sum(
        logits * hot, axis=1, keepdims=True
    )
    loss_out[...] = jnp.broadcast_to(per * valid, (IMG, 128))
    sig = jnp.where(logits >= 0.0, 1.0, ex) / (1.0 + ex)
    gl = (scale * (sig * real - hot)).astype(bf16)
    pooled_out[...] = pooled
    sinv_out[...] = sinv
    gp_out[...] = dot(gl, w[...], NT)
    half = jnp.where(sc[2] % 2 == 1, gl[:, 512:].astype(f32), gl[:, :512].astype(f32))
    gw[...] = dot(low, half.astype(bf16), TN)
    for p, r in enumerate(rel_order(2)):
        gh_out[p] = gw[rows_at(sc[0] ^ r, SUB), :].astype(bf16)
        gh_send[p] = gw[rows_at(sc[0] ^ (r + 1), SUB), :].astype(bf16)


def rel_order(first):
    m1, m2 = (2, 4) if first == 2 else (4, 2)
    return [(p >> 1) * m1 + (p & 1) * m2 for p in range(4)]


def back_kernel(sc, u, x2, x1, gx, mem, pooled, gp, sinv, heads, *rest):
    refs, w_all = eight(rest[:5]), rest[5]
    gu_out, gr_out, gm_out, gmid_out = rest[6:10]
    ga_out, small_out = rest[10:14], rest[14]
    w_t, w_o, grs, acc, sem_t, sem_o = rest[15:]
    j = pl.program_id(0)

    def out_rows():
        return row_copies(refs, sc[0], w_o, sem_o)

    @pl.when(j == 0)
    def _():
        for t in range(4):
            start(tile_copies(w_all, t, w_t.at[t], sem_t.at[t]))
        start(out_rows())
        scaled, inv = norm_stats(x2[...])
        f = scaled * gx[2:3, :]
        probe = gx[3:4, :]
        ones = heads[...]
        e = jnp.exp(dot_split(f * probe, ones, 3) * 0.125)
        m = mem[...]
        m3 = jnp.concatenate([m, m, m], axis=1)

        def spread(x):
            return dot(m3, jnp.concatenate(splits(x, 3), axis=0))

        gt = spread(gp[...])
        at = e * spread(sinv[...])
        gpp = dot_split(gp[...] * pooled[...], ones, 3)
        da = dot_split(gt * f, ones, 3)
        dc = at * (da - spread(gpp))
        dcb = dot_split(dc, ones, 2, NT) * 0.125
        df = dot_split(at, ones, 2, NT) * gt + dcb * probe
        gr = norm_back(df * gx[2:3, :], scaled, inv)
        grs[...] = gr
        gr_out[...] = gr.astype(bf16)
        small_out[2:3, :] = jnp.sum(df * scaled, axis=0, keepdims=True)
        small_out[3:4, :] = jnp.sum(dcb * f, axis=0, keepdims=True)
        small_out[0:1, :] = jnp.zeros((1, D), f32)
        small_out[4:8, :] = jnp.zeros((4, D), f32)
        acc[...] = jnp.zeros_like(acc)

    wait(tile_copies(w_all, j, w_t.at[j], sem_t.at[j]))
    gh = dot(gr_out[...], w_t[j, 1])
    v = u[...]
    t = gelu_tanh(v)
    slope = 0.5 * (1.0 + t) + 0.5 * v * (1.0 - t * t) * GELU_C * (1.0 + 0.134145 * v * v)
    gu = (gh * slope).astype(bf16)
    gu_out[...] = gu
    acc[...] += dot(gu, w_t[j, 0], NT)

    @pl.when(j == 3)
    def _():
        wait(out_rows())
        scaled, inv = norm_stats(x1[...])
        gb = acc[...]
        small_out[1:2, :] = jnp.sum(gb * scaled, axis=0, keepdims=True)
        gmid = grs[...] + norm_back(gb * gx[1:2, :], scaled, inv)
        gmid_out[...] = gmid
        low = gmid.astype(bf16)
        gm_out[...] = low
        for r in range(4):
            ga_out[r][...] = dot(low, w_o[:, lanes_at(sc[1] ^ r, OW)]).astype(bf16)


def wgrad_kernel(sc, gr, h, b, gu, gm, o0, o1, o2, o3, out, os):
    j = pl.program_id(0)

    @pl.when(j == 0)
    def _():
        for r, ref in enumerate((o0, o1, o2, o3)):
            os[r] = ref[...]

    parts = [
        (0, dot(b[...], gu[...], TN)),
        (D, dot(gr[...], h[...], TN)),
        (2 * D, dot(gm[...], os[sc[1] ^ j], TN)),
    ]
    for lo, value in parts:
        width = value.shape[1]
        for d in range(8):
            out[d, 0, :, lo : lo + width] = value[d * SUB : (d + 1) * SUB, :].astype(bf16)


def attn_back_kernel(sc, ql_a, ql_b, of_a, of_b, d0, d1, d2, d3, kx, vx, free, g_out, dq, dk, dv, dos):
    i = pl.program_id(0)
    nq = dk.shape[1] // BQ

    @pl.when(i == 0)
    def _():
        for n, ref in enumerate((d3, d1, d2, d0)):
            dos[n] = ref[...]

    @pl.when(i == 0)
    def _():
        dk[...] = jnp.zeros_like(dk)
        dv[...] = jnp.zeros_like(dv)

    @pl.when(i < nq)
    def _():
        n = i // 2
        block = 2 * (sc[1] ^ jnp.where(n < 2, 3 - 2 * n, 6 - 2 * n)) + i % 2
        mine = rows_at(block, BQ)
        lane = lax.broadcasted_iota(jnp.int32, (BQ, HD), 1)
        first = i < nq // 2
        of = jnp.where(first, of_a[...], of_b[...])
        do = dos[n, rows_at(i % 2, BQ), :].astype(f32)
        width = NH * HD
        head_r = lax.broadcasted_iota(jnp.int32, (width, width), 0) // HD
        head_c = lax.broadcasted_iota(jnp.int32, (width, width), 1) // HD
        same_head = (head_r == head_c).astype(f32).astype(bf16)
        deltas = dot_split(do[:, :width] * of, same_head, 3)
        dob, qb = [], []
        for h in range(NH):
            dof = do[:, h * HD : h * HD + HD]
            delta = deltas[:, h * HD : h * HD + HD]
            aux = jnp.zeros((BQ, HD), f32)
            for m, part in enumerate(splits(-delta, 3)):
                aux = jnp.where(lane == m, part.astype(f32), aux)
            dob.append(jnp.concatenate([dof, aux], axis=1).astype(bf16))
            q = jnp.where(first, ql_a[h].astype(f32), ql_b[h].astype(f32))
            qb.append(q.astype(bf16))
            dq[h, mine, :] = jnp.zeros((BQ, 128), f32)
        own_free = free[0:1, pl.ds(pl.multiple_of(block * BQ, BQ), BQ)]

        def tile(start_row, size):
            ks = pl.ds(pl.multiple_of(start_row, BQ), size)
            row = lax.broadcasted_iota(jnp.int32, (size, BQ), 0)
            col = lax.broadcasted_iota(jnp.int32, (size, BQ), 1)
            own = jnp.where(row + (start_row - block * BQ) == col, own_free, 0.0)
            pts = [jnp.exp(dot(kx[h, ks, :], qb[h], NT) + own) for h in range(NH)]
            dpts = [dot(vx[h, ks, :], dob[h], NT) for h in range(NH)]
            dsts = [(pts[h] * dpts[h]).astype(bf16) for h in range(NH)]
            for h in range(NH):
                dv[h, ks, :] += dot(pts[h].astype(bf16), dob[h])
                dk[h, ks, :] += dot(dsts[h], qb[h])
                dq[h, mine, :] += dot(dsts[h], kx[h, ks, :], TN)

        lo, hi = sc[8 + block], sc[16 + block]

        def step(j, carry):
            tile((lo + 2 * j) * BQ, 2 * BQ)
            return carry

        lax.fori_loop(0, (hi - lo) // 2, step, 0)

        @pl.when((hi - lo) % 2 == 1)
        def _():
            tile((hi - 1) * BQ, BQ)

    @pl.when(i >= nq)
    def _():
        rows = rows_at(i - nq, TOK)
        g_out[...] = jnp.concatenate(
            [ref[h, rows, :][:, :HD] for ref in (dq, dk, dv) for h in range(NH)], axis=1
        )


def mix_kernel(sc, grad, xh, inv, a, gain, avg, *rest):
    refs = rest[:4]
    g_send, g_one, g_own, in_keep, in_send, qg_out, gin, w, sems = rest[4:]
    n = pl.program_id(0)

    @pl.when(n == 0)
    def _():
        copies = row_copies(refs, sc[4], w, sems, IN_REL)
        start(copies)
        gin[...] = jnp.zeros_like(gin)
        qg_out[...] = jnp.zeros_like(qg_out)
        wait(copies)

    grads = grad[:, :QK]
    scaled = xh[...]
    ones = avg[...]
    qg_out[0:1, :] += jnp.sum(grads * scaled, axis=0, keepdims=True)
    dg = grads * gain[0:1, :]
    back = inv[...] * (
        dg - head_mean(dg, ones, 2) - scaled * head_mean(dg * scaled, ones, 2)
    )
    mix = jnp.concatenate([back, grad[:, QK:]], axis=1).astype(bf16)
    out = dot(mix, w[...], NT).astype(bf16)
    gin[...] += dot(a[...], mix, TN)

    @pl.when(n < 2)
    def _():
        g_send[0] = out

    @pl.when(n == 2)
    def _():
        g_one[...] = out

    @pl.when(n == 3)
    def _():
        g_own[...] = out
        size = D // 4
        for p in range(2):
            in_keep[p] = gin[rows_at(sc[4] ^ (2 * p), size), :].astype(bf16)
            in_send[p] = gin[rows_at(sc[4] ^ (2 * p + 1), size), :].astype(bf16)


def add(x, y):
    return x.astype(f32) + y.astype(f32)


def halve_kernel(sc, kept, got, keep_o, send_o):
    half = keep_o.shape[0]
    for n in range(half):
        keep_o[n] = add(kept[n], got[n]).astype(bf16)
        send_o[n] = add(kept[half + n], got[half + n]).astype(bf16)


def in_parts_kernel(sc, kept, got, a_out, b_out):
    half = a_out.shape[0]
    first = sc[5]
    mine, other = rows_at(first, half), rows_at(1 - first, half)
    a_out[...] = add(kept[mine, :], got[mine, :]).astype(bf16)
    b_out[...] = add(kept[other, :], got[other, :]).astype(bf16)


def share_z_kernel(sc, z0, z1, z2, z3, up_o, down_o, out_o, sq_o):
    rows = up_o.shape[0]
    total = add(z0[0], z1[...]) + add(z2[...], z3[...])
    up_o[...] = total[:, :D]
    down_o[...] = total[:, D : 2 * D]
    out_o[...] = dot(total[:, 2 * D :], eye(rows, rows), TN, HIGH)[:192, :]
    sq_o[...] = jnp.broadcast_to(jnp.sum(total * total, keepdims=True), sq_o.shape)


def share_kernel(sc, sq_z, in_a, in_b, h_own, h_got, kept, got, extra_row, in_o, head_o, row_o):
    rows = kept.shape[1]
    grad = add(in_a[...], in_b[...])
    in_o[...] = jnp.concatenate(
        [
            grad[:, part * NH * HD + h * HD : part * NH * HD + h * HD + HD]
            for h in range(NH)
            for part in range(3)
        ],
        axis=1,
    )
    head = ordered(sc[2] % 2 == 1, h_own[...], h_got[...])
    head_o[...] = head[:, :CLASSES]
    squares = jnp.sum(grad * grad, keepdims=True)
    once = jnp.where(sc[2] == 0, 1.0, 0.0)
    squares += once * jnp.sum(head * head, keepdims=True)
    row_o[:rows, :] = add(kept[0], got[0]).astype(bf16)
    lane = lax.broadcasted_iota(jnp.int32, (16, D + SMALL), 1)
    row = lax.broadcasted_iota(jnp.int32, (16, D + SMALL), 0)
    value = jnp.where(lane == 0, sq_z[0:1, 0:1] + squares, extra_row[0:1, :])
    tail = jnp.zeros((16, D + SMALL), f32)
    for n, part in enumerate(splits(value, 3)):
        tail = jnp.where(row == n, part.astype(f32), tail)
    row_o[rows:, :] = tail.astype(bf16)


def patch_sum_kernel(sc, own, q1, q2, q3, share_o, stats_o):
    rows = share_o.shape[0]
    total = add(own[...], q1[...]) + add(q2[...], q3[...])
    patch = total[:rows, :]
    share_o[...] = patch
    sums = total[rows : rows + 1, :SMALL] + total[rows + 1 : rows + 2, :SMALL]
    sums += total[rows + 2 : rows + 3, :SMALL]
    lane = lax.broadcasted_iota(jnp.int32, (8, SMALL), 1)
    squares = jnp.sum(patch * patch, keepdims=True)
    stats_o[...] = sums + jnp.where(lane == 0, squares, 0.0)


def tail_kernel(n_dp, sc, g_own, g_core, g_z, gmid, x0, gx, own, other, hot, small_b, qgrad,
                pk, ps, tile):
    grad = g_own[...].astype(f32) + g_core[0].astype(f32) + g_z[...].astype(f32)
    scaled, inv = norm_stats(x0[...])
    gain_a = jnp.sum(grad * scaled, axis=0, keepdims=True)
    ge = (gmid[...] + norm_back(grad * gx[0:1, :], scaled, inv)).astype(bf16)
    rows = jnp.where(sc[3] == 1, own[...], other[...])
    tile[:, :D] = dot(rows, ge, TN)
    row8 = lax.broadcasted_iota(jnp.int32, (8, D), 0)
    gains = jnp.where(row8 == 0, gain_a, small_b[...])
    small = dot(ge, hot[...], TN) + dot(gains, eye(8, SMALL, LANE_GAIN), TN)
    part = HD // n_dp
    kk = lax.broadcasted_iota(jnp.int32, (HD, D), 0)
    rr = lax.broadcasted_iota(jnp.int32, (HD, D), 1)
    spot = ((kk // part) * (D // n_dp) + kk % part == rr).astype(f32)
    lane = lax.broadcasted_iota(jnp.int32, (8, SMALL), 1)
    row = lax.broadcasted_iota(jnp.int32, (8, SMALL), 0)
    q_lane = ((lane == LANE_QG + row) & (row < 2)).astype(f32)
    q_cols = dot(qgrad[...], q_lane, TN, HIGH)
    small += dot(spot, q_cols, TN)
    tile[:, D:] = small
    for p, r in enumerate(rel_order(2)):
        pk[p] = tile[rows_at(sc[0] ^ r, SUB), :].astype(bf16)
        ps[p] = tile[rows_at(sc[0] ^ (r + 1), SUB), :].astype(bf16)


def update_kernel(stats, *rest):
    shares = rest[:6]
    state = rest[6:33]
    norm_out, loss_out, outs = rest[33], rest[34], rest[35:]
    total = stats[0:1, :]
    norm = jnp.sqrt(total)
    norm_out[...] = norm[:, 0:1]
    loss_out[...] = total[:, 1 : 1 + NB]
    factor = jnp.minimum(1.0, CLIP / (norm[:, 0:1] + 1e-06))
    s_in, s_out, s_up, s_down, s_patch, s_head = shares
    rows = s_patch.shape[0]
    small = dot(eye(SMALL, SMALL), s_patch[:, D:], NT, HIGH)
    part = state[24].shape[1]
    grads = [
        s_in[...],
        s_out[...],
        s_up[...],
        s_down[...],
        s_patch[:, :D],
        small[: 2 * GRID, :],
        s_head[...],
        small[LANE_GAIN : LANE_GAIN + 4, :],
        small[LANE_QG : LANE_QG + 2, :part],
    ]
    for n in range(9):
        master, first, second = state[3 * n : 3 * n + 3]
        clipped = grads[n] * factor
        first_new = BETA_ONE * first[...] + (1.0 - BETA_ONE) * clipped
        second_new = BETA_TWO * second[...] + (1.0 - BETA_TWO) * clipped * clipped
        matrix = n in (0, 1, 2, 3, 4, 6)
        rate = RATE_MATRIX if matrix else RATE_SMALL
        decay = DECAY if matrix else 0.0
        ratio = (
            first_new
            / (1.0 - BETA_ONE**STEP)
            / (jnp.sqrt(second_new / (1.0 - BETA_TWO**STEP)) + ADAM_EPS)
        )
        value = master[...]
        outs[3 * n][...] = value - rate * (ratio + decay * value)
        outs[3 * n + 1][...] = first_new
        outs[3 * n + 2][...] = second_new


ANY = pl.BlockSpec(memory_space=pl.ANY)


def without(kernel, count, deps):
    if not deps:
        return kernel
    return lambda *refs: kernel(*refs[:count], *refs[count + len(deps) :])


def call(kernel, grid, sc, ins, specs, outs, out_specs, scratch, us=5, deps=()):
    return pl.pallas_call(
        without(kernel, 1 + len(ins), deps),
        out_shape=outs,
        grid_spec=pltpu.PrefetchScalarGridSpec(
            num_scalar_prefetch=1,
            grid=grid,
            in_specs=list(specs) + [ANY] * len(deps),
            out_specs=out_specs,
            scratch_shapes=scratch,
        ),
        compiler_params=pltpu.CompilerParams(vmem_limit_bytes=VLIM),
        cost_estimate=pl.CostEstimate(
            flops=int(us * COST), bytes_accessed=1000, transcendentals=0
        ),
    )(sc, *ins, *deps)


def flat_call(kernel, sc, ins, outs, scratch=(), us=3, deps=()):
    return call(
        kernel,
        (1,),
        sc,
        ins,
        [whole(x.shape) for x in ins],
        outs,
        tuple(whole(o.shape) for o in outs),
        list(scratch),
        us,
        deps,
    )


def pass_on(x, deps):
    return pl.pallas_call(
        lambda *refs: None,
        out_shape=sds(x.shape, x.dtype),
        in_specs=[ANY] * (1 + len(deps)),
        out_specs=ANY,
        input_output_aliases={0: 0},
        cost_estimate=pl.CostEstimate(flops=0, bytes_accessed=1000, transcendentals=0),
    )(x, *deps)


def simple_call(kernel, ins, outs, us=3, deps=()):
    return pl.pallas_call(
        without(kernel, len(ins), deps),
        out_shape=outs,
        in_specs=[pl.BlockSpec(memory_space=pltpu.VMEM)] * len(ins) + [ANY] * len(deps),
        compiler_params=pltpu.CompilerParams(vmem_limit_bytes=VLIM),
        cost_estimate=pl.CostEstimate(
            flops=int(us * COST), bytes_accessed=1000, transcendentals=0
        ),
    )(*ins, *deps)


def whole(shape):
    return pl.BlockSpec(shape, lambda i, s: (0,) * len(shape))


def sds(shape, dtype):
    return jax.ShapeDtypeStruct(shape, dtype)


DMA = pltpu.SemaphoreType.DMA


def make_local(n_dp, n_mp):
    extra = n_dp // 8
    masks = [extra, 2 * extra, 4 * extra]
    low_bits = [b for b in (1, 2, 4, 8, 16, 32) if b < extra]
    col_low = [2 * b for b in low_bits]
    col_masks = [2 * extra, 4 * extra]

    def pp(x, dmask, zmask=0):
        perm = [
            (d * n_mp + z, (d ^ dmask) * n_mp + (z ^ zmask))
            for d in range(n_dp)
            for z in range(n_mp)
        ]
        return lax.ppermute(x, ("dp", "mp"), perm)

    def local(patches, segment, keep, pos_y, pos_x, labels, bucket, *state):
        masters = state[0::3]
        (attend_in, attend_out, expand, contract, patch_embed, pos_table, class_head,
         norm_gains, query_gains) = masters
        length = patches.shape[0]
        rows = patch_embed.shape[0]
        nq = length // BQ
        dp = lax.axis_index("dp")
        z = lax.axis_index("mp")
        core = dp % 2
        z1, z0 = z // 2, z % 2
        g = z0 + 2 * core
        me = dp // extra
        mecol = (dp // 2) // extra
        mine = core == z1

        def bit_of(mask):
            return (dp // mask) % 2 == 1

        def swap(flag, x, y, axis):
            return jnp.where(
                flag, jnp.concatenate([y, x], axis=axis), jnp.concatenate([x, y], axis=axis)
            )

        def pick4(parts, index, axis):
            odd, high = index % 2 == 1, index // 2 == 1
            lo = swap(odd, parts[0], parts[1], axis)
            hi = swap(odd, parts[2], parts[3], axis)
            return swap(high, lo, hi, axis)

        patch_w, t_w = pl.pallas_call(
            pack_kernel,
            out_shape=(
                sds((rows, D + SMALL), bf16),
                sds((rows, 2 * D), bf16),
            ),
            in_specs=[pl.BlockSpec(memory_space=pltpu.VMEM)] * 6
            + [pl.BlockSpec(memory_space=pltpu.SMEM)]
            + [pl.BlockSpec(memory_space=pltpu.VMEM)] * 2,
            compiler_params=pltpu.CompilerParams(vmem_limit_bytes=VLIM),
        )(patch_embed, pos_table, norm_gains, query_gains, segment.reshape(-1, 128),
          keep.reshape(-1, 128), bucket, expand, contract.T)
        w_all = lax.all_gather(t_w, ("dp", "mp"), axis=0, tiled=True)
        w_all = w_all.reshape(8, extra, n_mp, rows, 2 * D)
        if extra > 1:
            w_all = w_all.transpose(0, 2, 1, 3, 4)
        w_all = w_all.reshape(8, n_mp, SUB, 2 * D)

        perm_core = [
            (d * n_mp + zz, (d ^ 1) * n_mp + zz)
            for d in range(n_dp)
            for zz in range(n_mp)
            if d % 2 == zz // 2
        ]
        patches_in = lax.ppermute(patches, ("dp", "mp"), perm_core)
        meta = jnp.stack([segment, keep, pos_y, pos_x])
        tag = jnp.concatenate([labels, bucket, jnp.zeros((length - IMG - 1,), jnp.int32)])
        meta = jnp.concatenate([meta, tag[None]], axis=0)
        meta_in = lax.ppermute(meta, ("dp", "mp"), perm_core)
        meta = jnp.where(mine, meta, meta_in)

        def widen(x, low):
            for b in low:
                x = swap(bit_of(b), x, pp(x, b), -2)
            return x

        def across(x):
            one, two = pp(x, masks[1]), pp(x, masks[2])
            return [x, one, two, pp(one, masks[2])]

        def stack(parts, deps):
            high, width = parts[0].shape
            cuts = 1 if width < 2048 else 4
            step = width // cuts
            return pl.pallas_call(
                without(stack_kernel, 4, deps),
                out_shape=sds((4, high, width), bf16),
                grid=(cuts,),
                in_specs=[pl.BlockSpec((high, step), lambda i: (0, i))] * 4 + [ANY] * len(deps),
                out_specs=pl.BlockSpec((4, high, step), lambda i: (0, 0, i)),
                compiler_params=pltpu.CompilerParams(vmem_limit_bytes=VLIM),
                cost_estimate=pl.CostEstimate(flops=int(COST), bytes_accessed=1000, transcendentals=0),
            )(*parts, *deps)

        def direct(x):
            return [x] + [pp(x, m) for m in (masks[1], masks[2], masks[1] | masks[2])]

        def all8(parts, deps=()):
            stacked = stack(parts, deps)
            return parts + [pp(stacked, masks[0])], stacked

        patch_c = direct(widen(patch_w, low_bits))
        in_w, out_w = simple_call(
            pack_rest_kernel,
            [attend_in, attend_out],
            (sds((rows, 576), bf16), sds((rows, OW), bf16)),
            deps=[meta_in],
        )

        perm_a, perm_b, back_b = [], [], []
        for d in range(n_dp):
            for zz in range(n_mp):
                c, a1, a0 = d % 2, zz // 2, zz % 2
                src = d * n_mp + zz
                perm_a.append((src, (d - c + a1) * n_mp + a0 + 2 * c))
                perm_b.append((src, (d - c + a1) * n_mp + a0 + 2 * (1 - c)))
                back_b.append((src, (d - c + 1 - a1) * n_mp + a0 + 2 * c))
        in_a = lax.ppermute(in_w, ("dp", "mp"), perm_a)
        in_b = lax.ppermute(in_w, ("dp", "mp"), perm_b)
        patch_p, _ = all8(patch_c, [patches_in])
        in_own = widen(swap(z1 == 1, in_a, in_b, 0), col_low)
        in_one, in_two = pp(in_own, col_masks[0]), pp(in_own, col_masks[1])
        in_p = [in_own, in_one, in_two, pp(in_own, col_masks[0] | col_masks[1])]
        o_one, o_two = pp(out_w, 0, 1), pp(out_w, 0, 2)
        out_z = [out_w, o_one, o_two, pp(o_two, 0, 1)]

        seg, kp, py, px = meta[0], meta[1], meta[2], meta[3]
        labs = meta[4, :IMG]
        buck = meta[4, IMG]
        kept = (kp == 1) & (seg < IMG)
        ids = jnp.arange(128)[None, :]
        ids64 = ids[:, :64]
        hot_pos = ((py[:, None] == ids) | (px[:, None] + GRID == ids)).astype(bf16)
        match = seg[:, None] == ids64
        qaux = jnp.where((ids64 < IMG) & match, BIG, jnp.where(ids64 == IMG, 1.0, 0.0)).astype(bf16)
        kaux = jnp.where(
            (ids64 < IMG) & match & kept[:, None],
            1.0,
            jnp.where(
                ids64 == IMG,
                -BIG,
                jnp.where(
                    (ids64 > IMG) & (ids64 < IMG + 4),
                    1.0,
                    0.0,
                ),
            ),
        ).astype(bf16)
        vaux = jnp.broadcast_to(jnp.ones((64,), bf16), (TOK, 64))
        first_seg, last_seg = seg[::BQ], jnp.minimum(seg[BQ - 1 :: BQ], IMG - 1)
        lo = jnp.sum((seg[None, :] < first_seg[:, None]).astype(jnp.int32), axis=1) // BQ
        hi = (jnp.sum((seg[None, :] <= last_seg[:, None]).astype(jnp.int32), axis=1) + BQ - 1) // BQ
        blocks = jnp.arange(nq)
        lo, hi = jnp.minimum(lo, blocks), jnp.maximum(hi, blocks + 1)
        free_row = jnp.broadcast_to(jnp.where(kept, 0.0, BIG)[None, :], (8, length))
        sc = jnp.concatenate(
            [
                jnp.stack([me, g, z, mine.astype(jnp.int32), mecol, z1, z1, z1]),
                lo,
                hi,
            ]
        ).astype(jnp.int32)
        own_seg = lax.dynamic_slice_in_dim(seg, g * TOK, TOK, 0)
        own_kp = lax.dynamic_slice_in_dim(kept, g * TOK, TOK, 0)
        mem = (
            (own_seg[:, None] == jnp.arange(IMG)[None, :]) & own_kp[:, None]
        ).astype(bf16)
        valid = jnp.max(
            ((seg[None, :] == jnp.arange(IMG)[:, None]) & kept[None, :]).astype(f32), axis=1
        )
        lab_hot = (labs[:, None] == jnp.arange(CPAD)[None, :]).astype(f32)
        block = jnp.arange(128) // HD
        avg = jnp.where(block[:, None] == block[None, :], 1.0 / HD, 0.0).astype(bf16)
        heads = (jnp.arange(D)[:, None] // HD == ids).astype(bf16)

        nt = length // TOK
        a, x0, gx = call(
            x0_kernel,
            (nt,),
            sc,
            [patches, patches_in, hot_pos] + patch_p,
            [
                pl.BlockSpec((TOK, D), lambda i, s: (jnp.where(s[3] == 1, i, 0), 0)),
                pl.BlockSpec((TOK, D), lambda i, s: (jnp.where(s[3] == 1, 0, i), 0)),
                pl.BlockSpec((TOK, 128), lambda i, s: (i, 0)),
            ]
            + [ANY] * 5,
            (sds((length, D), bf16), sds((TOK, D), f32), sds((16, D), f32)),
            (pl.BlockSpec((TOK, D), lambda i, s: (i, 0)), whole((TOK, D)), whole((16, D))),
            [pltpu.VMEM((D, D + SMALL), bf16), DMA((8,))],
            10,
        )
        qcols = query_gains.shape[1]
        counts = jnp.sum(gx[LANE_COUNT - LANE_GAIN : LANE_COUNT - LANE_GAIN + NB], axis=1)
        image_total = jnp.sum(counts)
        qg = gx[4:6].reshape(2, n_dp, rows)[:, :, :qcols].reshape(2, 1, HD)
        gain = jnp.tile(qg * jnp.array([0.125, 1.0], f32)[:, None, None], (1, NH, 1))
        gain = jnp.pad(gain.reshape(1, QK), ((0, 7), (0, 0)))
        vt = jnp.stack([valid, valid / image_total], axis=1)
        vt = jnp.pad(vt, ((0, 0), (0, 126)))

        row_block = lambda width: pl.BlockSpec((TOK, width), lambda i, s: (i, 0))
        head_block = pl.BlockSpec((NH, TOK, 128), lambda i, s: (0, i, 0))
        qx, kx, vx, xh, inv = call(
            qkv_kernel,
            (nt,),
            sc,
            [a, qaux, kaux, vaux, gain, avg] + in_p,
            [row_block(D), row_block(64), row_block(64), whole((TOK, 64)), whole((8, QK)),
             whole((128, 128))]
            + [ANY] * 4,
            tuple([sds((NH, length, 128), bf16)] * 3 + [sds((length, QK), f32)] * 2),
            tuple([head_block] * 3 + [row_block(QK)] * 2),
            [pltpu.VMEM((D, 576), bf16), DMA((4,))],
            10,
        )
        f_w = flat_call(
            out_kernel, sc, out_z, (sds((rows, 4 * OW), bf16),), us=2, deps=[a]
        )[0]
        f_c = direct(widen(f_w, low_bits))
        per_tok = TOK // BQ
        def attend(rel, us, deps):
            half = nq // 2
            block = lambda i, s: 2 * (s[1] ^ jnp.where(i < 2, rel[0], rel[1])) + i % 2
            return call(
                lambda *refs: attn_kernel(rel, *refs),
                (half,),
                sc,
                [qx, kx, vx, free_row],
                [
                    pl.BlockSpec((NH, BQ, 128), lambda i, s: (0, block(i, s), 0)),
                    whole((NH, length, 128)),
                    whole((NH, length, 128)),
                    whole((8, length)),
                ],
                (
                    sds((TOK, OW), bf16),
                    sds((TOK, OW), bf16),
                    sds((half * BQ, NH * HD), f32),
                    sds((NH, half * BQ, 128), bf16),
                ),
                (
                    pl.BlockSpec((BQ, OW), lambda i, s: (jnp.minimum(i, 1), 0)),
                    pl.BlockSpec((BQ, OW), lambda i, s: (jnp.maximum(i - 2, 0), 0)),
                    pl.BlockSpec((BQ, NH * HD), lambda i, s: (i, 0)),
                    pl.BlockSpec((NH, BQ, 128), lambda i, s: (0, i, 0)),
                ),
                [pltpu.VMEM((NH, BQ, 128), f32)],
                us,
                deps,
            )

        o_3, o_1, of_a, ql_a = attend((3, 1), 11, [f_w])
        f_p, f_stack = all8(f_c, [o_1])
        o_2, o_0, of_b, ql_b = attend((2, 0), 11, [f_stack])
        head_w = simple_call(
            head_pack_kernel, [class_head], sds((rows, CPAD), bf16), deps=[o_0]
        )
        head_c = direct(widen(head_w, low_bits))

        def trade(parts):
            return [parts[0], pp(parts[1], 0, 1), pp(parts[2], 1, 0), pp(parts[3], 1, 1)]

        o_p = trade([o_0, o_1, o_2, o_3])
        tile_spec = pl.BlockSpec((TOK, D), lambda j, s: (0, j))
        x1, b, u, h, x2, ns = call(
            mlp_kernel,
            (4,),
            sc,
            o_p + [x0, gx, mem, heads] + f_p + [w_all],
            [whole((TOK, OW))] * 4
            + [whole((TOK, D)), whole((16, D)), whole((TOK, IMG)), whole((D, 128))]
            + [ANY] * 6,
            (
                sds((TOK, D), f32),
                sds((TOK, D), bf16),
                sds((TOK, HID), f32),
                sds((TOK, HID), bf16),
                sds((TOK, D), f32),
                sds((IMG, D + 128), f32),
            ),
            (whole((TOK, D)), whole((TOK, D)), tile_spec, tile_spec, whole((TOK, D)),
             whole((IMG, D + 128))),
            [
                pltpu.VMEM((D, 4 * OW), bf16),
                pltpu.VMEM((4, 2, D, D), bf16),
                DMA((8,)),
                DMA((4, 2, 8)),
            ],
            18,
        )
        head_p, _ = all8(head_c, [x1])
        ns = ns + pp(ns, 1, 0)
        half_shape = (4, SUB, CPAD // 2)
        pooled, gp, sinv, loss, gh, gh_send = call(
            head_kernel,
            (1,),
            sc,
            [ns, pp(ns, 0, 1), lab_hot, vt, heads] + head_p,
            [whole((IMG, D + 128))] * 2
            + [whole((IMG, CPAD)), whole((IMG, 128)), whole((D, 128))]
            + [ANY] * 5,
            (
                sds((IMG, D), f32),
                sds((IMG, D), f32),
                sds((IMG, 128), f32),
                sds((IMG, 128), f32),
                sds(half_shape, bf16),
                sds(half_shape, bf16),
            ),
            (
                whole((IMG, D)),
                whole((IMG, D)),
                whole((IMG, 128)),
                whole((IMG, 128)),
                whole(half_shape),
                whole(half_shape),
            ),
            [pltpu.VMEM((D, CPAD), bf16), pltpu.VMEM((D, CPAD // 2), f32), DMA((8,))],
            5,
        )

        gu, gr, gm, gmid, *ga_parts, small_b = call(
            back_kernel,
            (4,),
            sc,
            [u, x2, x1, gx, mem, pooled, gp, sinv, heads] + f_p + [w_all],
            [
                tile_spec,
                whole((TOK, D)),
                whole((TOK, D)),
                whole((16, D)),
                whole((TOK, IMG)),
                whole((IMG, D)),
                whole((IMG, D)),
                whole((IMG, 128)),
                whole((D, 128)),
            ]
            + [ANY] * 6,
            (
                sds((TOK, HID), bf16),
                sds((TOK, D), bf16),
                sds((TOK, D), bf16),
                sds((TOK, D), f32),
                sds((TOK, OW), bf16),
                sds((TOK, OW), bf16),
                sds((TOK, OW), bf16),
                sds((TOK, OW), bf16),
                sds((8, D), f32),
            ),
            (
                tile_spec,
                whole((TOK, D)),
                whole((TOK, D)),
                whole((TOK, D)),
                whole((TOK, OW)),
                whole((TOK, OW)),
                whole((TOK, OW)),
                whole((TOK, OW)),
                whole((8, D)),
            ),
            [
                pltpu.VMEM((4, 2, D, D), bf16),
                pltpu.VMEM((D, 4 * OW), bf16),
                pltpu.VMEM((TOK, D), f32),
                pltpu.VMEM((TOK, D), f32),
                DMA((4, 2, 8)),
                DMA((8,)),
            ],
            20,
        )
        do_p = trade(ga_parts)

        if extra == 1:
            gh_one = add(gh[:2], pp(gh[2:], masks[1])).astype(bf16)
        else:
            gh_one = add(gh, pp(gh_send, masks[0])).astype(bf16)

        tile_of = pl.BlockSpec((TOK, D), lambda j, s: (0, j))
        width = 2 * D + OW
        wgrad = call(
            wgrad_kernel,
            (4,),
            sc,
            [gr, h, b, gu, gm] + o_p,
            [whole((TOK, D)), tile_of, whole((TOK, D)), tile_of, whole((TOK, D))]
            + [whole((TOK, OW))] * 4,
            (sds((8, 4, SUB, width), bf16),),
            (pl.BlockSpec((8, 1, SUB, width), lambda j, s: (0, s[2] ^ j, 0, 0)),),
            [pltpu.VMEM((4, TOK, OW), bf16)],
            14,
            deps=[gh_one],
        )[0]
        wgrad = pass_on(wgrad, [do_p[1], do_p[2], do_p[3]])
        if extra > 1:
            wgrad = wgrad.reshape(8, 4, extra, rows, width).transpose(0, 2, 1, 3, 4)
        wgrad = wgrad.reshape(n_dp * 4 * rows, width)
        z_out = lax.psum_scatter(wgrad, "dp", scatter_dimension=0, tiled=True)
        z_out = z_out.reshape(4, rows, width)
        z_got = [pp(z_out[r], 0, r) for r in (1, 2, 3)]

        def low_rows(x, low):
            for b in reversed(low):
                half = x.shape[-2] // 2
                first, second = x[..., :half, :], x[..., half:, :]
                flag = bit_of(b)
                send = jnp.where(flag, first, second)
                stay = jnp.where(flag, second, first)
                x = add(stay, pp(send.astype(bf16), b))
            return x

        def scatter4(stay, low, m1, m2):
            x = add(stay[:2], pp(stay[2:].astype(bf16), m1))
            x = add(x[0].astype(bf16), pp(x[1].astype(bf16), m2))
            return low_rows(x, low)

        def core_sum(stay, send):
            return add(stay, pp(send, masks[0])).astype(bf16)

        def chip_sum(x, first):
            m1, m2 = (masks[1], masks[2]) if first == 2 else (masks[2], masks[1])
            return scatter4(x, low_bits, m1, m2)

        if extra == 1:
            gh_m2 = add(gh_one[0], pp(gh_one[1], masks[2])).astype(bf16)
        else:
            gh_m2 = (0.5 * chip_sum(gh_one, 2)).astype(bf16)

        def halves(pairs, us, deps=()):
            kept, got = pairs[0]
            out = sds((kept.shape[0] // 2,) + kept.shape[1:], bf16)
            return (tuple(flat_call(halve_kernel, sc, [kept, got], (out, out), us=us, deps=deps)),)

        gh = add(gh_m2, pp(gh_m2, 0, 2))
        gh_got = pp(gh, 0, 1)
        half = nq // 2
        grads = call(
            attn_back_kernel,
            (nq + nt,),
            sc,
            [ql_a, ql_b, of_a, of_b] + do_p + [kx, vx, free_row],
            [
                pl.BlockSpec((NH, BQ, 128), lambda i, s: (0, jnp.minimum(i, half - 1), 0)),
                pl.BlockSpec((NH, BQ, 128), lambda i, s: (0, jnp.clip(i - half, 0, half - 1), 0)),
                pl.BlockSpec((BQ, NH * HD), lambda i, s: (jnp.minimum(i, half - 1), 0)),
                pl.BlockSpec((BQ, NH * HD), lambda i, s: (jnp.clip(i - half, 0, half - 1), 0)),
            ]
            + [whole((TOK, OW))] * 4
            + [whole((NH, length, 128)), whole((NH, length, 128)), whole((8, length))],
            (sds((length, 576), f32),),
            (pl.BlockSpec((TOK, 576), lambda i, s: (jnp.maximum(i - nq, 0), 0)),),
            [
                pltpu.VMEM((NH, length, 128), f32),
                pltpu.VMEM((NH, length, 128), f32),
                pltpu.VMEM((NH, length, 128), f32),
                pltpu.VMEM((4, TOK, OW), bf16),
            ],
            35,
        )[0]
        rel_tok = lambda n, s: s[1] ^ jnp.where(n < 2, n + 2, 3 - n)
        tok_block = lambda width: pl.BlockSpec((TOK, width), lambda n, s: (rel_tok(n, s), 0))
        in_shape = (2, D // 4, 576)
        g_send, g_one, g_own, in_keep, in_send, qgrad = call(
            mix_kernel,
            (nt,),
            sc,
            [grads, xh, inv, a, gain, avg] + in_p,
            [tok_block(576), tok_block(QK), tok_block(QK), tok_block(D), whole((8, QK)),
             whole((128, 128))]
            + [ANY] * 4,
            (
                sds((2, TOK, D), bf16),
                sds((TOK, D), bf16),
                sds((TOK, D), bf16),
                sds(in_shape, bf16),
                sds(in_shape, bf16),
                sds((8, QK), f32),
            ),
            (
                pl.BlockSpec((1, TOK, D), lambda n, s: (jnp.minimum(n, 1), 0, 0)),
                whole((TOK, D)),
                whole((TOK, D)),
                whole(in_shape),
                whole(in_shape),
                whole((8, QK)),
            ),
            [pltpu.VMEM((D, 576), f32), pltpu.VMEM((D, 576), bf16), DMA((4,))],
            14,
            deps=[gh_m2],
        )
        g_core = pp(g_send, 1)
        g_z_in = add(g_one, g_core[1]).astype(bf16)
        g_z = pp(g_z_in, 0, 1)

        in_got = pp(in_send, col_masks[0])
        (ik, is_), = halves([(in_keep, in_got)], 2, deps=[g_z_in])
        is_got = pp(is_, col_masks[1])

        if extra == 1:
            in_a, in_b = flat_call(
                in_parts_kernel, sc, [ik[0], is_got[0]], (sds((rows, 576), bf16),) * 2, us=2,
                deps=[is_],
            )
        else:
            both = low_rows(add(ik[0], is_got[0]), col_low).astype(bf16).reshape(2, rows, 576)
            in_a = jnp.where(z1 == 1, both[1], both[0])
            in_b = jnp.where(z1 == 1, both[0], both[1])
        in_parts = in_a
        in_a = lax.ppermute(in_a, ("dp", "mp"), perm_a)
        in_b = lax.ppermute(in_b, ("dp", "mp"), back_b)
        qg_rows = qgrad[0].reshape(2, NH, HD).sum(axis=1) * jnp.array([0.125, 1.0], f32)[:, None]
        qg_rows = jnp.pad(qg_rows, ((0, 6), (0, 0)))
        hot_own = pl.BlockSpec((TOK, 128), lambda i, s: (s[1], 0))
        own_rows = pl.BlockSpec((TOK, D), lambda i, s: (s[1], 0))

        def tail_body(*refs):
            tail_kernel(n_dp, *refs)

        pk, ps = call(
            tail_body,
            (1,),
            sc,
            [g_own, g_core, g_z, gmid, x0, gx, patches, patches_in, hot_pos, small_b, qg_rows],
            [
                whole((TOK, D)),
                pl.BlockSpec((1, TOK, D), lambda i, s: (0, 0, 0)),
                whole((TOK, D)),
                whole((TOK, D)),
                whole((TOK, D)),
                whole((16, D)),
                own_rows,
                own_rows,
                hot_own,
                whole((8, D)),
                whole((8, HD)),
            ],
            (sds((4, SUB, D + SMALL), bf16), sds((4, SUB, D + SMALL), bf16)),
            (whole((4, SUB, D + SMALL)), whole((4, SUB, D + SMALL))),
            [pltpu.VMEM((D, D + SMALL), f32)],
            6,
            deps=[is_],
        )
        (pk1, ps1), = halves([(pk, pp(ps, masks[0]))], 2, deps=[z_out])
        ps1_got = pp(ps1, masks[1])
        (pk2, ps2), = halves([(pk1, ps1_got)], 2, deps=[gh, in_parts])
        ps2_got = pp(ps2, masks[2])
        s_up, s_down, s_out, sq_z = flat_call(
            share_z_kernel,
            sc,
            [z_out] + z_got,
            (
                sds((rows, D), f32),
                sds((rows, D), f32),
                sds((192, rows), f32),
                sds((8, 128), f32),
            ),
            us=3,
            deps=[ps2],
        )
        if extra == 1:
            p_ins = [pk2, ps2_got]
        else:
            total = low_rows(add(pk2[0], ps2_got[0]), low_bits).astype(bf16)[None]
            p_ins = [total, jnp.zeros_like(total)]
        wide = jnp.arange(D + SMALL)
        extra_row = jnp.where((wide == buck + 1) & (g == 0), jnp.sum(loss[:, 0]), 0.0)
        extra_row = jnp.broadcast_to(extra_row[None, :], (8, D + SMALL))
        s_in, s_head, mine_q = flat_call(
            share_kernel,
            sc,
            [sq_z, in_a, in_b, gh, gh_got] + p_ins + [extra_row],
            (
                sds((rows, 576), f32),
                sds((rows, CLASSES), f32),
                sds((rows + 16, D + SMALL), bf16),
            ),
            us=3,
            deps=[sq_z],
        )
        share_patch, stats = flat_call(
            patch_sum_kernel,
            sc,
            [mine_q, pp(mine_q, 0, 1), pp(mine_q, 0, 2), pp(mine_q, 0, 3)],
            (sds((rows, D + SMALL), f32), sds((8, SMALL), f32)),
            us=2,
        )
        stats = stats + pp(stats, 1)
        m = 2
        while m < n_dp:
            stats = (stats + pp(stats, m)) + (pp(stats, 2 * m) + pp(stats, 3 * m))
            m *= 4

        shares = [s_in, s_out, s_up, s_down, share_patch, s_head]
        turned = [x.T if n // 3 == 3 else x for n, x in enumerate(state)]
        news = simple_call(
            update_kernel,
            [stats] + shares + turned,
            tuple([sds((1, 1), f32), sds((1, NB), f32)] + [sds(s.shape, f32) for s in turned]),
            6,
        )
        outs = [x.T if n // 3 == 3 else x for n, x in enumerate(news[2:])]
        return (news[1].reshape(NB), counts, news[0].reshape(())) + tuple(outs)

    return local


def solution(mesh):
    shard = {
        "in": P("dp", "mp"),
        "out": P("mp", "dp"),
        "row": P("dp", None),
        "col": P(None, "dp"),
    }
    kinds = ["in", "out", "in", "out", "row", "col", "row", "col", "col"]
    triples = tuple(shard[k] for k in kinds for _ in range(3))
    in_specs = (P("dp", None),) + (P("dp"),) * 6 + triples
    out_specs = (P(), P(), P()) + triples
    return jax.shard_map(
        make_local(mesh.shape["dp"], mesh.shape["mp"]),
        mesh=mesh,
        in_specs=in_specs,
        out_specs=out_specs,
        check_vma=False,
    )
```

```python
import jax
import jax.numpy as jnp
from jax import lax
from jax.experimental import pallas as pl
from jax.experimental.pallas import tpu as pltpu
from jax.sharding import PartitionSpec as P

D = 768
HD = 64
HID = 3072
CLASSES = 1000
CPAD = 1024
GRID = 32
IMG = 16
NB = 4
STEP = 10
BQ = 256
TOK = 512
NH = 3
QK = 2 * NH * HD
SUB = D // 8
SMALL = 128
OW = 256
LANE_GAIN = 64
LANE_QG = 68
LANE_COUNT = 72

HIGH = lax.Precision.HIGHEST
NORM_EPS = 1e-06
CLIP = 0.1
BETA_ONE = 0.9
BETA_TWO = 0.95
RATE_MATRIX = 0.05
RATE_SMALL = 0.2
DECAY = 0.05
ADAM_EPS = 1e-08
BIG = 128.0

bf16 = jnp.bfloat16
f32 = jnp.float32
VLIM = 56 * 1024 * 1024
COST = 0.001 * 1.15e9

NN = (((1,), (0,)), ((), ()))
NT = (((1,), (1,)), ((), ()))
TN = (((0,), (0,)), ((), ()))


def dot(a, b, dims=NN, precision=None):
    return lax.dot_general(a, b, dims, precision=precision, preferred_element_type=f32)


def norm_stats(values):
    center = values - jnp.mean(values, axis=-1, keepdims=True)
    inv_std = lax.rsqrt(jnp.mean(center * center, axis=-1, keepdims=True) + NORM_EPS)
    return center * inv_std, inv_std


def norm_back(grad_scaled, scaled, inv_std):
    return inv_std * (
        grad_scaled
        - jnp.mean(grad_scaled, axis=-1, keepdims=True)
        - scaled * jnp.mean(grad_scaled * scaled, axis=-1, keepdims=True)
    )


def splits(x, n):
    out = []
    for _ in range(n - 1):
        part = x.astype(bf16)
        out.append(part)
        x = x - part.astype(f32)
    out.append(x.astype(bf16))
    return out


def dot_split(x, exact, n, dims=NN):
    total = None
    for part in splits(x, n):
        term = dot(part, exact, dims)
        total = term if total is None else total + term
    return total


def head_mean(x, ones, n):
    return jnp.concatenate(
        [dot_split(x[:, c : c + 128], ones, n) for c in range(0, QK, 128)], axis=1
    )


def eye(rows, cols, offset=0):
    row = lax.broadcasted_iota(jnp.int32, (rows, cols), 0)
    col = lax.broadcasted_iota(jnp.int32, (rows, cols), 1)
    return (row + offset == col).astype(f32)


def rows_at(index, size):
    return pl.ds(pl.multiple_of(index * size, size), size)


def pack_kernel(w_patch, w_pos, w_gain, w_qg, seg, keep, bucket, w_up, w_down,
                patch_o, t_o):
    rows = w_patch.shape[0]
    patch_o[:, :D] = w_patch[...].astype(bf16)
    low = lambda ref: ref[...].astype(bf16).astype(f32)
    small = dot(low(w_pos), eye(64, SMALL), TN)
    small += dot(low(w_gain), eye(4, SMALL, LANE_GAIN), TN)
    qg = dot(low(w_qg), eye(2, SMALL, LANE_QG), TN)
    small += dot(eye(rows, qg.shape[0]), qg)
    kept = keep[...] == 1
    count = jnp.zeros((1, 1), f32)
    for n in range(IMG):
        held = jnp.where((seg[...] == n) & kept, 1.0, 0.0)
        count += jnp.max(held, keepdims=True)
    row = lax.broadcasted_iota(jnp.int32, (rows, SMALL), 0)
    col = lax.broadcasted_iota(jnp.int32, (rows, SMALL), 1)
    small += jnp.where((row == 0) & (col == LANE_COUNT + bucket[0]), count, 0.0)
    patch_o[:, D:] = small.astype(bf16)

    t_o[:, :D] = w_up[...].astype(bf16)
    t_o[:, D:] = w_down[...].astype(bf16)


def pack_rest_kernel(w_in, w_out, in_o, out_o):
    rows = w_in.shape[0]
    w = w_in[...].astype(bf16)
    parts = [
        w[:, h * 192 + part * HD : h * 192 + part * HD + HD]
        for part in range(3)
        for h in range(NH)
    ]
    in_o[...] = jnp.concatenate(parts, axis=1)
    turned = dot(eye(rows, rows).astype(bf16), w_out[...].astype(bf16), NT)
    out_o[...] = jnp.concatenate([turned, jnp.zeros((rows, OW - 192), f32)], axis=1).astype(bf16)


def ordered(flag, x, y):
    return jnp.where(flag, jnp.concatenate([y, x], axis=1), jnp.concatenate([x, y], axis=1))


def lanes_at(index, width):
    return pl.ds(pl.multiple_of(index * width, width), width)


def out_kernel(sc, o0, o1, o2, o3, out):
    for r, ref in enumerate((o0, o1, o2, o3)):
        out[:, lanes_at(sc[2] ^ r, OW)] = ref[...]


def head_pack_kernel(head, out):
    out[...] = jnp.zeros_like(out)
    out[:, :CLASSES] = head[...].astype(bf16)


def eight(refs):
    return list(refs[:4]) + [refs[4].at[n] for n in range(4)]


REL = [0, 2, 4, 6, 1, 3, 5, 7]


def stack_kernel(a, b, c, d, out):
    for n, ref in enumerate((a, b, c, d)):
        out[n] = ref[...]


def row_copies(refs, me, dst, sems, rel=REL):
    out = []
    for n, ref in enumerate(refs):
        size = ref.shape[0]
        out.append(pltpu.make_async_copy(ref, dst.at[rows_at(me ^ rel[n], size), :], sems.at[n]))
    return out


def columns(refs, lo, width):
    return [ref.at[:, pl.ds(lo, width)] for ref in refs]


def start(copies):
    for copy in copies:
        copy.start()


def wait(copies):
    for copy in copies:
        copy.wait()


def x0_kernel(sc, own, other, hot, *rest):
    refs = eight(rest[:5])
    a_out, x0_out, gx_out, w, sems = rest[5:]
    i = pl.program_id(0)

    @pl.when(i == 0)
    def _():
        copies = row_copies(refs, sc[0], w, sems)
        start(copies)
        wait(copies)
        row = lax.broadcasted_iota(jnp.int32, (16, SMALL), 0)
        col = lax.broadcasted_iota(jnp.int32, (16, SMALL), 1)
        pick = (row + LANE_GAIN == col).astype(f32).astype(bf16)
        gx_out[...] = dot(pick, w[:, D:], NT)

    rows = jnp.where(sc[3] == 1, own[...], other[...])
    x0 = dot(rows, w[:, :D]) + dot(hot[...], w[:, D:], NT)
    scaled, _ = norm_stats(x0)
    a_out[...] = (scaled * gx_out[0:1, :]).astype(bf16)

    @pl.when(i == sc[1])
    def _():
        x0_out[...] = x0


IN_REL = [0, 1, 2, 3]


def qkv_kernel(sc, a, qaux, kaux, vaux, gain, avg, *rest):
    refs = rest[:4]
    qx, kx, vx, xh_out, inv_out, w, sems = rest[4:]
    i = pl.program_id(0)

    @pl.when(i == 0)
    def _():
        copies = row_copies(refs, sc[4], w, sems, IN_REL)
        start(copies)
        wait(copies)

    mixed = dot(a[...], w[...])
    qk = mixed[:, :QK]
    v = mixed[:, QK:].astype(bf16)
    ones = avg[...]
    center = qk - head_mean(qk, ones, 2)
    inv = lax.rsqrt(head_mean(center * center, ones, 2) + NORM_EPS)
    scaled = center * inv
    xh_out[...] = scaled
    inv_out[...] = inv
    low = (scaled * gain[0:1, :]).astype(bf16)
    qa, ka, va = qaux[...], kaux[...], vaux[...]
    for h in range(NH):
        qx[h] = jnp.concatenate([low[:, h * HD : h * HD + HD], qa], axis=1)
        kx[h] = jnp.concatenate([low[:, (NH + h) * HD : (NH + h) * HD + HD], ka], axis=1)
        vx[h] = jnp.concatenate([v[:, h * HD : h * HD + HD], va], axis=1)


def attn_kernel(rel, sc, qx, kx, vx, free, o_first, o_second, o_full, ql, acc):
    step_id = pl.program_id(0)
    i = 2 * (sc[1] ^ jnp.where(step_id < 2, rel[0], rel[1])) + step_id % 2
    acc[...] = jnp.zeros_like(acc)
    lo, hi = sc[8 + i], sc[16 + i]

    def tile(start_row, size):
        ks = pl.ds(pl.multiple_of(start_row, BQ), size)
        row = lax.broadcasted_iota(jnp.int32, (BQ, size), 0)
        col = lax.broadcasted_iota(jnp.int32, (BQ, size), 1)
        own = jnp.where(row + (i * BQ - start_row) == col, free[0:1, ks], 0.0)
        scores = [dot(qx[h], kx[h, ks, :], NT) + own for h in range(NH)]
        probs = [jnp.exp(s).astype(bf16) for s in scores]
        for h in range(NH):
            acc[h] += dot(probs[h], vx[h, ks, :])

    pairs = (hi - lo) // 2

    def step(j, carry):
        tile((lo + 2 * j) * BQ, 2 * BQ)
        return carry

    lax.fori_loop(0, pairs, step, 0)

    @pl.when((hi - lo) % 2 == 1)
    def _():
        tile((hi - 1) * BQ, BQ)

    lane = lax.broadcasted_iota(jnp.int32, (BQ, HD), 1)
    outs = []
    for h in range(NH):
        out = acc[h]
        total = out[:, HD:]
        outs.append(out[:, :HD] / total)
        aux = qx[h][:, HD:].astype(f32)
        for n, part in enumerate(splits(-jnp.log(total), 3)):
            aux = jnp.where(lane == IMG + 1 + n, part.astype(f32), aux)
        ql[h] = jnp.concatenate([qx[h][:, :HD], aux.astype(bf16)], axis=1)
    full = jnp.concatenate(outs, axis=1)
    o_full[...] = full
    low = jnp.concatenate([full, jnp.zeros((BQ, OW - NH * HD), f32)], axis=1).astype(bf16)

    @pl.when(step_id < 2)
    def _():
        o_first[...] = low

    @pl.when(step_id >= 2)
    def _():
        o_second[...] = low


GELU_C = 0.7978845608028654


def gelu_tanh(u):
    return jnp.tanh(GELU_C * (u + 0.044715 * u * u * u))


def mlp_tile(b, w, u_out, h_out):
    u = dot(b, w[0])
    u_out[...] = u
    h = (0.5 * u * (1.0 + gelu_tanh(u))).astype(bf16)
    h_out[...] = h
    return dot(h, w[1], NT)


def tile_copies(w_all, j, dst, sems):
    size = D // 8
    return [
        pltpu.make_async_copy(
            w_all.at[d, j, :, pl.ds(part * D, D)],
            dst.at[part, pl.ds(d * size, size), :],
            sems.at[part, d],
        )
        for part in range(2)
        for d in range(8)
    ]


def mlp_kernel(sc, o0, o1, o2, o3, x0, gx, mem, heads, *rest):
    refs, w_all = eight(rest[:5]), rest[5]
    x1_out, b_out, u_out, h_out, x2, ns_out, w_o, w_t, sem_o, sem_t = rest[6:]
    j = pl.program_id(0)

    @pl.when(j == 0)
    def _():
        first = row_copies(refs, sc[0], w_o, sem_o)
        start(first)
        for t in range(4):
            start(tile_copies(w_all, t, w_t.at[t], sem_t.at[t]))
        wait(first)
        x1 = x0[...]
        for r, ref in enumerate((o0, o1, o2, o3)):
            x1 += dot(ref[...], w_o[:, lanes_at(sc[1] ^ r, OW)], NT)
        x1_out[...] = x1
        b_out[...] = (norm_stats(x1)[0] * gx[1:2, :]).astype(bf16)
        x2[...] = x1

    wait(tile_copies(w_all, j, w_t.at[j], sem_t.at[j]))
    x2[...] += mlp_tile(b_out[...], w_t.at[j], u_out, h_out)

    @pl.when(j == 3)
    def _():
        f = norm_stats(x2[...])[0] * gx[2:3, :]
        ones = heads[...]
        e = jnp.exp(dot_split(f * gx[3:4, :], ones, 3) * 0.125)
        eb = dot_split(e, ones, 2, NT)
        m = mem[...]
        num = jnp.zeros((IMG, D), f32)
        for part in splits(eb * f, 3):
            num += dot(m, part, TN)
        den = jnp.zeros((IMG, 128), f32)
        for part in splits(e, 3):
            den += dot(m, part, TN)
        ns_out[:, :D] = num
        ns_out[:, D:] = den


def head_kernel(sc, ns_a, ns_b, lab, vt, heads, *rest):
    pooled_out, gp_out, sinv_out, loss_out, gh_out, gh_send, w, gw, sems = rest[5:]
    copies = row_copies(eight(rest[:5]), sc[0], w, sems)
    start(copies)
    ns = ns_a[...] + ns_b[...]
    valid = vt[:, 0:1]
    scale = vt[:, 1:2]
    total = jnp.where(valid > 0.0, ns[:, D:], 1.0)
    sinv = jnp.where(valid > 0.0, 1.0 / total, 0.0)
    lane = lax.broadcasted_iota(jnp.int32, (IMG, 128), 1)
    sinv = jnp.where(lane < D // HD, sinv, 0.0)
    pooled = ns[:, :D] * dot_split(sinv, heads[...], 3, NT)
    low = pooled.astype(bf16)
    wait(copies)
    logits = dot(low, w[...])
    cls = lax.broadcasted_iota(jnp.int32, (IMG, CPAD), 1)
    real = (cls < CLASSES).astype(f32)
    hot = lab[...]
    ex = jnp.exp(-jnp.abs(logits))
    soft = jnp.maximum(logits, 0.0) + jnp.log1p(ex)
    per = jnp.sum(soft * real, axis=1, keepdims=True) - jnp.sum(
        logits * hot, axis=1, keepdims=True
    )
    loss_out[...] = jnp.broadcast_to(per * valid, (IMG, 128))
    sig = jnp.where(logits >= 0.0, 1.0, ex) / (1.0 + ex)
    gl = (scale * (sig * real - hot)).astype(bf16)
    pooled_out[...] = pooled
    sinv_out[...] = sinv
    gp_out[...] = dot(gl, w[...], NT)
    half = jnp.where(sc[2] % 2 == 1, gl[:, 512:].astype(f32), gl[:, :512].astype(f32))
    gw[...] = dot(low, half.astype(bf16), TN)
    for p, r in enumerate(rel_order(2)):
        gh_out[p] = gw[rows_at(sc[0] ^ r, SUB), :].astype(bf16)
        gh_send[p] = gw[rows_at(sc[0] ^ (r + 1), SUB), :].astype(bf16)


def rel_order(first):
    m1, m2 = (2, 4) if first == 2 else (4, 2)
    return [(p >> 1) * m1 + (p & 1) * m2 for p in range(4)]


def back_kernel(sc, u, x2, x1, gx, mem, pooled, gp, sinv, heads, *rest):
    refs, w_all = eight(rest[:5]), rest[5]
    gu_out, gr_out, gm_out, gmid_out = rest[6:10]
    ga_out, small_out = rest[10:14], rest[14]
    w_t, w_o, grs, acc, sem_t, sem_o = rest[15:]
    j = pl.program_id(0)

    def out_rows():
        return row_copies(refs, sc[0], w_o, sem_o)

    @pl.when(j == 0)
    def _():
        for t in range(4):
            start(tile_copies(w_all, t, w_t.at[t], sem_t.at[t]))
        start(out_rows())
        scaled, inv = norm_stats(x2[...])
        f = scaled * gx[2:3, :]
        probe = gx[3:4, :]
        ones = heads[...]
        e = jnp.exp(dot_split(f * probe, ones, 3) * 0.125)
        m = mem[...]
        m3 = jnp.concatenate([m, m, m], axis=1)

        def spread(x):
            return dot(m3, jnp.concatenate(splits(x, 3), axis=0))

        gt = spread(gp[...])
        at = e * spread(sinv[...])
        gpp = dot_split(gp[...] * pooled[...], ones, 3)
        da = dot_split(gt * f, ones, 2)
        dc = at * (da - spread(gpp))
        dcb = dot_split(dc, ones, 2, NT) * 0.125
        df = dot_split(at, ones, 2, NT) * gt + dcb * probe
        gr = norm_back(df * gx[2:3, :], scaled, inv)
        grs[...] = gr
        gr_out[...] = gr.astype(bf16)
        small_out[2:3, :] = jnp.sum(df * scaled, axis=0, keepdims=True)
        small_out[3:4, :] = jnp.sum(dcb * f, axis=0, keepdims=True)
        small_out[0:1, :] = jnp.zeros((1, D), f32)
        small_out[4:8, :] = jnp.zeros((4, D), f32)
        acc[...] = jnp.zeros_like(acc)

    wait(tile_copies(w_all, j, w_t.at[j], sem_t.at[j]))
    gh = dot(gr_out[...], w_t[j, 1])
    v = u[...]
    t = gelu_tanh(v)
    slope = 0.5 * (1.0 + t) + 0.5 * v * (1.0 - t * t) * GELU_C * (1.0 + 0.134145 * v * v)
    gu = (gh * slope).astype(bf16)
    gu_out[...] = gu
    acc[...] += dot(gu, w_t[j, 0], NT)

    @pl.when(j == 3)
    def _():
        wait(out_rows())
        scaled, inv = norm_stats(x1[...])
        gb = acc[...]
        small_out[1:2, :] = jnp.sum(gb * scaled, axis=0, keepdims=True)
        gmid = grs[...] + norm_back(gb * gx[1:2, :], scaled, inv)
        gmid_out[...] = gmid
        low = gmid.astype(bf16)
        gm_out[...] = low
        for r in range(4):
            ga_out[r][...] = dot(low, w_o[:, lanes_at(sc[1] ^ r, OW)]).astype(bf16)


def wgrad_kernel(sc, gr, h, b, gu, gm, o0, o1, o2, o3, out, os):
    j = pl.program_id(0)

    @pl.when(j == 0)
    def _():
        for r, ref in enumerate((o0, o1, o2, o3)):
            os[r] = ref[...]

    parts = [
        (0, dot(b[...], gu[...], TN)),
        (D, dot(gr[...], h[...], TN)),
        (2 * D, dot(gm[...], os[sc[1] ^ j], TN)),
    ]
    for lo, value in parts:
        width = value.shape[1]
        for d in range(8):
            out[d, 0, :, lo : lo + width] = value[d * SUB : (d + 1) * SUB, :].astype(bf16)


def attn_back_kernel(sc, ql_a, ql_b, of_a, of_b, d0, d1, d2, d3, kx, vx, free, g_out, dq, dk, dv, dos):
    i = pl.program_id(0)
    nq = dk.shape[1] // BQ

    @pl.when(i == 0)
    def _():
        for n, ref in enumerate((d3, d1, d2, d0)):
            dos[n] = ref[...]

    @pl.when(i == 0)
    def _():
        dk[...] = jnp.zeros_like(dk)
        dv[...] = jnp.zeros_like(dv)

    @pl.when(i < nq)
    def _():
        n = i // 2
        block = 2 * (sc[1] ^ jnp.where(n < 2, 3 - 2 * n, 6 - 2 * n)) + i % 2
        mine = rows_at(block, BQ)
        lane = lax.broadcasted_iota(jnp.int32, (BQ, HD), 1)
        first = i < nq // 2
        of = jnp.where(first, of_a[...], of_b[...])
        do = dos[n, rows_at(i % 2, BQ), :].astype(f32)
        width = NH * HD
        head_r = lax.broadcasted_iota(jnp.int32, (width, width), 0) // HD
        head_c = lax.broadcasted_iota(jnp.int32, (width, width), 1) // HD
        same_head = (head_r == head_c).astype(f32).astype(bf16)
        deltas = dot_split(do[:, :width] * of, same_head, 3)
        dob, qb = [], []
        for h in range(NH):
            dof = do[:, h * HD : h * HD + HD]
            delta = deltas[:, h * HD : h * HD + HD]
            aux = jnp.zeros((BQ, HD), f32)
            for m, part in enumerate(splits(-delta, 3)):
                aux = jnp.where(lane == m, part.astype(f32), aux)
            dob.append(jnp.concatenate([dof, aux], axis=1).astype(bf16))
            q = jnp.where(first, ql_a[h].astype(f32), ql_b[h].astype(f32))
            qb.append(q.astype(bf16))
            dq[h, mine, :] = jnp.zeros((BQ, 128), f32)
        own_free = free[0:1, pl.ds(pl.multiple_of(block * BQ, BQ), BQ)]

        def tile(start_row, size):
            ks = pl.ds(pl.multiple_of(start_row, BQ), size)
            row = lax.broadcasted_iota(jnp.int32, (size, BQ), 0)
            col = lax.broadcasted_iota(jnp.int32, (size, BQ), 1)
            own = jnp.where(row + (start_row - block * BQ) == col, own_free, 0.0)
            pts = [jnp.exp(dot(kx[h, ks, :], qb[h], NT) + own) for h in range(NH)]
            dpts = [dot(vx[h, ks, :], dob[h], NT) for h in range(NH)]
            dsts = [(pts[h] * dpts[h]).astype(bf16) for h in range(NH)]
            for h in range(NH):
                dv[h, ks, :] += dot(pts[h].astype(bf16), dob[h])
                dk[h, ks, :] += dot(dsts[h], qb[h])
                dq[h, mine, :] += dot(dsts[h], kx[h, ks, :], TN)

        lo, hi = sc[8 + block], sc[16 + block]

        def step(j, carry):
            tile((lo + 2 * j) * BQ, 2 * BQ)
            return carry

        lax.fori_loop(0, (hi - lo) // 2, step, 0)

        @pl.when((hi - lo) % 2 == 1)
        def _():
            tile((hi - 1) * BQ, BQ)

    @pl.when(i >= nq)
    def _():
        rows = rows_at(i - nq, TOK)
        g_out[...] = jnp.concatenate(
            [ref[h, rows, :][:, :HD] for ref in (dq, dk, dv) for h in range(NH)], axis=1
        )


def mix_kernel(sc, grad, xh, inv, a, gain, avg, *rest):
    refs = rest[:4]
    g_send, g_one, g_own, in_keep, in_send, qg_out, gin, w, sems = rest[4:]
    n = pl.program_id(0)

    @pl.when(n == 0)
    def _():
        copies = row_copies(refs, sc[4], w, sems, IN_REL)
        start(copies)
        gin[...] = jnp.zeros_like(gin)
        qg_out[...] = jnp.zeros_like(qg_out)
        wait(copies)

    grads = grad[:, :QK]
    scaled = xh[...]
    ones = avg[...]
    qg_out[0:1, :] += jnp.sum(grads * scaled, axis=0, keepdims=True)
    dg = grads * gain[0:1, :]
    back = inv[...] * (
        dg - head_mean(dg, ones, 1) - scaled * head_mean(dg * scaled, ones, 1)
    )
    mix = jnp.concatenate([back, grad[:, QK:]], axis=1).astype(bf16)
    out = dot(mix, w[...], NT).astype(bf16)
    gin[...] += dot(a[...], mix, TN)

    @pl.when(n < 2)
    def _():
        g_send[0] = out

    @pl.when(n == 2)
    def _():
        g_one[...] = out

    @pl.when(n == 3)
    def _():
        g_own[...] = out
        size = D // 4
        for p in range(2):
            in_keep[p] = gin[rows_at(sc[4] ^ (2 * p), size), :].astype(bf16)
            in_send[p] = gin[rows_at(sc[4] ^ (2 * p + 1), size), :].astype(bf16)


def add(x, y):
    return x.astype(f32) + y.astype(f32)


def halve_kernel(sc, kept, got, keep_o, send_o):
    half = keep_o.shape[0]
    for n in range(half):
        keep_o[n] = add(kept[n], got[n]).astype(bf16)
        send_o[n] = add(kept[half + n], got[half + n]).astype(bf16)


def in_parts_kernel(sc, kept, got, a_out, b_out):
    half = a_out.shape[0]
    first = sc[5]
    mine, other = rows_at(first, half), rows_at(1 - first, half)
    a_out[...] = add(kept[mine, :], got[mine, :]).astype(bf16)
    b_out[...] = add(kept[other, :], got[other, :]).astype(bf16)


def share_z_kernel(sc, z0, z1, z2, z3, up_o, down_o, out_o, sq_o):
    rows = up_o.shape[0]
    total = add(z0[0], z1[...]) + add(z2[...], z3[...])
    up_o[...] = total[:, :D]
    down_o[...] = total[:, D : 2 * D]
    out_o[...] = dot(total[:, 2 * D :], eye(rows, rows), TN, HIGH)[:192, :]
    sq_o[...] = jnp.broadcast_to(jnp.sum(total * total, keepdims=True), sq_o.shape)


def share_kernel(sc, sq_z, in_a, in_b, h_own, h_got, kept, got, extra_row, in_o, head_o, row_o):
    rows = kept.shape[1]
    grad = add(in_a[...], in_b[...])
    in_o[...] = jnp.concatenate(
        [
            grad[:, part * NH * HD + h * HD : part * NH * HD + h * HD + HD]
            for h in range(NH)
            for part in range(3)
        ],
        axis=1,
    )
    head = ordered(sc[2] % 2 == 1, h_own[...], h_got[...])
    head_o[...] = head[:, :CLASSES]
    squares = jnp.sum(grad * grad, keepdims=True)
    once = jnp.where(sc[2] == 0, 1.0, 0.0)
    squares += once * jnp.sum(head * head, keepdims=True)
    row_o[:rows, :] = add(kept[0], got[0]).astype(bf16)
    lane = lax.broadcasted_iota(jnp.int32, (16, D + SMALL), 1)
    row = lax.broadcasted_iota(jnp.int32, (16, D + SMALL), 0)
    value = jnp.where(lane == 0, sq_z[0:1, 0:1] + squares, extra_row[0:1, :])
    tail = jnp.zeros((16, D + SMALL), f32)
    for n, part in enumerate(splits(value, 3)):
        tail = jnp.where(row == n, part.astype(f32), tail)
    row_o[rows:, :] = tail.astype(bf16)


def patch_sum_kernel(sc, own, q1, q2, q3, share_o, stats_o):
    rows = share_o.shape[0]
    total = add(own[...], q1[...]) + add(q2[...], q3[...])
    patch = total[:rows, :]
    share_o[...] = patch
    sums = total[rows : rows + 1, :SMALL] + total[rows + 1 : rows + 2, :SMALL]
    sums += total[rows + 2 : rows + 3, :SMALL]
    lane = lax.broadcasted_iota(jnp.int32, (8, SMALL), 1)
    squares = jnp.sum(patch * patch, keepdims=True)
    stats_o[...] = sums + jnp.where(lane == 0, squares, 0.0)


def tail_kernel(n_dp, sc, g_own, g_core, g_z, gmid, x0, gx, own, other, hot, small_b, qgrad,
                pk, ps, tile):
    grad = g_own[...].astype(f32) + g_core[0].astype(f32) + g_z[...].astype(f32)
    scaled, inv = norm_stats(x0[...])
    gain_a = jnp.sum(grad * scaled, axis=0, keepdims=True)
    ge = (gmid[...] + norm_back(grad * gx[0:1, :], scaled, inv)).astype(bf16)
    rows = jnp.where(sc[3] == 1, own[...], other[...])
    tile[:, :D] = dot(rows, ge, TN)
    row8 = lax.broadcasted_iota(jnp.int32, (8, D), 0)
    gains = jnp.where(row8 == 0, gain_a, small_b[...])
    small = dot(ge, hot[...], TN) + dot(gains, eye(8, SMALL, LANE_GAIN), TN)
    part = HD // n_dp
    kk = lax.broadcasted_iota(jnp.int32, (HD, D), 0)
    rr = lax.broadcasted_iota(jnp.int32, (HD, D), 1)
    spot = ((kk // part) * (D // n_dp) + kk % part == rr).astype(f32)
    lane = lax.broadcasted_iota(jnp.int32, (8, SMALL), 1)
    row = lax.broadcasted_iota(jnp.int32, (8, SMALL), 0)
    q_lane = ((lane == LANE_QG + row) & (row < 2)).astype(f32)
    q_cols = dot(qgrad[...], q_lane, TN, HIGH)
    small += dot(spot, q_cols, TN)
    tile[:, D:] = small
    for p, r in enumerate(rel_order(2)):
        pk[p] = tile[rows_at(sc[0] ^ r, SUB), :].astype(bf16)
        ps[p] = tile[rows_at(sc[0] ^ (r + 1), SUB), :].astype(bf16)


def update_kernel(stats, *rest):
    shares = rest[:6]
    state = rest[6:33]
    norm_out, loss_out, outs = rest[33], rest[34], rest[35:]
    total = stats[0:1, :]
    norm = jnp.sqrt(total)
    norm_out[...] = norm[:, 0:1]
    loss_out[...] = total[:, 1 : 1 + NB]
    factor = jnp.minimum(1.0, CLIP / (norm[:, 0:1] + 1e-06))
    s_in, s_out, s_up, s_down, s_patch, s_head = shares
    rows = s_patch.shape[0]
    small = dot(eye(SMALL, SMALL), s_patch[:, D:], NT, HIGH)
    part = state[24].shape[1]
    grads = [
        s_in[...],
        s_out[...],
        s_up[...],
        s_down[...],
        s_patch[:, :D],
        small[: 2 * GRID, :],
        s_head[...],
        small[LANE_GAIN : LANE_GAIN + 4, :],
        small[LANE_QG : LANE_QG + 2, :part],
    ]
    for n in range(9):
        master, first, second = state[3 * n : 3 * n + 3]
        clipped = grads[n] * factor
        first_new = BETA_ONE * first[...] + (1.0 - BETA_ONE) * clipped
        second_new = BETA_TWO * second[...] + (1.0 - BETA_TWO) * clipped * clipped
        matrix = n in (0, 1, 2, 3, 4, 6)
        rate = RATE_MATRIX if matrix else RATE_SMALL
        decay = DECAY if matrix else 0.0
        ratio = (
            first_new
            / (1.0 - BETA_ONE**STEP)
            / (jnp.sqrt(second_new / (1.0 - BETA_TWO**STEP)) + ADAM_EPS)
        )
        value = master[...]
        outs[3 * n][...] = value - rate * (ratio + decay * value)
        outs[3 * n + 1][...] = first_new
        outs[3 * n + 2][...] = second_new


ANY = pl.BlockSpec(memory_space=pl.ANY)


def without(kernel, count, deps):
    if not deps:
        return kernel
    return lambda *refs: kernel(*refs[:count], *refs[count + len(deps) :])


def call(kernel, grid, sc, ins, specs, outs, out_specs, scratch, us=5, deps=()):
    return pl.pallas_call(
        without(kernel, 1 + len(ins), deps),
        out_shape=outs,
        grid_spec=pltpu.PrefetchScalarGridSpec(
            num_scalar_prefetch=1,
            grid=grid,
            in_specs=list(specs) + [ANY] * len(deps),
            out_specs=out_specs,
            scratch_shapes=scratch,
        ),
        compiler_params=pltpu.CompilerParams(vmem_limit_bytes=VLIM),
        cost_estimate=pl.CostEstimate(
            flops=int(us * COST), bytes_accessed=1000, transcendentals=0
        ),
    )(sc, *ins, *deps)


def flat_call(kernel, sc, ins, outs, scratch=(), us=3, deps=()):
    return call(
        kernel,
        (1,),
        sc,
        ins,
        [whole(x.shape) for x in ins],
        outs,
        tuple(whole(o.shape) for o in outs),
        list(scratch),
        us,
        deps,
    )


def pass_on(x, deps):
    return pl.pallas_call(
        lambda *refs: None,
        out_shape=sds(x.shape, x.dtype),
        in_specs=[ANY] * (1 + len(deps)),
        out_specs=ANY,
        input_output_aliases={0: 0},
        cost_estimate=pl.CostEstimate(flops=0, bytes_accessed=1000, transcendentals=0),
    )(x, *deps)


def simple_call(kernel, ins, outs, us=3, deps=()):
    return pl.pallas_call(
        without(kernel, len(ins), deps),
        out_shape=outs,
        in_specs=[pl.BlockSpec(memory_space=pltpu.VMEM)] * len(ins) + [ANY] * len(deps),
        compiler_params=pltpu.CompilerParams(vmem_limit_bytes=VLIM),
        cost_estimate=pl.CostEstimate(
            flops=int(us * COST), bytes_accessed=1000, transcendentals=0
        ),
    )(*ins, *deps)


def whole(shape):
    return pl.BlockSpec(shape, lambda i, s: (0,) * len(shape))


def sds(shape, dtype):
    return jax.ShapeDtypeStruct(shape, dtype)


DMA = pltpu.SemaphoreType.DMA


def make_local(n_dp, n_mp):
    extra = n_dp // 8
    masks = [extra, 2 * extra, 4 * extra]
    low_bits = [b for b in (1, 2, 4, 8, 16, 32) if b < extra]
    col_low = [2 * b for b in low_bits]
    col_masks = [2 * extra, 4 * extra]

    def pp(x, dmask, zmask=0):
        perm = [
            (d * n_mp + z, (d ^ dmask) * n_mp + (z ^ zmask))
            for d in range(n_dp)
            for z in range(n_mp)
        ]
        return lax.ppermute(x, ("dp", "mp"), perm)

    def local(patches, segment, keep, pos_y, pos_x, labels, bucket, *state):
        masters = state[0::3]
        (attend_in, attend_out, expand, contract, patch_embed, pos_table, class_head,
         norm_gains, query_gains) = masters
        length = patches.shape[0]
        rows = patch_embed.shape[0]
        nq = length // BQ
        dp = lax.axis_index("dp")
        z = lax.axis_index("mp")
        core = dp % 2
        z1, z0 = z // 2, z % 2
        g = z0 + 2 * core
        me = dp // extra
        mecol = (dp // 2) // extra
        mine = core == z1

        def bit_of(mask):
            return (dp // mask) % 2 == 1

        def swap(flag, x, y, axis):
            return jnp.where(
                flag, jnp.concatenate([y, x], axis=axis), jnp.concatenate([x, y], axis=axis)
            )

        def pick4(parts, index, axis):
            odd, high = index % 2 == 1, index // 2 == 1
            lo = swap(odd, parts[0], parts[1], axis)
            hi = swap(odd, parts[2], parts[3], axis)
            return swap(high, lo, hi, axis)

        patch_w, t_w = pl.pallas_call(
            pack_kernel,
            out_shape=(
                sds((rows, D + SMALL), bf16),
                sds((rows, 2 * D), bf16),
            ),
            in_specs=[pl.BlockSpec(memory_space=pltpu.VMEM)] * 6
            + [pl.BlockSpec(memory_space=pltpu.SMEM)]
            + [pl.BlockSpec(memory_space=pltpu.VMEM)] * 2,
            compiler_params=pltpu.CompilerParams(vmem_limit_bytes=VLIM),
        )(patch_embed, pos_table, norm_gains, query_gains, segment.reshape(-1, 128),
          keep.reshape(-1, 128), bucket, expand, contract.T)
        w_all = lax.all_gather(t_w, ("dp", "mp"), axis=0, tiled=True)
        w_all = w_all.reshape(8, extra, n_mp, rows, 2 * D)
        if extra > 1:
            w_all = w_all.transpose(0, 2, 1, 3, 4)
        w_all = w_all.reshape(8, n_mp, SUB, 2 * D)

        perm_core = [
            (d * n_mp + zz, (d ^ 1) * n_mp + zz)
            for d in range(n_dp)
            for zz in range(n_mp)
            if d % 2 == zz // 2
        ]
        patches_in = lax.ppermute(patches, ("dp", "mp"), perm_core)
        meta = jnp.stack([segment, keep, pos_y, pos_x])
        tag = jnp.concatenate([labels, bucket, jnp.zeros((length - IMG - 1,), jnp.int32)])
        meta = jnp.concatenate([meta, tag[None]], axis=0)
        meta_in = lax.ppermute(meta, ("dp", "mp"), perm_core)
        meta = jnp.where(mine, meta, meta_in)

        def widen(x, low):
            for b in low:
                x = swap(bit_of(b), x, pp(x, b), -2)
            return x

        def across(x):
            one, two = pp(x, masks[1]), pp(x, masks[2])
            return [x, one, two, pp(one, masks[2])]

        def stack(parts, deps):
            high, width = parts[0].shape
            cuts = 1 if width < 2048 else 4
            step = width // cuts
            return pl.pallas_call(
                without(stack_kernel, 4, deps),
                out_shape=sds((4, high, width), bf16),
                grid=(cuts,),
                in_specs=[pl.BlockSpec((high, step), lambda i: (0, i))] * 4 + [ANY] * len(deps),
                out_specs=pl.BlockSpec((4, high, step), lambda i: (0, 0, i)),
                compiler_params=pltpu.CompilerParams(vmem_limit_bytes=VLIM),
                cost_estimate=pl.CostEstimate(flops=int(COST), bytes_accessed=1000, transcendentals=0),
            )(*parts, *deps)

        def direct(x):
            return [x] + [pp(x, m) for m in (masks[1], masks[2], masks[1] | masks[2])]

        def all8(parts, deps=()):
            stacked = stack(parts, deps)
            return parts + [pp(stacked, masks[0])], stacked

        patch_c = direct(widen(patch_w, low_bits))
        in_w, out_w = simple_call(
            pack_rest_kernel,
            [attend_in, attend_out],
            (sds((rows, 576), bf16), sds((rows, OW), bf16)),
            deps=[meta_in],
        )

        perm_a, perm_b, back_b = [], [], []
        for d in range(n_dp):
            for zz in range(n_mp):
                c, a1, a0 = d % 2, zz // 2, zz % 2
                src = d * n_mp + zz
                perm_a.append((src, (d - c + a1) * n_mp + a0 + 2 * c))
                perm_b.append((src, (d - c + a1) * n_mp + a0 + 2 * (1 - c)))
                back_b.append((src, (d - c + 1 - a1) * n_mp + a0 + 2 * c))
        in_a = lax.ppermute(in_w, ("dp", "mp"), perm_a)
        in_b = lax.ppermute(in_w, ("dp", "mp"), perm_b)
        patch_p, _ = all8(patch_c, [patches_in])
        in_own = widen(swap(z1 == 1, in_a, in_b, 0), col_low)
        in_one, in_two = pp(in_own, col_masks[0]), pp(in_own, col_masks[1])
        in_p = [in_own, in_one, in_two, pp(in_own, col_masks[0] | col_masks[1])]
        o_one, o_two = pp(out_w, 0, 1), pp(out_w, 0, 2)
        out_z = [out_w, o_one, o_two, pp(o_two, 0, 1)]

        seg, kp, py, px = meta[0], meta[1], meta[2], meta[3]
        labs = meta[4, :IMG]
        buck = meta[4, IMG]
        kept = (kp == 1) & (seg < IMG)
        ids = jnp.arange(128)[None, :]
        ids64 = ids[:, :64]
        hot_pos = ((py[:, None] == ids) | (px[:, None] + GRID == ids)).astype(bf16)
        match = seg[:, None] == ids64
        qaux = jnp.where((ids64 < IMG) & match, BIG, jnp.where(ids64 == IMG, 1.0, 0.0)).astype(bf16)
        kaux = jnp.where(
            (ids64 < IMG) & match & kept[:, None],
            1.0,
            jnp.where(
                ids64 == IMG,
                -BIG,
                jnp.where(
                    (ids64 > IMG) & (ids64 < IMG + 4),
                    1.0,
                    0.0,
                ),
            ),
        ).astype(bf16)
        vaux = jnp.broadcast_to(jnp.ones((64,), bf16), (TOK, 64))
        first_seg, last_seg = seg[::BQ], jnp.minimum(seg[BQ - 1 :: BQ], IMG - 1)
        lo = jnp.sum((seg[None, :] < first_seg[:, None]).astype(jnp.int32), axis=1) // BQ
        hi = (jnp.sum((seg[None, :] <= last_seg[:, None]).astype(jnp.int32), axis=1) + BQ - 1) // BQ
        blocks = jnp.arange(nq)
        lo, hi = jnp.minimum(lo, blocks), jnp.maximum(hi, blocks + 1)
        free_row = jnp.broadcast_to(jnp.where(kept, 0.0, BIG)[None, :], (8, length))
        sc = jnp.concatenate(
            [
                jnp.stack([me, g, z, mine.astype(jnp.int32), mecol, z1, z1, z1]),
                lo,
                hi,
            ]
        ).astype(jnp.int32)
        own_seg = lax.dynamic_slice_in_dim(seg, g * TOK, TOK, 0)
        own_kp = lax.dynamic_slice_in_dim(kept, g * TOK, TOK, 0)
        mem = (
            (own_seg[:, None] == jnp.arange(IMG)[None, :]) & own_kp[:, None]
        ).astype(bf16)
        valid = jnp.max(
            ((seg[None, :] == jnp.arange(IMG)[:, None]) & kept[None, :]).astype(f32), axis=1
        )
        lab_hot = (labs[:, None] == jnp.arange(CPAD)[None, :]).astype(f32)
        block = jnp.arange(128) // HD
        avg = jnp.where(block[:, None] == block[None, :], 1.0 / HD, 0.0).astype(bf16)
        heads = (jnp.arange(D)[:, None] // HD == ids).astype(bf16)

        nt = length // TOK
        a, x0, gx = call(
            x0_kernel,
            (nt,),
            sc,
            [patches, patches_in, hot_pos] + patch_p,
            [
                pl.BlockSpec((TOK, D), lambda i, s: (jnp.where(s[3] == 1, i, 0), 0)),
                pl.BlockSpec((TOK, D), lambda i, s: (jnp.where(s[3] == 1, 0, i), 0)),
                pl.BlockSpec((TOK, 128), lambda i, s: (i, 0)),
            ]
            + [ANY] * 5,
            (sds((length, D), bf16), sds((TOK, D), f32), sds((16, D), f32)),
            (pl.BlockSpec((TOK, D), lambda i, s: (i, 0)), whole((TOK, D)), whole((16, D))),
            [pltpu.VMEM((D, D + SMALL), bf16), DMA((8,))],
            10,
        )
        qcols = query_gains.shape[1]
        counts = jnp.sum(gx[LANE_COUNT - LANE_GAIN : LANE_COUNT - LANE_GAIN + NB], axis=1)
        image_total = jnp.sum(counts)
        qg = gx[4:6].reshape(2, n_dp, rows)[:, :, :qcols].reshape(2, 1, HD)
        gain = jnp.tile(qg * jnp.array([0.125, 1.0], f32)[:, None, None], (1, NH, 1))
        gain = jnp.pad(gain.reshape(1, QK), ((0, 7), (0, 0)))
        vt = jnp.stack([valid, valid / image_total], axis=1)
        vt = jnp.pad(vt, ((0, 0), (0, 126)))

        row_block = lambda width: pl.BlockSpec((TOK, width), lambda i, s: (i, 0))
        head_block = pl.BlockSpec((NH, TOK, 128), lambda i, s: (0, i, 0))
        qx, kx, vx, xh, inv = call(
            qkv_kernel,
            (nt,),
            sc,
            [a, qaux, kaux, vaux, gain, avg] + in_p,
            [row_block(D), row_block(64), row_block(64), whole((TOK, 64)), whole((8, QK)),
             whole((128, 128))]
            + [ANY] * 4,
            tuple([sds((NH, length, 128), bf16)] * 3 + [sds((length, QK), f32)] * 2),
            tuple([head_block] * 3 + [row_block(QK)] * 2),
            [pltpu.VMEM((D, 576), bf16), DMA((4,))],
            10,
        )
        f_w = flat_call(
            out_kernel, sc, out_z, (sds((rows, 4 * OW), bf16),), us=2, deps=[a]
        )[0]
        f_c = direct(widen(f_w, low_bits))
        per_tok = TOK // BQ
        def attend(rel, us, deps):
            half = nq // 2
            block = lambda i, s: 2 * (s[1] ^ jnp.where(i < 2, rel[0], rel[1])) + i % 2
            return call(
                lambda *refs: attn_kernel(rel, *refs),
                (half,),
                sc,
                [qx, kx, vx, free_row],
                [
                    pl.BlockSpec((NH, BQ, 128), lambda i, s: (0, block(i, s), 0)),
                    whole((NH, length, 128)),
                    whole((NH, length, 128)),
                    whole((8, length)),
                ],
                (
                    sds((TOK, OW), bf16),
                    sds((TOK, OW), bf16),
                    sds((half * BQ, NH * HD), f32),
                    sds((NH, half * BQ, 128), bf16),
                ),
                (
                    pl.BlockSpec((BQ, OW), lambda i, s: (jnp.minimum(i, 1), 0)),
                    pl.BlockSpec((BQ, OW), lambda i, s: (jnp.maximum(i - 2, 0), 0)),
                    pl.BlockSpec((BQ, NH * HD), lambda i, s: (i, 0)),
                    pl.BlockSpec((NH, BQ, 128), lambda i, s: (0, i, 0)),
                ),
                [pltpu.VMEM((NH, BQ, 128), f32)],
                us,
                deps,
            )

        o_3, o_1, of_a, ql_a = attend((3, 1), 11, [f_w])
        f_p, f_stack = all8(f_c, [o_1])
        o_2, o_0, of_b, ql_b = attend((2, 0), 11, [f_stack])
        head_w = simple_call(
            head_pack_kernel, [class_head], sds((rows, CPAD), bf16), deps=[o_0]
        )
        head_c = direct(widen(head_w, low_bits))

        def trade(parts):
            return [parts[0], pp(parts[1], 0, 1), pp(parts[2], 1, 0), pp(parts[3], 1, 1)]

        o_p = trade([o_0, o_1, o_2, o_3])
        tile_spec = pl.BlockSpec((TOK, D), lambda j, s: (0, j))
        x1, b, u, h, x2, ns = call(
            mlp_kernel,
            (4,),
            sc,
            o_p + [x0, gx, mem, heads] + f_p + [w_all],
            [whole((TOK, OW))] * 4
            + [whole((TOK, D)), whole((16, D)), whole((TOK, IMG)), whole((D, 128))]
            + [ANY] * 6,
            (
                sds((TOK, D), f32),
                sds((TOK, D), bf16),
                sds((TOK, HID), f32),
                sds((TOK, HID), bf16),
                sds((TOK, D), f32),
                sds((IMG, D + 128), f32),
            ),
            (whole((TOK, D)), whole((TOK, D)), tile_spec, tile_spec, whole((TOK, D)),
             whole((IMG, D + 128))),
            [
                pltpu.VMEM((D, 4 * OW), bf16),
                pltpu.VMEM((4, 2, D, D), bf16),
                DMA((8,)),
                DMA((4, 2, 8)),
            ],
            18,
        )
        head_p, _ = all8(head_c, [x1])
        ns = ns + pp(ns, 1, 0)
        half_shape = (4, SUB, CPAD // 2)
        pooled, gp, sinv, loss, gh, gh_send = call(
            head_kernel,
            (1,),
            sc,
            [ns, pp(ns, 0, 1), lab_hot, vt, heads] + head_p,
            [whole((IMG, D + 128))] * 2
            + [whole((IMG, CPAD)), whole((IMG, 128)), whole((D, 128))]
            + [ANY] * 5,
            (
                sds((IMG, D), f32),
                sds((IMG, D), f32),
                sds((IMG, 128), f32),
                sds((IMG, 128), f32),
                sds(half_shape, bf16),
                sds(half_shape, bf16),
            ),
            (
                whole((IMG, D)),
                whole((IMG, D)),
                whole((IMG, 128)),
                whole((IMG, 128)),
                whole(half_shape),
                whole(half_shape),
            ),
            [pltpu.VMEM((D, CPAD), bf16), pltpu.VMEM((D, CPAD // 2), f32), DMA((8,))],
            5,
        )

        gu, gr, gm, gmid, *ga_parts, small_b = call(
            back_kernel,
            (4,),
            sc,
            [u, x2, x1, gx, mem, pooled, gp, sinv, heads] + f_p + [w_all],
            [
                tile_spec,
                whole((TOK, D)),
                whole((TOK, D)),
                whole((16, D)),
                whole((TOK, IMG)),
                whole((IMG, D)),
                whole((IMG, D)),
                whole((IMG, 128)),
                whole((D, 128)),
            ]
            + [ANY] * 6,
            (
                sds((TOK, HID), bf16),
                sds((TOK, D), bf16),
                sds((TOK, D), bf16),
                sds((TOK, D), f32),
                sds((TOK, OW), bf16),
                sds((TOK, OW), bf16),
                sds((TOK, OW), bf16),
                sds((TOK, OW), bf16),
                sds((8, D), f32),
            ),
            (
                tile_spec,
                whole((TOK, D)),
                whole((TOK, D)),
                whole((TOK, D)),
                whole((TOK, OW)),
                whole((TOK, OW)),
                whole((TOK, OW)),
                whole((TOK, OW)),
                whole((8, D)),
            ),
            [
                pltpu.VMEM((4, 2, D, D), bf16),
                pltpu.VMEM((D, 4 * OW), bf16),
                pltpu.VMEM((TOK, D), f32),
                pltpu.VMEM((TOK, D), f32),
                DMA((4, 2, 8)),
                DMA((8,)),
            ],
            20,
        )
        do_p = trade(ga_parts)

        if extra == 1:
            gh_one = add(gh[:2], pp(gh[2:], masks[1])).astype(bf16)
        else:
            gh_one = add(gh, pp(gh_send, masks[0])).astype(bf16)

        tile_of = pl.BlockSpec((TOK, D), lambda j, s: (0, j))
        width = 2 * D + OW
        wgrad = call(
            wgrad_kernel,
            (4,),
            sc,
            [gr, h, b, gu, gm] + o_p,
            [whole((TOK, D)), tile_of, whole((TOK, D)), tile_of, whole((TOK, D))]
            + [whole((TOK, OW))] * 4,
            (sds((8, 4, SUB, width), bf16),),
            (pl.BlockSpec((8, 1, SUB, width), lambda j, s: (0, s[2] ^ j, 0, 0)),),
            [pltpu.VMEM((4, TOK, OW), bf16)],
            14,
            deps=[gh_one],
        )[0]
        wgrad = pass_on(wgrad, [do_p[1], do_p[2], do_p[3]])
        if extra > 1:
            wgrad = wgrad.reshape(8, 4, extra, rows, width).transpose(0, 2, 1, 3, 4)
        wgrad = wgrad.reshape(n_dp * 4 * rows, width)
        z_out = lax.psum_scatter(wgrad, "dp", scatter_dimension=0, tiled=True)
        z_out = z_out.reshape(4, rows, width)
        z_got = [pp(z_out[r], 0, r) for r in (1, 2, 3)]

        def low_rows(x, low):
            for b in reversed(low):
                half = x.shape[-2] // 2
                first, second = x[..., :half, :], x[..., half:, :]
                flag = bit_of(b)
                send = jnp.where(flag, first, second)
                stay = jnp.where(flag, second, first)
                x = add(stay, pp(send.astype(bf16), b))
            return x

        def scatter4(stay, low, m1, m2):
            x = add(stay[:2], pp(stay[2:].astype(bf16), m1))
            x = add(x[0].astype(bf16), pp(x[1].astype(bf16), m2))
            return low_rows(x, low)

        def core_sum(stay, send):
            return add(stay, pp(send, masks[0])).astype(bf16)

        def chip_sum(x, first):
            m1, m2 = (masks[1], masks[2]) if first == 2 else (masks[2], masks[1])
            return scatter4(x, low_bits, m1, m2)

        if extra == 1:
            gh_m2 = add(gh_one[0], pp(gh_one[1], masks[2])).astype(bf16)
        else:
            gh_m2 = (0.5 * chip_sum(gh_one, 2)).astype(bf16)

        def halves(pairs, us, deps=()):
            kept, got = pairs[0]
            out = sds((kept.shape[0] // 2,) + kept.shape[1:], bf16)
            return (tuple(flat_call(halve_kernel, sc, [kept, got], (out, out), us=us, deps=deps)),)

        gh = add(gh_m2, pp(gh_m2, 0, 2))
        gh_got = pp(gh, 0, 1)
        half = nq // 2
        grads = call(
            attn_back_kernel,
            (nq + nt,),
            sc,
            [ql_a, ql_b, of_a, of_b] + do_p + [kx, vx, free_row],
            [
                pl.BlockSpec((NH, BQ, 128), lambda i, s: (0, jnp.minimum(i, half - 1), 0)),
                pl.BlockSpec((NH, BQ, 128), lambda i, s: (0, jnp.clip(i - half, 0, half - 1), 0)),
                pl.BlockSpec((BQ, NH * HD), lambda i, s: (jnp.minimum(i, half - 1), 0)),
                pl.BlockSpec((BQ, NH * HD), lambda i, s: (jnp.clip(i - half, 0, half - 1), 0)),
            ]
            + [whole((TOK, OW))] * 4
            + [whole((NH, length, 128)), whole((NH, length, 128)), whole((8, length))],
            (sds((length, 576), f32),),
            (pl.BlockSpec((TOK, 576), lambda i, s: (jnp.maximum(i - nq, 0), 0)),),
            [
                pltpu.VMEM((NH, length, 128), f32),
                pltpu.VMEM((NH, length, 128), f32),
                pltpu.VMEM((NH, length, 128), f32),
                pltpu.VMEM((4, TOK, OW), bf16),
            ],
            35,
        )[0]
        rel_tok = lambda n, s: s[1] ^ jnp.where(n < 2, n + 2, 3 - n)
        tok_block = lambda width: pl.BlockSpec((TOK, width), lambda n, s: (rel_tok(n, s), 0))
        in_shape = (2, D // 4, 576)
        g_send, g_one, g_own, in_keep, in_send, qgrad = call(
            mix_kernel,
            (nt,),
            sc,
            [grads, xh, inv, a, gain, avg] + in_p,
            [tok_block(576), tok_block(QK), tok_block(QK), tok_block(D), whole((8, QK)),
             whole((128, 128))]
            + [ANY] * 4,
            (
                sds((2, TOK, D), bf16),
                sds((TOK, D), bf16),
                sds((TOK, D), bf16),
                sds(in_shape, bf16),
                sds(in_shape, bf16),
                sds((8, QK), f32),
            ),
            (
                pl.BlockSpec((1, TOK, D), lambda n, s: (jnp.minimum(n, 1), 0, 0)),
                whole((TOK, D)),
                whole((TOK, D)),
                whole(in_shape),
                whole(in_shape),
                whole((8, QK)),
            ),
            [pltpu.VMEM((D, 576), f32), pltpu.VMEM((D, 576), bf16), DMA((4,))],
            14,
            deps=[gh_m2],
        )
        g_core = pp(g_send, 1)
        g_z_in = add(g_one, g_core[1]).astype(bf16)
        g_z = pp(g_z_in, 0, 1)

        in_got = pp(in_send, col_masks[0])
        (ik, is_), = halves([(in_keep, in_got)], 2, deps=[g_z_in])
        is_got = pp(is_, col_masks[1])

        if extra == 1:
            in_a, in_b = flat_call(
                in_parts_kernel, sc, [ik[0], is_got[0]], (sds((rows, 576), bf16),) * 2, us=2,
                deps=[is_],
            )
        else:
            both = low_rows(add(ik[0], is_got[0]), col_low).astype(bf16).reshape(2, rows, 576)
            in_a = jnp.where(z1 == 1, both[1], both[0])
            in_b = jnp.where(z1 == 1, both[0], both[1])
        in_parts = in_a
        in_a = lax.ppermute(in_a, ("dp", "mp"), perm_a)
        in_b = lax.ppermute(in_b, ("dp", "mp"), back_b)
        qg_rows = qgrad[0].reshape(2, NH, HD).sum(axis=1) * jnp.array([0.125, 1.0], f32)[:, None]
        qg_rows = jnp.pad(qg_rows, ((0, 6), (0, 0)))
        hot_own = pl.BlockSpec((TOK, 128), lambda i, s: (s[1], 0))
        own_rows = pl.BlockSpec((TOK, D), lambda i, s: (s[1], 0))

        def tail_body(*refs):
            tail_kernel(n_dp, *refs)

        pk, ps = call(
            tail_body,
            (1,),
            sc,
            [g_own, g_core, g_z, gmid, x0, gx, patches, patches_in, hot_pos, small_b, qg_rows],
            [
                whole((TOK, D)),
                pl.BlockSpec((1, TOK, D), lambda i, s: (0, 0, 0)),
                whole((TOK, D)),
                whole((TOK, D)),
                whole((TOK, D)),
                whole((16, D)),
                own_rows,
                own_rows,
                hot_own,
                whole((8, D)),
                whole((8, HD)),
            ],
            (sds((4, SUB, D + SMALL), bf16), sds((4, SUB, D + SMALL), bf16)),
            (whole((4, SUB, D + SMALL)), whole((4, SUB, D + SMALL))),
            [pltpu.VMEM((D, D + SMALL), f32)],
            6,
            deps=[is_],
        )
        (pk1, ps1), = halves([(pk, pp(ps, masks[0]))], 2, deps=[z_out])
        ps1_got = pp(ps1, masks[1])
        (pk2, ps2), = halves([(pk1, ps1_got)], 2, deps=[gh, in_parts])
        ps2_got = pp(ps2, masks[2])
        s_up, s_down, s_out, sq_z = flat_call(
            share_z_kernel,
            sc,
            [z_out] + z_got,
            (
                sds((rows, D), f32),
                sds((rows, D), f32),
                sds((192, rows), f32),
                sds((8, 128), f32),
            ),
            us=3,
            deps=[ps2],
        )
        if extra == 1:
            p_ins = [pk2, ps2_got]
        else:
            total = low_rows(add(pk2[0], ps2_got[0]), low_bits).astype(bf16)[None]
            p_ins = [total, jnp.zeros_like(total)]
        wide = jnp.arange(D + SMALL)
        extra_row = jnp.where((wide == buck + 1) & (g == 0), jnp.sum(loss[:, 0]), 0.0)
        extra_row = jnp.broadcast_to(extra_row[None, :], (8, D + SMALL))
        s_in, s_head, mine_q = flat_call(
            share_kernel,
            sc,
            [sq_z, in_a, in_b, gh, gh_got] + p_ins + [extra_row],
            (
                sds((rows, 576), f32),
                sds((rows, CLASSES), f32),
                sds((rows + 16, D + SMALL), bf16),
            ),
            us=3,
            deps=[sq_z],
        )
        share_patch, stats = flat_call(
            patch_sum_kernel,
            sc,
            [mine_q, pp(mine_q, 0, 1), pp(mine_q, 0, 2), pp(mine_q, 0, 3)],
            (sds((rows, D + SMALL), f32), sds((8, SMALL), f32)),
            us=2,
        )
        stats = stats + pp(stats, 1)
        m = 2
        while m < n_dp:
            stats = (stats + pp(stats, m)) + (pp(stats, 2 * m) + pp(stats, 3 * m))
            m *= 4

        shares = [s_in, s_out, s_up, s_down, share_patch, s_head]
        turned = [x.T if n // 3 == 3 else x for n, x in enumerate(state)]
        news = simple_call(
            update_kernel,
            [stats] + shares + turned,
            tuple([sds((1, 1), f32), sds((1, NB), f32)] + [sds(s.shape, f32) for s in turned]),
            6,
        )
        outs = [x.T if n // 3 == 3 else x for n, x in enumerate(news[2:])]
        return (news[1].reshape(NB), counts, news[0].reshape(())) + tuple(outs)

    return local


def solution(mesh):
    shard = {
        "in": P("dp", "mp"),
        "out": P("mp", "dp"),
        "row": P("dp", None),
        "col": P(None, "dp"),
    }
    kinds = ["in", "out", "in", "out", "row", "col", "row", "col", "col"]
    triples = tuple(shard[k] for k in kinds for _ in range(3))
    in_specs = (P("dp", None),) + (P("dp"),) * 6 + triples
    out_specs = (P(), P(), P()) + triples
    return jax.shard_map(
        make_local(mesh.shape["dp"], mesh.shape["mp"]),
        mesh=mesh,
        in_specs=in_specs,
        out_specs=out_specs,
        check_vma=False,
    )
```
